32 devices in a mesh: dp: 8 (over z, core), tensor: 4 (over y, x).
Axes of the slice: x: 2, y: 2, z: 4, core: 2. Of those that a mesh axis runs over, the one named last changes fastest.
Arguments:
- tokens: bfloat16 [16, 2048, 1280], P('dp', 'tensor'), may hold values from -6 to 6
- segments: int32 [16, 2048], P('dp'), may hold values from 0 to 255, as said below
- attn_gain: float32 [1280], replicated, may hold values from 0.1 to 1.9
- w_query: bfloat16 [1280, 1280], P('dp', 'tensor'), may hold values from -0.15625 to 0.15625
- w_key: bfloat16 [1280, 1280], P('dp', 'tensor'), may hold values from -0.15625 to 0.15625
- w_value: bfloat16 [1280, 1280], P('dp', 'tensor'), may hold values from -0.15625 to 0.15625
- w_out: bfloat16 [1280, 1280], P('tensor', 'dp'), may hold values from -1 to 1
- query_scale: float32 [80], replicated, may hold values from 0 to 1.5
- mlp_gain: float32 [1280], replicated, may hold values from 0.1 to 1.9
- w_up: bfloat16 [1280, 1280], P('dp', 'tensor'), may hold values from -0.15625 to 0.15625
- w_down: bfloat16 [1280, 1280], P('tensor', 'dp'), may hold values from -0.15625 to 0.15625
- cotangent: bfloat16 [16, 2048, 1280], P('dp', 'tensor'), may hold values from -6 to 6
Outputs:
- block_out: bfloat16 [16, 2048, 1280], P('dp', 'tensor')
- input_grad: float32 [16, 2048, 1280], P('dp', 'tensor')
- grad_attn_gain: float32 [1280], replicated
- grad_query: float32 [1280, 1280], P('dp', 'tensor')
- grad_key: float32 [1280, 1280], P('dp', 'tensor')
- grad_value: float32 [1280, 1280], P('dp', 'tensor')
- grad_out: float32 [1280, 1280], P('tensor', 'dp')
- grad_query_scale: float32 [80], replicated
- grad_mlp_gain: float32 [1280], replicated
- grad_up: float32 [1280, 1280], P('dp', 'tensor')
- grad_down: float32 [1280, 1280], P('tensor', 'dp')
The draws below stay inside these ranges and needn't reach their ends.
Inputs may be any that keep to these rules, and one draw needn't show every extreme that they name: `segments`: each row holds the document numbers of one sequence: they start at 0, never fall and rise by at most 1 from one position to the next. In every aligned group of 2 rows (the sequences of one index of dp) one row is a single document.
All inputs are finite; a program needn't handle non-finite values.
Results may differ from the reference program's by a relative error of at most 0.012.
The reference program's roundings to bfloat16 on the way count: a program that leaves them out, or rounds other values in their place, can miss the bound.
Values may be sent and summed in bfloat16 or wider, within the bound.
A program may use at most 320 MiB of HBM per device.

```python
import math
import jax
import jax.numpy as jnp
from jax import lax

D = 1280
H = 16
HD = 80
FF = 1280
SEQ_LEN = 2048
SEQ_DEV = 2
NSEQ = 16


def draw_segments(key, part):
    key = jax.random.fold_in(key, 11)
    rate_key, flag_key, pick_key = jax.random.split(key, 3)
    rate_pick = jax.random.randint(rate_key, (NSEQ, 1), 0, 4)
    period = jnp.left_shift(jnp.int32(8), 2 * rate_pick)
    raw_bits = jax.random.randint(flag_key, (NSEQ, SEQ_LEN), 0, 1 << 20)
    start_flags = (raw_bits % period == 0).astype(jnp.int32)
    single_pick = jax.random.randint(pick_key, (NSEQ // SEQ_DEV, 1), 0, SEQ_DEV)
    row_place = (jnp.arange(NSEQ) % SEQ_DEV).reshape(NSEQ // SEQ_DEV, SEQ_DEV)
    single_rows = (row_place == single_pick).reshape(NSEQ, 1)
    dense_place = (single_pick[0, 0] + 1) % SEQ_DEV
    dense_rows = (jnp.arange(NSEQ) == dense_place).reshape(NSEQ, 1)
    eighth_cols = (jnp.arange(SEQ_LEN) % 8 == 0).astype(jnp.int32)[None, :]
    start_flags = jnp.where(dense_rows, jnp.maximum(start_flags, eighth_cols), start_flags)
    later_cols = (jnp.arange(SEQ_LEN) > 0).astype(jnp.int32)[None, :]
    start_flags = jnp.where(single_rows, 0, start_flags) * later_cols
    counted = jnp.cumsum(start_flags, axis=1)
    return jnp.minimum(counted, SEQ_LEN // 8 - 1).astype(jnp.int32)


def strengthened(values, own_key, source, target, shards_of, factor):
    def block_of(dim):
        return (jnp.arange(values.shape[dim]) // (values.shape[dim] // shards_of)).reshape((-1,) + (1,) * (values.ndim - 1 - dim))

    one_side = jax.random.permutation(own_key, shards_of)[block_of(target)]
    other_side = (block_of(target) + shards_of // 2) % shards_of
    return jnp.where((block_of(source) == one_side) | (block_of(source) == other_side), factor * values, values)


def shard_levels(rng, shape, cuts, least, top_value):
    level, own = 1.0, jax.random.fold_in(rng, 6)
    for dim, blocks in cuts:
        steps = jnp.exp(jax.random.uniform(jax.random.fold_in(own, dim), (blocks,), jnp.float32, least / len(cuts), top_value / len(cuts)))
        level = level * jnp.repeat(steps, shape[dim] // blocks).reshape([-1 if axis == dim else 1 for axis in range(len(shape))])
    return level


def bell_draw(rng, shape, width, most, cuts=(), held_as=jnp.bfloat16):
    values = jax.random.normal(rng, shape, jnp.float32) * width
    if len(cuts) > 0:
        values = shard_levels(rng, shape, cuts, -0.22, 0.18) * values
    return jnp.clip(values, min=-most, max=most).astype(held_as)


def noise_with(own_key, extent, scale, limit, cuts, heavy, held_as=jnp.bfloat16):
    entries = scale * jax.random.normal(own_key, extent, jnp.float32)
    if cuts:
        entries = entries * shard_levels(own_key, extent, cuts, -0.22, 0.18)
    return jnp.clip(strengthened(entries, jax.random.fold_in(own_key, 3), *heavy), -limit, limit).astype(held_as)


def setup_inputs(seed: int = 0) -> dict:
    seeds = jax.random.split(jax.random.key(seed), 13)
    return {
        "tokens": bell_draw(seeds[0], (NSEQ, SEQ_LEN, D), 1.0, 6.0, ((0, 8), (1, 4))),
        "segments": draw_segments(jax.random.fold_in(seeds[12], 71), 0),
        "attn_gain": jnp.clip(1.0 + 0.18 * jax.random.normal(seeds[2], (D,), jnp.float32), 0.1, 1.9),
        "w_query": bell_draw(seeds[3], (D, H * HD), D ** -0.5, 0.15625, ((0, 8), (1, 4))),
        "w_key": bell_draw(seeds[4], (D, H * HD), D ** -0.5, 0.15625, ((0, 8), (1, 4))),
        "w_value": bell_draw(seeds[5], (D, H * HD), D ** -0.5, 0.15625, ((0, 8), (1, 4))),
        "w_out": bell_draw(seeds[6], (H * HD, D), (H * HD // 32) ** -0.5, 1.0, ((0, 4), (1, 8))),
        "query_scale": jnp.clip(jax.random.uniform(seeds[7], (HD,), jnp.float32, 0.0, 1.5), 0.0, 1.5),
        "mlp_gain": jnp.clip(1.0 + 0.18 * jax.random.normal(seeds[8], (D,), jnp.float32), 0.1, 1.9),
        "w_up": bell_draw(seeds[9], (D, FF), D ** -0.5, 0.15625, ((0, 8), (1, 4))),
        "w_down": bell_draw(seeds[10], (FF, D), FF ** -0.5, 0.15625, ((0, 4), (1, 8))),
        "cotangent": noise_with(seeds[11], (NSEQ, SEQ_LEN, D), 1.0, 6.0, ((0, 8), (1, 4)), (0, 2, 8, 2.0)),
    }


@jax.custom_vjp
def low(v):
    return lax.optimization_barrier(v.astype(jnp.bfloat16)).astype(jnp.float32)

@jax.custom_vjp
def low_back(v):
    return v

def low_keep(v):
    return (low(v), None)

def low_pass(kept, grad):
    return (grad,)

def back_keep(v):
    return (v, None)

def back_low(kept, grad):
    return (low(grad),)
low.defvjp(low_keep, low_pass)
low_back.defvjp(back_keep, back_low)
norm_eps = 1e-06
scale_base = 1.442695041
masked_fill = -1e+30
highest = lax.Precision.HIGHEST

def rms_normed(source, gain_vec):
    inverse = lax.rsqrt(lax.optimization_barrier(jnp.mean(source * source, axis=-1, keepdims=True)) + norm_eps)
    return source * inverse * gain_vec

def attend_one(pieces):
    query_rows, key_rows, value_rows, seg_row = pieces
    scores = low_back(jnp.dot(query_rows, key_rows.T, precision=highest))
    places = jnp.arange(SEQ_LEN)
    allowed = (seg_row[:, None] == seg_row[None, :]) & (places[:, None] >= places[None, :])
    masked = jnp.where(allowed, scores, masked_fill)
    row_top = lax.optimization_barrier(jnp.max(masked, axis=-1, keepdims=True))
    weights = jnp.exp(masked - row_top)
    probs = low(weights / lax.optimization_barrier(jnp.sum(weights, axis=-1, keepdims=True)))
    return jnp.dot(probs, value_rows, precision=highest)

def by_head(source):
    return source.reshape(NSEQ, SEQ_LEN, H, HD).transpose(0, 2, 1, 3).reshape(NSEQ * H, SEQ_LEN, HD)

def layer(inputs, attn_gain, w_query, w_key, w_value, w_out, query_scale, mlp_gain, w_up, w_down, segments):
    flat_in = inputs.reshape(NSEQ * SEQ_LEN, D)
    attn_in = low(rms_normed(flat_in, attn_gain))
    queries = low_back(jnp.dot(attn_in, w_query, precision=highest))
    keys_r = low(low_back(jnp.dot(attn_in, w_key, precision=highest)))
    values_r = low(low_back(jnp.dot(attn_in, w_value, precision=highest)))
    per_dim = scale_base / math.sqrt(HD) * jax.nn.softplus(query_scale)
    scaled = low((queries.reshape(-1, H, HD) * per_dim).reshape(-1, H * HD))
    seg_rows = jnp.repeat(segments, H, axis=0)
    heads_out = lax.map(jax.checkpoint(attend_one), (by_head(scaled), by_head(keys_r), by_head(values_r), seg_rows))
    merged = heads_out.reshape(NSEQ, H, SEQ_LEN, HD).transpose(0, 2, 1, 3).reshape(NSEQ * SEQ_LEN, H * HD)
    mixed = low(low_back(merged))
    attn = low_back(jnp.dot(mixed, w_out, precision=highest))
    middle = flat_in + attn
    mlp_in = low(rms_normed(middle, mlp_gain))
    up_proj = low_back(jnp.dot(mlp_in, w_up, precision=highest))
    hidden = low(jax.nn.silu(up_proj))
    branch = low_back(jnp.dot(hidden, w_down, precision=highest))
    return (middle + branch).reshape(NSEQ, SEQ_LEN, D)

def reference(tokens, segments, attn_gain, w_query, w_key, w_value, w_out, query_scale, mlp_gain, w_up, w_down, cotangent):
    floats = [source.astype(jnp.float32) for source in (tokens, attn_gain, w_query, w_key, w_value, w_out, query_scale, mlp_gain, w_up, w_down)]

    def forward(inputs, gain_one, query_w, key_w, value_w, out_w, scale_param, gain_two, up_w, down_w):
        return layer(inputs, gain_one, query_w, key_w, value_w, out_w, scale_param, gain_two, up_w, down_w, segments)
    output, pullback = jax.vjp(forward, *floats)
    gradients = pullback(cotangent.astype(jnp.float32))
    return (output.astype(jnp.bfloat16), gradients[0], gradients[1], gradients[2], gradients[3], gradients[4], gradients[5], gradients[6], gradients[7], gradients[8], gradients[9])
```

```python
import math, functools
import jax, jax.numpy as jnp
from jax import lax
from jax.experimental import pallas as pl
from jax.experimental.pallas import tpu as pltpu
HD=80
BQ=256
NEG=-1e30
f32=jnp.float32; bf16=jnp.bfloat16
NT=(((1,),(1,)),((),()))
NN=(((1,),(0,)),((),()))
TN=(((0,),(0,)),((),()))
def dot(a,b,dims=NN): return lax.dot_general(a,b,dims,preferred_element_type=f32)

def merge(*gens):
    gens=list(gens)
    while gens:
        for g in list(gens):
            try: next(g)
            except StopIteration: gens.remove(g)

def fwd_kernel(hb, first_ref, last_ref, x_ref, wt_ref, pd_ref, segk_ref, segq_ref,
               qt_ref, kt_ref, k_ref, v_ref, ot_ref, lse_ref, vt_scr, s_scr, m_scr, l_scr, acc_scr):
    L=x_ref.shape[0]; nb=L//BQ; W=hb*HD
    CH=512
    for c in range(L//CH):
        cs=slice(c*CH,(c+1)*CH)
        r=dot(wt_ref[...],x_ref[cs,:],NT)
        qt_ref[:,cs]=(r[:W]*pd_ref[:,:1]).astype(bf16)
        kt_ref[:,cs]=r[W:2*W].astype(bf16)
        vt_scr[:,cs]=r[2*W:].astype(bf16)
        for h in range(hb):
            k_ref[h,cs,:]=r[W+h*HD:W+(h+1)*HD].T.astype(bf16)
            v_ref[h,cs,:]=r[2*W+h*HD:2*W+(h+1)*HD].T.astype(bf16)
    rowi=lax.broadcasted_iota(jnp.int32,(BQ,BQ),0)
    coli=lax.broadcasted_iota(jnp.int32,(BQ,BQ),1)
    hs=[slice(h*HD,(h+1)*HD) for h in range(hb)]
    single = first_ref[0]==last_ref[nb-1]
    @pl.when(single)
    def _():
        units=[(i,h) for i in range(nb) for h in range(hb)]
        st={}
        def phase_a(u):
            i,h=units[u]; c0=i*BQ
            qi=qt_ref[hs[h],c0:c0+BQ]
            m8=None
            for j in range(i+1):
                s=dot(k_ref[h,j*BQ:(j+1)*BQ,:],qi)
                if j==i: s=jnp.where(rowi<=coli,s,NEG)
                s_scr[u%2,j*BQ:(j+1)*BQ,:]=s
                mm=s.reshape(BQ//8,8,BQ).max(0)
                m8=mm if m8 is None else jnp.maximum(m8,mm)
                yield
            st[u]=m8.max(0,keepdims=True)
        def phase_b(u):
            i,h=units[u]; c0=i*BQ
            m=st[u]; l8=None; acc=None
            for j in range(i+1):
                p=jnp.exp(s_scr[u%2,j*BQ:(j+1)*BQ,:]-m)
                ll=p.reshape(BQ//8,8,BQ).sum(0)
                l8=ll if l8 is None else l8+ll
                pv=dot(vt_scr[hs[h],j*BQ:(j+1)*BQ],p.astype(bf16))
                acc=pv if acc is None else acc+pv
                yield
            l=l8.sum(0,keepdims=True)
            ot_ref[hs[h],c0:c0+BQ]=(acc*(1.0/l)).astype(bf16)
            lse_ref[h,:,c0:c0+BQ]=m+jnp.log(l)
        merge(phase_a(0))
        for u in range(len(units)):
            gs=[phase_b(u)]
            if u+1<len(units): gs=[phase_a(u+1)]+gs
            merge(*gs)
    @pl.when(jnp.logical_not(single))
    def _():
        def qblock(i,_):
            c0=pl.multiple_of(i*BQ,BQ)
            def cnt(j,a): return a+jnp.where(last_ref[j]<first_ref[i],1,0)
            j0=lax.fori_loop(0,i,cnt,jnp.int32(0))
            m_scr[...]=jnp.full_like(m_scr,NEG); l_scr[...]=jnp.zeros_like(l_scr); acc_scr[...]=jnp.zeros_like(acc_scr)
            def step(j,_):
                r0=pl.multiple_of(j*BQ,BQ)
                sk=segk_ref[pl.ds(r0,BQ),:]
                ok=(jnp.concatenate([sk]*(BQ//128),axis=1)==segq_ref[:,pl.ds(c0,BQ)])&(rowi+r0<=coli+c0)
                for h in range(hb):
                    s=dot(k_ref[h,pl.ds(r0,BQ),:],qt_ref[hs[h],pl.ds(c0,BQ)])
                    s=jnp.where(ok,s,NEG)
                    mo=m_scr[h]
                    m=jnp.maximum(mo,s.max(0,keepdims=True))
                    al=jnp.exp(mo-m)
                    p=jnp.where(ok,jnp.exp(s-m),0.0)
                    l_scr[h]=l_scr[h]*al+p.sum(0,keepdims=True)
                    acc_scr[hs[h],:]=acc_scr[hs[h],:]*al+dot(vt_scr[hs[h],pl.ds(r0,BQ)],p.astype(bf16))
                    m_scr[h]=m
                return 0
            lax.fori_loop(j0,i+1,step,0)
            for h in range(hb):
                ot_ref[hs[h],pl.ds(c0,BQ)]=(acc_scr[hs[h],:]*(1.0/l_scr[h])).astype(bf16)
                lse_ref[h,:,pl.ds(c0,BQ)]=m_scr[h]+jnp.log(l_scr[h])
            return 0
        lax.fori_loop(0,nb,qblock,0)

def attn_fwd(first,last,x,wt,pd,segk,segq):
    L,D=x.shape; W=wt.shape[0]//3; hb=W//HD
    V=pl.BlockSpec(memory_space=pltpu.VMEM); S=pl.BlockSpec(memory_space=pltpu.SMEM)
    hd=jax.ShapeDtypeStruct((hb,L,HD),bf16); td=jax.ShapeDtypeStruct((W,L),bf16)
    flops=2*L*D*3*W+2*2*L*L//2*256*hb
    return pl.pallas_call(functools.partial(fwd_kernel,hb),
        out_shape=(td,td,hd,hd,td,jax.ShapeDtypeStruct((hb,1,L),f32)),
        in_specs=[S,S,V,V,V,V,V],out_specs=(V,)*6,
        scratch_shapes=[pltpu.VMEM((W,L),bf16),pltpu.VMEM((2,L,BQ),f32),
            pltpu.VMEM((hb,1,BQ),f32),pltpu.VMEM((hb,1,BQ),f32),pltpu.VMEM((W,BQ),f32)],
        compiler_params=pltpu.CompilerParams(vmem_limit_bytes=56*2**20),
        cost_estimate=pl.CostEstimate(flops=flops,bytes_accessed=x.size*2+wt.size*2+4*L*W*2,transcendentals=L*L//2*hb),
        name="attn_fwd")(first,last,x,wt,pd,segk,segq)

def bwd_kernel(hb, first_ref, last_ref, qt_ref, kt_ref, k_ref, v_ref, ot_ref, dot_ref, lse_ref, pd_ref, segk_ref, segq_ref,
               g_ref, sc_ref, p_scr, ds_scr, dq_scr, dl_scr, dv_scr, dk_scr):
    W=hb*HD; L=qt_ref.shape[1]; nb=L//BQ
    rowi=lax.broadcasted_iota(jnp.int32,(BQ,BQ),0)
    coli=lax.broadcasted_iota(jnp.int32,(BQ,BQ),1)
    hs=[slice(h*HD,(h+1)*HD) for h in range(hb)]
    for h in range(hb):
        dl_scr[h]=(dot_ref[hs[h],:].astype(f32)*ot_ref[hs[h],:].astype(f32)).sum(0,keepdims=True)
    single = first_ref[0]==last_ref[nb-1]
    @pl.when(single)
    def _():
        units=[(j,h,i) for j in range(nb) for h in range(hb) for i in range(j,nb)]
        acc={}
        def phase_a(u):
            j,h,i=units[u]; js=slice(j*BQ,(j+1)*BQ); cs=slice(i*BQ,(i+1)*BQ)
            H2=BQ//2
            for a in range(2):
                ks=slice(j*BQ+a*H2,j*BQ+(a+1)*H2)
                s=dot(k_ref[h,ks,:],qt_ref[hs[h],cs])
                dp=dot(v_ref[h,ks,:],dot_ref[hs[h],cs])
                if j==i: s=jnp.where(rowi[a*H2:(a+1)*H2]<=coli[a*H2:(a+1)*H2],s,NEG)
                p=jnp.exp(s-lse_ref[h,:,cs])
                p_scr[u%2,a*H2:(a+1)*H2,:]=p.astype(bf16)
                ds_scr[u%2,a*H2:(a+1)*H2,:]=(p*(dp-dl_scr[h,:,cs])).astype(bf16)
                yield
        def phase_b(u):
            j,h,i=units[u]; js=slice(j*BQ,(j+1)*BQ); cs=slice(i*BQ,(i+1)*BQ)
            p=p_scr[u%2]; ds=ds_scr[u%2]
            dv=dot(dot_ref[hs[h],cs],p,NT); dk=dot(qt_ref[hs[h],cs],ds,NT)
            if i==j: dv_scr[h]=dv; dk_scr[h]=dk
            else: dv_scr[h]+=dv; dk_scr[h]+=dk
            yield
            dq=dot(kt_ref[hs[h],js],ds)
            if j==0: dq_scr[hs[h],cs]=dq
            else: dq_scr[hs[h],cs]+=dq
            if i==nb-1:
                g_ref[W+h*HD:W+(h+1)*HD,js]=dk_scr[h].astype(bf16)
                g_ref[2*W+h*HD:2*W+(h+1)*HD,js]=dv_scr[h].astype(bf16)
            yield
        merge(phase_a(0))
        for u in range(len(units)):
            gs=[phase_b(u)]
            if u+1<len(units): gs=[phase_a(u+1)]+gs
            merge(*gs)
    @pl.when(jnp.logical_not(single))
    def _():
        dq_scr[...]=jnp.zeros_like(dq_scr)
        def kblock(j,_):
            r0=pl.multiple_of(j*BQ,BQ)
            def cnt(i,a): return a+jnp.where(first_ref[i]<=last_ref[j],1,0)
            iend=lax.fori_loop(j,nb,cnt,j)
            dv_scr[...]=jnp.zeros_like(dv_scr); dk_scr[...]=jnp.zeros_like(dk_scr)
            sk=segk_ref[pl.ds(r0,BQ),:]
            sk=jnp.concatenate([sk]*(BQ//128),axis=1)
            def step(i,_):
                c0=pl.multiple_of(i*BQ,BQ); cs=pl.ds(c0,BQ)
                ok=(sk==segq_ref[:,cs])&(rowi+r0<=coli+c0)
                for h in range(hb):
                    qt=qt_ref[hs[h],cs]; do=dot_ref[hs[h],cs]
                    s=dot(k_ref[h,pl.ds(r0,BQ),:],qt)
                    dp=dot(v_ref[h,pl.ds(r0,BQ),:],do)
                    p=jnp.exp(jnp.where(ok,s-lse_ref[h,:,cs],NEG))
                    ds=(p*(dp-dl_scr[h,:,cs])).astype(bf16)
                    dv_scr[h]+=dot(do,p.astype(bf16),NT)
                    dk_scr[h]+=dot(qt,ds,NT)
                    dq_scr[hs[h],cs]+=dot(kt_ref[hs[h],pl.ds(r0,BQ)],ds)
                return 0
            lax.fori_loop(j,iend,step,0)
            for h in range(hb):
                g_ref[W+h*HD:W+(h+1)*HD,pl.ds(r0,BQ)]=dk_scr[h].astype(bf16)
                g_ref[2*W+h*HD:2*W+(h+1)*HD,pl.ds(r0,BQ)]=dv_scr[h].astype(bf16)
            return 0
        lax.fori_loop(0,nb,kblock,0)
    dq=dq_scr[...]
    g_ref[:W,:]=(dq*pd_ref[:,:1]).astype(bf16)
    sc=(dq*qt_ref[...].astype(f32)).sum(1,keepdims=True)
    sc_ref[...]=jnp.broadcast_to(sc/pd_ref[:,:1],sc_ref.shape)

def attn_bwd(first,last,qt,kt,k,v,ot,dot_,lse,pd,segk,segq):
    W,L=qt.shape; hb=W//HD
    V=pl.BlockSpec(memory_space=pltpu.VMEM); S=pl.BlockSpec(memory_space=pltpu.SMEM)
    flops=5*2*L*L//2*256*hb
    return pl.pallas_call(functools.partial(bwd_kernel,hb),
        out_shape=(jax.ShapeDtypeStruct((3*W,L),bf16),jax.ShapeDtypeStruct((W,128),f32)),
        in_specs=[S,S]+[V]*10,out_specs=(V,)*2,
        scratch_shapes=[pltpu.VMEM((2,BQ,BQ),bf16),pltpu.VMEM((2,BQ,BQ),bf16),pltpu.VMEM((W,L),f32),
            pltpu.VMEM((hb,1,L),f32),pltpu.VMEM((hb,HD,BQ),f32),pltpu.VMEM((hb,HD,BQ),f32)],
        compiler_params=pltpu.CompilerParams(vmem_limit_bytes=56*2**20),
        cost_estimate=pl.CostEstimate(flops=flops,bytes_accessed=8*L*W*2,transcendentals=L*L//2*hb),
        name="attn_bwd")(first,last,qt,kt,k,v,ot,dot_,lse,pd,segk,segq)


import itertools
from jax.sharding import Mesh, PartitionSpec as P

AXES=("zz","core","q","s")
norm_eps = 1e-06
scale_base = 1.442695041

def silu_slope(u):
    sg=jax.nn.sigmoid(u)
    return sg*(1.0+u*(1.0-sg))

def make_local(Z, C):
    sizes=(Z,2,4,C)
    coords=list(itertools.product(*[range(n) for n in sizes]))
    lin={c:i for i,c in enumerate(coords)}
    G=2*C
    def pp(x, fn):
        return lax.ppermute(x, AXES, [(lin[c], lin[fn(*c)]) for c in coords])
    def unxor(parts, idx):
        b=1
        while b<len(parts):
            c=(idx & b)!=0
            parts=[jnp.where(c,parts[a^b],parts[a]) for a in range(len(parts))]
            b*=2
        return parts
    def allsum(v):
        for ax,n in enumerate(sizes):
            b=1
            while b<n:
                v=v+pp(v,lambda *c,ax=ax,b=b: tuple(ci^b if i==ax else ci for i,ci in enumerate(c)))
                b*=2
        return v
    def gsend(x, gamma):
        gc,gs=divmod(gamma,C)
        return pp(x, lambda z,k,q,s: (z,k^gc,q,s^gs))

    def local(tokens, segments, attn_gain, w_query, w_key, w_value, w_out, query_scale, mlp_gain, w_up, w_down, cotangent):
        zi,k,qi,si=[lax.axis_index(a) for a in AXES]
        R,Pn,D=tokens.shape; L=segments.shape[1]
        n=Pn//G
        N=4*C*n
        Dd,Ct=w_query.shape; Ch=Ct//2; W=Ch; hb=W//HD
        g0=k*C+si
        k0=k==0
        q0=2*(k^(qi//2))+qi%2
        rounds=list(itertools.product(range(2),range(2),range(C)))

        def spread(x):
            got=[]
            for eta,rho,sg in rounds:
                r=(qi%2)^rho; h=(qi//2)^k^eta; s2=si^sg
                piece=lax.dynamic_slice(x,(r,(h*C+s2)*n,0),(1,n,D))[0]
                got.append(pp(piece, lambda z,kk,q,s: (z,(q//2)^kk^eta,2*kk+((q%2)^rho),s^sg)))
            return jnp.concatenate(unxor(got,q0*C+si),0)
        def collect(y):
            parts=unxor([y[i*n:(i+1)*n] for i in range(4*C)],q0*C+si)
            got=[]
            for idx,(eta,rho,sg) in enumerate(rounds):
                got.append(pp(parts[idx], lambda z,kk,q,s: (z,q//2,(2*(kk^(q//2))+q%2)^(2*eta+rho),s^sg)))
            ab=unxor(got,((qi//2)^k)*(2*C)+(qi%2)*C+si)
            rows=[jnp.concatenate([ab[(h*2+r)*C+s2] for h in range(2) for s2 in range(C)],0) for r in range(R)]
            return jnp.stack(rows,0)
        def gatherD(shards):
            lo=jnp.concatenate([w[:,:Ch] for w in shards],1); hi=jnp.concatenate([w[:,Ch:] for w in shards],1)
            keep=jnp.where(k0,lo,hi); send=jnp.where(k0,hi,lo)
            recv=pp(send,lambda z,kk,q,s:(z,1-kk,q,s))
            rows=jnp.concatenate([jnp.where(k0,keep,recv),jnp.where(k0,recv,keep)],0)
            parts=[rows]+[pp(rows,lambda z,kk,q,s:(z^j,kk,q,s)) for j in range(1,Z)]
            full=jnp.concatenate(unxor(parts,zi),0)
            return full.T
        def gatherQ(block):
            return [block]+[pp(block,lambda z,kk,q,s:(z,kk,q^m,s)) for m in range(1,4)]
        def reduceD(acc, recvs, nw):
            for t in recvs: acc=acc+t.astype(f32)
            a=acc.astype(bf16).T
            rel=unxor([a[z*2*Dd:(z+1)*2*Dd] for z in range(Z)],zi)
            tot=rel[0].astype(f32)
            for j in range(1,Z):
                tot=tot+pp(rel[j],lambda z,kk,q,s:(z^j,kk,q,s)).astype(f32)
            keep=jnp.where(k0,tot[:Dd],tot[Dd:]); send=jnp.where(k0,tot[Dd:],tot[:Dd])
            recv=pp(send,lambda z,kk,q,s:(z,1-kk,q,s))
            lo=jnp.where(k0,keep,recv); hi=jnp.where(k0,recv,keep)
            return [jnp.concatenate([lo[:,i*Ch:(i+1)*Ch],hi[:,i*Ch:(i+1)*Ch]],1) for i in range(nw)]
        def tok_lanes(xT):
            return [jnp.concatenate([xT[:,(b*G+g)*n:(b*G+g+1)*n] for b in range(4*C)],1) for g in range(G)]
        def tok_rows_join(parts):
            return jnp.concatenate([parts[g][b*n:(b+1)*n] for b in range(4*C) for g in range(G)],0)
        def tok_lanes_join(parts):
            return jnp.concatenate([parts[g][:,b*n:(b+1)*n] for b in range(4*C) for g in range(G)],1)

        x_b=spread(tokens)
        wt0=gatherD([w_query,w_key,w_value])
        wts=gatherQ(wt0)
        seg_o=pp(segments,lambda z,kk,q,s:(z,1-kk,q,s))
        seg2=jnp.where(k==qi//2,segments,seg_o)
        seg=jnp.where(qi%2==0,seg2[0],seg2[1])
        first=seg[::BQ]; last=seg[BQ-1::BQ]
        segk=jnp.broadcast_to(seg[:,None],(L,128)); segq=seg[None]
        x=x_b.astype(f32)
        inv1=lax.rsqrt(jnp.mean(x*x,axis=-1,keepdims=True)+norm_eps)
        ain_own=(x*inv1*attn_gain).astype(bf16)
        ain=tok_rows_join(unxor([ain_own]+[gsend(ain_own,g) for g in range(1,G)],g0))
        per_dim=scale_base/math.sqrt(HD)*jax.nn.softplus(query_scale)
        pd=jnp.broadcast_to(jnp.tile(per_dim,hb)[:,None],(W,128))

        saved=[]
        for m in range(4):
            saved.append(attn_fwd(first,last,ain,wts[m],pd,segk,segq))
        mixT=jnp.concatenate([sv[4] for sv in saved],0)
        rel=unxor(tok_lanes(mixT),g0)
        mixT_own=jnp.concatenate([rel[0]]+[gsend(rel[g],g) for g in range(1,G)],0)

        w3=gatherQ(gatherD([w_out.T,w_up,w_down.T]))
        def whole(i):
            mine=jnp.concatenate([w3[m][i*Ch:(i+1)*Ch] for m in range(4)],0)
            return jnp.concatenate([mine]+[gsend(mine,g) for g in range(1,G)],0)
        wo,wu,wd=whole(0),whole(1),whole(2)
        cot=spread(cotangent)

        attn=dot(mixT_own,wo,TN)
        middle=x+attn
        inv2=lax.rsqrt(jnp.mean(middle*middle,axis=-1,keepdims=True)+norm_eps)
        norm2=middle*inv2
        mlp_in=(norm2*mlp_gain).astype(bf16)
        up=dot(mlp_in,wu,NT)
        hid=jax.nn.silu(up).astype(bf16)
        block=(middle+dot(hid,wd)).astype(bf16)
        block_out=collect(block)
        gup=(dot(cot,wd,NT)*silu_slope(up)).astype(bf16)
        gmlp=dot(gup,wu)
        dn=gmlp*mlp_gain
        gmid=cot.astype(f32)+inv2*(dn-norm2*jnp.mean(dn*norm2,axis=-1,keepdims=True))
        mlp_gain_part=jnp.sum(gmlp*norm2,axis=0)
        gattn=gmid.astype(bf16)
        gmixT=dot(wo,gattn,NT).astype(bf16)
        K=gmixT.shape[0]//G
        doT=tok_lanes_join(unxor([gmixT[:K]]+[gsend(gmixT[g*K:(g+1)*K],g) for g in range(1,G)],g0))
        g3=[dot(mixT_own,gattn),dot(gup,mlp_in,TN),dot(hid,cot,TN)]

        def fold(gs):
            K4=4*Ch
            mine=[t[:K4] for t in gs]
            for g in range(1,G):
                for i,t in enumerate(gs):
                    mine[i]=mine[i]+gsend(t[g*K4:(g+1)*K4].astype(bf16),g).astype(f32)
            blocks=[jnp.concatenate([t[m*Ch:(m+1)*Ch] for t in mine],0) for m in range(4)]
            recvs=[pp(blocks[m].astype(bf16),lambda z,kk,q,s:(z,kk,q^m,s)) for m in range(1,4)]
            return reduceD(blocks[0],recvs,len(gs))
        g_out,g_up,g_down=fold(g3)
        grad_out=g_out.T; grad_up=g_up; grad_down=g_down.T

        gT=[None]*4; dW=[None]*4; sc=0.0
        for m in (3,2,1,0):
            qt,kt,kn,vn,ot,lse=saved[m]
            gT[m],s_=attn_bwd(first,last,qt,kt,kn,vn,ot,doT[m*W:(m+1)*W],lse,pd,segk,segq)
            sc=sc+s_[:,0]
            dW[m]=dot(gT[m],ain)
        recvs=[pp(dW[m].astype(bf16),lambda z,kk,q,s:(z,kk,q^m,s)) for m in range(1,4)]
        grad_query,grad_key,grad_value=reduceD(dW[0],recvs,3)
        gTall=jnp.concatenate(gT,0); wtall=jnp.concatenate(wts,0)
        grel=unxor(tok_lanes(gTall),g0)
        gain=0.0
        for g in range(1,G):
            gain=gain+gsend(dot(grel[g],wtall,TN).astype(bf16),g).astype(f32)
        gain=gain+dot(grel[0],wtall,TN)
        norm1=x*inv1
        dn1=gain*attn_gain
        gin=gmid+inv1*(dn1-norm1*jnp.mean(dn1*norm1,axis=-1,keepdims=True))
        attn_gain_part=jnp.sum(gain*norm1,axis=0)
        input_grad=collect(gin.astype(bf16)).astype(f32)

        scale_part=jnp.sum(sc.reshape(hb,HD),axis=0)*(scale_base/math.sqrt(HD))*jax.nn.sigmoid(query_scale)
        grad_mlp_gain=allsum(mlp_gain_part)
        late=allsum(jnp.concatenate([attn_gain_part,scale_part]))
        return (block_out,input_grad,late[:D],grad_query,grad_key,grad_value,grad_out,late[D:],grad_mlp_gain,grad_up,grad_down)
    return local

def solution(mesh):
    dp,T=mesh.shape["dp"],mesh.shape["tensor"]
    Z,C=dp//2,T//4
    fine=Mesh(mesh.devices.reshape(Z,2,4,C),AXES)
    dpx=("zz","core"); tx=("q","s")
    in_specs=(P(dpx,tx,None),P(dpx,None),P(),P(dpx,tx),P(dpx,tx),P(dpx,tx),P(tx,dpx),P(),P(),P(dpx,tx),P(tx,dpx),P(dpx,tx,None))
    out_specs=(P(dpx,tx,None),P(dpx,tx,None),P(),P(dpx,tx),P(dpx,tx),P(dpx,tx),P(tx,dpx),P(),P(),P(dpx,tx),P(tx,dpx))
    return jax.shard_map(make_local(Z,C),mesh=fine,in_specs=in_specs,out_specs=out_specs,check_vma=False)
```

```python
import functools
import itertools
import math
import jax, jax.numpy as jnp
from jax import lax
from jax.experimental import pallas as pl
from jax.experimental.pallas import tpu as pltpu
from jax.sharding import Mesh, PartitionSpec as P

AXES=("zz","core","q","s")
norm_eps = 1e-06
HD=80
BQ=256
NEG=-1e30
f32=jnp.float32; bf16=jnp.bfloat16
NT=(((1,),(1,)),((),()))
NN=(((1,),(0,)),((),()))
TN=(((0,),(0,)),((),()))
def dot(a,b,dims=NN): return lax.dot_general(a,b,dims,preferred_element_type=f32)

def merge(*gens):
    gens=list(gens)
    while gens:
        for g in list(gens):
            try: next(g)
            except StopIteration: gens.remove(g)

def fwd_kernel(hb, first_ref, last_ref, x_ref, wt_ref, pd_ref, segk_ref, segq_ref,
               qt_ref, kt_ref, k_ref, v_ref, ot_ref, lse_ref, vt_scr, s_scr, m_scr, l_scr, acc_scr):
    L=x_ref.shape[0]; nb=L//BQ; W=hb*HD
    CH=512
    for c in range(L//CH):
        cs=slice(c*CH,(c+1)*CH)
        r=dot(wt_ref[...],x_ref[cs,:],NT)
        qt_ref[:,cs]=(r[:W]*pd_ref[:,:1]).astype(bf16)
        kt_ref[:,cs]=r[W:2*W].astype(bf16)
        vt_scr[:,cs]=r[2*W:].astype(bf16)
        for h in range(hb):
            k_ref[h,cs,:]=r[W+h*HD:W+(h+1)*HD].T.astype(bf16)
            v_ref[h,cs,:]=r[2*W+h*HD:2*W+(h+1)*HD].T.astype(bf16)
    rowi=lax.broadcasted_iota(jnp.int32,(BQ,BQ),0)
    coli=lax.broadcasted_iota(jnp.int32,(BQ,BQ),1)
    hs=[slice(h*HD,(h+1)*HD) for h in range(hb)]
    single = first_ref[0]==last_ref[nb-1]
    @pl.when(single)
    def _():
        units=[(i,h) for i in range(nb) for h in range(hb)]
        st={}
        def phase_a(u):
            i,h=units[u]; c0=i*BQ
            qi=qt_ref[hs[h],c0:c0+BQ]
            m8=None
            for j in range(i+1):
                s=dot(k_ref[h,j*BQ:(j+1)*BQ,:],qi)
                if j==i: s=jnp.where(rowi<=coli,s,NEG)
                s_scr[u%2,j*BQ:(j+1)*BQ,:]=s
                mm=s.reshape(BQ//8,8,BQ).max(0)
                m8=mm if m8 is None else jnp.maximum(m8,mm)
                yield
            st[u]=m8.max(0,keepdims=True)
        def phase_b(u):
            i,h=units[u]; c0=i*BQ
            m=st[u]; l8=None; acc=None
            for j in range(i+1):
                p=jnp.exp(s_scr[u%2,j*BQ:(j+1)*BQ,:]-m)
                ll=p.reshape(BQ//8,8,BQ).sum(0)
                l8=ll if l8 is None else l8+ll
                pv=dot(vt_scr[hs[h],j*BQ:(j+1)*BQ],p.astype(bf16))
                acc=pv if acc is None else acc+pv
                yield
            l=l8.sum(0,keepdims=True)
            ot_ref[hs[h],c0:c0+BQ]=(acc*(1.0/l)).astype(bf16)
            lse_ref[h,:,c0:c0+BQ]=m+jnp.log(l)
        merge(phase_a(0))
        for u in range(len(units)):
            gs=[phase_b(u)]
            if u+1<len(units): gs=[phase_a(u+1)]+gs
            merge(*gs)
    @pl.when(jnp.logical_not(single))
    def _():
        def qblock(i,_):
            c0=pl.multiple_of(i*BQ,BQ)
            def cnt(j,a): return a+jnp.where(last_ref[j]<first_ref[i],1,0)
            j0=lax.fori_loop(0,i,cnt,jnp.int32(0))
            m_scr[...]=jnp.full_like(m_scr,NEG); l_scr[...]=jnp.zeros_like(l_scr); acc_scr[...]=jnp.zeros_like(acc_scr)
            def step(j,_):
                r0=pl.multiple_of(j*BQ,BQ)
                sk=segk_ref[pl.ds(r0,BQ),:]
                ok=(jnp.concatenate([sk]*(BQ//128),axis=1)==segq_ref[:,pl.ds(c0,BQ)])&(rowi+r0<=coli+c0)
                for h in range(hb):
                    s=dot(k_ref[h,pl.ds(r0,BQ),:],qt_ref[hs[h],pl.ds(c0,BQ)])
                    s=jnp.where(ok,s,NEG)
                    mo=m_scr[h]
                    m=jnp.maximum(mo,s.max(0,keepdims=True))
                    al=jnp.exp(mo-m)
                    p=jnp.where(ok,jnp.exp(s-m),0.0)
                    l_scr[h]=l_scr[h]*al+p.sum(0,keepdims=True)
                    acc_scr[hs[h],:]=acc_scr[hs[h],:]*al+dot(vt_scr[hs[h],pl.ds(r0,BQ)],p.astype(bf16))
                    m_scr[h]=m
                return 0
            lax.fori_loop(j0,i+1,step,0)
            for h in range(hb):
                ot_ref[hs[h],pl.ds(c0,BQ)]=(acc_scr[hs[h],:]*(1.0/l_scr[h])).astype(bf16)
                lse_ref[h,:,pl.ds(c0,BQ)]=m_scr[h]+jnp.log(l_scr[h])
            return 0
        lax.fori_loop(0,nb,qblock,0)

def attn_fwd(first,last,x,wt,pd,segk,segq):
    L,D=x.shape; W=wt.shape[0]//3; hb=W//HD
    V=pl.BlockSpec(memory_space=pltpu.VMEM); S=pl.BlockSpec(memory_space=pltpu.SMEM)
    hd=jax.ShapeDtypeStruct((hb,L,HD),bf16); td=jax.ShapeDtypeStruct((W,L),bf16)
    flops=2*L*D*3*W+2*2*L*L//2*256*hb
    return pl.pallas_call(functools.partial(fwd_kernel,hb),
        out_shape=(td,td,hd,hd,td,jax.ShapeDtypeStruct((hb,1,L),f32)),
        in_specs=[S,S,V,V,V,V,V],out_specs=(V,)*6,
        scratch_shapes=[pltpu.VMEM((W,L),bf16),pltpu.VMEM((2,L,BQ),f32),
            pltpu.VMEM((hb,1,BQ),f32),pltpu.VMEM((hb,1,BQ),f32),pltpu.VMEM((W,BQ),f32)],
        compiler_params=pltpu.CompilerParams(vmem_limit_bytes=56*2**20),
        cost_estimate=pl.CostEstimate(flops=flops,bytes_accessed=x.size*2+wt.size*2+4*L*W*2,transcendentals=L*L//2*hb),
        name="attn_fwd")(first,last,x,wt,pd,segk,segq)

def bwd_kernel(hb, first_ref, last_ref, qt_ref, kt_ref, k_ref, v_ref, ot_ref, dot_ref, lse_ref, pd_ref, segk_ref, segq_ref,
               g_ref, sc_ref, p_scr, ds_scr, dq_scr, dl_scr, dv_scr, dk_scr):
    W=hb*HD; L=qt_ref.shape[1]; nb=L//BQ
    rowi=lax.broadcasted_iota(jnp.int32,(BQ,BQ),0)
    coli=lax.broadcasted_iota(jnp.int32,(BQ,BQ),1)
    hs=[slice(h*HD,(h+1)*HD) for h in range(hb)]
    for h in range(hb):
        dl_scr[h]=(dot_ref[hs[h],:].astype(f32)*ot_ref[hs[h],:].astype(f32)).sum(0,keepdims=True)
    single = first_ref[0]==last_ref[nb-1]
    @pl.when(single)
    def _():
        units=[(j,h,i) for j in range(nb) for h in range(hb) for i in range(j,nb)]
        acc={}
        def phase_a(u):
            j,h,i=units[u]; js=slice(j*BQ,(j+1)*BQ); cs=slice(i*BQ,(i+1)*BQ)
            H2=BQ//2
            for a in range(2):
                ks=slice(j*BQ+a*H2,j*BQ+(a+1)*H2)
                s=dot(k_ref[h,ks,:],qt_ref[hs[h],cs])
                dp=dot(v_ref[h,ks,:],dot_ref[hs[h],cs])
                if j==i: s=jnp.where(rowi[a*H2:(a+1)*H2]<=coli[a*H2:(a+1)*H2],s,NEG)
                p=jnp.exp(s-lse_ref[h,:,cs])
                p_scr[u%2,a*H2:(a+1)*H2,:]=p.astype(bf16)
                ds_scr[u%2,a*H2:(a+1)*H2,:]=(p*(dp-dl_scr[h,:,cs])).astype(bf16)
                yield
        def phase_b(u):
            j,h,i=units[u]; js=slice(j*BQ,(j+1)*BQ); cs=slice(i*BQ,(i+1)*BQ)
            p=p_scr[u%2]; ds=ds_scr[u%2]
            dv=dot(dot_ref[hs[h],cs],p,NT); dk=dot(qt_ref[hs[h],cs],ds,NT)
            if i==j: dv_scr[h]=dv; dk_scr[h]=dk
            else: dv_scr[h]+=dv; dk_scr[h]+=dk
            yield
            dq=dot(kt_ref[hs[h],js],ds)
            if j==0: dq_scr[hs[h],cs]=dq
            else: dq_scr[hs[h],cs]+=dq
            if i==nb-1:
                g_ref[W+h*HD:W+(h+1)*HD,js]=dk_scr[h].astype(bf16)
                g_ref[2*W+h*HD:2*W+(h+1)*HD,js]=dv_scr[h].astype(bf16)
            yield
        merge(phase_a(0))
        for u in range(len(units)):
            gs=[phase_b(u)]
            if u+1<len(units): gs=[phase_a(u+1)]+gs
            merge(*gs)
    @pl.when(jnp.logical_not(single))
    def _():
        dq_scr[...]=jnp.zeros_like(dq_scr)
        def kblock(j,_):
            r0=pl.multiple_of(j*BQ,BQ)
            def cnt(i,a): return a+jnp.where(first_ref[i]<=last_ref[j],1,0)
            iend=lax.fori_loop(j,nb,cnt,j)
            dv_scr[...]=jnp.zeros_like(dv_scr); dk_scr[...]=jnp.zeros_like(dk_scr)
            sk=segk_ref[pl.ds(r0,BQ),:]
            sk=jnp.concatenate([sk]*(BQ//128),axis=1)
            def step(i,_):
                c0=pl.multiple_of(i*BQ,BQ); cs=pl.ds(c0,BQ)
                ok=(sk==segq_ref[:,cs])&(rowi+r0<=coli+c0)
                for h in range(hb):
                    qt=qt_ref[hs[h],cs]; do=dot_ref[hs[h],cs]
                    s=dot(k_ref[h,pl.ds(r0,BQ),:],qt)
                    dp=dot(v_ref[h,pl.ds(r0,BQ),:],do)
                    p=jnp.exp(jnp.where(ok,s-lse_ref[h,:,cs],NEG))
                    ds=(p*(dp-dl_scr[h,:,cs])).astype(bf16)
                    dv_scr[h]+=dot(do,p.astype(bf16),NT)
                    dk_scr[h]+=dot(qt,ds,NT)
                    dq_scr[hs[h],cs]+=dot(kt_ref[hs[h],pl.ds(r0,BQ)],ds)
                return 0
            lax.fori_loop(j,iend,step,0)
            for h in range(hb):
                g_ref[W+h*HD:W+(h+1)*HD,pl.ds(r0,BQ)]=dk_scr[h].astype(bf16)
                g_ref[2*W+h*HD:2*W+(h+1)*HD,pl.ds(r0,BQ)]=dv_scr[h].astype(bf16)
            return 0
        lax.fori_loop(0,nb,kblock,0)
    dq=dq_scr[...]
    g_ref[:W,:]=(dq*pd_ref[:,:1]).astype(bf16)
    sc=(dq*qt_ref[...].astype(f32)).sum(1,keepdims=True)
    sc_ref[...]=jnp.broadcast_to(sc/pd_ref[:,:1],sc_ref.shape)

def attn_bwd(first,last,qt,kt,k,v,ot,dot_,lse,pd,segk,segq):
    W,L=qt.shape; hb=W//HD
    V=pl.BlockSpec(memory_space=pltpu.VMEM); S=pl.BlockSpec(memory_space=pltpu.SMEM)
    flops=5*2*L*L//2*256*hb
    return pl.pallas_call(functools.partial(bwd_kernel,hb),
        out_shape=(jax.ShapeDtypeStruct((3*W,L),bf16),jax.ShapeDtypeStruct((W,128),f32)),
        in_specs=[S,S]+[V]*10,out_specs=(V,)*2,
        scratch_shapes=[pltpu.VMEM((2,BQ,BQ),bf16),pltpu.VMEM((2,BQ,BQ),bf16),pltpu.VMEM((W,L),f32),
            pltpu.VMEM((hb,1,L),f32),pltpu.VMEM((hb,HD,BQ),f32),pltpu.VMEM((hb,HD,BQ),f32)],
        compiler_params=pltpu.CompilerParams(vmem_limit_bytes=56*2**20),
        cost_estimate=pl.CostEstimate(flops=flops,bytes_accessed=8*L*W*2,transcendentals=L*L//2*hb),
        name="attn_bwd")(first,last,qt,kt,k,v,ot,dot_,lse,pd,segk,segq)


MESH=pl.DeviceIdType.MESH

def pro_kernel(Z, C, n, x_ref, w_ref, gain_ref, xo_ref, ain_ref, wt_ref, d3_ref, wd_scr,
               tok_s, tok_r, ain_s, ain_r, w_s, w_r, d_s, d_r):
    z,k,q,s=[lax.axis_index(a) for a in AXES]
    G=2*C; g0=k*C+s
    bar=pltpu.get_barrier_semaphore()
    plane=[(a,b,c) for a in range(2) for b in range(4) for c in range(C)][1:]
    column=[(j,a) for j in range(1,Z) for a in range(2)]
    for a,b,c in plane:
        pl.semaphore_signal(bar,inc=1,device_id=(z,lax.rem(k+a,2),lax.rem(q+b,4),lax.rem(s+c,C)),device_id_type=MESH)
    for j,a in column:
        pl.semaphore_signal(bar,inc=1,device_id=(lax.rem(z+j,Z),lax.rem(k+a,2),q,s),device_id_type=MESH)
    pl.semaphore_wait(bar,len(plane)+len(column))
    def rcopy(src,dst,ss,rs,dev):
        return pltpu.make_async_remote_copy(src_ref=src,dst_ref=dst,send_sem=ss,recv_sem=rs,device_id=dev,device_id_type=MESH)
    toks=[]
    for r in range(2):
        for h in range(2):
            for s2 in range(C):
                i=(r*2+h)*C+s2
                mine=(k==h)&(q==2*k+r)&(s==s2)
                src=x_ref.at[r,pl.ds((h*C+s2)*n,n),:]
                cp=rcopy(src,xo_ref.at[q*C+s],tok_s.at[i],tok_r.at[q*C+s],(z,h,2*k+r,s2))
                loc=pltpu.make_async_copy(src,xo_ref.at[q*C+s],tok_r.at[q*C+s])
                @pl.when(mine)
                def _(loc=loc): loc.start()
                @pl.when(jnp.logical_not(mine))
                def _(cp=cp): cp.start()
                toks.append((mine,cp))
    ws=[]
    for j in range(Z):
        for a in range(2):
            kk=lax.rem(k+a,2)
            if j==0 and a==0:
                pltpu.make_async_copy(w_ref.at[k],wd_scr.at[2*z+k],w_r.at[2*z+k]).start()
            else:
                cp=rcopy(w_ref.at[kk],wd_scr.at[2*z+k],w_s.at[j*2+a],w_r.at[2*z+k],(lax.rem(z+j,Z),kk,q,s))
                cp.start(); ws.append(cp)
    qd=3-q
    dcp=rcopy(w_ref,d3_ref,d_s,d_r,(z,k,qd,s))
    dcp.start()
    ains=[]
    peers=[(gc,gs) for gc in range(2) for gs in range(C)][1:]
    for j in range(4*C):
        rcopy(xo_ref.at[j],xo_ref.at[j],tok_s.at[0],tok_r.at[j],(z,1-k,q,s)).wait_recv()
        x=xo_ref[j].astype(f32)
        inv=lax.rsqrt(jnp.mean(x*x,axis=-1,keepdims=True)+norm_eps)
        slot=j*G+g0
        ain_ref[slot]=(x*inv*gain_ref[...]).astype(bf16)
        for i,(gc,gs) in enumerate(peers):
            cp=rcopy(ain_ref.at[slot],ain_ref.at[slot],ain_s.at[i*4*C+j],ain_r.at[slot],(z,lax.rem(k+gc,2),q,lax.rem(s+gs,C)))
            cp.start(); ains.append(cp)
    for i in range(2*Z):
        rcopy(wd_scr.at[i],wd_scr.at[i],w_s.at[0],w_r.at[i],(z,1-k,q,s)).wait_recv()
    transpose_rows(wd_scr,wt_ref)
    dcp.wait()
    for j in range(4*C):
        for gc,gs in peers:
            slot=j*G+lax.rem(k+gc,2)*C+lax.rem(s+gs,C)
            rcopy(ain_ref.at[slot],ain_ref.at[slot],ain_s.at[0],ain_r.at[slot],(z,1-k,q,s)).wait_recv()
    for mine,cp in toks:
        @pl.when(jnp.logical_not(mine))
        def _(cp=cp): cp.wait_send()
    for cp in ws+ains: cp.wait_send()

def transpose_rows(src, dst):
    P_,rows,cols=src.shape
    per=max(1,640//rows)
    for i in range(P_//per):
        dst[:,i*per*rows:(i+1)*per*rows]=src[i*per:(i+1)*per].reshape(per*rows,cols).T

def prologue(Z, C, tokens, w2h, gain):
    R,Pn,D=tokens.shape; G=2*C; n=Pn//G; _,Dd,nC=w2h.shape
    V=pl.BlockSpec(memory_space=pltpu.VMEM); A=pl.BlockSpec(memory_space=pl.ANY)
    S=pltpu.SemaphoreType.DMA
    xo,ain,wt,d3=pl.pallas_call(functools.partial(pro_kernel,Z,C,n),
        out_shape=(jax.ShapeDtypeStruct((4*C,n,D),bf16),jax.ShapeDtypeStruct((4*C*G,n,D),bf16),
                   jax.ShapeDtypeStruct((nC,D),bf16),jax.ShapeDtypeStruct((2,Dd,nC),bf16)),
        in_specs=[A,V,V],out_specs=(V,)*4,
        scratch_shapes=[pltpu.VMEM((2*Z,Dd,nC),bf16),S((4*C,)),S((4*C,)),S((4*C*(G-1),)),S((4*C*G,)),S((2*Z,)),S((2*Z,)),S,S],
        compiler_params=pltpu.CompilerParams(collective_id=0,has_side_effects=True,vmem_limit_bytes=56*2**20),
        cost_estimate=pl.CostEstimate(flops=10**10,bytes_accessed=10**8,transcendentals=0),
        name="prologue")(tokens,w2h,gain[None])
    return xo.reshape(4*C*n,D),ain.reshape(4*C*G*n,D),wt,d3

def assemble_kernel(Z, zi_ref, *refs):
    parts,out,scr=refs[:Z],refs[Z],refs[Z+1]
    for j in range(Z):
        scr[zi_ref[0]^j]=parts[j][...]
    transpose_rows(scr,out)

def assemble(zi, parts):
    Z=len(parts); rows,nC=parts[0].shape
    V=pl.BlockSpec(memory_space=pltpu.VMEM)
    return pl.pallas_call(functools.partial(assemble_kernel,Z),out_shape=jax.ShapeDtypeStruct((nC,Z*rows),bf16),
        in_specs=[pl.BlockSpec(memory_space=pltpu.SMEM)]+[V]*Z,out_specs=V,
        scratch_shapes=[pltpu.VMEM((Z,rows,nC),bf16)],
        compiler_params=pltpu.CompilerParams(vmem_limit_bytes=56*2**20),name="assemble")(zi[None],*parts)

def split_kernel(Z, nr, zi_ref, own_ref, *refs):
    recvs,outs,scr=refs[:nr],refs[nr:nr+Z],refs[nr+Z]
    nC,D=own_ref.shape; rows=D//Z
    per=max(1,640//rows)
    for i in range(Z//per):
        ls=slice(i*per*rows,(i+1)*per*rows)
        t=own_ref[:,ls].astype(f32)
        for r in recvs: t=t+r[:,ls].astype(f32)
        scr[i*per:(i+1)*per]=t.T.reshape(per,rows,nC)
    for j in range(Z):
        outs[j][...]=scr[zi_ref[0]^j].astype(outs[j].dtype)

def split(zi, Z, own, recvs):
    nC,D=own.shape
    V=pl.BlockSpec(memory_space=pltpu.VMEM)
    return pl.pallas_call(functools.partial(split_kernel,Z,len(recvs)),
        out_shape=tuple(jax.ShapeDtypeStruct((D//Z,nC),f32 if j==0 else bf16) for j in range(Z)),
        in_specs=[pl.BlockSpec(memory_space=pltpu.SMEM)]+[V]*(1+len(recvs)),out_specs=(V,)*Z,
        scratch_shapes=[pltpu.VMEM((Z,D//Z,nC),f32)],
        compiler_params=pltpu.CompilerParams(vmem_limit_bytes=56*2**20),name="split")(zi[None],own,*recvs)


scale_base = 1.442695041

def silu_slope(u):
    sg=jax.nn.sigmoid(u)
    return sg*(1.0+u*(1.0-sg))

def make_local(Z, C):
    sizes=(Z,2,4,C)
    coords=list(itertools.product(*[range(n) for n in sizes]))
    lin={c:i for i,c in enumerate(coords)}
    G=2*C
    def pp(x, fn):
        return lax.ppermute(x, AXES, [(lin[c], lin[fn(*c)]) for c in coords])
    def unxor(parts, idx):
        b=1
        while b<len(parts):
            c=(idx & b)!=0
            parts=[jnp.where(c,parts[a^b],parts[a]) for a in range(len(parts))]
            b*=2
        return parts
    def allsum(v):
        for ax,n in enumerate(sizes):
            b=1
            while b<n:
                v=v+pp(v,lambda *c,ax=ax,b=b: tuple(ci^b if i==ax else ci for i,ci in enumerate(c)))
                b*=2
        return v
    def gsend(x, gamma):
        gc,gs=divmod(gamma,C)
        return pp(x, lambda z,k,q,s: (z,k^gc,q,s^gs))

    def after(x, *deps):
        return lax.optimization_barrier((x,)+deps)[0] if deps else x

    def local(tokens, segments, attn_gain, w_query, w_key, w_value, w_out, query_scale, mlp_gain, w_up, w_down, cotangent):
        zi,k,qi,si=[lax.axis_index(a) for a in AXES]
        R,Pn,D=tokens.shape; L=segments.shape[1]
        n=Pn//G
        N=4*C*n
        Dd,Ct=w_query.shape; Ch=Ct//2; W=Ch; hb=W//HD
        g0=k*C+si
        k0=k==0
        q0=2*(k^(qi//2))+qi%2
        rounds=list(itertools.product(range(2),range(2),range(C)))

        def spread(x):
            got=[]
            for eta,rho,sg in rounds:
                r=(qi%2)^rho; h=(qi//2)^k^eta; s2=si^sg
                piece=lax.dynamic_slice(x,(r,(h*C+s2)*n,0),(1,n,D))[0]
                got.append(pp(piece, lambda z,kk,q,s: (z,(q//2)^kk^eta,2*kk+((q%2)^rho),s^sg)))
            return jnp.concatenate(unxor(got,q0*C+si),0)
        def collect(y):
            parts=unxor([y[i*n:(i+1)*n] for i in range(4*C)],q0*C+si)
            got=[]
            for idx,(eta,rho,sg) in enumerate(rounds):
                got.append(pp(parts[idx], lambda z,kk,q,s: (z,q//2,(2*(kk^(q//2))+q%2)^(2*eta+rho),s^sg)))
            ab=unxor(got,((qi//2)^k)*(2*C)+(qi%2)*C+si)
            rows=[jnp.concatenate([ab[(h*2+r)*C+s2] for h in range(2) for s2 in range(C)],0) for r in range(R)]
            return jnp.stack(rows,0)
        def halves(shards):
            return jnp.stack([jnp.concatenate([w[:,h*Ch:(h+1)*Ch] for w in shards],1) for h in range(2)],0)
        def gatherD(w2h, *deps):
            keep=jnp.where(k0,w2h[0],w2h[1]); send=jnp.where(k0,w2h[1],w2h[0])
            recv=pp(send,lambda z,kk,q,s:(z,1-kk,q,s))
            rows=jnp.concatenate([jnp.where(k0,keep,recv),jnp.where(k0,recv,keep)],0)
            rows=after(rows,*deps)
            parts=[rows]+[pp(rows,lambda z,kk,q,s:(z^j,kk,q,s)) for j in range(1,Z)]
            return assemble(zi,parts),parts[-1]
        def chip(x, m):
            return pp(x,lambda z,kk,q,s:(z,kk,q^m,s))
        def reduceZ(rel):
            tot=rel[0]
            for j in range(1,Z):
                tot=tot+pp(rel[j],lambda z,kk,q,s:(z^j,kk,q,s)).astype(f32)
            return tot
        def finish(tot, nw):
            keep=jnp.where(k0,tot[:Dd],tot[Dd:]); send=jnp.where(k0,tot[Dd:],tot[:Dd])
            recv=pp(send,lambda z,kk,q,s:(z,1-kk,q,s))
            lo=jnp.where(k0,keep,recv); hi=jnp.where(k0,recv,keep)
            return [jnp.concatenate([lo[:,i*Ch:(i+1)*Ch],hi[:,i*Ch:(i+1)*Ch]],1) for i in range(nw)]
        def tok_lanes(xT):
            return [jnp.concatenate([xT[:,(b*G+g)*n:(b*G+g+1)*n] for b in range(4*C)],1) for g in range(G)]
        def tok_rows_join(parts):
            return jnp.concatenate([parts[g][b*n:(b+1)*n] for b in range(4*C) for g in range(G)],0)
        def tok_lanes_join(parts):
            return jnp.concatenate([parts[g][:,b*n:(b+1)*n] for b in range(4*C) for g in range(G)],1)

        wq2=halves([w_query,w_key,w_value]); wo2=halves([w_out.T,w_up,w_down.T])
        x_b,ain,wt0,d3=prologue(Z,C,tokens,wq2,attn_gain)
        x=x_b.astype(f32)
        wt1,wt2=chip(wt0,1),chip(wt0,2)
        wt3,z3=gatherD(d3)
        wts=[wt0,wt1,wt2,wt3]
        seg_o=pp(segments,lambda z,kk,q,s:(z,1-kk,q,s))
        seg2=jnp.where(k==qi//2,segments,seg_o)
        seg=jnp.where(qi%2==0,seg2[0],seg2[1])
        first=seg[::BQ]; last=seg[BQ-1::BQ]
        segk=jnp.broadcast_to(seg[:,None],(L,128)); segq=seg[None]
        per_dim=scale_base/math.sqrt(HD)*jax.nn.softplus(query_scale)
        pd=jnp.broadcast_to(jnp.tile(per_dim,hb)[:,None],(W,128))

        wo2=after(wo2,wt0)
        u0,z0=gatherD(wo2,z3)
        o3=chip(after(wo2,wt1,wt2),3)
        cot=spread(after(cotangent,o3))
        u1,u2=chip(u0,1),chip(u0,2)
        u3,_=gatherD(o3,z0)

        saved=[attn_fwd(first,last,ain,wts[m],pd,segk,segq) for m in range(4)]
        mixT=jnp.concatenate([sv[4] for sv in saved],0)
        rel=unxor(tok_lanes(mixT),g0)
        mixT_own=jnp.concatenate([rel[0]]+[gsend(rel[g],g) for g in range(1,G)],0)
        w3=[u0,u1,u2,u3]
        def whole(i):
            mine=jnp.concatenate([w3[m][i*Ch:(i+1)*Ch] for m in range(4)],0)
            return jnp.concatenate([mine]+[gsend(mine,g) for g in range(1,G)],0)
        wo,wu,wd=whole(0),whole(1),whole(2)

        inv1=lax.rsqrt(jnp.mean(x*x,axis=-1,keepdims=True)+norm_eps)
        attn=dot(mixT_own,wo,TN)
        middle=x+attn
        inv2=lax.rsqrt(jnp.mean(middle*middle,axis=-1,keepdims=True)+norm_eps)
        norm2=middle*inv2
        mlp_in=(norm2*mlp_gain).astype(bf16)
        up=dot(mlp_in,wu,NT)
        hid=jax.nn.silu(up).astype(bf16)
        block=(middle+dot(hid,wd)).astype(bf16)
        block_out=collect(block)
        gup=(dot(cot,wd,NT)*silu_slope(up)).astype(bf16)
        gmlp=dot(gup,wu)
        dn=gmlp*mlp_gain
        gmid=cot.astype(f32)+inv2*(dn-norm2*jnp.mean(dn*norm2,axis=-1,keepdims=True))
        mlp_gain_part=jnp.sum(gmlp*norm2,axis=0)
        gattn=gmid.astype(bf16)
        gmixT=dot(wo,gattn,NT).astype(bf16)
        K=gmixT.shape[0]//G
        doT=tok_lanes_join(unxor([gmixT[:K]]+[gsend(gmixT[g*K:(g+1)*K],g) for g in range(1,G)],g0))
        g3=[dot(mixT_own,gattn),dot(gup,mlp_in,TN),dot(hid,cot,TN)]

        K4=4*Ch
        mine=list(g3)
        mine=[t[:K4] for t in g3]
        for g in range(1,G):
            for i,t in enumerate(g3):
                mine[i]=mine[i]+gsend(t[g*K4:(g+1)*K4].astype(bf16),g).astype(f32)
        fb=[jnp.concatenate([t[m*Ch:(m+1)*Ch] for t in mine],0) for m in range(4)]
        gT=[None]*4; dW=[None]*4; sc=0.0
        def bwd(m,*deps):
            qt,kt,kn,vn,ot,lse=saved[m]
            qt=after(qt,*deps)
            gT[m],s_=attn_bwd(first,last,qt,kt,kn,vn,ot,doT[m*W:(m+1)*W],lse,pd,segk,segq)
            return s_[:,0]
        sc=sc+bwd(3)
        dW[3]=dot(gT[3],ain).astype(bf16)
        fr=[chip(fb[m].astype(bf16),m) for m in (1,2)]
        f3=reduceZ(split(zi,Z,fb[3],[]))
        sc=sc+bwd(1,gT[3],fb[0])
        dW[1]=dot(gT[1],ain).astype(bf16)
        q1=chip(dW[1],1)
        f0=reduceZ(split(zi,Z,fb[0],fr))
        f3=chip(f3.astype(bf16),3)
        sc=sc+bwd(2,gT[1],fr[0],fr[1])
        dW[2]=dot(gT[2],ain).astype(bf16)
        q2=chip(dW[2],2)
        q3=reduceZ(split(zi,Z,after(dW[3],f0),[]))
        sc=sc+bwd(0,gT[2],f0,q1)
        q3=chip(after(q3,gT[0]).astype(bf16),3)
        g_out,g_up,g_down=finish(f0+f3.astype(f32),3)
        grad_out=g_out.T; grad_up=g_up; grad_down=g_down.T
        gTall=jnp.concatenate(gT,0); wtall=jnp.concatenate(wts,0)
        grel=unxor(tok_lanes(gTall),g0)
        gain=0.0
        for g in range(1,G):
            gain=gain+gsend(dot(grel[g],wtall,TN).astype(bf16),g).astype(f32)
        gain=gain+dot(grel[0],wtall,TN)
        norm1=x*inv1
        dn1=gain*attn_gain
        gin=gmid+inv1*(dn1-norm1*jnp.mean(dn1*norm1,axis=-1,keepdims=True))
        attn_gain_part=jnp.sum(gain*norm1,axis=0)
        ginb=gin.astype(bf16)
        input_grad=collect(ginb).astype(f32)
        dW[0]=dot(after(gT[0],ginb),ain)
        q0s=reduceZ(split(zi,Z,dW[0],[q1,q2]))
        grad_query,grad_key,grad_value=finish(q0s+q3.astype(f32),3)

        scale_part=jnp.sum(sc.reshape(hb,HD),axis=0)*(scale_base/math.sqrt(HD))*jax.nn.sigmoid(query_scale)
        grad_mlp_gain=allsum(mlp_gain_part)
        late=allsum(jnp.concatenate([attn_gain_part,scale_part]))
        return (block_out,input_grad,late[:D],grad_query,grad_key,grad_value,grad_out,late[D:],grad_mlp_gain,grad_up,grad_down)
    return local

def solution(mesh):
    dp,T=mesh.shape["dp"],mesh.shape["tensor"]
    Z,C=dp//2,T//4
    fine=Mesh(mesh.devices.reshape(Z,2,4,C),AXES)
    dpx=("zz","core"); tx=("q","s")
    in_specs=(P(dpx,tx,None),P(dpx,None),P(),P(dpx,tx),P(dpx,tx),P(dpx,tx),P(tx,dpx),P(),P(),P(dpx,tx),P(tx,dpx),P(dpx,tx,None))
    out_specs=(P(dpx,tx,None),P(dpx,tx,None),P(),P(dpx,tx),P(dpx,tx),P(dpx,tx),P(tx,dpx),P(),P(),P(dpx,tx),P(tx,dpx))
    return jax.shard_map(make_local(Z,C),mesh=fine,in_specs=in_specs,out_specs=out_specs,check_vma=False)
```

```python
import functools
import itertools
import math
import jax, jax.numpy as jnp
from jax import lax
from jax.experimental import pallas as pl
from jax.experimental.pallas import tpu as pltpu
from jax.sharding import Mesh, PartitionSpec as P

AXES=("zz","core","q","s")
norm_eps = 1e-06
HD=80
BQ=256
NEG=-1e30
f32=jnp.float32; bf16=jnp.bfloat16
NT=(((1,),(1,)),((),()))
NN=(((1,),(0,)),((),()))
TN=(((0,),(0,)),((),()))
def dot(a,b,dims=NN): return lax.dot_general(a,b,dims,preferred_element_type=f32)

def merge(*gens):
    gens=list(gens)
    while gens:
        for g in list(gens):
            try: next(g)
            except StopIteration: gens.remove(g)

def fwd_kernel(hb, first_ref, last_ref, x_ref, wt_ref, pd_ref, segk_ref, segq_ref,
               qt_ref, kt_ref, k_ref, v_ref, ot_ref, lse_ref, vt_scr, s_scr, m_scr, l_scr, acc_scr):
    L=x_ref.shape[0]; nb=L//BQ; W=hb*HD
    CH=512
    for c in range(L//CH):
        cs=slice(c*CH,(c+1)*CH)
        r=dot(wt_ref[...],x_ref[cs,:],NT)
        qt_ref[:,cs]=(r[:W]*pd_ref[:,:1]).astype(bf16)
        kt_ref[:,cs]=r[W:2*W].astype(bf16)
        vt_scr[:,cs]=r[2*W:].astype(bf16)
        for h in range(hb):
            k_ref[h,cs,:]=r[W+h*HD:W+(h+1)*HD].T.astype(bf16)
            v_ref[h,cs,:]=r[2*W+h*HD:2*W+(h+1)*HD].T.astype(bf16)
    rowi=lax.broadcasted_iota(jnp.int32,(BQ,BQ),0)
    coli=lax.broadcasted_iota(jnp.int32,(BQ,BQ),1)
    hs=[slice(h*HD,(h+1)*HD) for h in range(hb)]
    single = first_ref[0]==last_ref[nb-1]
    @pl.when(single)
    def _():
        units=[(i,h) for i in range(nb) for h in range(hb)]
        st={}
        def phase_a(u):
            i,h=units[u]; c0=i*BQ
            qi=qt_ref[hs[h],c0:c0+BQ]
            m8=None
            for j in range(i+1):
                s=dot(k_ref[h,j*BQ:(j+1)*BQ,:],qi)
                if j==i: s=jnp.where(rowi<=coli,s,NEG)
                s_scr[u%2,j*BQ:(j+1)*BQ,:]=s
                mm=s.reshape(BQ//8,8,BQ).max(0)
                m8=mm if m8 is None else jnp.maximum(m8,mm)
                yield
            st[u]=m8.max(0,keepdims=True)
        def phase_b(u):
            i,h=units[u]; c0=i*BQ
            m=st[u]; l8=None; acc=None
            for j in range(i+1):
                p=jnp.exp(s_scr[u%2,j*BQ:(j+1)*BQ,:]-m)
                ll=p.reshape(BQ//8,8,BQ).sum(0)
                l8=ll if l8 is None else l8+ll
                pv=dot(vt_scr[hs[h],j*BQ:(j+1)*BQ],p.astype(bf16))
                acc=pv if acc is None else acc+pv
                yield
            l=l8.sum(0,keepdims=True)
            ot_ref[hs[h],c0:c0+BQ]=(acc*(1.0/l)).astype(bf16)
            lse_ref[h,:,c0:c0+BQ]=m+jnp.log(l)
        merge(phase_a(0))
        for u in range(len(units)):
            gs=[phase_b(u)]
            if u+1<len(units): gs=[phase_a(u+1)]+gs
            merge(*gs)
    @pl.when(jnp.logical_not(single))
    def _():
        def qblock(i,_):
            c0=pl.multiple_of(i*BQ,BQ)
            def cnt(j,a): return a+jnp.where(last_ref[j]<first_ref[i],1,0)
            j0=lax.fori_loop(0,i,cnt,jnp.int32(0))
            m_scr[...]=jnp.full_like(m_scr,NEG); l_scr[...]=jnp.zeros_like(l_scr); acc_scr[...]=jnp.zeros_like(acc_scr)
            def step(j,_):
                r0=pl.multiple_of(j*BQ,BQ)
                sk=segk_ref[pl.ds(r0,BQ),:]
                ok=(jnp.concatenate([sk]*(BQ//128),axis=1)==segq_ref[:,pl.ds(c0,BQ)])&(rowi+r0<=coli+c0)
                for h in range(hb):
                    s=dot(k_ref[h,pl.ds(r0,BQ),:],qt_ref[hs[h],pl.ds(c0,BQ)])
                    s=jnp.where(ok,s,NEG)
                    mo=m_scr[h]
                    m=jnp.maximum(mo,s.max(0,keepdims=True))
                    al=jnp.exp(mo-m)
                    p=jnp.where(ok,jnp.exp(s-m),0.0)
                    l_scr[h]=l_scr[h]*al+p.sum(0,keepdims=True)
                    acc_scr[hs[h],:]=acc_scr[hs[h],:]*al+dot(vt_scr[hs[h],pl.ds(r0,BQ)],p.astype(bf16))
                    m_scr[h]=m
                return 0
            lax.fori_loop(j0,i+1,step,0)
            for h in range(hb):
                ot_ref[hs[h],pl.ds(c0,BQ)]=(acc_scr[hs[h],:]*(1.0/l_scr[h])).astype(bf16)
                lse_ref[h,:,pl.ds(c0,BQ)]=m_scr[h]+jnp.log(l_scr[h])
            return 0
        lax.fori_loop(0,nb,qblock,0)

def attn_fwd(first,last,x,wt,pd,segk,segq):
    L,D=x.shape; W=wt.shape[0]//3; hb=W//HD
    V=pl.BlockSpec(memory_space=pltpu.VMEM); S=pl.BlockSpec(memory_space=pltpu.SMEM)
    hd=jax.ShapeDtypeStruct((hb,L,HD),bf16); td=jax.ShapeDtypeStruct((W,L),bf16)
    flops=2*L*D*3*W+2*2*L*L//2*256*hb
    return pl.pallas_call(functools.partial(fwd_kernel,hb),
        out_shape=(td,td,hd,hd,td,jax.ShapeDtypeStruct((hb,1,L),f32)),
        in_specs=[S,S,V,V,V,V,V],out_specs=(V,)*6,
        scratch_shapes=[pltpu.VMEM((W,L),bf16),pltpu.VMEM((2,L,BQ),f32),
            pltpu.VMEM((hb,1,BQ),f32),pltpu.VMEM((hb,1,BQ),f32),pltpu.VMEM((W,BQ),f32)],
        compiler_params=pltpu.CompilerParams(vmem_limit_bytes=56*2**20),
        cost_estimate=pl.CostEstimate(flops=flops,bytes_accessed=x.size*2+wt.size*2+4*L*W*2,transcendentals=L*L//2*hb),
        name="attn_fwd")(first,last,x,wt,pd,segk,segq)

def bwd_kernel(hb, first_ref, last_ref, qt_ref, kt_ref, k_ref, v_ref, ot_ref, dot_ref, lse_ref, pd_ref, segk_ref, segq_ref,
               g_ref, sc_ref, p_scr, ds_scr, dq_scr, dl_scr, dv_scr, dk_scr):
    W=hb*HD; L=qt_ref.shape[1]; nb=L//BQ
    rowi=lax.broadcasted_iota(jnp.int32,(BQ,BQ),0)
    coli=lax.broadcasted_iota(jnp.int32,(BQ,BQ),1)
    hs=[slice(h*HD,(h+1)*HD) for h in range(hb)]
    for h in range(hb):
        dl_scr[h]=(dot_ref[hs[h],:].astype(f32)*ot_ref[hs[h],:].astype(f32)).sum(0,keepdims=True)
    single = first_ref[0]==last_ref[nb-1]
    @pl.when(single)
    def _():
        units=[(j,h,i) for j in range(nb) for h in range(hb) for i in range(j,nb)]
        acc={}
        def phase_a(u):
            j,h,i=units[u]; js=slice(j*BQ,(j+1)*BQ); cs=slice(i*BQ,(i+1)*BQ)
            H2=BQ//2
            for a in range(2):
                ks=slice(j*BQ+a*H2,j*BQ+(a+1)*H2)
                s=dot(k_ref[h,ks,:],qt_ref[hs[h],cs])
                dp=dot(v_ref[h,ks,:],dot_ref[hs[h],cs])
                if j==i: s=jnp.where(rowi[a*H2:(a+1)*H2]<=coli[a*H2:(a+1)*H2],s,NEG)
                p=jnp.exp(s-lse_ref[h,:,cs])
                p_scr[u%2,a*H2:(a+1)*H2,:]=p.astype(bf16)
                ds_scr[u%2,a*H2:(a+1)*H2,:]=(p*(dp-dl_scr[h,:,cs])).astype(bf16)
                yield
        def phase_b(u):
            j,h,i=units[u]; js=slice(j*BQ,(j+1)*BQ); cs=slice(i*BQ,(i+1)*BQ)
            p=p_scr[u%2]; ds=ds_scr[u%2]
            dv=dot(dot_ref[hs[h],cs],p,NT); dk=dot(qt_ref[hs[h],cs],ds,NT)
            if i==j: dv_scr[h]=dv; dk_scr[h]=dk
            else: dv_scr[h]+=dv; dk_scr[h]+=dk
            yield
            dq=dot(kt_ref[hs[h],js],ds)
            if j==0: dq_scr[hs[h],cs]=dq
            else: dq_scr[hs[h],cs]+=dq
            if i==nb-1:
                g_ref[W+h*HD:W+(h+1)*HD,js]=dk_scr[h].astype(bf16)
                g_ref[2*W+h*HD:2*W+(h+1)*HD,js]=dv_scr[h].astype(bf16)
            yield
        merge(phase_a(0))
        for u in range(len(units)):
            gs=[phase_b(u)]
            if u+1<len(units): gs=[phase_a(u+1)]+gs
            merge(*gs)
    @pl.when(jnp.logical_not(single))
    def _():
        dq_scr[...]=jnp.zeros_like(dq_scr)
        def kblock(j,_):
            r0=pl.multiple_of(j*BQ,BQ)
            def cnt(i,a): return a+jnp.where(first_ref[i]<=last_ref[j],1,0)
            iend=lax.fori_loop(j,nb,cnt,j)
            dv_scr[...]=jnp.zeros_like(dv_scr); dk_scr[...]=jnp.zeros_like(dk_scr)
            sk=segk_ref[pl.ds(r0,BQ),:]
            sk=jnp.concatenate([sk]*(BQ//128),axis=1)
            def step(i,_):
                c0=pl.multiple_of(i*BQ,BQ); cs=pl.ds(c0,BQ)
                ok=(sk==segq_ref[:,cs])&(rowi+r0<=coli+c0)
                for h in range(hb):
                    qt=qt_ref[hs[h],cs]; do=dot_ref[hs[h],cs]
                    s=dot(k_ref[h,pl.ds(r0,BQ),:],qt)
                    dp=dot(v_ref[h,pl.ds(r0,BQ),:],do)
                    p=jnp.exp(jnp.where(ok,s-lse_ref[h,:,cs],NEG))
                    ds=(p*(dp-dl_scr[h,:,cs])).astype(bf16)
                    dv_scr[h]+=dot(do,p.astype(bf16),NT)
                    dk_scr[h]+=dot(qt,ds,NT)
                    dq_scr[hs[h],cs]+=dot(kt_ref[hs[h],pl.ds(r0,BQ)],ds)
                return 0
            lax.fori_loop(j,iend,step,0)
            for h in range(hb):
                g_ref[W+h*HD:W+(h+1)*HD,pl.ds(r0,BQ)]=dk_scr[h].astype(bf16)
                g_ref[2*W+h*HD:2*W+(h+1)*HD,pl.ds(r0,BQ)]=dv_scr[h].astype(bf16)
            return 0
        lax.fori_loop(0,nb,kblock,0)
    dq=dq_scr[...]
    g_ref[:W,:]=(dq*pd_ref[:,:1]).astype(bf16)
    sc=(dq*qt_ref[...].astype(f32)).sum(1,keepdims=True)
    sc_ref[...]=jnp.broadcast_to(sc/pd_ref[:,:1],sc_ref.shape)

def attn_bwd(first,last,qt,kt,k,v,ot,dot_,lse,pd,segk,segq):
    W,L=qt.shape; hb=W//HD
    V=pl.BlockSpec(memory_space=pltpu.VMEM); S=pl.BlockSpec(memory_space=pltpu.SMEM)
    flops=5*2*L*L//2*256*hb
    return pl.pallas_call(functools.partial(bwd_kernel,hb),
        out_shape=(jax.ShapeDtypeStruct((3*W,L),bf16),jax.ShapeDtypeStruct((W,128),f32)),
        in_specs=[S,S]+[V]*10,out_specs=(V,)*2,
        scratch_shapes=[pltpu.VMEM((2,BQ,BQ),bf16),pltpu.VMEM((2,BQ,BQ),bf16),pltpu.VMEM((W,L),f32),
            pltpu.VMEM((hb,1,L),f32),pltpu.VMEM((hb,HD,BQ),f32),pltpu.VMEM((hb,HD,BQ),f32)],
        compiler_params=pltpu.CompilerParams(vmem_limit_bytes=56*2**20),
        cost_estimate=pl.CostEstimate(flops=flops,bytes_accessed=8*L*W*2,transcendentals=L*L//2*hb),
        name="attn_bwd")(first,last,qt,kt,k,v,ot,dot_,lse,pd,segk,segq)


MESH=pl.DeviceIdType.MESH

def rcopy(src,dst,ss,rs,dev):
    return pltpu.make_async_remote_copy(src_ref=src,dst_ref=dst,send_sem=ss,recv_sem=rs,device_id=dev,device_id_type=MESH)

def transpose_rows(src, dst):
    P_,rows,cols=src.shape
    per=max(1,640//rows)
    for i in range(P_//per):
        dst[:,i*per*rows:(i+1)*per*rows]=src[i*per:(i+1)*per].reshape(per*rows,cols).T

def partner(q, m):
    return (q,q+1-2*lax.rem(q,2),lax.rem(q+2,4),3-q)[m]

def greet(Z, C):
    z,k,q,s=[lax.axis_index(a) for a in AXES]
    bar=pltpu.get_barrier_semaphore()
    plane=list(itertools.product(range(2),range(4),range(C)))[1:]
    column=[(j,a) for j in range(1,Z) for a in range(2)]
    for a,b,c in plane:
        pl.semaphore_signal(bar,inc=1,device_id=(z,lax.rem(k+a,2),lax.rem(q+b,4),lax.rem(s+c,C)),device_id_type=MESH)
    for j,a in column:
        pl.semaphore_signal(bar,inc=1,device_id=(lax.rem(z+j,Z),lax.rem(k+a,2),q,s),device_id_type=MESH)
    pl.semaphore_wait(bar,len(plane)+len(column))

def col_copies(Z, src, dst, ss, rs):
    z,k,q,s=[lax.axis_index(a) for a in AXES]
    out=[]
    for j in range(Z):
        for a in range(2):
            kk=lax.rem(k+a,2)
            if j==0 and a==0: out.append(pltpu.make_async_copy(src.at[k],dst.at[2*z+k],rs.at[2*z+k]))
            else: out.append(rcopy(src.at[kk],dst.at[2*z+k],ss.at[j*2+a],rs.at[2*z+k],(lax.rem(z+j,Z),kk,q,s)))
    return out

def spread_copies(C, n, src, dst, ss, rs):
    z,k,q,s=[lax.axis_index(a) for a in AXES]
    out=[]
    for r in range(2):
        for h in range(2):
            for s2 in range(C):
                i=(r*2+h)*C+s2
                piece=src.at[r,pl.ds((h*C+s2)*n,n),:]
                out.append(((k==h)&(q==2*k+r)&(s==s2),pltpu.make_async_copy(piece,dst.at[q*C+s],rs.at[q*C+s]),
                            rcopy(piece,dst.at[q*C+s],ss.at[i],rs.at[q*C+s],(z,h,2*k+r,s2))))
    return out

def spread_start(cps):
    for mine,loc,cp in cps:
        @pl.when(mine)
        def _(loc=loc): loc.start()
        @pl.when(jnp.logical_not(mine))
        def _(cp=cp): cp.start()

def spread_sent(cps):
    for mine,loc,cp in cps:
        @pl.when(jnp.logical_not(mine))
        def _(cp=cp): cp.wait_send()

def arrived(ref, sem):
    z,k,q,s=[lax.axis_index(a) for a in AXES]
    rcopy(ref,ref,sem,sem,(z,1-k,q,s)).wait_recv()

def fwd_kernel(Z, C, n, x_ref, w1_ref, w2_ref, cot_ref, gain_ref, pd_ref, segk_ref, segq_ref,
               xo_ref, ain_ref, wts_ref, w2o_ref, coto_ref, mix_ref, qt_ref, kt_ref, k_ref, v_ref, ot_ref, lse_ref,
               wa_scr, wb_scr, wc_scr, wd_scr, d3_scr, o3_scr, w2_scr, vt_scr, s_scr,
               tok_s, tok_r, ain_s, ain_r, a_s, a_r, b_s, b_r, c_s, c_r, dd_s, dd_r, d3_s, o3_s, do_r,
               wt_s, wt_r, w2_s, w2_r, gr_s, gr_r, loc_s, cot_s, cot_r, mix_s, mix_r):
    z,k,q,s=[lax.axis_index(a) for a in AXES]
    G=2*C; g0=k*C+s; NB=4*C
    D=gain_ref.shape[1]; L=segq_ref.shape[1]; W=pd_ref.shape[0]; hb=W//HD; nb=L//BQ
    peers=list(itertools.product(range(2),range(C)))[1:]
    pdev=[(z,lax.rem(k+gc,2),q,lax.rem(s+gs,C)) for gc,gs in peers]
    pidx=[lax.rem(k+gc,2)*C+lax.rem(s+gs,C) for gc,gs in peers]
    back=[gc*C+(C-gs)%C for gc,gs in peers]
    fore=[gc*C+gs for gc,gs in peers]
    chipdev=[(z,k,partner(q,m),s) for m in range(4)]
    toks=spread_copies(C,n,x_ref,xo_ref,tok_s,tok_r)
    cots=spread_copies(C,n,cot_ref,coto_ref,cot_s,cot_r)
    ca=col_copies(Z,w1_ref,wa_scr,a_s,a_r)
    cb=col_copies(Z,w2_ref,wb_scr,b_s,b_r)
    cc=col_copies(Z,d3_scr,wc_scr,c_s,c_r)
    cd=col_copies(Z,o3_scr,wd_scr,dd_s,dd_r)
    d3=rcopy(w1_ref,d3_scr,d3_s,do_r.at[0],chipdev[3])
    o3=rcopy(w2_ref,o3_scr,o3_s,do_r.at[1],chipdev[3])
    wcp=[rcopy(wts_ref.at[0],wts_ref.at[m],wt_s.at[m],wt_r.at[m],chipdev[m]) for m in (1,2)]
    w2cp=[rcopy(w2_scr.at[0],w2_scr.at[m],w2_s.at[m],w2_r.at[m],chipdev[m]) for m in (1,2)]
    grp=[[rcopy(w2_scr.at[m],w2o_ref.at[back[i],m],gr_s.at[i,m],gr_r.at[back[i],m],pdev[i]) for i in range(G-1)] for m in range(4)]
    loc=[pltpu.make_async_copy(w2_scr.at[m],w2o_ref.at[0,m],loc_s.at[m]) for m in range(4)]
    def share(m):
        loc[m].start()
        for cp in grp[m]: cp.start()
    greet(Z,C)
    spread_start(toks)
    for cp in ca: cp.start()
    ains=[]
    for j in range(NB):
        arrived(xo_ref.at[j],tok_r.at[j])
        x=xo_ref[j].astype(f32)
        inv=lax.rsqrt(jnp.mean(x*x,axis=-1,keepdims=True)+norm_eps)
        slot=j*G+g0
        ain_ref[slot]=(x*inv*gain_ref[...]).astype(bf16)
        for i in range(G-1):
            cp=rcopy(ain_ref.at[slot],ain_ref.at[slot],ain_s.at[i,j],ain_r.at[slot],pdev[i])
            cp.start(); ains.append(cp)
    for i in range(2*Z): arrived(wa_scr.at[i],a_r.at[i])
    transpose_rows(wa_scr,wts_ref.at[0])
    for cp in wcp: cp.start()
    for cp in cb: cp.start()
    d3.start(); o3.start()
    for j in range(NB):
        for i in range(G-1): arrived(ain_ref.at[j*G+pidx[i]],ain_r.at[j*G+pidx[i]])
    rowi=lax.broadcasted_iota(jnp.int32,(BQ,BQ),0)
    coli=lax.broadcasted_iota(jnp.int32,(BQ,BQ),1)
    hs=[slice(h*HD,(h+1)*HD) for h in range(hb)]
    CH=512; per=CH//n; sub=BQ//n

    def block(m,_):
        @pl.when(m==1)
        def _():
            arrived(wts_ref.at[1],wt_r.at[1])
            for i in range(2*Z): arrived(wb_scr.at[i],b_r.at[i])
            transpose_rows(wb_scr,w2_scr.at[0])
            for cp in w2cp: cp.start()
            share(0)
            arrived(d3_scr,do_r.at[0])
            for cp in cc: cp.start()
        @pl.when(m==2)
        def _():
            arrived(wts_ref.at[2],wt_r.at[2])
            arrived(o3_scr,do_r.at[1])
            for cp in cd: cp.start()
        @pl.when(m==3)
        def _():
            for i in range(2*Z): arrived(wc_scr.at[i],c_r.at[i])
            transpose_rows(wc_scr,wts_ref.at[3])
            spread_start(cots)
        for c in range(L//CH):
            cs=slice(c*CH,(c+1)*CH)
            r=dot(wts_ref[m],ain_ref[c*per:(c+1)*per].reshape(CH,D),NT)
            qt_ref[m,:,cs]=(r[:W]*pd_ref[:,:1]).astype(bf16)
            kt_ref[m,:,cs]=r[W:2*W].astype(bf16)
            vt_scr[:,cs]=r[2*W:].astype(bf16)
            for h in range(hb):
                k_ref[m*hb+h,cs,:]=r[W+h*HD:W+(h+1)*HD].T.astype(bf16)
                v_ref[m*hb+h,cs,:]=r[2*W+h*HD:2*W+(h+1)*HD].T.astype(bf16)
        units=[(i,h) for i in range(nb) for h in range(hb)]
        st={}
        def phase_a(u):
            i,h=units[u]; c0=i*BQ
            qi=qt_ref[m,hs[h],c0:c0+BQ]
            sq=segq_ref[:,c0:c0+BQ]
            m8=None
            for j in range(i+1):
                t=dot(k_ref[m*hb+h,j*BQ:(j+1)*BQ,:],qi)
                sk=segk_ref[j*BQ:(j+1)*BQ,:]
                ok=jnp.concatenate([sk]*(BQ//128),axis=1)==sq
                if j==i: ok=ok&(rowi<=coli)
                t=jnp.where(ok,t,NEG)
                s_scr[u%2,j*BQ:(j+1)*BQ,:]=t
                mm=t.reshape(BQ//8,8,BQ).max(0)
                m8=mm if m8 is None else jnp.maximum(m8,mm)
                yield
            st[u]=m8.max(0,keepdims=True)
        def phase_b(u):
            i,h=units[u]; c0=i*BQ
            mx=st[u]; l8=None; acc=None
            for j in range(i+1):
                p=jnp.exp(s_scr[u%2,j*BQ:(j+1)*BQ,:]-mx)
                ll=p.reshape(BQ//8,8,BQ).sum(0)
                l8=ll if l8 is None else l8+ll
                pv=dot(vt_scr[hs[h],j*BQ:(j+1)*BQ],p.astype(bf16))
                acc=pv if acc is None else acc+pv
                yield
            l=l8.sum(0,keepdims=True)
            o=(acc*(1.0/l)).astype(bf16)
            for t in range(sub): ot_ref[i*sub+t,m,hs[h],:]=o[:,t*n:(t+1)*n]
            lse_ref[m*hb+h,:,c0:c0+BQ]=mx+jnp.log(l)
        merge(phase_a(0))
        for u in range(len(units)):
            gs=[phase_b(u)]
            if u+1<len(units): gs=[phase_a(u+1)]+gs
            merge(*gs)
        for b in range(NB):
            mix_ref[b,0,m]=ot_ref[b*G+g0,m]
            for i in range(G-1):
                rcopy(ot_ref.at[b*G+pidx[i],m],mix_ref.at[b,back[i],m],mix_s.at[i,b,m],mix_r.at[back[i],b,m],pdev[i]).start()
        return 0
    lax.fori_loop(0,4,block,0)
    for m in (1,2):
        arrived(w2_scr.at[m],w2_r.at[m])
        share(m)
    for i in range(2*Z): arrived(wd_scr.at[i],dd_r.at[i])
    transpose_rows(wd_scr,w2_scr.at[3])
    share(3)
    for j in range(NB): arrived(coto_ref.at[j],cot_r.at[j])
    for i in range(G-1):
        for b in range(NB):
            for m in range(4):
                arrived(mix_ref.at[b,fore[i],m],mix_r.at[fore[i],b,m])
                rcopy(ot_ref.at[b*G+pidx[i],m],mix_ref.at[b,back[i],m],mix_s.at[i,b,m],mix_r.at[back[i],b,m],pdev[i]).wait_send()
        for m in range(4): arrived(w2o_ref.at[fore[i],m],gr_r.at[fore[i],m])
    for m in range(4):
        loc[m].wait()
        for cp in grp[m]: cp.wait_send()
    for cps in (ca,cb,cc,cd):
        for cp in cps[1:]: cp.wait_send()
    for cp in wcp+w2cp+ains+[d3,o3]: cp.wait_send()
    spread_sent(toks); spread_sent(cots)

def forward(Z, C, tokens, w1h, w2h, cot, gain, pd, segk, segq):
    R,Pn,D=tokens.shape; G=2*C; n=Pn//G; _,Dd,nC=w1h.shape; NB=4*C
    L=segq.shape[1]; W=pd.shape[0]; hb=W//HD
    V=pl.BlockSpec(memory_space=pltpu.VMEM); A=pl.BlockSpec(memory_space=pl.ANY)
    S=lambda *sh: pltpu.SemaphoreType.DMA(sh) if sh else pltpu.SemaphoreType.DMA
    B=lambda *sh: jax.ShapeDtypeStruct(sh,bf16)
    col=pltpu.VMEM((2*Z,Dd,nC),bf16); half=pltpu.VMEM((2,Dd,nC),bf16)
    return pl.pallas_call(functools.partial(fwd_kernel,Z,C,n),
        out_shape=(B(NB,n,D),B(NB*G,n,D),B(4,nC,D),B(G,4,nC,D),B(NB,n,D),B(NB,G,4,W,n),B(4,W,L),B(4,W,L),
                   B(4*hb,L,HD),B(4*hb,L,HD),B(NB*G,4,W,n),jax.ShapeDtypeStruct((4*hb,1,L),f32)),
        in_specs=[A,A,A,A,V,V,V,V],out_specs=(V,V,V,A,A,V,V,V,V,V,V,V),
        scratch_shapes=[col,col,col,col,half,half,pltpu.VMEM((4,nC,D),bf16),pltpu.VMEM((W,L),bf16),pltpu.VMEM((2,L,BQ),f32),
            S(NB),S(NB),S(G-1,NB),S(NB*G),S(2*Z),S(2*Z),S(2*Z),S(2*Z),S(2*Z),S(2*Z),S(2*Z),S(2*Z),S(),S(),S(2),
            S(4),S(4),S(4),S(4),S(G-1,4),S(G,4),S(4),S(NB),S(NB),S(G-1,NB,4),S(G,NB,4)],
        compiler_params=pltpu.CompilerParams(collective_id=0,has_side_effects=True,vmem_limit_bytes=60*2**20),
        cost_estimate=pl.CostEstimate(flops=3*10**10,bytes_accessed=10**8,transcendentals=0),
        name="forward")(tokens,w1h,w2h,cot,gain[None],pd,segk,segq)


def assemble_kernel(Z, zi_ref, *refs):
    parts,out,scr=refs[:Z],refs[Z],refs[Z+1]
    for j in range(Z):
        scr[zi_ref[0]^j]=parts[j][...]
    transpose_rows(scr,out)

def assemble(zi, parts):
    Z=len(parts); rows,nC=parts[0].shape
    V=pl.BlockSpec(memory_space=pltpu.VMEM)
    return pl.pallas_call(functools.partial(assemble_kernel,Z),out_shape=jax.ShapeDtypeStruct((nC,Z*rows),bf16),
        in_specs=[pl.BlockSpec(memory_space=pltpu.SMEM)]+[V]*Z,out_specs=V,
        scratch_shapes=[pltpu.VMEM((Z,rows,nC),bf16)],
        compiler_params=pltpu.CompilerParams(vmem_limit_bytes=56*2**20),name="assemble")(zi[None],*parts)

def split_kernel(Z, nr, zi_ref, own_ref, *refs):
    recvs,outs,scr=refs[:nr],refs[nr:nr+Z],refs[nr+Z]
    nC,D=own_ref.shape; rows=D//Z
    per=max(1,640//rows)
    for i in range(Z//per):
        ls=slice(i*per*rows,(i+1)*per*rows)
        t=own_ref[:,ls].astype(f32)
        for r in recvs: t=t+r[:,ls].astype(f32)
        scr[i*per:(i+1)*per]=t.T.reshape(per,rows,nC)
    for j in range(Z):
        outs[j][...]=scr[zi_ref[0]^j].astype(outs[j].dtype)

def split(zi, Z, own, recvs):
    nC,D=own.shape
    V=pl.BlockSpec(memory_space=pltpu.VMEM)
    return pl.pallas_call(functools.partial(split_kernel,Z,len(recvs)),
        out_shape=tuple(jax.ShapeDtypeStruct((D//Z,nC),f32 if j==0 else bf16) for j in range(Z)),
        in_specs=[pl.BlockSpec(memory_space=pltpu.SMEM)]+[V]*(1+len(recvs)),out_specs=(V,)*Z,
        scratch_shapes=[pltpu.VMEM((Z,D//Z,nC),f32)],
        compiler_params=pltpu.CompilerParams(vmem_limit_bytes=56*2**20),name="split")(zi[None],own,*recvs)


scale_base = 1.442695041

def silu_slope(u):
    sg=jax.nn.sigmoid(u)
    return sg*(1.0+u*(1.0-sg))

def make_local(Z, C):
    sizes=(Z,2,4,C)
    coords=list(itertools.product(*[range(n) for n in sizes]))
    lin={c:i for i,c in enumerate(coords)}
    G=2*C
    def pp(x, fn):
        return lax.ppermute(x, AXES, [(lin[c], lin[fn(*c)]) for c in coords])
    def unxor(parts, idx):
        b=1
        while b<len(parts):
            c=(idx & b)!=0
            parts=[jnp.where(c,parts[a^b],parts[a]) for a in range(len(parts))]
            b*=2
        return parts
    def allsum(v):
        for ax,n in enumerate(sizes):
            b=1
            while b<n:
                v=v+pp(v,lambda *c,ax=ax,b=b: tuple(ci^b if i==ax else ci for i,ci in enumerate(c)))
                b*=2
        return v
    def gsend(x, gamma):
        gc,gs=divmod(gamma,C)
        return pp(x, lambda z,k,q,s: (z,k^gc,q,s^gs))

    def after(x, *deps):
        return lax.optimization_barrier((x,)+deps)[0] if deps else x

    def local(tokens, segments, attn_gain, w_query, w_key, w_value, w_out, query_scale, mlp_gain, w_up, w_down, cotangent):
        zi,k,qi,si=[lax.axis_index(a) for a in AXES]
        R,Pn,D=tokens.shape; L=segments.shape[1]
        n=Pn//G
        N=4*C*n
        Dd,Ct=w_query.shape; Ch=Ct//2; W=Ch; hb=W//HD
        g0=k*C+si
        k0=k==0
        q0=2*(k^(qi//2))+qi%2
        rounds=list(itertools.product(range(2),range(2),range(C)))

        def spread(x):
            got=[]
            for eta,rho,sg in rounds:
                r=(qi%2)^rho; h=(qi//2)^k^eta; s2=si^sg
                piece=lax.dynamic_slice(x,(r,(h*C+s2)*n,0),(1,n,D))[0]
                got.append(pp(piece, lambda z,kk,q,s: (z,(q//2)^kk^eta,2*kk+((q%2)^rho),s^sg)))
            return jnp.concatenate(unxor(got,q0*C+si),0)
        def collect(y):
            parts=unxor([y[i*n:(i+1)*n] for i in range(4*C)],q0*C+si)
            got=[]
            for idx,(eta,rho,sg) in enumerate(rounds):
                got.append(pp(parts[idx], lambda z,kk,q,s: (z,q//2,(2*(kk^(q//2))+q%2)^(2*eta+rho),s^sg)))
            ab=unxor(got,((qi//2)^k)*(2*C)+(qi%2)*C+si)
            rows=[jnp.concatenate([ab[(h*2+r)*C+s2] for h in range(2) for s2 in range(C)],0) for r in range(R)]
            return jnp.stack(rows,0)
        def halves(shards):
            return jnp.stack([jnp.concatenate([w[:,h*Ch:(h+1)*Ch] for w in shards],1) for h in range(2)],0)
        def gatherD(w2h, *deps):
            keep=jnp.where(k0,w2h[0],w2h[1]); send=jnp.where(k0,w2h[1],w2h[0])
            recv=pp(send,lambda z,kk,q,s:(z,1-kk,q,s))
            rows=jnp.concatenate([jnp.where(k0,keep,recv),jnp.where(k0,recv,keep)],0)
            rows=after(rows,*deps)
            parts=[rows]+[pp(rows,lambda z,kk,q,s:(z^j,kk,q,s)) for j in range(1,Z)]
            return assemble(zi,parts),parts[-1]
        def chip(x, m):
            return pp(x,lambda z,kk,q,s:(z,kk,q^m,s))
        def reduceZ(rel):
            tot=rel[0]
            for j in range(1,Z):
                tot=tot+pp(rel[j],lambda z,kk,q,s:(z^j,kk,q,s)).astype(f32)
            return tot
        def finish(tot, nw):
            keep=jnp.where(k0,tot[:Dd],tot[Dd:]); send=jnp.where(k0,tot[Dd:],tot[:Dd])
            recv=pp(send,lambda z,kk,q,s:(z,1-kk,q,s))
            lo=jnp.where(k0,keep,recv); hi=jnp.where(k0,recv,keep)
            return [jnp.concatenate([lo[:,i*Ch:(i+1)*Ch],hi[:,i*Ch:(i+1)*Ch]],1) for i in range(nw)]
        def tok_lanes(xT):
            return [jnp.concatenate([xT[:,(b*G+g)*n:(b*G+g+1)*n] for b in range(4*C)],1) for g in range(G)]
        def tok_rows_join(parts):
            return jnp.concatenate([parts[g][b*n:(b+1)*n] for b in range(4*C) for g in range(G)],0)
        def tok_lanes_join(parts):
            return jnp.concatenate([parts[g][:,b*n:(b+1)*n] for b in range(4*C) for g in range(G)],1)

        seg_o=pp(segments,lambda z,kk,q,s:(z,1-kk,q,s))
        seg2=jnp.where(k==qi//2,segments,seg_o)
        seg=jnp.where(qi%2==0,seg2[0],seg2[1])
        first=seg[::BQ]; last=seg[BQ-1::BQ]
        segk=jnp.broadcast_to(seg[:,None],(L,128)); segq=seg[None]
        per_dim=scale_base/math.sqrt(HD)*jax.nn.softplus(query_scale)
        pd=jnp.broadcast_to(jnp.tile(per_dim,hb)[:,None],(W,128))
        w1h=halves([w_query,w_key,w_value]); w2h=halves([w_out.T,w_up,w_down.T])
        xo,ain,wts,w2o,cot,mix,qt,kt,kn,vn,ot,lse=forward(Z,C,tokens,w1h,w2h,cotangent,attn_gain,pd,segk,segq)
        x=xo.reshape(N,D).astype(f32); ain=ain.reshape(L,D); cot=cot.reshape(N,D)
        otT=jnp.concatenate([ot[i] for i in range(4*C*G)],-1)
        saved=[(qt[m],kt[m],kn[m*hb:(m+1)*hb],vn[m*hb:(m+1)*hb],otT[m],lse[m*hb:(m+1)*hb]) for m in range(4)]
        mixT_own=jnp.concatenate([mix[b].reshape(G*4*W,n) for b in range(4*C)],1)
        wo,wu,wd=[w2o[:,:,i*Ch:(i+1)*Ch].reshape(G*4*Ch,D) for i in range(3)]

        inv1=lax.rsqrt(jnp.mean(x*x,axis=-1,keepdims=True)+norm_eps)
        attn=dot(mixT_own,wo,TN)
        middle=x+attn
        inv2=lax.rsqrt(jnp.mean(middle*middle,axis=-1,keepdims=True)+norm_eps)
        norm2=middle*inv2
        mlp_in=(norm2*mlp_gain).astype(bf16)
        up=dot(mlp_in,wu,NT)
        hid=jax.nn.silu(up).astype(bf16)
        block=(middle+dot(hid,wd)).astype(bf16)
        block_out=collect(block)
        gup=(dot(cot,wd,NT)*silu_slope(up)).astype(bf16)
        gmlp=dot(gup,wu)
        dn=gmlp*mlp_gain
        gmid=cot.astype(f32)+inv2*(dn-norm2*jnp.mean(dn*norm2,axis=-1,keepdims=True))
        mlp_gain_part=jnp.sum(gmlp*norm2,axis=0)
        gattn=gmid.astype(bf16)
        gmixT=dot(wo,gattn,NT).astype(bf16)
        K=gmixT.shape[0]//G
        doT=tok_lanes_join(unxor([gmixT[:K]]+[gsend(gmixT[g*K:(g+1)*K],g) for g in range(1,G)],g0))
        g3=[dot(mixT_own,gattn),dot(gup,mlp_in,TN),dot(hid,cot,TN)]

        K4=4*Ch
        mine=list(g3)
        mine=[t[:K4] for t in g3]
        for g in range(1,G):
            for i,t in enumerate(g3):
                mine[i]=mine[i]+gsend(t[g*K4:(g+1)*K4].astype(bf16),g).astype(f32)
        fb=[jnp.concatenate([t[m*Ch:(m+1)*Ch] for t in mine],0) for m in range(4)]
        gT=[None]*4; dW=[None]*4; sc=0.0
        def bwd(m,*deps):
            qt,kt,kn,vn,ot,lse=saved[m]
            qt=after(qt,*deps)
            gT[m],s_=attn_bwd(first,last,qt,kt,kn,vn,ot,doT[m*W:(m+1)*W],lse,pd,segk,segq)
            return s_[:,0]
        sc=sc+bwd(3)
        dW[3]=dot(gT[3],ain).astype(bf16)
        fr=[chip(fb[m].astype(bf16),m) for m in (1,2)]
        f3=reduceZ(split(zi,Z,fb[3],[]))
        sc=sc+bwd(1,gT[3],fb[0])
        dW[1]=dot(gT[1],ain).astype(bf16)
        q1=chip(dW[1],1)
        f0=reduceZ(split(zi,Z,fb[0],fr))
        f3=chip(f3.astype(bf16),3)
        sc=sc+bwd(2,gT[1],fr[0],fr[1])
        dW[2]=dot(gT[2],ain).astype(bf16)
        q2=chip(dW[2],2)
        q3=reduceZ(split(zi,Z,after(dW[3],f0),[]))
        sc=sc+bwd(0,gT[2],f0,q1)
        q3=chip(after(q3,gT[0]).astype(bf16),3)
        g_out,g_up,g_down=finish(f0+f3.astype(f32),3)
        grad_out=g_out.T; grad_up=g_up; grad_down=g_down.T
        gTall=jnp.concatenate(gT,0); wtall=jnp.concatenate(wts,0)
        grel=unxor(tok_lanes(gTall),g0)
        gain=0.0
        for g in range(1,G):
            gain=gain+gsend(dot(grel[g],wtall,TN).astype(bf16),g).astype(f32)
        gain=gain+dot(grel[0],wtall,TN)
        norm1=x*inv1
        dn1=gain*attn_gain
        gin=gmid+inv1*(dn1-norm1*jnp.mean(dn1*norm1,axis=-1,keepdims=True))
        attn_gain_part=jnp.sum(gain*norm1,axis=0)
        ginb=gin.astype(bf16)
        input_grad=collect(ginb).astype(f32)
        dW[0]=dot(after(gT[0],ginb),ain)
        q0s=reduceZ(split(zi,Z,dW[0],[q1,q2]))
        grad_query,grad_key,grad_value=finish(q0s+q3.astype(f32),3)

        scale_part=jnp.sum(sc.reshape(hb,HD),axis=0)*(scale_base/math.sqrt(HD))*jax.nn.sigmoid(query_scale)
        grad_mlp_gain=allsum(mlp_gain_part)
        late=allsum(jnp.concatenate([attn_gain_part,scale_part]))
        return (block_out,input_grad,late[:D],grad_query,grad_key,grad_value,grad_out,late[D:],grad_mlp_gain,grad_up,grad_down)
    return local

def solution(mesh):
    dp,T=mesh.shape["dp"],mesh.shape["tensor"]
    Z,C=dp//2,T//4
    fine=Mesh(mesh.devices.reshape(Z,2,4,C),AXES)
    dpx=("zz","core"); tx=("q","s")
    in_specs=(P(dpx,tx,None),P(dpx,None),P(),P(dpx,tx),P(dpx,tx),P(dpx,tx),P(tx,dpx),P(),P(),P(dpx,tx),P(tx,dpx),P(dpx,tx,None))
    out_specs=(P(dpx,tx,None),P(dpx,tx,None),P(),P(dpx,tx),P(dpx,tx),P(dpx,tx),P(tx,dpx),P(),P(),P(dpx,tx),P(tx,dpx))
    return jax.shard_map(make_local(Z,C),mesh=fine,in_specs=in_specs,out_specs=out_specs,check_vma=False)
```

```python
import functools
import itertools
import math
import jax, jax.numpy as jnp
from jax import lax
from jax.experimental import pallas as pl
from jax.experimental.pallas import tpu as pltpu
from jax.sharding import Mesh, PartitionSpec as P

AXES=("zz","core","q","s")
norm_eps = 1e-06
HD=80
BQ=256
NEG=-1e30
f32=jnp.float32; bf16=jnp.bfloat16
NT=(((1,),(1,)),((),()))
NN=(((1,),(0,)),((),()))
TN=(((0,),(0,)),((),()))
def dot(a,b,dims=NN): return lax.dot_general(a,b,dims,preferred_element_type=f32)

def merge(*gens):
    gens=list(gens)
    while gens:
        for g in list(gens):
            try: next(g)
            except StopIteration: gens.remove(g)

def fwd_kernel(hb, first_ref, last_ref, x_ref, wt_ref, pd_ref, segk_ref, segq_ref,
               qt_ref, kt_ref, k_ref, v_ref, ot_ref, lse_ref, vt_scr, s_scr, m_scr, l_scr, acc_scr):
    L=x_ref.shape[0]; nb=L//BQ; W=hb*HD
    CH=512
    for c in range(L//CH):
        cs=slice(c*CH,(c+1)*CH)
        r=dot(wt_ref[...],x_ref[cs,:],NT)
        qt_ref[:,cs]=(r[:W]*pd_ref[:,:1]).astype(bf16)
        kt_ref[:,cs]=r[W:2*W].astype(bf16)
        vt_scr[:,cs]=r[2*W:].astype(bf16)
        for h in range(hb):
            k_ref[h,cs,:]=r[W+h*HD:W+(h+1)*HD].T.astype(bf16)
            v_ref[h,cs,:]=r[2*W+h*HD:2*W+(h+1)*HD].T.astype(bf16)
    rowi=lax.broadcasted_iota(jnp.int32,(BQ,BQ),0)
    coli=lax.broadcasted_iota(jnp.int32,(BQ,BQ),1)
    hs=[slice(h*HD,(h+1)*HD) for h in range(hb)]
    single = first_ref[0]==last_ref[nb-1]
    @pl.when(single)
    def _():
        units=[(i,h) for i in range(nb) for h in range(hb)]
        st={}
        def phase_a(u):
            i,h=units[u]; c0=i*BQ
            qi=qt_ref[hs[h],c0:c0+BQ]
            m8=None
            for j in range(i+1):
                s=dot(k_ref[h,j*BQ:(j+1)*BQ,:],qi)
                if j==i: s=jnp.where(rowi<=coli,s,NEG)
                s_scr[u%2,j*BQ:(j+1)*BQ,:]=s
                mm=s.reshape(BQ//8,8,BQ).max(0)
                m8=mm if m8 is None else jnp.maximum(m8,mm)
                yield
            st[u]=m8.max(0,keepdims=True)
        def phase_b(u):
            i,h=units[u]; c0=i*BQ
            m=st[u]; l8=None; acc=None
            for j in range(i+1):
                p=jnp.exp(s_scr[u%2,j*BQ:(j+1)*BQ,:]-m)
                ll=p.reshape(BQ//8,8,BQ).sum(0)
                l8=ll if l8 is None else l8+ll
                pv=dot(vt_scr[hs[h],j*BQ:(j+1)*BQ],p.astype(bf16))
                acc=pv if acc is None else acc+pv
                yield
            l=l8.sum(0,keepdims=True)
            ot_ref[hs[h],c0:c0+BQ]=(acc*(1.0/l)).astype(bf16)
            lse_ref[h,:,c0:c0+BQ]=m+jnp.log(l)
        merge(phase_a(0))
        for u in range(len(units)):
            gs=[phase_b(u)]
            if u+1<len(units): gs=[phase_a(u+1)]+gs
            merge(*gs)
    @pl.when(jnp.logical_not(single))
    def _():
        def qblock(i,_):
            c0=pl.multiple_of(i*BQ,BQ)
            def cnt(j,a): return a+jnp.where(last_ref[j]<first_ref[i],1,0)
            j0=lax.fori_loop(0,i,cnt,jnp.int32(0))
            m_scr[...]=jnp.full_like(m_scr,NEG); l_scr[...]=jnp.zeros_like(l_scr); acc_scr[...]=jnp.zeros_like(acc_scr)
            def step(j,_):
                r0=pl.multiple_of(j*BQ,BQ)
                sk=segk_ref[pl.ds(r0,BQ),:]
                ok=(jnp.concatenate([sk]*(BQ//128),axis=1)==segq_ref[:,pl.ds(c0,BQ)])&(rowi+r0<=coli+c0)
                for h in range(hb):
                    s=dot(k_ref[h,pl.ds(r0,BQ),:],qt_ref[hs[h],pl.ds(c0,BQ)])
                    s=jnp.where(ok,s,NEG)
                    mo=m_scr[h]
                    m=jnp.maximum(mo,s.max(0,keepdims=True))
                    al=jnp.exp(mo-m)
                    p=jnp.where(ok,jnp.exp(s-m),0.0)
                    l_scr[h]=l_scr[h]*al+p.sum(0,keepdims=True)
                    acc_scr[hs[h],:]=acc_scr[hs[h],:]*al+dot(vt_scr[hs[h],pl.ds(r0,BQ)],p.astype(bf16))
                    m_scr[h]=m
                return 0
            lax.fori_loop(j0,i+1,step,0)
            for h in range(hb):
                ot_ref[hs[h],pl.ds(c0,BQ)]=(acc_scr[hs[h],:]*(1.0/l_scr[h])).astype(bf16)
                lse_ref[h,:,pl.ds(c0,BQ)]=m_scr[h]+jnp.log(l_scr[h])
            return 0
        lax.fori_loop(0,nb,qblock,0)

def attn_fwd(first,last,x,wt,pd,segk,segq):
    L,D=x.shape; W=wt.shape[0]//3; hb=W//HD
    V=pl.BlockSpec(memory_space=pltpu.VMEM); S=pl.BlockSpec(memory_space=pltpu.SMEM)
    hd=jax.ShapeDtypeStruct((hb,L,HD),bf16); td=jax.ShapeDtypeStruct((W,L),bf16)
    flops=2*L*D*3*W+2*2*L*L//2*256*hb
    return pl.pallas_call(functools.partial(fwd_kernel,hb),
        out_shape=(td,td,hd,hd,td,jax.ShapeDtypeStruct((hb,1,L),f32)),
        in_specs=[S,S,V,V,V,V,V],out_specs=(V,)*6,
        scratch_shapes=[pltpu.VMEM((W,L),bf16),pltpu.VMEM((2,L,BQ),f32),
            pltpu.VMEM((hb,1,BQ),f32),pltpu.VMEM((hb,1,BQ),f32),pltpu.VMEM((W,BQ),f32)],
        compiler_params=pltpu.CompilerParams(vmem_limit_bytes=56*2**20),
        cost_estimate=pl.CostEstimate(flops=flops,bytes_accessed=x.size*2+wt.size*2+4*L*W*2,transcendentals=L*L//2*hb),
        name="attn_fwd")(first,last,x,wt,pd,segk,segq)

def bwd_kernel(hb, first_ref, last_ref, qt_ref, kt_ref, k_ref, v_ref, ot_ref, dot_ref, lse_ref, pd_ref, segk_ref, segq_ref,
               g_ref, sc_ref, p_scr, ds_scr, dq_scr, dl_scr, dv_scr, dk_scr):
    W=hb*HD; L=qt_ref.shape[1]; nb=L//BQ
    rowi=lax.broadcasted_iota(jnp.int32,(BQ,BQ),0)
    coli=lax.broadcasted_iota(jnp.int32,(BQ,BQ),1)
    hs=[slice(h*HD,(h+1)*HD) for h in range(hb)]
    for h in range(hb):
        dl_scr[h]=(dot_ref[hs[h],:].astype(f32)*ot_ref[hs[h],:].astype(f32)).sum(0,keepdims=True)
    single = first_ref[0]==last_ref[nb-1]
    @pl.when(single)
    def _():
        units=[(j,h,i) for j in range(nb) for h in range(hb) for i in range(j,nb)]
        acc={}
        def phase_a(u):
            j,h,i=units[u]; js=slice(j*BQ,(j+1)*BQ); cs=slice(i*BQ,(i+1)*BQ)
            H2=BQ//2
            for a in range(2):
                ks=slice(j*BQ+a*H2,j*BQ+(a+1)*H2)
                s=dot(k_ref[h,ks,:],qt_ref[hs[h],cs])
                dp=dot(v_ref[h,ks,:],dot_ref[hs[h],cs])
                if j==i: s=jnp.where(rowi[a*H2:(a+1)*H2]<=coli[a*H2:(a+1)*H2],s,NEG)
                p=jnp.exp(s-lse_ref[h,:,cs])
                p_scr[u%2,a*H2:(a+1)*H2,:]=p.astype(bf16)
                ds_scr[u%2,a*H2:(a+1)*H2,:]=(p*(dp-dl_scr[h,:,cs])).astype(bf16)
                yield
        def phase_b(u):
            j,h,i=units[u]; js=slice(j*BQ,(j+1)*BQ); cs=slice(i*BQ,(i+1)*BQ)
            p=p_scr[u%2]; ds=ds_scr[u%2]
            dv=dot(dot_ref[hs[h],cs],p,NT); dk=dot(qt_ref[hs[h],cs],ds,NT)
            if i==j: dv_scr[h]=dv; dk_scr[h]=dk
            else: dv_scr[h]+=dv; dk_scr[h]+=dk
            yield
            dq=dot(kt_ref[hs[h],js],ds)
            if j==0: dq_scr[hs[h],cs]=dq
            else: dq_scr[hs[h],cs]+=dq
            if i==nb-1:
                g_ref[W+h*HD:W+(h+1)*HD,js]=dk_scr[h].astype(bf16)
                g_ref[2*W+h*HD:2*W+(h+1)*HD,js]=dv_scr[h].astype(bf16)
            yield
        merge(phase_a(0))
        for u in range(len(units)):
            gs=[phase_b(u)]
            if u+1<len(units): gs=[phase_a(u+1)]+gs
            merge(*gs)
    @pl.when(jnp.logical_not(single))
    def _():
        dq_scr[...]=jnp.zeros_like(dq_scr)
        def kblock(j,_):
            r0=pl.multiple_of(j*BQ,BQ)
            def cnt(i,a): return a+jnp.where(first_ref[i]<=last_ref[j],1,0)
            iend=lax.fori_loop(j,nb,cnt,j)
            dv_scr[...]=jnp.zeros_like(dv_scr); dk_scr[...]=jnp.zeros_like(dk_scr)
            sk=segk_ref[pl.ds(r0,BQ),:]
            sk=jnp.concatenate([sk]*(BQ//128),axis=1)
            def step(i,_):
                c0=pl.multiple_of(i*BQ,BQ); cs=pl.ds(c0,BQ)
                ok=(sk==segq_ref[:,cs])&(rowi+r0<=coli+c0)
                for h in range(hb):
                    qt=qt_ref[hs[h],cs]; do=dot_ref[hs[h],cs]
                    s=dot(k_ref[h,pl.ds(r0,BQ),:],qt)
                    dp=dot(v_ref[h,pl.ds(r0,BQ),:],do)
                    p=jnp.exp(jnp.where(ok,s-lse_ref[h,:,cs],NEG))
                    ds=(p*(dp-dl_scr[h,:,cs])).astype(bf16)
                    dv_scr[h]+=dot(do,p.astype(bf16),NT)
                    dk_scr[h]+=dot(qt,ds,NT)
                    dq_scr[hs[h],cs]+=dot(kt_ref[hs[h],pl.ds(r0,BQ)],ds)
                return 0
            lax.fori_loop(j,iend,step,0)
            for h in range(hb):
                g_ref[W+h*HD:W+(h+1)*HD,pl.ds(r0,BQ)]=dk_scr[h].astype(bf16)
                g_ref[2*W+h*HD:2*W+(h+1)*HD,pl.ds(r0,BQ)]=dv_scr[h].astype(bf16)
            return 0
        lax.fori_loop(0,nb,kblock,0)
    dq=dq_scr[...]
    g_ref[:W,:]=(dq*pd_ref[:,:1]).astype(bf16)
    sc=(dq*qt_ref[...].astype(f32)).sum(1,keepdims=True)
    sc_ref[...]=jnp.broadcast_to(sc/pd_ref[:,:1],sc_ref.shape)

def attn_bwd(first,last,qt,kt,k,v,ot,dot_,lse,pd,segk,segq):
    W,L=qt.shape; hb=W//HD
    V=pl.BlockSpec(memory_space=pltpu.VMEM); S=pl.BlockSpec(memory_space=pltpu.SMEM)
    flops=5*2*L*L//2*256*hb
    return pl.pallas_call(functools.partial(bwd_kernel,hb),
        out_shape=(jax.ShapeDtypeStruct((3*W,L),bf16),jax.ShapeDtypeStruct((W,128),f32)),
        in_specs=[S,S]+[V]*10,out_specs=(V,)*2,
        scratch_shapes=[pltpu.VMEM((2,BQ,BQ),bf16),pltpu.VMEM((2,BQ,BQ),bf16),pltpu.VMEM((W,L),f32),
            pltpu.VMEM((hb,1,L),f32),pltpu.VMEM((hb,HD,BQ),f32),pltpu.VMEM((hb,HD,BQ),f32)],
        compiler_params=pltpu.CompilerParams(vmem_limit_bytes=56*2**20),
        cost_estimate=pl.CostEstimate(flops=flops,bytes_accessed=8*L*W*2,transcendentals=L*L//2*hb),
        name="attn_bwd")(first,last,qt,kt,k,v,ot,dot_,lse,pd,segk,segq)


MESH=pl.DeviceIdType.MESH

def rcopy(src,dst,ss,rs,dev):
    return pltpu.make_async_remote_copy(src_ref=src,dst_ref=dst,send_sem=ss,recv_sem=rs,device_id=dev,device_id_type=MESH)

def transpose_rows(src, dst):
    P_,rows,cols=src.shape
    per=max(1,640//rows)
    for i in range(P_//per):
        dst[:,i*per*rows:(i+1)*per*rows]=src[i*per:(i+1)*per].reshape(per*rows,cols).T

def partner(q, m):
    return (q,q+1-2*lax.rem(q,2),lax.rem(q+2,4),3-q)[m]

def greet(Z, C):
    z,k,q,s=[lax.axis_index(a) for a in AXES]
    bar=pltpu.get_barrier_semaphore()
    plane=list(itertools.product(range(2),range(4),range(C)))[1:]
    column=[(j,a) for j in range(1,Z) for a in range(2)]
    for a,b,c in plane:
        pl.semaphore_signal(bar,inc=1,device_id=(z,lax.rem(k+a,2),lax.rem(q+b,4),lax.rem(s+c,C)),device_id_type=MESH)
    for j,a in column:
        pl.semaphore_signal(bar,inc=1,device_id=(lax.rem(z+j,Z),lax.rem(k+a,2),q,s),device_id_type=MESH)
    pl.semaphore_wait(bar,len(plane)+len(column))

def col_copies(Z, src, dst, ss, rs):
    z,k,q,s=[lax.axis_index(a) for a in AXES]
    out=[]
    for j in range(Z):
        for a in range(2):
            kk=lax.rem(k+a,2)
            if j==0 and a==0: out.append(pltpu.make_async_copy(src.at[k],dst.at[2*z+k],rs.at[2*z+k]))
            else: out.append(rcopy(src.at[kk],dst.at[2*z+k],ss.at[j*2+a],rs.at[2*z+k],(lax.rem(z+j,Z),kk,q,s)))
    return out

def spread_copies(C, n, src, dst, ss, rs):
    z,k,q,s=[lax.axis_index(a) for a in AXES]
    out=[]
    for r in range(2):
        for h in range(2):
            for s2 in range(C):
                i=(r*2+h)*C+s2
                piece=src.at[r,pl.ds((h*C+s2)*n,n),:]
                out.append(((k==h)&(q==2*k+r)&(s==s2),pltpu.make_async_copy(piece,dst.at[q*C+s],rs.at[q*C+s]),
                            rcopy(piece,dst.at[q*C+s],ss.at[i],rs.at[q*C+s],(z,h,2*k+r,s2))))
    return out

def spread_start(cps):
    for mine,loc,cp in cps:
        @pl.when(mine)
        def _(loc=loc): loc.start()
        @pl.when(jnp.logical_not(mine))
        def _(cp=cp): cp.start()

def spread_sent(cps):
    for mine,loc,cp in cps:
        @pl.when(jnp.logical_not(mine))
        def _(cp=cp): cp.wait_send()

def arrived(ref, sem):
    z,k,q,s=[lax.axis_index(a) for a in AXES]
    rcopy(ref,ref,sem,sem,(z,1-k,q,s)).wait_recv()

def fwd_kernel(Z, C, n, x_ref, w1_ref, w2_ref, cot_ref, gain_ref, pd_ref, segk_ref, segq_ref,
               xo_ref, ain_ref, wts_ref, w2o_ref, coto_ref, mix_ref, qkv_ref, ot_ref, lse_ref,
               wa_scr, wb_scr, wc_scr, wd_scr, d3_scr, o3_scr, w2_scr, k_scr, s_scr,
               tok_s, tok_r, ain_s, ain_r, a_s, a_r, b_s, b_r, c_s, c_r, dd_s, dd_r, d3_s, o3_s, do_r,
               wt_s, wt_r, w2_s, w2_r, gr_s, gr_r, loc_s, cot_s, cot_r, mix_s, mix_r):
    z,k,q,s=[lax.axis_index(a) for a in AXES]
    G=2*C; g0=k*C+s; NB=4*C
    D=gain_ref.shape[1]; L=segq_ref.shape[1]; W=pd_ref.shape[0]; hb=W//HD; nb=L//BQ
    peers=list(itertools.product(range(2),range(C)))[1:]
    pdev=[(z,lax.rem(k+gc,2),q,lax.rem(s+gs,C)) for gc,gs in peers]
    pidx=[lax.rem(k+gc,2)*C+lax.rem(s+gs,C) for gc,gs in peers]
    back=[gc*C+(C-gs)%C for gc,gs in peers]
    fore=[gc*C+gs for gc,gs in peers]
    chipdev=[(z,k,partner(q,m),s) for m in range(4)]
    toks=spread_copies(C,n,x_ref,xo_ref,tok_s,tok_r)
    cots=spread_copies(C,n,cot_ref,coto_ref,cot_s,cot_r)
    ca=col_copies(Z,w1_ref,wa_scr,a_s,a_r)
    cb=col_copies(Z,w2_ref,wb_scr,b_s,b_r)
    cc=col_copies(Z,d3_scr,wc_scr,c_s,c_r)
    cd=col_copies(Z,o3_scr,wd_scr,dd_s,dd_r)
    d3=rcopy(w1_ref,d3_scr,d3_s,do_r.at[0],chipdev[3])
    o3=rcopy(w2_ref,o3_scr,o3_s,do_r.at[1],chipdev[3])
    wcp=[rcopy(wts_ref.at[0],wts_ref.at[m],wt_s.at[m],wt_r.at[m],chipdev[m]) for m in (1,2)]
    w2cp=[rcopy(w2_scr.at[0],w2_scr.at[m],w2_s.at[m],w2_r.at[m],chipdev[m]) for m in (1,2)]
    grp=[[rcopy(w2_scr.at[m],w2o_ref.at[back[i],m],gr_s.at[i,m],gr_r.at[back[i],m],pdev[i]) for i in range(G-1)] for m in range(4)]
    loc=[pltpu.make_async_copy(w2_scr.at[m],w2o_ref.at[0,m],loc_s.at[m]) for m in range(4)]
    def share(m):
        loc[m].start()
        for cp in grp[m]: cp.start()
    greet(Z,C)
    spread_start(toks)
    for cp in ca: cp.start()
    ains=[]
    for j in range(NB):
        arrived(xo_ref.at[j],tok_r.at[j])
        x=xo_ref[j].astype(f32)
        inv=lax.rsqrt(jnp.mean(x*x,axis=-1,keepdims=True)+norm_eps)
        slot=j*G+g0
        ain_ref[slot]=(x*inv*gain_ref[...]).astype(bf16)
        for i in range(G-1):
            cp=rcopy(ain_ref.at[slot],ain_ref.at[slot],ain_s.at[i,j],ain_r.at[slot],pdev[i])
            cp.start(); ains.append(cp)
    for i in range(2*Z): arrived(wa_scr.at[i],a_r.at[i])
    transpose_rows(wa_scr,wts_ref.at[0])
    for cp in wcp: cp.start()
    for cp in cb: cp.start()
    d3.start(); o3.start()
    for j in range(NB):
        for i in range(G-1): arrived(ain_ref.at[j*G+pidx[i]],ain_r.at[j*G+pidx[i]])
    rowi=lax.broadcasted_iota(jnp.int32,(BQ,BQ),0)
    coli=lax.broadcasted_iota(jnp.int32,(BQ,BQ),1)
    hs=[slice(h*HD,(h+1)*HD) for h in range(hb)]
    CH=512; per=CH//n; sub=BQ//n

    def block(m,_):
        @pl.when(m==1)
        def _():
            arrived(wts_ref.at[1],wt_r.at[1])
            for i in range(2*Z): arrived(wb_scr.at[i],b_r.at[i])
            transpose_rows(wb_scr,w2_scr.at[0])
            for cp in w2cp: cp.start()
            share(0)
            arrived(d3_scr,do_r.at[0])
            for cp in cc: cp.start()
        @pl.when(m==2)
        def _():
            arrived(wts_ref.at[2],wt_r.at[2])
            arrived(o3_scr,do_r.at[1])
            for cp in cd: cp.start()
        @pl.when(m==3)
        def _():
            for i in range(2*Z): arrived(wc_scr.at[i],c_r.at[i])
            transpose_rows(wc_scr,wts_ref.at[3])
            spread_start(cots)
        for c in range(L//CH):
            cs=slice(c*CH,(c+1)*CH)
            r=dot(wts_ref[m],ain_ref[c*per:(c+1)*per].reshape(CH,D),NT)
            qkv_ref[m,:W,cs]=(r[:W]*pd_ref[:,:1]).astype(bf16)
            qkv_ref[m,W:,cs]=r[W:].astype(bf16)
            for h in range(hb):
                k_scr[h,cs,:]=r[W+h*HD:W+(h+1)*HD].T.astype(bf16)
        units=[(i,h) for i in range(nb) for h in range(hb)]
        st={}
        def phase_a(u):
            i,h=units[u]; c0=i*BQ
            qi=qkv_ref[m,hs[h],c0:c0+BQ]
            sq=segq_ref[:,c0:c0+BQ]
            m8=None
            for j in range(i+1):
                t=dot(k_scr[h,j*BQ:(j+1)*BQ,:],qi)
                sk=segk_ref[j*BQ:(j+1)*BQ,:]
                ok=jnp.concatenate([sk]*(BQ//128),axis=1)==sq
                if j==i: ok=ok&(rowi<=coli)
                t=jnp.where(ok,t,NEG)
                s_scr[u%2,j*BQ:(j+1)*BQ,:]=t
                mm=t.reshape(BQ//8,8,BQ).max(0)
                m8=mm if m8 is None else jnp.maximum(m8,mm)
                yield
            st[u]=m8.max(0,keepdims=True)
        def phase_b(u):
            i,h=units[u]; c0=i*BQ
            mx=st[u]; l8=None; acc=None
            for j in range(i+1):
                p=jnp.exp(s_scr[u%2,j*BQ:(j+1)*BQ,:]-mx)
                ll=p.reshape(BQ//8,8,BQ).sum(0)
                l8=ll if l8 is None else l8+ll
                pv=dot(qkv_ref[m,2*W+h*HD:2*W+(h+1)*HD,j*BQ:(j+1)*BQ],p.astype(bf16))
                acc=pv if acc is None else acc+pv
                yield
            l=l8.sum(0,keepdims=True)
            o=(acc*(1.0/l)).astype(bf16)
            for t in range(sub): ot_ref[i*sub+t,m,hs[h],:]=o[:,t*n:(t+1)*n]
            lse_ref[m*hb+h,:,c0:c0+BQ]=mx+jnp.log(l)
        merge(phase_a(0))
        for u in range(len(units)):
            gs=[phase_b(u)]
            if u+1<len(units): gs=[phase_a(u+1)]+gs
            merge(*gs)
        for b in range(NB):
            mix_ref[b,0,m]=ot_ref[b*G+g0,m]
            for i in range(G-1):
                rcopy(ot_ref.at[b*G+pidx[i],m],mix_ref.at[b,back[i],m],mix_s.at[i,b,m],mix_r.at[back[i],b,m],pdev[i]).start()
        return 0
    lax.fori_loop(0,4,block,0)
    for m in (1,2):
        arrived(w2_scr.at[m],w2_r.at[m])
        share(m)
    for i in range(2*Z): arrived(wd_scr.at[i],dd_r.at[i])
    transpose_rows(wd_scr,w2_scr.at[3])
    share(3)
    for j in range(NB): arrived(coto_ref.at[j],cot_r.at[j])
    for i in range(G-1):
        for b in range(NB):
            for m in range(4):
                arrived(mix_ref.at[b,fore[i],m],mix_r.at[fore[i],b,m])
                rcopy(ot_ref.at[b*G+pidx[i],m],mix_ref.at[b,back[i],m],mix_s.at[i,b,m],mix_r.at[back[i],b,m],pdev[i]).wait_send()
        for m in range(4): arrived(w2o_ref.at[fore[i],m],gr_r.at[fore[i],m])
    for m in range(4):
        loc[m].wait()
        for cp in grp[m]: cp.wait_send()
    for cps in (ca,cb,cc,cd):
        for cp in cps[1:]: cp.wait_send()
    for cp in wcp+w2cp+ains+[d3,o3]: cp.wait_send()
    spread_sent(toks); spread_sent(cots)

def forward(Z, C, tokens, w1h, w2h, cot, gain, pd, segk, segq):
    R,Pn,D=tokens.shape; G=2*C; n=Pn//G; _,Dd,nC=w1h.shape; NB=4*C
    L=segq.shape[1]; W=pd.shape[0]; hb=W//HD
    V=pl.BlockSpec(memory_space=pltpu.VMEM); A=pl.BlockSpec(memory_space=pl.ANY)
    S=lambda *sh: pltpu.SemaphoreType.DMA(sh) if sh else pltpu.SemaphoreType.DMA
    B=lambda *sh: jax.ShapeDtypeStruct(sh,bf16)
    col=pltpu.VMEM((2*Z,Dd,nC),bf16); half=pltpu.VMEM((2,Dd,nC),bf16)
    return pl.pallas_call(functools.partial(fwd_kernel,Z,C,n),
        out_shape=(B(NB,n,D),B(NB*G,n,D),B(4,nC,D),B(G,4,nC,D),B(NB,n,D),B(NB,G,4,W,n),B(4,nC,L),
                   B(NB*G,4,W,n),jax.ShapeDtypeStruct((4*hb,1,L),f32)),
        in_specs=[A,A,A,A,V,V,V,V],out_specs=(V,V,V,A,A,V,V,V,V),
        scratch_shapes=[col,col,col,col,half,half,pltpu.VMEM((4,nC,D),bf16),pltpu.VMEM((hb,L,HD),bf16),pltpu.VMEM((2,L,BQ),f32),
            S(NB),S(NB),S(G-1,NB),S(NB*G),S(2*Z),S(2*Z),S(2*Z),S(2*Z),S(2*Z),S(2*Z),S(2*Z),S(2*Z),S(),S(),S(2),
            S(4),S(4),S(4),S(4),S(G-1,4),S(G,4),S(4),S(NB),S(NB),S(G-1,NB,4),S(G,NB,4)],
        compiler_params=pltpu.CompilerParams(collective_id=0,has_side_effects=True,vmem_limit_bytes=60*2**20),
        cost_estimate=pl.CostEstimate(flops=3*10**10,bytes_accessed=10**8,transcendentals=0),
        name="forward")(tokens,w1h,w2h,cot,gain[None],pd,segk,segq)


def bwd_kernel(Z, C, n, qkv_ref, ot_ref, do_ref, lse_ref, pd_ref, segk_ref, segq_ref, ain_ref, wts_ref,
               xo_ref, gmid_ref, gain_ref, vec_ref, fb_ref,
               gi_ref, gwm_ref, gwq_ref, vo_ref,
               kv_scr, k_scr, v_scr, p_scr, ds_scr, dq_scr, dl_scr, dv_scr, dk_scr, a_scr, st_scr, dw_scr, qr_scr, fr_scr, zs_scr, zr_scr, t3_scr, t3r_scr, ot_scr, do_scr,
               dx_scr, dxr_scr, own_scr, xb_scr, gb_scr, va_scr, vb_scr, vs_scr, sc_scr,
               fs, frs, qs, qrs, zss, zrs, t3s, t3rs, cs_, crs, dxs, dxrs, gis, girs, ld, al, otl, dol, kvl, xl, vas, vars_, vbs, vbrs):
    z,k,q,s=[lax.axis_index(a) for a in AXES]
    G=2*C; g0=k*C+s; NB=4*C
    D=gain_ref.shape[1]; L=segq_ref.shape[1]; W=pd_ref.shape[0]; hb=W//HD; nb=L//BQ; sub=BQ//n
    nC=3*W; Dd=gwm_ref.shape[1]
    peers=list(itertools.product(range(2),range(C)))[1:]
    pdev=[(z,lax.rem(k+gc,2),q,lax.rem(s+gs,C)) for gc,gs in peers]
    pidx=[lax.rem(k+gc,2)*C+lax.rem(s+gs,C) for gc,gs in peers]
    back=[gc*C+(C-gs)%C for gc,gs in peers]
    fore=[gc*C+gs for gc,gs in peers]
    chipdev=[(z,k,partner(q,m),s) for m in range(4)]
    core=(z,1-k,q,s)
    zdev=[lax.rem(z+j,Z) for j in range(Z)]
    fcp={m: rcopy(fb_ref.at[m],fr_scr.at[m-1],fs.at[m],frs.at[m],chipdev[m]) for m in (1,2)}
    qcp={m: rcopy(dw_scr.at[m-1],qr_scr.at[m-1],qs.at[m],qrs.at[m],chipdev[m]) for m in (1,2)}
    zcp=[[rcopy(zs_scr.at[e%2,zdev[j]],zr_scr.at[e,z],zss.at[e,j],zrs.at[e,z],(zdev[j],k,q,s)) for j in range(1,Z)] for e in range(4)]
    t3cp=[rcopy(t3_scr.at[e],t3r_scr.at[e],t3s.at[e],t3rs.at[e],chipdev[3]) for e in range(2)]
    gws=(gwm_ref,gwq_ref)
    ccp=[rcopy(t3_scr.at[e,pl.ds(pl.multiple_of((1-k)*Dd,Dd),Dd),:],gws[e].at[k],cs_.at[e],crs.at[e],core) for e in range(2)]
    def load(src,dst,i):
        cp=pltpu.make_async_copy(src,dst,ld.at[i]); cp.start(); return cp
    def zsend(e, value):
        rows=D//Z; per=max(1,640//rows)
        for i in range(Z//per):
            ls=slice(i*per*rows,(i+1)*per*rows)
            zs_scr[e%2,i*per:(i+1)*per]=value(ls).T.reshape(per,rows,nC).astype(bf16)
        for cp in zcp[e]: cp.start()
    def zsum(e):
        for cp in zcp[e]: cp.wait_send()
        t=zs_scr[e%2,z].astype(f32)
        for j in range(1,Z):
            arrived(zr_scr.at[e,zdev[j]],zrs.at[e,zdev[j]])
            t=t+zr_scr[e,zdev[j]].astype(f32)
        return t
    def diag(e):
        t3_scr[e]=zsum(e)
        t3cp[e].start()
    def final(e):
        t=zsum(2+e)
        arrived(t3r_scr.at[e],t3rs.at[e])
        t=t+t3r_scr[e]
        t3cp[e].wait_send()
        t3_scr[e]=t
        ccp[e].start()
        gws[e][k]=t3_scr[e,pl.ds(pl.multiple_of(k*Dd,Dd),Dd),:]
    kvcp=[pltpu.make_async_copy(qkv_ref.at[m],kv_scr.at[m],kvl.at[m]) for m in range(4)]
    for m in (3,2,1,0): kvcp[m].start()
    acp=pltpu.make_async_copy(ain_ref,a_scr,al)
    acp.start()
    def otcp(m): return pltpu.make_async_copy(ot_ref.at[:,m],ot_scr,otl)
    otcp(3).start()
    def docp(idx): return pltpu.make_async_copy(do_ref.at[:,3-idx],do_scr.at[lax.rem(idx,2)],dol.at[lax.rem(idx,2)])
    docp(0).start()
    greet(Z,C)
    for m in (1,2): fcp[m].start()
    load(fb_ref.at[3],st_scr,0).wait()
    zsend(0,lambda ls: st_scr[:,ls].astype(f32))
    sc_scr[...]=jnp.zeros_like(sc_scr)
    rowi=lax.broadcasted_iota(jnp.int32,(BQ,BQ),0)
    coli=lax.broadcasted_iota(jnp.int32,(BQ,BQ),1)
    hs=[slice(h*HD,(h+1)*HD) for h in range(hb)]
    H2=BQ//2

    def block(idx,_):
        m=3-idx
        pltpu.make_async_copy(qkv_ref.at[m],kv_scr.at[m],kvl.at[m]).wait()
        for h in range(hb):
            k_scr[h]=kv_scr[m,W+h*HD:W+(h+1)*HD,:].T
            v_scr[h]=kv_scr[m,2*W+h*HD:2*W+(h+1)*HD,:].T
        slot=lax.rem(idx,2)
        docp(idx).wait()
        @pl.when(idx<3)
        def _(): docp(idx+1).start()
        def tile(h,i):
            return jnp.concatenate([do_scr[slot,i*sub+t,hs[h],:] for t in range(sub)],1) if sub>1 else do_scr[slot,i,hs[h],:]
        otcp(m).wait()
        for i in range(nb):
            for h in range(hb):
                for t in range(sub):
                    B_=i*sub+t
                    dl_scr[h,:,B_*n:(B_+1)*n]=(do_scr[slot,B_,hs[h],:].astype(f32)*ot_scr[B_,hs[h],:].astype(f32)).sum(0,keepdims=True)
        @pl.when(m>0)
        def _(): otcp(m-1).start()
        units=[(j,h,i) for j in range(nb) for h in range(hb) for i in range(j,nb)]
        def phase_a(u):
            j,h,i=units[u]; cs=slice(i*BQ,(i+1)*BQ)
            for a in range(2):
                ks=slice(j*BQ+a*H2,j*BQ+(a+1)*H2)
                t=dot(k_scr[h,ks,:],kv_scr[m,hs[h],cs])
                dp=dot(v_scr[h,ks,:],tile(h,i))
                sk=segk_ref[ks,:]
                ok=jnp.concatenate([sk]*(BQ//128),axis=1)==segq_ref[:,cs]
                if j==i: ok=ok&(rowi[a*H2:(a+1)*H2]<=coli[a*H2:(a+1)*H2])
                p=jnp.exp(jnp.where(ok,t-lse_ref[m*hb+h,:,cs],NEG))
                p_scr[u%2,a*H2:(a+1)*H2,:]=p.astype(bf16)
                ds_scr[u%2,a*H2:(a+1)*H2,:]=(p*(dp-dl_scr[h,:,cs])).astype(bf16)
                yield
        def phase_b(u):
            j,h,i=units[u]; js=slice(j*BQ,(j+1)*BQ); cs=slice(i*BQ,(i+1)*BQ)
            p=p_scr[u%2]; ds=ds_scr[u%2]
            dv=dot(tile(h,i),p,NT); dk=dot(kv_scr[m,hs[h],cs],ds,NT)
            if i==j: dv_scr[h]=dv; dk_scr[h]=dk
            else: dv_scr[h]+=dv; dk_scr[h]+=dk
            yield
            dq=dot(kv_scr[m,W+h*HD:W+(h+1)*HD,js],ds)
            if j==0: dq_scr[hs[h],cs]=dq
            else: dq_scr[hs[h],cs]+=dq
            if i==nb-1:
                kv_scr[m,W+h*HD:W+(h+1)*HD,js]=dk_scr[h].astype(bf16)
                kv_scr[m,2*W+h*HD:2*W+(h+1)*HD,js]=dv_scr[h].astype(bf16)
            yield
        merge(phase_a(0))
        for u in range(len(units)):
            gs=[phase_b(u)]
            if u+1<len(units): gs=[phase_a(u+1)]+gs
            merge(*gs)
        dq=dq_scr[...]
        sc_scr[...]+=(dq*kv_scr[m,:W,:].astype(f32)).sum(1,keepdims=True)/pd_ref[:,:1]
        kv_scr[m,:W,:]=(dq*pd_ref[:,:1]).astype(bf16)
        @pl.when(idx==0)
        def _():
            acp.wait()
            zsend(1,lambda ls: dwt(3,ls))
        @pl.when((idx==1)|(idx==2))
        def _():
            for c in range(D//256):
                ls=slice(c*256,(c+1)*256)
                dw_scr[m-1,:,ls]=dwt(m,ls).astype(bf16)
        @pl.when(idx==1)
        def _():
            qcp[2].start()
            diag(0)
            ld0=load(fb_ref.at[0],st_scr,0)
            for m2 in (1,2): arrived(fr_scr.at[m2-1],frs.at[m2])
            ld0.wait()
            zsend(2,lambda ls: st_scr[:,ls].astype(f32)+fr_scr[0,:,ls].astype(f32)+fr_scr[1,:,ls].astype(f32))
        @pl.when(idx==2)
        def _():
            qcp[1].start()
            diag(1)
        return 0
    def dwt(m,ls):
        return dot(kv_scr[m],a_scr[:,ls])
    lax.fori_loop(0,4,block,0)
    for m2 in (1,2): arrived(qr_scr.at[m2-1],qrs.at[m2])
    zsend(3,lambda ls: dwt(0,ls)+qr_scr[0,:,ls].astype(f32)+qr_scr[1,:,ls].astype(f32))
    wcp=[pltpu.make_async_copy(wts_ref.at[m],a_scr.at[pl.ds(m*nC,nC),:],kvl.at[m]) for m in range(4)]
    for cp in wcp: cp.start()
    for cp in wcp: cp.wait()

    def chunk(i):
        gl=kv_scr[:,:,pl.ds(pl.multiple_of(i*BQ,BQ),BQ)].reshape(4*nC,BQ)
        return dot(gl,a_scr[:4*nC,:],TN)
    def xload(b):
        return [pltpu.make_async_copy(xo_ref.at[b],xb_scr.at[b%2],xl.at[0,b%2]),pltpu.make_async_copy(gmid_ref.at[b],gb_scr.at[b%2],xl.at[1,b%2])]
    for cp in xload(0): cp.start()
    dxcp=[[rcopy(dx_scr.at[i,b],dxr_scr.at[back[i]-1,b],dxs.at[i,b],dxrs.at[back[i],b],pdev[i]) for b in range(NB)] for i in range(G-1)]
    for b in range(NB):
        if sub==1:
            for i in range(G-1):
                dx_scr[i,b]=chunk(b*G+pidx[i]).astype(bf16)
                dxcp[i][b].start()
        else:
            own_scr[...]=chunk(b)
            for i in range(G-1):
                dx_scr[i,b]=own_scr[pl.ds(pl.multiple_of(pidx[i]*n,n),n),:].astype(bf16)
                dxcp[i][b].start()
    gicp=[]
    gpart=None
    for b in range(NB):
        if b+1<NB:
            for cp in xload(b+1): cp.start()
        if sub==1:
            gain=chunk(b*G+g0)
        else:
            own_scr[...]=chunk(b)
            gain=own_scr[pl.ds(pl.multiple_of(g0*n,n),n),:]
        for i in range(G-1):
            arrived(dxr_scr.at[fore[i]-1,b],dxrs.at[fore[i],b])
            gain=gain+dxr_scr[fore[i]-1,b].astype(f32)
        for cp in xload(b): cp.wait()
        x=xb_scr[b%2].astype(f32)
        inv=lax.rsqrt(jnp.mean(x*x,axis=-1,keepdims=True)+norm_eps)
        nx=x*inv
        dn=gain*gain_ref[...]
        gin=gb_scr[b%2]+inv*(dn-nx*jnp.mean(dn*nx,axis=-1,keepdims=True))
        gp=(gain*nx).reshape(n//8,8,D).sum(0)
        gpart=gp if gpart is None else gpart+gp
        dxcp[0][b].wait_send()
        dx_scr[0,b]=gin.astype(bf16)
        dst=gi_ref.at[lax.rem(q,2),pl.ds(pl.multiple_of((k*C+s)*n,n),n),:]
        rs=girs.at[(lax.rem(q,2)*2+k)*C+s]
        mine=(lax.div(q,2)==k)&(q==b//C)&(s==b%C)
        gicp.append((mine,pltpu.make_async_copy(dx_scr.at[0,b],dst,rs),rcopy(dx_scr.at[0,b],dst,gis.at[b],rs,(z,lax.div(q,2),b//C,b%C))))
        spread_start(gicp[-1:])
    vs_scr[...]=jnp.zeros_like(vs_scr)
    vs_scr[0:1,:]=gpart.sum(0,keepdims=True)
    vs_scr[1:2,:]=vec_ref[...]
    sc=sc_scr[0:HD,:]
    for h in range(1,hb): sc=sc+sc_scr[h*HD:(h+1)*HD,:]
    vs_scr[2:3,0:HD]=sc.T[0:1,:]
    me=(k*4+q)*C+s
    va_scr[me]=vs_scr[...]
    plane=list(itertools.product(range(2),range(4),range(C)))[1:]
    vacp=[rcopy(vs_scr,va_scr.at[me],vas.at[i],vars_.at[me],(z,lax.rem(k+a,2),lax.rem(q+b,4),lax.rem(s+c,C))) for i,(a,b,c) in enumerate(plane)]
    for cp in vacp: cp.start()
    final(0)
    for a,b,c in plane:
        o=(lax.rem(k+a,2)*4+lax.rem(q+b,4))*C+lax.rem(s+c,C)
        arrived(va_scr.at[o],vars_.at[o])
    t=va_scr[0]
    for i in range(1,8*C): t=t+va_scr[i]
    vb_scr[z]=t
    vbcp=[rcopy(vb_scr.at[z],vb_scr.at[z],vbs.at[j],vbrs.at[z],(zdev[j],k,q,s)) for j in range(1,Z)]
    for cp in vbcp: cp.start()
    final(1)
    for j in range(1,Z): arrived(vb_scr.at[zdev[j]],vbrs.at[zdev[j]])
    t=vb_scr[0]
    for i in range(1,Z): t=t+vb_scr[i]
    vo_ref[...]=t
    for e in range(2):
        arrived(gws[e].at[1-k],crs.at[e])
        ccp[e].wait_send()
    for r in range(2):
        for h in range(2):
            for s2 in range(C):
                arrived(gi_ref.at[r,pl.ds((h*C+s2)*n,n),:],girs.at[(r*2+h)*C+s2])
    spread_sent(gicp)
    for i in range(1,G-1):
        for b in range(NB): dxcp[i][b].wait_send()
    for m in (1,2):
        fcp[m].wait_send(); qcp[m].wait_send()
    for cp in vacp+vbcp: cp.wait_send()

def backward(Z, C, qkv, ot, do, lse, pd, segk, segq, ain, wts, xo, gmid, gain, vec, fb, R, Pn, Dd):
    NB,n,D=xo.shape; G=2*C; nC=wts.shape[1]; W=pd.shape[0]; hb=W//HD; L=segq.shape[1]
    V=pl.BlockSpec(memory_space=pltpu.VMEM); A=pl.BlockSpec(memory_space=pl.ANY)
    S=lambda *sh: pltpu.SemaphoreType.DMA(sh) if sh else pltpu.SemaphoreType.DMA
    M=lambda *sh: pltpu.VMEM(sh,bf16)
    F=lambda *sh: pltpu.VMEM(sh,f32)
    gw=jax.ShapeDtypeStruct((2,Dd,nC),f32)
    return pl.pallas_call(functools.partial(bwd_kernel,Z,C,n),
        out_shape=(jax.ShapeDtypeStruct((R,Pn,D),bf16),gw,gw,jax.ShapeDtypeStruct((8,D),f32)),
        in_specs=[A,A,A,V,V,V,V,A,A,A,A,V,V,A],out_specs=(A,V,V,V),
        scratch_shapes=[M(4,nC,L),M(hb,L,HD),M(hb,L,HD),M(2,BQ,BQ),M(2,BQ,BQ),F(W,L),F(hb,1,L),F(hb,HD,BQ),F(hb,HD,BQ),M(L,D),
            M(nC,D),M(2,nC,D),M(2,nC,D),M(2,nC,D),M(2,Z,D//Z,nC),M(4,Z,D//Z,nC),F(2,D//Z,nC),F(2,D//Z,nC),M(NB*G,W,n),M(2,NB*G,W,n),
            M(G-1,NB,n,D),M(G-1,NB,n,D),F(BQ,D) if n<BQ else F(8,128),M(2,n,D),F(2,n,D),F(8*C,8,D),F(Z,8,D),F(8,D),F(W,1),
            S(4),S(4),S(4),S(4),S(4,Z),S(4,Z),S(2),S(2),S(2),S(2),S(G,NB),S(G,NB),S(NB),S(4*C),S(4),S(),S(),S(2),S(4),S(2,2),S(8*C),S(8*C),S(Z),S(Z)],
        compiler_params=pltpu.CompilerParams(collective_id=1,has_side_effects=True,vmem_limit_bytes=58*2**20),
        cost_estimate=pl.CostEstimate(flops=6*10**10,bytes_accessed=10**8,transcendentals=0),
        name="backward")(qkv,ot,do,lse,pd,segk,segq,ain.reshape(L,D),wts,xo,gmid,gain[None],vec[None],fb)


scale_base = 1.442695041

def silu_slope(u):
    sg=jax.nn.sigmoid(u)
    return sg*(1.0+u*(1.0-sg))

def make_local(Z, C):
    sizes=(Z,2,4,C)
    coords=list(itertools.product(*[range(n) for n in sizes]))
    lin={c:i for i,c in enumerate(coords)}
    G=2*C
    def pp(x, fn):
        return lax.ppermute(x, AXES, [(lin[c], lin[fn(*c)]) for c in coords])
    def unxor(parts, idx):
        b=1
        while b<len(parts):
            c=(idx & b)!=0
            parts=[jnp.where(c,parts[a^b],parts[a]) for a in range(len(parts))]
            b*=2
        return parts
    def allsum(v):
        for ax,n in enumerate(sizes):
            b=1
            while b<n:
                v=v+pp(v,lambda *c,ax=ax,b=b: tuple(ci^b if i==ax else ci for i,ci in enumerate(c)))
                b*=2
        return v
    def gsend(x, gamma):
        gc,gs=divmod(gamma,C)
        return pp(x, lambda z,k,q,s: (z,k^gc,q,s^gs))

    def after(x, *deps):
        return lax.optimization_barrier((x,)+deps)[0] if deps else x

    def local(tokens, segments, attn_gain, w_query, w_key, w_value, w_out, query_scale, mlp_gain, w_up, w_down, cotangent):
        zi,k,qi,si=[lax.axis_index(a) for a in AXES]
        R,Pn,D=tokens.shape; L=segments.shape[1]
        n=Pn//G
        N=4*C*n
        Dd,Ct=w_query.shape; Ch=Ct//2; W=Ch; hb=W//HD
        g0=k*C+si
        k0=k==0
        q0=2*(k^(qi//2))+qi%2
        rounds=list(itertools.product(range(2),range(2),range(C)))

        def spread(x):
            got=[]
            for eta,rho,sg in rounds:
                r=(qi%2)^rho; h=(qi//2)^k^eta; s2=si^sg
                piece=lax.dynamic_slice(x,(r,(h*C+s2)*n,0),(1,n,D))[0]
                got.append(pp(piece, lambda z,kk,q,s: (z,(q//2)^kk^eta,2*kk+((q%2)^rho),s^sg)))
            return jnp.concatenate(unxor(got,q0*C+si),0)
        def collect(y):
            parts=unxor([y[i*n:(i+1)*n] for i in range(4*C)],q0*C+si)
            got=[]
            for idx,(eta,rho,sg) in enumerate(rounds):
                got.append(pp(parts[idx], lambda z,kk,q,s: (z,q//2,(2*(kk^(q//2))+q%2)^(2*eta+rho),s^sg)))
            ab=unxor(got,((qi//2)^k)*(2*C)+(qi%2)*C+si)
            rows=[jnp.concatenate([ab[(h*2+r)*C+s2] for h in range(2) for s2 in range(C)],0) for r in range(R)]
            return jnp.stack(rows,0)
        def halves(shards):
            return jnp.stack([jnp.concatenate([w[:,h*Ch:(h+1)*Ch] for w in shards],1) for h in range(2)],0)
        def gatherD(w2h, *deps):
            keep=jnp.where(k0,w2h[0],w2h[1]); send=jnp.where(k0,w2h[1],w2h[0])
            recv=pp(send,lambda z,kk,q,s:(z,1-kk,q,s))
            rows=jnp.concatenate([jnp.where(k0,keep,recv),jnp.where(k0,recv,keep)],0)
            rows=after(rows,*deps)
            parts=[rows]+[pp(rows,lambda z,kk,q,s:(z^j,kk,q,s)) for j in range(1,Z)]
            return assemble(zi,parts),parts[-1]
        def chip(x, m):
            return pp(x,lambda z,kk,q,s:(z,kk,q^m,s))
        def reduceZ(rel):
            tot=rel[0]
            for j in range(1,Z):
                tot=tot+pp(rel[j],lambda z,kk,q,s:(z^j,kk,q,s)).astype(f32)
            return tot
        def finish(tot, nw):
            keep=jnp.where(k0,tot[:Dd],tot[Dd:]); send=jnp.where(k0,tot[Dd:],tot[:Dd])
            recv=pp(send,lambda z,kk,q,s:(z,1-kk,q,s))
            lo=jnp.where(k0,keep,recv); hi=jnp.where(k0,recv,keep)
            return [jnp.concatenate([lo[:,i*Ch:(i+1)*Ch],hi[:,i*Ch:(i+1)*Ch]],1) for i in range(nw)]
        def tok_lanes(xT):
            return [jnp.concatenate([xT[:,(b*G+g)*n:(b*G+g+1)*n] for b in range(4*C)],1) for g in range(G)]
        def tok_rows_join(parts):
            return jnp.concatenate([parts[g][b*n:(b+1)*n] for b in range(4*C) for g in range(G)],0)
        def tok_lanes_join(parts):
            return jnp.concatenate([parts[g][:,b*n:(b+1)*n] for b in range(4*C) for g in range(G)],1)

        seg_o=pp(segments,lambda z,kk,q,s:(z,1-kk,q,s))
        seg2=jnp.where(k==qi//2,segments,seg_o)
        seg=jnp.where(qi%2==0,seg2[0],seg2[1])
        first=seg[::BQ]; last=seg[BQ-1::BQ]
        segk=jnp.broadcast_to(seg[:,None],(L,128)); segq=seg[None]
        per_dim=scale_base/math.sqrt(HD)*jax.nn.softplus(query_scale)
        pd=jnp.broadcast_to(jnp.tile(per_dim,hb)[:,None],(W,128))
        w1h=halves([w_query,w_key,w_value]); w2h=halves([w_out.T,w_up,w_down.T])
        xo,ain,wts,w2o,cot,mix,qkv,ot,lse=forward(Z,C,tokens,w1h,w2h,cotangent,attn_gain,pd,segk,segq)
        x=xo.reshape(N,D).astype(f32); cot=cot.reshape(N,D)
        mixT_own=jnp.concatenate([mix[b].reshape(G*4*W,n) for b in range(4*C)],1)
        wo,wu,wd=[w2o[:,:,i*Ch:(i+1)*Ch].reshape(G*4*Ch,D) for i in range(3)]

        inv1=lax.rsqrt(jnp.mean(x*x,axis=-1,keepdims=True)+norm_eps)
        attn=dot(mixT_own,wo,TN)
        middle=x+attn
        inv2=lax.rsqrt(jnp.mean(middle*middle,axis=-1,keepdims=True)+norm_eps)
        norm2=middle*inv2
        mlp_in=(norm2*mlp_gain).astype(bf16)
        up=dot(mlp_in,wu,NT)
        hid=jax.nn.silu(up).astype(bf16)
        block=(middle+dot(hid,wd)).astype(bf16)
        block_out=collect(block)
        gup=(dot(cot,wd,NT)*silu_slope(up)).astype(bf16)
        gmlp=dot(gup,wu)
        dn=gmlp*mlp_gain
        gmid=cot.astype(f32)+inv2*(dn-norm2*jnp.mean(dn*norm2,axis=-1,keepdims=True))
        mlp_gain_part=jnp.sum(gmlp*norm2,axis=0)
        gattn=gmid.astype(bf16)
        gmixT=dot(wo,gattn,NT).astype(bf16)
        K=gmixT.shape[0]//G
        gparts=unxor([gmixT[:K]]+[gsend(gmixT[g*K:(g+1)*K],g) for g in range(1,G)],g0)
        do=jnp.stack([gparts[g][:,b*n:(b+1)*n].reshape(4,W,n) for b in range(4*C) for g in range(G)],0)
        g3=[dot(mixT_own,gattn),dot(gup,mlp_in,TN),dot(hid,cot,TN)]

        K4=4*Ch
        mine=list(g3)
        mine=[t[:K4] for t in g3]
        for g in range(1,G):
            for i,t in enumerate(g3):
                mine[i]=mine[i]+gsend(t[g*K4:(g+1)*K4].astype(bf16),g).astype(f32)
        fb=[jnp.concatenate([t[m*Ch:(m+1)*Ch] for t in mine],0) for m in range(4)]
        fbb=jnp.stack(fb,0).astype(bf16)
        gi,gwm,gwq,vo=backward(Z,C,qkv,ot,do,lse,pd,segk,segq,ain,wts,xo,gmid.reshape(4*C,n,D),attn_gain,mlp_gain_part,fbb,R,Pn,Dd)
        input_grad=gi.astype(f32)
        def cols(gw,i):
            return jnp.concatenate([gw[0,:,i*Ch:(i+1)*Ch],gw[1,:,i*Ch:(i+1)*Ch]],1)
        grad_query,grad_key,grad_value=[cols(gwq,i) for i in range(3)]
        grad_out=cols(gwm,0).T; grad_up=cols(gwm,1); grad_down=cols(gwm,2).T
        grad_query_scale=vo[2,:HD]*(scale_base/math.sqrt(HD))*jax.nn.sigmoid(query_scale)
        return (block_out,input_grad,vo[0],grad_query,grad_key,grad_value,grad_out,grad_query_scale,vo[1],grad_up,grad_down)
    return local

def solution(mesh):
    dp,T=mesh.shape["dp"],mesh.shape["tensor"]
    Z,C=dp//2,T//4
    fine=Mesh(mesh.devices.reshape(Z,2,4,C),AXES)
    dpx=("zz","core"); tx=("q","s")
    in_specs=(P(dpx,tx,None),P(dpx,None),P(),P(dpx,tx),P(dpx,tx),P(dpx,tx),P(tx,dpx),P(),P(),P(dpx,tx),P(tx,dpx),P(dpx,tx,None))
    out_specs=(P(dpx,tx,None),P(dpx,tx,None),P(),P(dpx,tx),P(dpx,tx),P(dpx,tx),P(tx,dpx),P(),P(),P(dpx,tx),P(tx,dpx))
    return jax.shard_map(make_local(Z,C),mesh=fine,in_specs=in_specs,out_specs=out_specs,check_vma=False)
```

```python
import functools
import itertools
import math
import jax, jax.numpy as jnp
from jax import lax
from jax.experimental import pallas as pl
from jax.experimental.pallas import tpu as pltpu
from jax.sharding import Mesh, PartitionSpec as P

AXES=("zz","core","q","s")
norm_eps = 1e-06
HD=80
BQ=256
NEG=-1e30
f32=jnp.float32; bf16=jnp.bfloat16
NT=(((1,),(1,)),((),()))
NN=(((1,),(0,)),((),()))
TN=(((0,),(0,)),((),()))
def dot(a,b,dims=NN): return lax.dot_general(a,b,dims,preferred_element_type=f32)

def merge(*gens):
    gens=list(gens)
    while gens:
        for g in list(gens):
            try: next(g)
            except StopIteration: gens.remove(g)


MESH=pl.DeviceIdType.MESH
scale_base = 1.442695041

def rcopy(src,dst,ss,rs,dev):
    return pltpu.make_async_remote_copy(src_ref=src,dst_ref=dst,send_sem=ss,recv_sem=rs,device_id=dev,device_id_type=MESH)

def transpose_rows(src, dst):
    P_,rows,cols=src.shape
    per=max(1,640//rows)
    for i in range(P_//per):
        dst[:,i*per*rows:(i+1)*per*rows]=src[i*per:(i+1)*per].reshape(per*rows,cols).T

def partner(q, m):
    return (q,q+1-2*lax.rem(q,2),lax.rem(q+2,4),3-q)[m]

def greet(Z, C):
    z,k,q,s=[lax.axis_index(a) for a in AXES]
    bar=pltpu.get_barrier_semaphore()
    plane=list(itertools.product(range(2),range(4),range(C)))[1:]
    column=[(j,a) for j in range(1,Z) for a in range(2)]
    for a,b,c in plane:
        pl.semaphore_signal(bar,inc=1,device_id=(z,lax.rem(k+a,2),lax.rem(q+b,4),lax.rem(s+c,C)),device_id_type=MESH)
    for j,a in column:
        pl.semaphore_signal(bar,inc=1,device_id=(lax.rem(z+j,Z),lax.rem(k+a,2),q,s),device_id_type=MESH)
    pl.semaphore_wait(bar,len(plane)+len(column))

def col_copies(Z, src, dst, ss, rs):
    z,k,q,s=[lax.axis_index(a) for a in AXES]
    out=[]
    for j in range(Z):
        for a in range(2):
            kk=lax.rem(k+a,2)
            if j==0 and a==0: out.append(pltpu.make_async_copy(src.at[k],dst.at[2*z+k],rs.at[2*z+k]))
            else: out.append(rcopy(src.at[kk],dst.at[2*z+k],ss.at[j*2+a],rs.at[2*z+k],(lax.rem(z+j,Z),kk,q,s)))
    return out

def spread_copies(C, n, src, dst, ss, rs):
    z,k,q,s=[lax.axis_index(a) for a in AXES]
    out=[]
    for rr in range(2):
        r=lax.rem(q+rr,2)
        for h in range(2):
            for s2 in range(C):
                i=(rr*2+h)*C+s2
                piece=src.at[r,pl.ds((h*C+s2)*n,n),:]
                out.append((rr,(k==h)&(q==2*k+r)&(s==s2),pltpu.make_async_copy(piece,dst.at[q*C+s],rs.at[q*C+s]),
                            rcopy(piece,dst.at[q*C+s],ss.at[i],rs.at[q*C+s],(z,h,2*k+r,s2))))
    return out

def is_home(): return lax.axis_index("core")==lax.div(lax.axis_index("q"),2)

def spread_near(cps, do):
    for rr,mine,loc,cp in cps:
        if rr==0:
            @pl.when(mine)
            def _(loc=loc):
                if do=="start": loc.start()
            @pl.when(jnp.logical_not(mine))
            def _(cp=cp): cp.start() if do=="start" else cp.wait_send()
        else:
            @pl.when(is_home())
            def _(cp=cp): cp.start() if do=="start" else cp.wait_send()

def spread_far(cps, do):
    for rr,mine,loc,cp in cps:
        if rr==1:
            @pl.when(jnp.logical_not(is_home()))
            def _(cp=cp): cp.start() if do=="start" else cp.wait_send()

def near_blocks(C):
    q=lax.axis_index("q")
    return [partner(q,m)*C+t for m in range(3) for t in range(C)]

def far_blocks(C):
    q=lax.axis_index("q")
    return [partner(q,3)*C+t for t in range(C)]

def spread_start(cps):
    for mine,loc,cp in cps:
        @pl.when(mine)
        def _(loc=loc): loc.start()
        @pl.when(jnp.logical_not(mine))
        def _(cp=cp): cp.start()

def spread_sent(cps):
    for mine,loc,cp in cps:
        @pl.when(jnp.logical_not(mine))
        def _(cp=cp): cp.wait_send()

def home_copies(C, n, src, dst, ss, rs):
    z,k,q,s=[lax.axis_index(a) for a in AXES]
    out=[]
    for b in range(4*C):
        to=dst.at[lax.rem(q,2),pl.ds(pl.multiple_of((k*C+s)*n,n),n),:]
        sem=rs.at[(lax.rem(q,2)*2+k)*C+s]
        out.append(((lax.div(q,2)==k)&(q==b//C)&(s==b%C),pltpu.make_async_copy(src.at[b],to,sem),
                    rcopy(src.at[b],to,ss.at[b],sem,(z,lax.div(q,2),b//C,b%C))))
    return out

def home_arrived(C, n, dst, rs):
    for r in range(2):
        for h in range(2):
            for s2 in range(C):
                arrived(dst.at[r,pl.ds((h*C+s2)*n,n),:],rs.at[(r*2+h)*C+s2])

def arrived(ref, sem):
    z,k,q,s=[lax.axis_index(a) for a in AXES]
    rcopy(ref,ref,sem,sem,(z,1-k,q,s)).wait_recv()

def fwd_kernel(Z, C, n, x_ref, w1_ref, w2_ref, cot_ref, gain_ref, pd_ref, seg_ref,
               xo_ref, ain_ref, wts_ref, w2o_ref, mix_ref, qkv_ref, ot_ref, lse_ref, segk_ref, segq_ref, coto_ref,
               xo_scr, ain_scr, wts_scr, qkv_scr, ot_scr, wa_scr, wb_scr, wd_scr, o3_scr, w2_scr, k_scr, s_scr, so_scr,
               tok_s, tok_r, ain_s, ain_r, a_s, a_r, b_s, b_r, dd_s, dd_r, o3_s, o3_r,
               wt_s, wt_r, hf_s, hf_r, w2_s, w2_r, gr_s, gr_r, loc_s, mix_s, mix_r, mixl, sg_s, sg_r, out_s, qo_s, cot_s, cot_r):
    z,k,q,s=[lax.axis_index(a) for a in AXES]
    G=2*C; g0=k*C+s; NB=4*C
    D=gain_ref.shape[1]; L=seg_ref.shape[1]; W=pd_ref.shape[0]; hb=W//HD; nb=L//BQ; nC=3*W
    peers=list(itertools.product(range(2),range(C)))[1:]
    pdev=[(z,lax.rem(k+gc,2),q,lax.rem(s+gs,C)) for gc,gs in peers]
    pidx=[lax.rem(k+gc,2)*C+lax.rem(s+gs,C) for gc,gs in peers]
    back=[gc*C+(C-gs)%C for gc,gs in peers]
    fore=[gc*C+gs for gc,gs in peers]
    chipdev=[(z,k,partner(q,m),s) for m in range(4)]
    toks=spread_copies(C,n,x_ref,xo_scr,tok_s,tok_r)
    cots=spread_copies(C,n,cot_ref,coto_ref,cot_s,cot_r)
    ca=col_copies(Z,w1_ref,wa_scr,a_s,a_r)
    cb=col_copies(Z,w2_ref,wb_scr,b_s,b_r)
    cd=col_copies(Z,o3_scr,wd_scr,dd_s,dd_r)
    o3=rcopy(w2_ref,o3_scr,o3_s,o3_r,chipdev[3])
    wcp=[rcopy(wts_scr.at[0],wts_scr.at[m],wt_s.at[m],wt_r.at[m],chipdev[m]) for m in (1,2)]
    h1=nC//32*16; half=[pl.ds(0,h1),pl.ds(h1,nC-h1)]
    hcp=[rcopy(wts_scr.at[1,half[0]],wts_scr.at[3,half[0]],hf_s.at[0],hf_r.at[0],chipdev[2]),
         rcopy(wts_scr.at[2,half[1]],wts_scr.at[3,half[1]],hf_s.at[1],hf_r.at[1],chipdev[1])]
    save=[pltpu.make_async_copy(xo_scr,xo_ref,out_s.at[0]),pltpu.make_async_copy(ain_scr,ain_ref,out_s.at[1])]
    wsave=[pltpu.make_async_copy(wts_scr.at[m],wts_ref.at[m],out_s.at[2+m]) for m in range(4)]
    def qsave(m): return [pltpu.make_async_copy(qkv_scr.at[m],qkv_ref.at[m],qo_s.at[0,m]),pltpu.make_async_copy(ot_scr.at[:,m],ot_ref.at[:,m],qo_s.at[1,m])]
    w2cp=[rcopy(w2_scr.at[0],w2_scr.at[m],w2_s.at[m],w2_r.at[m],chipdev[m]) for m in (1,2)]
    grp=[[rcopy(w2_scr.at[m],w2o_ref.at[back[i],m],gr_s.at[i,m],gr_r.at[back[i],m],pdev[i]) for i in range(G-1)] for m in range(4)]
    loc=[pltpu.make_async_copy(w2_scr.at[m],w2o_ref.at[0,m],loc_s.at[m]) for m in range(4)]
    def share(m):
        loc[m].start()
        for cp in grp[m]: cp.start()
    sgc=rcopy(seg_ref,so_scr,sg_s,sg_r,(z,1-k,q,s))
    greet(Z,C)
    sgc.start()
    for cp in ca: cp.start()
    spread_near(toks,"start"); spread_far(toks,"start")
    o3.start()
    sgc.wait_recv()
    sg=jnp.where(k==lax.div(q,2),seg_ref[...],so_scr[...])
    sg=jnp.where(lax.rem(q,2)==0,sg[0:1],sg[1:2]).astype(f32)
    segq_ref[...]=sg
    for c in range(L//BQ):
        segk_ref[c*BQ:(c+1)*BQ,:]=jnp.broadcast_to(sg[:,c*BQ:(c+1)*BQ],(128,BQ)).T
    for i in range(2*Z): arrived(wa_scr.at[i],a_r.at[i])
    for cp in cb: cp.start()
    transpose_rows(wa_scr,wts_scr.at[0])
    for cp in wcp: cp.start()
    wsave[0].start()
    ains=[]
    for j in range(NB):
        arrived(xo_scr.at[j],tok_r.at[j])
        x=xo_scr[j].astype(f32)
        inv=lax.rsqrt(jnp.mean(x*x,axis=-1,keepdims=True)+norm_eps)
        slot=j*G+g0
        ain_scr[slot]=(x*inv*gain_ref[...]).astype(bf16)
        for i in range(G-1):
            cp=rcopy(ain_scr.at[slot],ain_scr.at[slot],ain_s.at[i,j],ain_r.at[slot],pdev[i])
            cp.start(); ains.append(cp)
    for j in range(NB):
        for i in range(G-1): arrived(ain_scr.at[j*G+pidx[i]],ain_r.at[j*G+pidx[i]])
    for cp in save: cp.start()
    rowi=lax.broadcasted_iota(jnp.int32,(BQ,BQ),0)
    coli=lax.broadcasted_iota(jnp.int32,(BQ,BQ),1)
    hs=[slice(h*HD,(h+1)*HD) for h in range(hb)]
    CH=512; per=CH//n; sub=BQ//n

    def block(m,_):
        @pl.when(m==1)
        def _():
            for i in range(2*Z): arrived(wb_scr.at[i],b_r.at[i])
            arrived(o3_scr,o3_r)
            for cp in cd: cp.start()
            transpose_rows(wb_scr,w2_scr.at[0])
            for i in (1,2): arrived(wts_scr.at[i],wt_r.at[i])
            for cp in hcp+wsave[1:3]: cp.start()
            share(0)
        @pl.when(m==2)
        def _():
            for cp in w2cp: cp.start()
        @pl.when(m==3)
        def _():
            for i in range(2): arrived(wts_scr.at[3,half[i]],hf_r.at[i])
            wsave[3].start()
            spread_near(cots,"start")
        for c in range(L//CH):
            cs=slice(c*CH,(c+1)*CH)
            r=dot(wts_scr[m],ain_scr[c*per:(c+1)*per].reshape(CH,D),NT)
            qkv_scr[m,:W,cs]=(r[:W]*pd_ref[:,:1]).astype(bf16)
            qkv_scr[m,W:,cs]=r[W:].astype(bf16)
            for h in range(hb):
                k_scr[h,cs,:]=r[W+h*HD:W+(h+1)*HD].T.astype(bf16)
        units=[(i,h) for i in range(nb) for h in range(hb)]
        st={}
        def phase_a(u):
            i,h=units[u]; c0=i*BQ
            qi=qkv_scr[m,hs[h],c0:c0+BQ]
            sq=segq_ref[:,c0:c0+BQ]
            m8=None
            for j in range(i+1):
                t=dot(k_scr[h,j*BQ:(j+1)*BQ,:],qi)
                sk=segk_ref[j*BQ:(j+1)*BQ,:]
                ok=jnp.concatenate([sk]*(BQ//128),axis=1)==sq
                if j==i: ok=ok&(rowi<=coli)
                t=jnp.where(ok,t,NEG)
                s_scr[u%2,j*BQ:(j+1)*BQ,:]=t
                mm=t.reshape(BQ//8,8,BQ).max(0)
                m8=mm if m8 is None else jnp.maximum(m8,mm)
                yield
            st[u]=m8.max(0,keepdims=True)
        def phase_b(u):
            i,h=units[u]; c0=i*BQ
            mx=st[u]; l8=None; acc=None
            for j in range(i+1):
                p=jnp.exp(s_scr[u%2,j*BQ:(j+1)*BQ,:]-mx)
                ll=p.reshape(BQ//8,8,BQ).sum(0)
                l8=ll if l8 is None else l8+ll
                pv=dot(qkv_scr[m,2*W+h*HD:2*W+(h+1)*HD,j*BQ:(j+1)*BQ],p.astype(bf16))
                acc=pv if acc is None else acc+pv
                yield
            l=l8.sum(0,keepdims=True)
            o=(acc*(1.0/l)).astype(bf16)
            for t in range(sub): ot_scr[i*sub+t,m,hs[h],:]=o[:,t*n:(t+1)*n]
            lse_ref[m*hb+h,:,c0:c0+BQ]=mx+jnp.log(l)
        merge(phase_a(0))
        for u in range(len(units)):
            gs=[phase_b(u)]
            if u+1<len(units): gs=[phase_a(u+1)]+gs
            merge(*gs)
        for b in range(NB):
            pltpu.make_async_copy(ot_scr.at[b*G+g0,m],mix_ref.at[b,0,m],mixl.at[b,m]).start()
            for i in range(G-1):
                rcopy(ot_scr.at[b*G+pidx[i],m],mix_ref.at[b,back[i],m],mix_s.at[i,b,m],mix_r.at[back[i],b,m],pdev[i]).start()
        for cp in qsave(m): cp.start()
        return 0
    lax.fori_loop(0,4,block,0)
    for m in (1,2):
        arrived(w2_scr.at[m],w2_r.at[m])
        share(m)
    for i in range(2*Z): arrived(wd_scr.at[i],dd_r.at[i])
    transpose_rows(wd_scr,w2_scr.at[3])
    share(3)
    for i in range(G-1):
        for b in range(NB):
            for m in range(4):
                arrived(mix_ref.at[b,fore[i],m],mix_r.at[fore[i],b,m])
                rcopy(ot_scr.at[b*G+pidx[i],m],mix_ref.at[b,back[i],m],mix_s.at[i,b,m],mix_r.at[back[i],b,m],pdev[i]).wait_send()
        for m in range(4): arrived(w2o_ref.at[fore[i],m],gr_r.at[fore[i],m])
    for m in range(4):
        loc[m].wait()
        for cp in grp[m]: cp.wait_send()
    for cps in (ca,cb,cd):
        for cp in cps[1:]: cp.wait_send()
    for cp in wcp+hcp+w2cp+ains+[o3,sgc]: cp.wait_send()
    spread_near(toks,"sent"); spread_far(toks,"sent"); spread_near(cots,"sent")
    for b in near_blocks(C): arrived(coto_ref.at[b],cot_r.at[b])
    for cp in save+wsave: cp.wait()
    for m in range(4):
        for cp in qsave(m): cp.wait()
        for b in range(NB): pltpu.make_async_copy(ot_scr.at[b*G+g0,m],mix_ref.at[b,0,m],mixl.at[b,m]).wait()

def forward(Z, C, tokens, w1h, w2h, cot, gain, pd, seg):
    R,Pn,D=tokens.shape; G=2*C; n=Pn//G; _,Dd,nC=w1h.shape; NB=4*C
    L=seg.shape[1]; W=pd.shape[0]; hb=W//HD
    V=pl.BlockSpec(memory_space=pltpu.VMEM); A=pl.BlockSpec(memory_space=pl.ANY)
    S=lambda *sh: pltpu.SemaphoreType.DMA(sh) if sh else pltpu.SemaphoreType.DMA
    B=lambda *sh: jax.ShapeDtypeStruct(sh,bf16)
    F=lambda *sh: jax.ShapeDtypeStruct(sh,f32)
    M=lambda *sh: pltpu.VMEM(sh,bf16)
    col=M(2*Z,Dd,nC)
    return pl.pallas_call(functools.partial(fwd_kernel,Z,C,n),
        out_shape=(B(NB,n,D),B(NB*G,n,D),B(4,nC,D),B(G,4,nC,D),B(NB,G,4,W,n),B(4,nC,L),B(NB*G,4,W,n),F(4*hb,1,L),F(L,128),F(1,L),B(NB,n,D)),
        in_specs=[A,A,A,A,V,V,V],out_specs=(A,A,A,A,A,A,A,V,V,V,A),
        scratch_shapes=[M(NB,n,D),M(NB*G,n,D),M(4,nC,D),M(4,nC,L),M(NB*G,4,W,n),col,col,col,M(2,Dd,nC),M(4,nC,D),M(hb,L,HD),
            pltpu.VMEM((2,L,BQ),f32),pltpu.VMEM((R,L),jnp.int32),
            S(NB),S(NB),S(G-1,NB),S(NB*G),S(2*Z),S(2*Z),S(2*Z),S(2*Z),S(2*Z),S(2*Z),S(),S(),
            S(4),S(4),S(2),S(2),S(4),S(4),S(G-1,4),S(G,4),S(4),S(G-1,NB,4),S(G,NB,4),S(NB,4),S(),S(),S(6),S(2,4),S(NB),S(NB)],
        compiler_params=pltpu.CompilerParams(collective_id=0,has_side_effects=True,vmem_limit_bytes=60*2**20),
        cost_estimate=pl.CostEstimate(flops=3*10**10,bytes_accessed=10**8,transcendentals=0),
        name="forward")(tokens,w1h,w2h,cot,gain.reshape(1,D),pd,seg)

def prep_kernel(Ch, wq_ref, wk_ref, wv_ref, wo_ref, wu_ref, wd_ref, qs_ref, w1_ref, w2_ref, pd_ref):
    for ref,three in ((w1_ref,(wq_ref[...],wk_ref[...],wv_ref[...])),(w2_ref,(wo_ref[...],wu_ref[...],wd_ref[...]))):
        for i,w in enumerate(three):
            for h in range(2): ref[h,:,i*Ch:(i+1)*Ch]=w[:,h*Ch:(h+1)*Ch]
    v=qs_ref[...]
    per_dim=scale_base/math.sqrt(HD)*(jnp.maximum(v,0.0)+jnp.log(1.0+jnp.exp(-jnp.abs(v))))
    col=jnp.broadcast_to(per_dim,(128,HD)).T
    for h in range(pd_ref.shape[0]//HD): pd_ref[h*HD:(h+1)*HD,:]=col

def prep(wq, wk, wv, wo, wu, wd, qs):
    Dd,Ct=wq.shape; Ch=Ct//2
    B=jax.ShapeDtypeStruct((2,Dd,3*Ch),bf16)
    return pl.pallas_call(functools.partial(prep_kernel,Ch),out_shape=(B,B,jax.ShapeDtypeStruct((Ch,128),f32)),
        compiler_params=pltpu.CompilerParams(vmem_limit_bytes=60*2**20),name="prep")(wq,wk,wv,wo.T,wu,wd.T,qs.reshape(1,-1))


def mid_kernel(Z, C, n, mix_ref, w2_ref, xo_ref, cot_ref, coto_ref, gain_ref,
               bo_ref, bh_ref, do_ref, gm_ref, fb_ref, vec_ref,
               wo_scr, wu_scr, wd_scr, mi_scr, hid_scr, gup_scr, ga_scr, gt_scr, gs_scr, gr_scr, co_scr, up_scr, mid_scr,
               wl, dos, dors, dol, gss, grs, cot_s, cot_r, out_s, fo_s, bos, bors):
    z,k,q,s=[lax.axis_index(a) for a in AXES]
    G=2*C; g0=k*C+s; NB=4*C
    D=gain_ref.shape[1]; K4=wo_scr.shape[0]//G; Ch=K4//4; N=NB*n
    peers=list(itertools.product(range(2),range(C)))[1:]
    pdev=[(z,lax.rem(k+gc,2),q,lax.rem(s+gs,C)) for gc,gs in peers]
    pidx=[lax.rem(k+gc,2)*C+lax.rem(s+gs,C) for gc,gs in peers]
    back=[gc*C+(C-gs)%C for gc,gs in peers]
    fore=[gc*C+gs for gc,gs in peers]
    wcp=[]
    for i,dst in enumerate((wo_scr,wu_scr,wd_scr)):
        wcp.append([pltpu.make_async_copy(w2_ref.at[g,m,pl.ds(i*Ch,Ch),:],dst.at[pl.ds((g*4+m)*Ch,Ch),:],wl.at[i,g,m]) for g in range(G) for m in range(4)])
        for cp in wcp[i]: cp.start()
    cots=spread_copies(C,n,cot_ref,co_scr,cot_s,cot_r)
    greet(Z,C)
    spread_far(cots,"start")
    for b in near_blocks(C): pltpu.make_async_copy(coto_ref.at[b],co_scr.at[b],cot_r.at[b]).start()
    order=[partner(q,m)*C+(lax.rem(s+t,C)) for m in range(4) for t in range(C)]
    def rows(b): return pl.ds(pl.multiple_of(b*n,n),n)
    outs=[]
    def put(src,dst,sem):
        cp=pltpu.make_async_copy(src,dst,sem); cp.start(); outs.append(cp)
    vec_ref[...]=jnp.zeros_like(vec_ref)
    for cp in wcp[0]: cp.wait()
    for e,b in enumerate(order):
        attn=dot(mix_ref[b].reshape(G*K4,n),wo_scr[...],TN)
        middle=xo_ref[b].astype(f32)+attn
        mid_scr[b]=middle
        inv=lax.rsqrt(jnp.mean(middle*middle,axis=-1,keepdims=True)+norm_eps)
        mi_scr[rows(b),:]=(middle*inv*gain_ref[...]).astype(bf16)
        if e==0:
            for cp in wcp[1]+wcp[2]: cp.wait()
        up=dot(mi_scr[rows(b),:],wu_scr[...],NT)
        up_scr[b]=up
        hid_scr[rows(b),:]=(up*(1.0/(1.0+jnp.exp(-up)))).astype(bf16)
        gs_scr[rows(b),:]=(middle+dot(hid_scr[rows(b),:],wd_scr[...])).astype(bf16)
        put(gs_scr.at[rows(b)],bo_ref.at[b],out_s.at[0,e])
    exch=[]
    home=[]
    boouts=list(outs); outs=[]
    for e,b in enumerate(order):
        if e<3*C: pltpu.make_async_copy(coto_ref.at[b],co_scr.at[b],cot_r.at[b]).wait()
        else: arrived(co_scr.at[b],cot_r.at[b])
        boouts[e].wait()
        dst=bh_ref.at[lax.rem(q,2),pl.ds(pl.multiple_of((k*C+s)*n,n),n),:]
        rs=bors.at[(lax.rem(q,2)*2+k)*C+s]
        mine=is_home()&(b==q*C+s)
        home.append((mine,pltpu.make_async_copy(bo_ref.at[b],dst,rs),rcopy(bo_ref.at[b],dst,bos.at[e],rs,(z,lax.div(q,2),lax.div(b,C),lax.rem(b,C)))))
        spread_start(home[-1:])
        gh=dot(co_scr[b],wd_scr[...],NT)
        up=up_scr[b]
        sg=1.0/(1.0+jnp.exp(-up))
        gup_scr[rows(b),:]=(gh*(sg*(1.0+up*(1.0-sg)))).astype(bf16)
        gmlp=dot(gup_scr[rows(b),:],wu_scr[...])
        middle=mid_scr[b]
        inv=lax.rsqrt(jnp.mean(middle*middle,axis=-1,keepdims=True)+norm_eps)
        n2=middle*inv
        dn=gmlp*gain_ref[...]
        gm=co_scr[b].astype(f32)+inv*(dn-n2*jnp.mean(dn*n2,axis=-1,keepdims=True))
        vec_ref[...]+=(gmlp*n2).reshape(n//8,8,D).sum(0)
        mid_scr[b]=gm
        put(mid_scr.at[b],gm_ref.at[b],out_s.at[1,e])
        ga_scr[rows(b),:]=gm.astype(bf16)
        gt_scr[b]=dot(wo_scr[...],ga_scr[rows(b),:],NT).astype(bf16).reshape(G,4,Ch,n)
        lc=pltpu.make_async_copy(gt_scr.at[b,0],do_ref.at[b*G+g0],dol.at[e])
        lc.start(); exch.append(lc)
        for i in range(G-1):
            cp=rcopy(gt_scr.at[b,fore[i]],do_ref.at[b*G+g0],dos.at[i,e],dors.at[b*G+g0],pdev[i])
            cp.start(); exch.append(cp)
    def wgrad(i,g):
        cs=slice(g*K4,(g+1)*K4)
        if i==0: return dot(jnp.concatenate([mix_ref[b,g].reshape(K4,n) for b in range(NB)],1),ga_scr[...])
        if i==1: return dot(gup_scr[:,cs],mi_scr[...],TN)
        return dot(hid_scr[:,cs],co_scr[...].reshape(N,D),TN)
    for cp in outs: cp.wait()
    outs=[]
    def part(j,i): return pl.ds((j*3+i)*K4,K4)
    gcp=[[None]*3 for j in range(G-1)]
    for j in range(G-1):
        for i in range(3):
            gs_scr[part(j,i),:]=wgrad(i,fore[j]).astype(bf16)
            gcp[j][i]=rcopy(gs_scr.at[part(j,i)],gr_scr.at[back[j]-1,i],gss.at[j,i],grs.at[back[j]-1,i],pdev[j])
            gcp[j][i].start()
    for i in range(3):
        t=wgrad(i,0)
        for j in range(G-1):
            arrived(gr_scr.at[fore[j]-1,i],grs.at[fore[j]-1,i])
            t=t+gr_scr[fore[j]-1,i].astype(f32)
        gcp[0][i].wait_send()
        gs_scr[part(0,i),:]=t.astype(bf16)
        for m in range(4):
            put(gs_scr.at[pl.ds(i*K4+m*Ch,Ch)],fb_ref.at[m,pl.ds(i*Ch,Ch)],fo_s.at[i,m])
    for b in range(NB):
        for i in range(G-1): arrived(do_ref.at[b*G+pidx[i]],dors.at[b*G+pidx[i]])
    for i,cp in enumerate(exch):
        if i%G==0: cp.wait()
        else: cp.wait_send()
    for cps in gcp[1:]:
        for cp in cps: cp.wait_send()
    spread_far(cots,"sent")
    home_arrived(C,n,bh_ref,bors)
    spread_sent(home)
    for cp in outs: cp.wait()

def middle(Z, C, mix, w2o, xo, cot, coto, gain):
    NB,n,D=xo.shape; G=2*C; nC=w2o.shape[2]; Ch=nC//3; K4=4*Ch; N=NB*n
    V=pl.BlockSpec(memory_space=pltpu.VMEM); A=pl.BlockSpec(memory_space=pl.ANY)
    S=lambda *sh: pltpu.SemaphoreType.DMA(sh)
    M=lambda *sh: pltpu.VMEM(sh,bf16)
    B=lambda *sh: jax.ShapeDtypeStruct(sh,bf16)
    return pl.pallas_call(functools.partial(mid_kernel,Z,C,n),
        out_shape=(B(NB,n,D),B(*cot.shape),B(NB*G,4,Ch,n),jax.ShapeDtypeStruct((NB,n,D),f32),B(4,nC,D),jax.ShapeDtypeStruct((8,D),f32)),
        in_specs=[V,A,V,A,A,V],out_specs=(A,A,A,A,A,V),
        scratch_shapes=[M(G*K4,D)]*3+[M(N,G*K4) if i in (1,2) else M(N,D) for i in range(4)]+[M(NB,G,4,Ch,n),M((G-1)*3*K4,D),M(G-1,3,K4,D),M(NB,n,D),pltpu.VMEM((NB,n,G*K4),f32),pltpu.VMEM((NB,n,D),f32),
            S(3,G,4),S(G-1,NB),S(NB*G),S(NB),S(G-1,3),S(G-1,3),S(NB),S(NB),S(2,NB),S(3,4),S(NB),S(4*C)],
        compiler_params=pltpu.CompilerParams(collective_id=2,has_side_effects=True,vmem_limit_bytes=60*2**20),
        cost_estimate=pl.CostEstimate(flops=3*10**10,bytes_accessed=10**8,transcendentals=0),
        name="middle")(mix,w2o,xo,cot,coto,gain.reshape(1,D))

def bwd_kernel(Z, C, n, qkv_ref, ot_ref, do_ref, lse_ref, pd_ref, segk_ref, segq_ref, ain_ref, wts_ref,
               xo_ref, gmid_ref, gain_ref, vec_ref, fb_ref,
               gi_ref, gwm_ref, gwq_ref, vo_ref,
               kv_scr, k_scr, v_scr, p_scr, ds_scr, dq_scr, dl_scr, dv_scr, dk_scr, a_scr, st_scr, dw_scr, qr_scr, fr_scr, zs_scr, zr_scr, t3_scr, t3r_scr, tb_scr, ot_scr, do_scr,
               dx_scr, dxr_scr, own_scr, xb_scr, gb_scr, va_scr, vb_scr, vs_scr, sc_scr,
               fs, frs, qs, qrs, zss, zrs, t3s, t3rs, cs_, crs, dxs, dxrs, gis, girs, ld, al, otl, dol, kvl, xl, vas, vars_, vbs, vbrs):
    z,k,q,s=[lax.axis_index(a) for a in AXES]
    G=2*C; g0=k*C+s; NB=4*C
    D=gain_ref.shape[1]; L=segq_ref.shape[1]; W=pd_ref.shape[0]; hb=W//HD; nb=L//BQ; sub=BQ//n
    nC=3*W; Dd=gwm_ref.shape[1]
    peers=list(itertools.product(range(2),range(C)))[1:]
    pdev=[(z,lax.rem(k+gc,2),q,lax.rem(s+gs,C)) for gc,gs in peers]
    pidx=[lax.rem(k+gc,2)*C+lax.rem(s+gs,C) for gc,gs in peers]
    back=[gc*C+(C-gs)%C for gc,gs in peers]
    fore=[gc*C+gs for gc,gs in peers]
    chipdev=[(z,k,partner(q,m),s) for m in range(4)]
    core=(z,1-k,q,s)
    zdev=[lax.rem(z+j,Z) for j in range(Z)]
    fcp={m: rcopy(fb_ref.at[m],fr_scr.at[m-1],fs.at[m],frs.at[m],chipdev[m]) for m in (1,2)}
    qcp={m: rcopy(dw_scr.at[m-1],qr_scr.at[m-1],qs.at[m],qrs.at[m],chipdev[m]) for m in (1,2)}
    zcp=[[rcopy(zs_scr.at[e%2,zdev[j]],zr_scr.at[e,z],zss.at[e,j],zrs.at[e,z],(zdev[j],k,q,s)) for j in range(1,Z)] for e in range(4)]
    t3cp=[rcopy(tb_scr.at[e],t3r_scr.at[e],t3s.at[e],t3rs.at[e],chipdev[3]) for e in range(2)]
    gws=(gwm_ref,gwq_ref)
    ccp=[rcopy(t3_scr.at[e,pl.ds(pl.multiple_of((1-k)*Dd,Dd),Dd),:],gws[e].at[k],cs_.at[e],crs.at[e],core) for e in range(2)]
    def load(src,dst,i):
        cp=pltpu.make_async_copy(src,dst,ld.at[i]); cp.start(); return cp
    def zsend(e, value):
        rows=D//Z; per=max(1,640//rows)
        for i in range(Z//per):
            ls=slice(i*per*rows,(i+1)*per*rows)
            zs_scr[e%2,i*per:(i+1)*per]=value(ls).T.reshape(per,rows,nC).astype(bf16)
        for cp in zcp[e]: cp.start()
    def zsum(e):
        for cp in zcp[e]: cp.wait_send()
        t=zs_scr[e%2,z].astype(f32)
        for j in range(1,Z):
            arrived(zr_scr.at[e,zdev[j]],zrs.at[e,zdev[j]])
            t=t+zr_scr[e,zdev[j]].astype(f32)
        return t
    def diag(e):
        tb_scr[e]=zsum(e).astype(bf16)
        t3cp[e].start()
    def final(e):
        t=zsum(2+e)
        arrived(t3r_scr.at[e],t3rs.at[e])
        t=t+t3r_scr[e].astype(f32)
        t3cp[e].wait_send()
        t3_scr[e]=t
        ccp[e].start()
        gws[e][k]=t3_scr[e,pl.ds(pl.multiple_of(k*Dd,Dd),Dd),:]
    kvcp=[pltpu.make_async_copy(qkv_ref.at[m],kv_scr.at[m],kvl.at[m]) for m in range(4)]
    for m in (3,2,1,0): kvcp[m].start()
    acp=pltpu.make_async_copy(ain_ref,a_scr,al)
    acp.start()
    def otcp(m): return pltpu.make_async_copy(ot_ref.at[:,m],ot_scr,otl)
    otcp(3).start()
    def docp(idx): return pltpu.make_async_copy(do_ref.at[:,3-idx],do_scr.at[lax.rem(idx,2)],dol.at[lax.rem(idx,2)])
    docp(0).start()
    greet(Z,C)
    for m in (1,2): fcp[m].start()
    load(fb_ref.at[3],st_scr,0).wait()
    zsend(0,lambda ls: st_scr[:,ls].astype(f32))
    sc_scr[...]=jnp.zeros_like(sc_scr)
    rowi=lax.broadcasted_iota(jnp.int32,(BQ,BQ),0)
    coli=lax.broadcasted_iota(jnp.int32,(BQ,BQ),1)
    hs=[slice(h*HD,(h+1)*HD) for h in range(hb)]
    H2=BQ//2

    def block(idx,_):
        m=3-idx
        pltpu.make_async_copy(qkv_ref.at[m],kv_scr.at[m],kvl.at[m]).wait()
        for h in range(hb):
            k_scr[h]=kv_scr[m,W+h*HD:W+(h+1)*HD,:].T
            v_scr[h]=kv_scr[m,2*W+h*HD:2*W+(h+1)*HD,:].T
        slot=lax.rem(idx,2)
        docp(idx).wait()
        @pl.when(idx<3)
        def _(): docp(idx+1).start()
        def tile(h,i):
            return jnp.concatenate([do_scr[slot,i*sub+t,hs[h],:] for t in range(sub)],1) if sub>1 else do_scr[slot,i,hs[h],:]
        otcp(m).wait()
        for i in range(nb):
            for h in range(hb):
                for t in range(sub):
                    B_=i*sub+t
                    dl_scr[h,:,B_*n:(B_+1)*n]=(do_scr[slot,B_,hs[h],:].astype(f32)*ot_scr[B_,hs[h],:].astype(f32)).sum(0,keepdims=True)
        @pl.when(m>0)
        def _(): otcp(m-1).start()
        units=[(j,h,i) for j in range(nb) for h in range(hb) for i in range(j,nb)]
        def phase_a(u):
            j,h,i=units[u]; cs=slice(i*BQ,(i+1)*BQ)
            for a in range(2):
                ks=slice(j*BQ+a*H2,j*BQ+(a+1)*H2)
                t=dot(k_scr[h,ks,:],kv_scr[m,hs[h],cs])
                dp=dot(v_scr[h,ks,:],tile(h,i))
                sk=segk_ref[ks,:]
                ok=jnp.concatenate([sk]*(BQ//128),axis=1)==segq_ref[:,cs]
                if j==i: ok=ok&(rowi[a*H2:(a+1)*H2]<=coli[a*H2:(a+1)*H2])
                p=jnp.exp(jnp.where(ok,t-lse_ref[m*hb+h,:,cs],NEG))
                p_scr[u%2,a*H2:(a+1)*H2,:]=p.astype(bf16)
                ds_scr[u%2,a*H2:(a+1)*H2,:]=(p*(dp-dl_scr[h,:,cs])).astype(bf16)
                yield
        def phase_b(u):
            j,h,i=units[u]; js=slice(j*BQ,(j+1)*BQ); cs=slice(i*BQ,(i+1)*BQ)
            p=p_scr[u%2]; ds=ds_scr[u%2]
            dv=dot(tile(h,i),p,NT); dk=dot(kv_scr[m,hs[h],cs],ds,NT)
            if i==j: dv_scr[h]=dv; dk_scr[h]=dk
            else: dv_scr[h]+=dv; dk_scr[h]+=dk
            yield
            dq=dot(kv_scr[m,W+h*HD:W+(h+1)*HD,js],ds)
            if j==0: dq_scr[hs[h],cs]=dq
            else: dq_scr[hs[h],cs]+=dq
            if i==nb-1:
                kv_scr[m,W+h*HD:W+(h+1)*HD,js]=dk_scr[h].astype(bf16)
                kv_scr[m,2*W+h*HD:2*W+(h+1)*HD,js]=dv_scr[h].astype(bf16)
            yield
        merge(phase_a(0))
        for u in range(len(units)):
            gs=[phase_b(u)]
            if u+1<len(units): gs=[phase_a(u+1)]+gs
            merge(*gs)
        dq=dq_scr[...]
        sc_scr[...]+=(dq*kv_scr[m,:W,:].astype(f32)).sum(1,keepdims=True)/pd_ref[:,:1]
        kv_scr[m,:W,:]=(dq*pd_ref[:,:1]).astype(bf16)
        @pl.when(idx==0)
        def _():
            acp.wait()
            zsend(1,lambda ls: dwt(3,ls))
        @pl.when((idx==1)|(idx==2))
        def _():
            for c in range(D//256):
                ls=slice(c*256,(c+1)*256)
                dw_scr[m-1,:,ls]=dwt(m,ls).astype(bf16)
        @pl.when(idx==1)
        def _():
            qcp[2].start()
            diag(0)
            ld0=load(fb_ref.at[0],st_scr,0)
            for m2 in (1,2): arrived(fr_scr.at[m2-1],frs.at[m2])
            ld0.wait()
            zsend(2,lambda ls: st_scr[:,ls].astype(f32)+fr_scr[0,:,ls].astype(f32)+fr_scr[1,:,ls].astype(f32))
        @pl.when(idx==2)
        def _():
            qcp[1].start()
            diag(1)
        return 0
    def dwt(m,ls):
        return dot(kv_scr[m],a_scr[:,ls])
    lax.fori_loop(0,4,block,0)
    for m2 in (1,2): arrived(qr_scr.at[m2-1],qrs.at[m2])
    zsend(3,lambda ls: dwt(0,ls)+qr_scr[0,:,ls].astype(f32)+qr_scr[1,:,ls].astype(f32))
    wcp=[pltpu.make_async_copy(wts_ref.at[m],a_scr.at[pl.ds(m*nC,nC),:],kvl.at[m]) for m in range(4)]
    for cp in wcp: cp.start()
    for cp in wcp: cp.wait()

    def chunk(i):
        gl=kv_scr[:,:,pl.ds(pl.multiple_of(i*BQ,BQ),BQ)].reshape(4*nC,BQ)
        return dot(gl,a_scr[:4*nC,:],TN)
    def xload(b):
        return [pltpu.make_async_copy(xo_ref.at[b],xb_scr.at[b%2],xl.at[0,b%2]),pltpu.make_async_copy(gmid_ref.at[b],gb_scr.at[b%2],xl.at[1,b%2])]
    for cp in xload(0): cp.start()
    dxcp=[[rcopy(dx_scr.at[i,b],dxr_scr.at[back[i]-1,b],dxs.at[i,b],dxrs.at[back[i],b],pdev[i]) for b in range(NB)] for i in range(G-1)]
    for b in range(NB):
        if sub==1:
            for i in range(G-1):
                dx_scr[i,b]=chunk(b*G+pidx[i]).astype(bf16)
                dxcp[i][b].start()
        else:
            own_scr[...]=chunk(b)
            for i in range(G-1):
                dx_scr[i,b]=own_scr[pl.ds(pl.multiple_of(pidx[i]*n,n),n),:].astype(bf16)
                dxcp[i][b].start()
    gicp=home_copies(C,n,dx_scr.at[0],gi_ref,gis,girs)
    gpart=None
    for b in range(NB):
        if b+1<NB:
            for cp in xload(b+1): cp.start()
        if sub==1:
            gain=chunk(b*G+g0)
        else:
            own_scr[...]=chunk(b)
            gain=own_scr[pl.ds(pl.multiple_of(g0*n,n),n),:]
        for i in range(G-1):
            arrived(dxr_scr.at[fore[i]-1,b],dxrs.at[fore[i],b])
            gain=gain+dxr_scr[fore[i]-1,b].astype(f32)
        for cp in xload(b): cp.wait()
        x=xb_scr[b%2].astype(f32)
        inv=lax.rsqrt(jnp.mean(x*x,axis=-1,keepdims=True)+norm_eps)
        nx=x*inv
        dn=gain*gain_ref[...]
        gin=gb_scr[b%2]+inv*(dn-nx*jnp.mean(dn*nx,axis=-1,keepdims=True))
        gp=(gain*nx).reshape(n//8,8,D).sum(0)
        gpart=gp if gpart is None else gpart+gp
        dxcp[0][b].wait_send()
        dx_scr[0,b]=gin.astype(bf16)
        spread_start(gicp[b:b+1])
    vs_scr[...]=jnp.zeros_like(vs_scr)
    vs_scr[0:1,:]=gpart.sum(0,keepdims=True)
    vs_scr[1:2,:]=vec_ref[...].sum(0,keepdims=True)
    sc=sc_scr[0:HD,:]
    for h in range(1,hb): sc=sc+sc_scr[h*HD:(h+1)*HD,:]
    vs_scr[2:3,0:HD]=sc.T[0:1,:]
    me=(k*4+q)*C+s
    va_scr[me]=vs_scr[...]
    plane=list(itertools.product(range(2),range(4),range(C)))[1:]
    vacp=[rcopy(vs_scr,va_scr.at[me],vas.at[i],vars_.at[me],(z,lax.rem(k+a,2),lax.rem(q+b,4),lax.rem(s+c,C))) for i,(a,b,c) in enumerate(plane)]
    for cp in vacp: cp.start()
    final(0)
    for a,b,c in plane:
        o=(lax.rem(k+a,2)*4+lax.rem(q+b,4))*C+lax.rem(s+c,C)
        arrived(va_scr.at[o],vars_.at[o])
    t=va_scr[0]
    for i in range(1,8*C): t=t+va_scr[i]
    vb_scr[z]=t
    vbcp=[rcopy(vb_scr.at[z],vb_scr.at[z],vbs.at[j],vbrs.at[z],(zdev[j],k,q,s)) for j in range(1,Z)]
    for cp in vbcp: cp.start()
    final(1)
    for j in range(1,Z): arrived(vb_scr.at[zdev[j]],vbrs.at[zdev[j]])
    t=vb_scr[0]
    for i in range(1,Z): t=t+vb_scr[i]
    vo_ref[...]=t
    for e in range(2):
        arrived(gws[e].at[1-k],crs.at[e])
        ccp[e].wait_send()
    home_arrived(C,n,gi_ref,girs)
    spread_sent(gicp)
    for i in range(1,G-1):
        for b in range(NB): dxcp[i][b].wait_send()
    for m in (1,2):
        fcp[m].wait_send(); qcp[m].wait_send()
    for cp in vacp+vbcp: cp.wait_send()

def backward(Z, C, qkv, ot, do, lse, pd, segk, segq, ain, wts, xo, gmid, gain, vec, fb, R, Pn, Dd):
    NB,n,D=xo.shape; G=2*C; nC=wts.shape[1]; W=pd.shape[0]; hb=W//HD; L=segq.shape[1]
    V=pl.BlockSpec(memory_space=pltpu.VMEM); A=pl.BlockSpec(memory_space=pl.ANY)
    S=lambda *sh: pltpu.SemaphoreType.DMA(sh) if sh else pltpu.SemaphoreType.DMA
    M=lambda *sh: pltpu.VMEM(sh,bf16)
    F=lambda *sh: pltpu.VMEM(sh,f32)
    gw=jax.ShapeDtypeStruct((2,Dd,nC),f32)
    return pl.pallas_call(functools.partial(bwd_kernel,Z,C,n),
        out_shape=(jax.ShapeDtypeStruct((R,Pn,D),bf16),gw,gw,jax.ShapeDtypeStruct((8,D),f32)),
        in_specs=[A,A,A,V,V,V,V,A,A,A,A,V,V,A],out_specs=(A,V,V,V),
        scratch_shapes=[M(4,nC,L),M(hb,L,HD),M(hb,L,HD),M(2,BQ,BQ),M(2,BQ,BQ),F(W,L),F(hb,1,L),F(hb,HD,BQ),F(hb,HD,BQ),M(L,D),
            M(nC,D),M(2,nC,D),M(2,nC,D),M(2,nC,D),M(2,Z,D//Z,nC),M(4,Z,D//Z,nC),F(2,D//Z,nC),M(2,D//Z,nC),M(2,D//Z,nC),M(NB*G,W,n),M(2,NB*G,W,n),
            M(G-1,NB,n,D),M(G-1,NB,n,D),F(BQ,D) if n<BQ else F(8,128),M(2,n,D),F(2,n,D),F(8*C,8,D),F(Z,8,D),F(8,D),F(W,1),
            S(4),S(4),S(4),S(4),S(4,Z),S(4,Z),S(2),S(2),S(2),S(2),S(G,NB),S(G,NB),S(NB),S(4*C),S(4),S(),S(),S(2),S(4),S(2,2),S(8*C),S(8*C),S(Z),S(Z)],
        compiler_params=pltpu.CompilerParams(collective_id=1,has_side_effects=True,vmem_limit_bytes=58*2**20),
        cost_estimate=pl.CostEstimate(flops=6*10**10,bytes_accessed=10**8,transcendentals=0),
        name="backward")(qkv,ot,do,lse,pd,segk,segq,ain.reshape(L,D),wts,xo,gmid,gain.reshape(1,D),vec,fb)

def finish_kernel(Ch, gi_ref, gwm_ref, gwq_ref, vo_ref, sf_ref, ig_ref, gq_ref, gk_ref, gv_ref, go_ref, gu_ref, gd_ref, ga_ref, gs_ref, gm_ref):
    ig_ref[...]=gi_ref[...].astype(f32)
    @pl.when(pl.program_id(0)==0)
    def _():
        def cols(ref,i):
            return jnp.concatenate([ref[0,:,i*Ch:(i+1)*Ch],ref[1,:,i*Ch:(i+1)*Ch]],1)
        for i,o in enumerate((gq_ref,gk_ref,gv_ref)): o[...]=cols(gwq_ref,i)
        go_ref[...]=cols(gwm_ref,0)
        gu_ref[...]=cols(gwm_ref,1)
        gd_ref[...]=cols(gwm_ref,2)
        ga_ref[...]=vo_ref[0,:]
        gm_ref[...]=vo_ref[1,:]
        gs_ref[...]=vo_ref[2,0:HD]*sf_ref[0,:]

def finish(gi, gwm, gwq, vo, sf):
    R,Pn,D=gi.shape; _,Dd,nC=gwm.shape; Ch=nC//3; T=4
    F=lambda *sh: jax.ShapeDtypeStruct(sh,f32)
    full=lambda *sh: pl.BlockSpec(sh,lambda i: (0,)*len(sh))
    row=pl.BlockSpec((R,Pn//T,D),lambda i:(0,i,0))
    shapes=[(Dd,2*Ch)]*6+[(D,),(HD,),(D,)]
    return pl.pallas_call(functools.partial(finish_kernel,Ch),grid=(T,),
        out_shape=(F(R,Pn,D),)+tuple(F(*sh) for sh in shapes),
        in_specs=[row,full(2,Dd,nC),full(2,Dd,nC),full(8,D),full(1,HD)],
        out_specs=(row,)+tuple(full(*sh) for sh in shapes),
        compiler_params=pltpu.CompilerParams(vmem_limit_bytes=60*2**20),
        name="finish")(gi,gwm,gwq,vo,sf.reshape(1,HD))


def make_local(Z, C):
    def local(tokens, segments, attn_gain, w_query, w_key, w_value, w_out, query_scale, mlp_gain, w_up, w_down, cotangent):
        R,Pn,D=tokens.shape
        Dd=w_query.shape[0]

        w1h,w2h,pd=prep(w_query,w_key,w_value,w_out,w_up,w_down,query_scale)
        xo,ain,wts,w2o,mix,qkv,ot,lse,segk,segq,coto=forward(Z,C,tokens,w1h,w2h,cotangent,attn_gain,pd,segments)
        _,block_out,do,gmid,fb,vec=middle(Z,C,mix,w2o,xo,cotangent,coto,mlp_gain)
        gi,gwm,gwq,vo=backward(Z,C,qkv,ot,do,lse,pd,segk,segq,ain,wts,xo,gmid,attn_gain,vec,fb,R,Pn,Dd)
        sf=(scale_base/math.sqrt(HD))*jax.nn.sigmoid(query_scale)
        ig,gq,gk,gv,go,gu,gd,ga,gs,gm=finish(gi,gwm,gwq,vo,sf)
        return (block_out,ig,ga,gq,gk,gv,go.T,gs,gm,gu,gd.T)
    return local

def solution(mesh):
    dp,T=mesh.shape["dp"],mesh.shape["tensor"]
    Z,C=dp//2,T//4
    fine=Mesh(mesh.devices.reshape(Z,2,4,C),AXES)
    dpx=("zz","core"); tx=("q","s")
    in_specs=(P(dpx,tx,None),P(dpx,None),P(),P(dpx,tx),P(dpx,tx),P(dpx,tx),P(tx,dpx),P(),P(),P(dpx,tx),P(tx,dpx),P(dpx,tx,None))
    out_specs=(P(dpx,tx,None),P(dpx,tx,None),P(),P(dpx,tx),P(dpx,tx),P(dpx,tx),P(tx,dpx),P(),P(),P(dpx,tx),P(tx,dpx))
    return jax.shard_map(make_local(Z,C),mesh=fine,in_specs=in_specs,out_specs=out_specs,check_vma=False)
```

```python
import functools
import itertools
import math
import jax, jax.numpy as jnp
from jax import lax
from jax.experimental import pallas as pl
from jax.experimental.pallas import tpu as pltpu
from jax.sharding import Mesh, PartitionSpec as P

AXES=("zz","core","q","s")
norm_eps = 1e-06
HD=80
BQ=256
NEG=-1e30
f32=jnp.float32; bf16=jnp.bfloat16
NT=(((1,),(1,)),((),()))
NN=(((1,),(0,)),((),()))
TN=(((0,),(0,)),((),()))
def dot(a,b,dims=NN): return lax.dot_general(a,b,dims,preferred_element_type=f32)

def merge(*gens):
    gens=list(gens)
    while gens:
        for g in list(gens):
            try: next(g)
            except StopIteration: gens.remove(g)


MESH=pl.DeviceIdType.MESH
scale_base = 1.442695041

def rcopy(src,dst,ss,rs,dev):
    return pltpu.make_async_remote_copy(src_ref=src,dst_ref=dst,send_sem=ss,recv_sem=rs,device_id=dev,device_id_type=MESH)

def transpose_rows(src, dst):
    P_,rows,cols=src.shape
    per=max(1,640//rows)
    for i in range(P_//per):
        dst[:,i*per*rows:(i+1)*per*rows]=src[i*per:(i+1)*per].reshape(per*rows,cols).T

def partner(q, m):
    return (q,q+1-2*lax.rem(q,2),lax.rem(q+2,4),3-q)[m]

def greet(Z, C):
    z,k,q,s=[lax.axis_index(a) for a in AXES]
    bar=pltpu.get_barrier_semaphore()
    plane=list(itertools.product(range(2),range(4),range(C)))[1:]
    column=[(j,a) for j in range(1,Z) for a in range(2)]
    for a,b,c in plane:
        pl.semaphore_signal(bar,inc=1,device_id=(z,lax.rem(k+a,2),lax.rem(q+b,4),lax.rem(s+c,C)),device_id_type=MESH)
    for j,a in column:
        pl.semaphore_signal(bar,inc=1,device_id=(lax.rem(z+j,Z),lax.rem(k+a,2),q,s),device_id_type=MESH)
    pl.semaphore_wait(bar,len(plane)+len(column))

def col_copies(Z, src, dst, ss, rs):
    z,k,q,s=[lax.axis_index(a) for a in AXES]
    out=[]
    for j in range(Z):
        for a in range(2):
            kk=lax.rem(k+a,2)
            if j==0 and a==0: out.append(pltpu.make_async_copy(src.at[k],dst.at[2*z+k],rs.at[2*z+k]))
            else: out.append(rcopy(src.at[kk],dst.at[2*z+k],ss.at[j*2+a],rs.at[2*z+k],(lax.rem(z+j,Z),kk,q,s)))
    return out

def spread_copies(C, n, src, dst, ss, rs):
    z,k,q,s=[lax.axis_index(a) for a in AXES]
    out=[]
    for rr in range(2):
        r=lax.rem(q+rr,2)
        for h in range(2):
            for s2 in range(C):
                i=(rr*2+h)*C+s2
                piece=src.at[r,pl.ds((h*C+s2)*n,n),:]
                out.append((rr,(k==h)&(q==2*k+r)&(s==s2),pltpu.make_async_copy(piece,dst.at[q*C+s],rs.at[q*C+s]),
                            rcopy(piece,dst.at[q*C+s],ss.at[i],rs.at[q*C+s],(z,h,2*k+r,s2))))
    return out

def is_home(): return lax.axis_index("core")==lax.div(lax.axis_index("q"),2)

def spread_near(cps, do):
    for rr,mine,loc,cp in cps:
        if rr==0:
            @pl.when(mine)
            def _(loc=loc):
                if do=="start": loc.start()
            @pl.when(jnp.logical_not(mine))
            def _(cp=cp): cp.start() if do=="start" else cp.wait_send()
        else:
            @pl.when(is_home())
            def _(cp=cp): cp.start() if do=="start" else cp.wait_send()

def spread_far(cps, do):
    for rr,mine,loc,cp in cps:
        if rr==1:
            @pl.when(jnp.logical_not(is_home()))
            def _(cp=cp): cp.start() if do=="start" else cp.wait_send()

def near_blocks(C):
    q=lax.axis_index("q")
    return [partner(q,m)*C+t for m in range(3) for t in range(C)]

def far_blocks(C):
    q=lax.axis_index("q")
    return [partner(q,3)*C+t for t in range(C)]

def spread_start(cps):
    for mine,loc,cp in cps:
        @pl.when(mine)
        def _(loc=loc): loc.start()
        @pl.when(jnp.logical_not(mine))
        def _(cp=cp): cp.start()

def spread_sent(cps):
    for mine,loc,cp in cps:
        @pl.when(jnp.logical_not(mine))
        def _(cp=cp): cp.wait_send()

def home_copies(C, n, src, dst, ss, rs):
    z,k,q,s=[lax.axis_index(a) for a in AXES]
    out=[]
    for b in range(4*C):
        to=dst.at[lax.rem(q,2),pl.ds(pl.multiple_of((k*C+s)*n,n),n),:]
        sem=rs.at[(lax.rem(q,2)*2+k)*C+s]
        out.append(((lax.div(q,2)==k)&(q==b//C)&(s==b%C),pltpu.make_async_copy(src.at[b],to,sem),
                    rcopy(src.at[b],to,ss.at[b],sem,(z,lax.div(q,2),b//C,b%C))))
    return out

def home_arrived(C, n, dst, rs):
    for r in range(2):
        for h in range(2):
            for s2 in range(C):
                arrived(dst.at[r,pl.ds((h*C+s2)*n,n),:],rs.at[(r*2+h)*C+s2])

def arrived(ref, sem):
    z,k,q,s=[lax.axis_index(a) for a in AXES]
    rcopy(ref,ref,sem,sem,(z,1-k,q,s)).wait_recv()

def fwd_kernel(Z, C, n, x_ref, w1_ref, w2_ref, cot_ref, gain_ref, pd_ref, seg_ref,
               xo_ref, ain_ref, wts_ref, w2o_ref, mix_ref, qkv_ref, ot_ref, lse_ref, segk_ref, segq_ref, coto_ref,
               xo_scr, ain_scr, wts_scr, qkv_scr, ot_scr, wa_scr, wb_scr, wd_scr, o3_scr, w2_scr, k_scr, s_scr, so_scr,
               tok_s, tok_r, ain_s, ain_r, a_s, a_r, b_s, b_r, dd_s, dd_r, o3_s, o3_r,
               wt_s, wt_r, hf_s, hf_r, w2_s, w2_r, gr_s, gr_r, loc_s, mix_s, mix_r, mixl, sg_s, sg_r, out_s, qo_s, cot_s, cot_r):
    z,k,q,s=[lax.axis_index(a) for a in AXES]
    G=2*C; g0=k*C+s; NB=4*C
    D=gain_ref.shape[1]; L=seg_ref.shape[1]; W=pd_ref.shape[0]; hb=W//HD; nb=L//BQ; nC=3*W
    peers=list(itertools.product(range(2),range(C)))[1:]
    pdev=[(z,lax.rem(k+gc,2),q,lax.rem(s+gs,C)) for gc,gs in peers]
    pidx=[lax.rem(k+gc,2)*C+lax.rem(s+gs,C) for gc,gs in peers]
    back=[gc*C+(C-gs)%C for gc,gs in peers]
    fore=[gc*C+gs for gc,gs in peers]
    chipdev=[(z,k,partner(q,m),s) for m in range(4)]
    toks=spread_copies(C,n,x_ref,xo_scr,tok_s,tok_r)
    cots=spread_copies(C,n,cot_ref,coto_ref,cot_s,cot_r)
    ca=col_copies(Z,w1_ref,wa_scr,a_s,a_r)
    cb=col_copies(Z,w2_ref,wb_scr,b_s,b_r)
    cd=col_copies(Z,o3_scr,wd_scr,dd_s,dd_r)
    o3=rcopy(w2_ref,o3_scr,o3_s,o3_r,chipdev[3])
    wcp=[rcopy(wts_scr.at[0],wts_scr.at[m],wt_s.at[m],wt_r.at[m],chipdev[m]) for m in (1,2)]
    h1=nC//32*16; half=[pl.ds(0,h1),pl.ds(h1,nC-h1)]
    hcp=[rcopy(wts_scr.at[1,half[0]],wts_scr.at[3,half[0]],hf_s.at[0],hf_r.at[0],chipdev[2]),
         rcopy(wts_scr.at[2,half[1]],wts_scr.at[3,half[1]],hf_s.at[1],hf_r.at[1],chipdev[1])]
    save=[pltpu.make_async_copy(xo_scr,xo_ref,out_s.at[0]),pltpu.make_async_copy(ain_scr,ain_ref,out_s.at[1])]
    wsave=[pltpu.make_async_copy(wts_scr.at[m],wts_ref.at[m],out_s.at[2+m]) for m in range(4)]
    def qsave(m): return [pltpu.make_async_copy(qkv_scr.at[m],qkv_ref.at[m],qo_s.at[0,m]),pltpu.make_async_copy(ot_scr.at[:,m],ot_ref.at[:,m],qo_s.at[1,m])]
    w2cp=[rcopy(w2_scr.at[0],w2_scr.at[m],w2_s.at[m],w2_r.at[m],chipdev[m]) for m in (1,2)]
    grp=[[rcopy(w2_scr.at[m],w2o_ref.at[back[i],m],gr_s.at[i,m],gr_r.at[back[i],m],pdev[i]) for i in range(G-1)] for m in range(4)]
    loc=[pltpu.make_async_copy(w2_scr.at[m],w2o_ref.at[0,m],loc_s.at[m]) for m in range(4)]
    def share(m):
        loc[m].start()
        for cp in grp[m]: cp.start()
    sgc=rcopy(seg_ref,so_scr,sg_s,sg_r,(z,1-k,q,s))
    greet(Z,C)
    sgc.start()
    for cp in ca: cp.start()
    spread_near(toks,"start"); spread_far(toks,"start")
    o3.start()
    sgc.wait_recv()
    sg=jnp.where(k==lax.div(q,2),seg_ref[...],so_scr[...])
    sg=jnp.where(lax.rem(q,2)==0,sg[0:1],sg[1:2]).astype(f32)
    segq_ref[...]=sg
    for c in range(L//BQ):
        segk_ref[c*BQ:(c+1)*BQ,:]=jnp.broadcast_to(sg[:,c*BQ:(c+1)*BQ],(128,BQ)).T
    for i in range(2*Z): arrived(wa_scr.at[i],a_r.at[i])
    for cp in cb: cp.start()
    transpose_rows(wa_scr,wts_scr.at[0])
    for cp in wcp: cp.start()
    wsave[0].start()
    ains=[]
    for j in range(NB):
        arrived(xo_scr.at[j],tok_r.at[j])
        x=xo_scr[j].astype(f32)
        inv=lax.rsqrt(jnp.mean(x*x,axis=-1,keepdims=True)+norm_eps)
        slot=j*G+g0
        ain_scr[slot]=(x*inv*gain_ref[...]).astype(bf16)
        for i in range(G-1):
            cp=rcopy(ain_scr.at[slot],ain_scr.at[slot],ain_s.at[i,j],ain_r.at[slot],pdev[i])
            cp.start(); ains.append(cp)
    for j in range(NB):
        for i in range(G-1): arrived(ain_scr.at[j*G+pidx[i]],ain_r.at[j*G+pidx[i]])
    for cp in save: cp.start()
    rowi=lax.broadcasted_iota(jnp.int32,(BQ,BQ),0)
    coli=lax.broadcasted_iota(jnp.int32,(BQ,BQ),1)
    hs=[slice(h*HD,(h+1)*HD) for h in range(hb)]
    CH=512; per=CH//n; sub=BQ//n

    def block(m,_):
        @pl.when(m==1)
        def _():
            for i in range(2*Z): arrived(wb_scr.at[i],b_r.at[i])
            arrived(o3_scr,o3_r)
            for cp in cd: cp.start()
            transpose_rows(wb_scr,w2_scr.at[0])
            for i in (1,2): arrived(wts_scr.at[i],wt_r.at[i])
            for cp in hcp+wsave[1:3]: cp.start()
            share(0)
        @pl.when(m==2)
        def _():
            for cp in w2cp: cp.start()
        @pl.when(m==3)
        def _():
            for i in range(2): arrived(wts_scr.at[3,half[i]],hf_r.at[i])
            wsave[3].start()
            spread_near(cots,"start")
        for c in range(L//CH):
            cs=slice(c*CH,(c+1)*CH)
            r=dot(wts_scr[m],ain_scr[c*per:(c+1)*per].reshape(CH,D),NT)
            qkv_scr[m,:W,cs]=(r[:W]*pd_ref[:,:1]).astype(bf16)
            qkv_scr[m,W:,cs]=r[W:].astype(bf16)
            for h in range(hb):
                k_scr[h,cs,:]=r[W+h*HD:W+(h+1)*HD].T.astype(bf16)
        units=[(i,h) for i in range(nb) for h in range(hb)]
        st={}
        def phase_a(u):
            i,h=units[u]; c0=i*BQ
            qi=qkv_scr[m,hs[h],c0:c0+BQ]
            sq=segq_ref[:,c0:c0+BQ]
            m8=None
            for j in range(i+1):
                t=dot(k_scr[h,j*BQ:(j+1)*BQ,:],qi)
                sk=segk_ref[j*BQ:(j+1)*BQ,:]
                ok=jnp.concatenate([sk]*(BQ//128),axis=1)==sq
                if j==i: ok=ok&(rowi<=coli)
                t=jnp.where(ok,t,NEG)
                s_scr[u%2,j*BQ:(j+1)*BQ,:]=t
                mm=t.reshape(BQ//8,8,BQ).max(0)
                m8=mm if m8 is None else jnp.maximum(m8,mm)
                yield
            st[u]=m8.max(0,keepdims=True)
        def phase_b(u):
            i,h=units[u]; c0=i*BQ
            mx=st[u]; l8=None; acc=None
            for j in range(i+1):
                p=jnp.exp(s_scr[u%2,j*BQ:(j+1)*BQ,:]-mx)
                ll=p.reshape(BQ//8,8,BQ).sum(0)
                l8=ll if l8 is None else l8+ll
                pv=dot(qkv_scr[m,2*W+h*HD:2*W+(h+1)*HD,j*BQ:(j+1)*BQ],p.astype(bf16))
                acc=pv if acc is None else acc+pv
                yield
            l=l8.sum(0,keepdims=True)
            o=(acc*(1.0/l)).astype(bf16)
            for t in range(sub): ot_scr[i*sub+t,m,hs[h],:]=o[:,t*n:(t+1)*n]
            lse_ref[m*hb+h,:,c0:c0+BQ]=mx+jnp.log(l)
        merge(phase_a(0))
        for u in range(len(units)):
            gs=[phase_b(u)]
            if u+1<len(units): gs=[phase_a(u+1)]+gs
            merge(*gs)
        for b in range(NB):
            pltpu.make_async_copy(ot_scr.at[b*G+g0,m],mix_ref.at[b,0,m],mixl.at[b,m]).start()
            for i in range(G-1):
                rcopy(ot_scr.at[b*G+pidx[i],m],mix_ref.at[b,back[i],m],mix_s.at[i,b,m],mix_r.at[back[i],b,m],pdev[i]).start()
        for cp in qsave(m): cp.start()
        return 0
    lax.fori_loop(0,4,block,0)
    for m in (1,2):
        arrived(w2_scr.at[m],w2_r.at[m])
        share(m)
    for i in range(2*Z): arrived(wd_scr.at[i],dd_r.at[i])
    transpose_rows(wd_scr,w2_scr.at[3])
    share(3)
    for i in range(G-1):
        for b in range(NB):
            for m in range(4):
                arrived(mix_ref.at[b,fore[i],m],mix_r.at[fore[i],b,m])
                rcopy(ot_scr.at[b*G+pidx[i],m],mix_ref.at[b,back[i],m],mix_s.at[i,b,m],mix_r.at[back[i],b,m],pdev[i]).wait_send()
        for m in range(4): arrived(w2o_ref.at[fore[i],m],gr_r.at[fore[i],m])
    for m in range(4):
        loc[m].wait()
        for cp in grp[m]: cp.wait_send()
    for cps in (ca,cb,cd):
        for cp in cps[1:]: cp.wait_send()
    for cp in wcp+hcp+w2cp+ains+[o3,sgc]: cp.wait_send()
    spread_near(toks,"sent"); spread_far(toks,"sent"); spread_near(cots,"sent")
    for b in near_blocks(C): arrived(coto_ref.at[b],cot_r.at[b])
    for cp in save+wsave: cp.wait()
    for m in range(4):
        for cp in qsave(m): cp.wait()
        for b in range(NB): pltpu.make_async_copy(ot_scr.at[b*G+g0,m],mix_ref.at[b,0,m],mixl.at[b,m]).wait()

def forward(Z, C, tokens, w1h, w2h, cot, gain, pd, seg):
    R,Pn,D=tokens.shape; G=2*C; n=Pn//G; _,Dd,nC=w1h.shape; NB=4*C
    L=seg.shape[1]; W=pd.shape[0]; hb=W//HD
    V=pl.BlockSpec(memory_space=pltpu.VMEM); A=pl.BlockSpec(memory_space=pl.ANY)
    S=lambda *sh: pltpu.SemaphoreType.DMA(sh) if sh else pltpu.SemaphoreType.DMA
    B=lambda *sh: jax.ShapeDtypeStruct(sh,bf16)
    F=lambda *sh: jax.ShapeDtypeStruct(sh,f32)
    M=lambda *sh: pltpu.VMEM(sh,bf16)
    col=M(2*Z,Dd,nC)
    return pl.pallas_call(functools.partial(fwd_kernel,Z,C,n),
        out_shape=(B(NB,n,D),B(NB*G,n,D),B(4,nC,D),B(G,4,nC,D),B(NB,G,4,W,n),B(4,nC,L),B(NB*G,4,W,n),F(4*hb,1,L),F(L,128),F(1,L),B(NB,n,D)),
        in_specs=[A,A,A,A,V,V,V],out_specs=(A,A,A,A,A,A,A,V,V,V,A),
        scratch_shapes=[M(NB,n,D),M(NB*G,n,D),M(4,nC,D),M(4,nC,L),M(NB*G,4,W,n),col,col,col,M(2,Dd,nC),M(4,nC,D),M(hb,L,HD),
            pltpu.VMEM((2,L,BQ),f32),pltpu.VMEM((R,L),jnp.int32),
            S(NB),S(NB),S(G-1,NB),S(NB*G),S(2*Z),S(2*Z),S(2*Z),S(2*Z),S(2*Z),S(2*Z),S(),S(),
            S(4),S(4),S(2),S(2),S(4),S(4),S(G-1,4),S(G,4),S(4),S(G-1,NB,4),S(G,NB,4),S(NB,4),S(),S(),S(6),S(2,4),S(NB),S(NB)],
        compiler_params=pltpu.CompilerParams(collective_id=0,has_side_effects=True,vmem_limit_bytes=60*2**20),
        cost_estimate=pl.CostEstimate(flops=3*10**10,bytes_accessed=10**8,transcendentals=0),
        name="forward")(tokens,w1h,w2h,cot,gain.reshape(1,D),pd,seg)

def prep_kernel(Ch, wq_ref, wk_ref, wv_ref, wo_ref, wu_ref, wd_ref, qs_ref, w1_ref, w2_ref, pd_ref):
    for ref,three in ((w1_ref,(wq_ref[...],wk_ref[...],wv_ref[...])),(w2_ref,(wo_ref[...],wu_ref[...],wd_ref[...]))):
        for i,w in enumerate(three):
            for h in range(2): ref[h,:,i*Ch:(i+1)*Ch]=w[:,h*Ch:(h+1)*Ch]
    v=qs_ref[...]
    per_dim=scale_base/math.sqrt(HD)*(jnp.maximum(v,0.0)+jnp.log(1.0+jnp.exp(-jnp.abs(v))))
    col=jnp.broadcast_to(per_dim,(128,HD)).T
    for h in range(pd_ref.shape[0]//HD): pd_ref[h*HD:(h+1)*HD,:]=col

def prep(wq, wk, wv, wo, wu, wd, qs):
    Dd,Ct=wq.shape; Ch=Ct//2
    B=jax.ShapeDtypeStruct((2,Dd,3*Ch),bf16)
    return pl.pallas_call(functools.partial(prep_kernel,Ch),out_shape=(B,B,jax.ShapeDtypeStruct((Ch,128),f32)),
        compiler_params=pltpu.CompilerParams(vmem_limit_bytes=60*2**20),name="prep")(wq,wk,wv,wo.T,wu,wd.T,qs.reshape(1,-1))


def mid_kernel(Z, C, n, mix_ref, w2_ref, xo_ref, cot_ref, coto_ref, gain_ref,
               bo_ref, bh_ref, do_ref, gm_ref, fb_ref, vec_ref,
               wo_scr, wu_scr, wd_scr, mi_scr, hid_scr, gup_scr, ga_scr, gt_scr, gs_scr, gr_scr, co_scr, up_scr, mid_scr,
               wl, dos, dors, dol, gss, grs, cot_s, cot_r, out_s, fo_s, bos, bors):
    z,k,q,s=[lax.axis_index(a) for a in AXES]
    G=2*C; g0=k*C+s; NB=4*C
    D=gain_ref.shape[1]; K4=wo_scr.shape[0]//G; Ch=K4//4; N=NB*n
    peers=list(itertools.product(range(2),range(C)))[1:]
    pdev=[(z,lax.rem(k+gc,2),q,lax.rem(s+gs,C)) for gc,gs in peers]
    pidx=[lax.rem(k+gc,2)*C+lax.rem(s+gs,C) for gc,gs in peers]
    back=[gc*C+(C-gs)%C for gc,gs in peers]
    fore=[gc*C+gs for gc,gs in peers]
    wcp=[]
    for i,dst in enumerate((wo_scr,wu_scr,wd_scr)):
        wcp.append([pltpu.make_async_copy(w2_ref.at[g,m,pl.ds(i*Ch,Ch),:],dst.at[pl.ds((g*4+m)*Ch,Ch),:],wl.at[i,g,m]) for g in range(G) for m in range(4)])
        for cp in wcp[i]: cp.start()
    cots=spread_copies(C,n,cot_ref,co_scr,cot_s,cot_r)
    greet(Z,C)
    spread_far(cots,"start")
    for b in near_blocks(C): pltpu.make_async_copy(coto_ref.at[b],co_scr.at[b],cot_r.at[b]).start()
    order=[partner(q,m)*C+(lax.rem(s+t,C)) for m in range(4) for t in range(C)]
    def rows(b): return pl.ds(pl.multiple_of(b*n,n),n)
    outs=[]
    def put(src,dst,sem):
        cp=pltpu.make_async_copy(src,dst,sem); cp.start(); outs.append(cp)
    vec_ref[...]=jnp.zeros_like(vec_ref)
    for cp in wcp[0]: cp.wait()
    for e,b in enumerate(order):
        attn=dot(mix_ref[b].reshape(G*K4,n),wo_scr[...],TN)
        middle=xo_ref[b].astype(f32)+attn
        mid_scr[b]=middle
        inv=lax.rsqrt(jnp.mean(middle*middle,axis=-1,keepdims=True)+norm_eps)
        mi_scr[rows(b),:]=(middle*inv*gain_ref[...]).astype(bf16)
        if e==0:
            for cp in wcp[1]+wcp[2]: cp.wait()
        up=dot(mi_scr[rows(b),:],wu_scr[...],NT)
        up_scr[b]=up
        hid_scr[rows(b),:]=(up*(1.0/(1.0+jnp.exp(-up)))).astype(bf16)
        gs_scr[rows(b),:]=(middle+dot(hid_scr[rows(b),:],wd_scr[...])).astype(bf16)
        put(gs_scr.at[rows(b)],bo_ref.at[b],out_s.at[0,e])
    exch=[]
    home=[]
    boouts=list(outs); outs=[]
    for e,b in enumerate(order):
        if e<3*C: pltpu.make_async_copy(coto_ref.at[b],co_scr.at[b],cot_r.at[b]).wait()
        else: arrived(co_scr.at[b],cot_r.at[b])
        boouts[e].wait()
        dst=bh_ref.at[lax.rem(q,2),pl.ds(pl.multiple_of((k*C+s)*n,n),n),:]
        rs=bors.at[(lax.rem(q,2)*2+k)*C+s]
        mine=is_home()&(b==q*C+s)
        home.append((mine,pltpu.make_async_copy(bo_ref.at[b],dst,rs),rcopy(bo_ref.at[b],dst,bos.at[e],rs,(z,lax.div(q,2),lax.div(b,C),lax.rem(b,C)))))
        spread_start(home[-1:])
        gh=dot(co_scr[b],wd_scr[...],NT)
        up=up_scr[b]
        sg=1.0/(1.0+jnp.exp(-up))
        gup_scr[rows(b),:]=(gh*(sg*(1.0+up*(1.0-sg)))).astype(bf16)
        gmlp=dot(gup_scr[rows(b),:],wu_scr[...])
        middle=mid_scr[b]
        inv=lax.rsqrt(jnp.mean(middle*middle,axis=-1,keepdims=True)+norm_eps)
        n2=middle*inv
        dn=gmlp*gain_ref[...]
        gm=co_scr[b].astype(f32)+inv*(dn-n2*jnp.mean(dn*n2,axis=-1,keepdims=True))
        vec_ref[...]+=(gmlp*n2).reshape(n//8,8,D).sum(0)
        mid_scr[b]=gm
        put(mid_scr.at[b],gm_ref.at[b],out_s.at[1,e])
        ga_scr[rows(b),:]=gm.astype(bf16)
        gt_scr[b]=dot(wo_scr[...],ga_scr[rows(b),:],NT).astype(bf16).reshape(G,4,Ch,n)
        lc=pltpu.make_async_copy(gt_scr.at[b,0],do_ref.at[b*G+g0],dol.at[e])
        lc.start(); exch.append(lc)
        for i in range(G-1):
            cp=rcopy(gt_scr.at[b,fore[i]],do_ref.at[b*G+g0],dos.at[i,e],dors.at[b*G+g0],pdev[i])
            cp.start(); exch.append(cp)
    def wgrad(i,g):
        cs=slice(g*K4,(g+1)*K4)
        if i==0: return dot(jnp.concatenate([mix_ref[b,g].reshape(K4,n) for b in range(NB)],1),ga_scr[...])
        if i==1: return dot(gup_scr[:,cs],mi_scr[...],TN)
        return dot(hid_scr[:,cs],co_scr[...].reshape(N,D),TN)
    for cp in outs: cp.wait()
    outs=[]
    def part(j,i): return pl.ds((j*3+i)*K4,K4)
    gcp=[[None]*3 for j in range(G-1)]
    for j in range(G-1):
        for i in range(3):
            gs_scr[part(j,i),:]=wgrad(i,fore[j]).astype(bf16)
            gcp[j][i]=rcopy(gs_scr.at[part(j,i)],gr_scr.at[back[j]-1,i],gss.at[j,i],grs.at[back[j]-1,i],pdev[j])
            gcp[j][i].start()
    for i in range(3):
        t=wgrad(i,0)
        for j in range(G-1):
            arrived(gr_scr.at[fore[j]-1,i],grs.at[fore[j]-1,i])
            t=t+gr_scr[fore[j]-1,i].astype(f32)
        gcp[0][i].wait_send()
        gs_scr[part(0,i),:]=t.astype(bf16)
        for m in range(4):
            put(gs_scr.at[pl.ds(i*K4+m*Ch,Ch)],fb_ref.at[m,pl.ds(i*Ch,Ch)],fo_s.at[i,m])
    for b in range(NB):
        for i in range(G-1): arrived(do_ref.at[b*G+pidx[i]],dors.at[b*G+pidx[i]])
    for i,cp in enumerate(exch):
        if i%G==0: cp.wait()
        else: cp.wait_send()
    for cps in gcp[1:]:
        for cp in cps: cp.wait_send()
    spread_far(cots,"sent")
    home_arrived(C,n,bh_ref,bors)
    spread_sent(home)
    for cp in outs: cp.wait()

def middle(Z, C, mix, w2o, xo, cot, coto, gain):
    NB,n,D=xo.shape; G=2*C; nC=w2o.shape[2]; Ch=nC//3; K4=4*Ch; N=NB*n
    V=pl.BlockSpec(memory_space=pltpu.VMEM); A=pl.BlockSpec(memory_space=pl.ANY)
    S=lambda *sh: pltpu.SemaphoreType.DMA(sh)
    M=lambda *sh: pltpu.VMEM(sh,bf16)
    B=lambda *sh: jax.ShapeDtypeStruct(sh,bf16)
    return pl.pallas_call(functools.partial(mid_kernel,Z,C,n),
        out_shape=(B(NB,n,D),B(*cot.shape),B(NB*G,4,Ch,n),jax.ShapeDtypeStruct((NB,n,D),f32),B(4,nC,D),jax.ShapeDtypeStruct((8,D),f32)),
        in_specs=[V,A,V,A,A,V],out_specs=(A,A,A,A,A,V),
        scratch_shapes=[M(G*K4,D)]*3+[M(N,G*K4) if i in (1,2) else M(N,D) for i in range(4)]+[M(NB,G,4,Ch,n),M((G-1)*3*K4,D),M(G-1,3,K4,D),M(NB,n,D),pltpu.VMEM((NB,n,G*K4),f32),pltpu.VMEM((NB,n,D),f32),
            S(3,G,4),S(G-1,NB),S(NB*G),S(NB),S(G-1,3),S(G-1,3),S(NB),S(NB),S(2,NB),S(3,4),S(NB),S(4*C)],
        compiler_params=pltpu.CompilerParams(collective_id=2,has_side_effects=True,vmem_limit_bytes=60*2**20),
        cost_estimate=pl.CostEstimate(flops=3*10**10,bytes_accessed=10**8,transcendentals=0),
        name="middle")(mix,w2o,xo,cot,coto,gain.reshape(1,D))

def bwd_kernel(Z, C, n, qkv_ref, ot_ref, do_ref, lse_ref, pd_ref, segk_ref, segq_ref, ain_ref, wts_ref,
               xo_ref, gmid_ref, gain_ref, vec_ref, fb_ref,
               gi_ref, gwm_ref, gwq_ref, vo_ref,
               kv_scr, k_scr, v_scr, p_scr, ds_scr, dq_scr, dl_scr, a_scr, dw_scr, qr_scr, big_scr, zs_scr, zr_scr, t3_scr, t3r_scr, tb_scr, ot_scr, do_scr,
               dxr_scr, own_scr, xb_scr, gb_scr, va_scr, vb_scr, vs_scr, sc_scr,
               fs, frs, qs, qrs, zss, zrs, t3s, t3rs, cs_, crs, dxs, dxrs, gis, girs, ld, al, otl, dol, kvl, xl, vas, vars_, vbs, vbrs):
    z,k,q,s=[lax.axis_index(a) for a in AXES]
    G=2*C; g0=k*C+s; NB=4*C
    D=gain_ref.shape[1]; L=segq_ref.shape[1]; W=pd_ref.shape[0]; hb=W//HD; nb=L//BQ; sub=BQ//n
    nC=3*W; Dd=gwm_ref.shape[1]
    peers=list(itertools.product(range(2),range(C)))[1:]
    pdev=[(z,lax.rem(k+gc,2),q,lax.rem(s+gs,C)) for gc,gs in peers]
    pidx=[lax.rem(k+gc,2)*C+lax.rem(s+gs,C) for gc,gs in peers]
    back=[gc*C+(C-gs)%C for gc,gs in peers]
    fore=[gc*C+gs for gc,gs in peers]
    chipdev=[(z,k,partner(q,m),s) for m in range(4)]
    core=(z,1-k,q,s)
    zdev=[lax.rem(z+j,Z) for j in range(Z)]
    def frow(m): return big_scr.at[pl.ds((m-1)*nC,nC)]
    def dxat(i,e): return big_scr.at[pl.ds((i*NB+e)*n,n)]
    fcp={m: rcopy(fb_ref.at[m],frow(m),fs.at[m],frs.at[m],chipdev[m]) for m in (1,2)}
    qcp={m: rcopy(dw_scr.at[m-1],qr_scr.at[m-1],qs.at[m],qrs.at[m],chipdev[m]) for m in (1,2)}
    zcp=[[rcopy(zs_scr.at[e%2,zdev[j]],zr_scr.at[e,z],zss.at[e,j],zrs.at[e,z],(zdev[j],k,q,s)) for j in range(1,Z)] for e in range(4)]
    t3cp=[rcopy(tb_scr.at[e],t3r_scr.at[e],t3s.at[e],t3rs.at[e],chipdev[3]) for e in range(2)]
    gws=(gwm_ref,gwq_ref)
    ccp=[rcopy(t3_scr.at[e,pl.ds(pl.multiple_of((1-k)*Dd,Dd),Dd),:],gws[e].at[k],cs_.at[e],crs.at[e],core) for e in range(2)]
    def load(src,dst,i):
        cp=pltpu.make_async_copy(src,dst,ld.at[i]); cp.start(); return cp
    def zsend(e, value):
        rows=D//Z; per=max(1,640//rows)
        for i in range(Z//per):
            ls=slice(i*per*rows,(i+1)*per*rows)
            zs_scr[e%2,i*per:(i+1)*per]=value(ls).T.reshape(per,rows,nC).astype(bf16)
        for cp in zcp[e]: cp.start()
    def zsum(e):
        for cp in zcp[e]: cp.wait_send()
        t=zs_scr[e%2,z].astype(f32)
        for j in range(1,Z):
            arrived(zr_scr.at[e,zdev[j]],zrs.at[e,zdev[j]])
            t=t+zr_scr[e,zdev[j]].astype(f32)
        return t
    def diag(e):
        tb_scr[e]=zsum(e).astype(bf16)
        t3cp[e].start()
    def final(e):
        t=zsum(2+e)
        arrived(t3r_scr.at[e],t3rs.at[e])
        t=t+t3r_scr[e].astype(f32)
        t3cp[e].wait_send()
        t3_scr[e]=t
        ccp[e].start()
        gws[e][k]=t3_scr[e,pl.ds(pl.multiple_of(k*Dd,Dd),Dd),:]
    kvcp=[pltpu.make_async_copy(qkv_ref.at[m],kv_scr.at[m],kvl.at[m]) for m in range(4)]
    for m in (3,2,1,0): kvcp[m].start()
    acp=pltpu.make_async_copy(ain_ref,a_scr,al)
    acp.start()
    def otcp(m): return pltpu.make_async_copy(ot_ref.at[:,m],ot_scr,otl)
    otcp(3).start()
    def docp(idx): return pltpu.make_async_copy(do_ref.at[:,3-idx],do_scr.at[lax.rem(idx,2)],dol.at[lax.rem(idx,2)])
    docp(0).start()
    greet(Z,C)
    for m in (1,2): fcp[m].start()
    load(fb_ref.at[3],dw_scr.at[0],0).wait()
    zsend(0,lambda ls: dw_scr[0,:,ls].astype(f32))
    sc_scr[...]=jnp.zeros_like(sc_scr)
    rowi=lax.broadcasted_iota(jnp.int32,(BQ,BQ),0)
    coli=lax.broadcasted_iota(jnp.int32,(BQ,BQ),1)
    hs=[slice(h*HD,(h+1)*HD) for h in range(hb)]

    def block(idx,_):
        m=3-idx
        pltpu.make_async_copy(qkv_ref.at[m],kv_scr.at[m],kvl.at[m]).wait()
        for h in range(hb):
            k_scr[h]=kv_scr[m,W+h*HD:W+(h+1)*HD,:].T
            v_scr[h]=kv_scr[m,2*W+h*HD:2*W+(h+1)*HD,:].T
        slot=lax.rem(idx,2)
        docp(idx).wait()
        @pl.when(idx<3)
        def _(): docp(idx+1).start()
        def tile(h,i):
            return jnp.concatenate([do_scr[slot,i*sub+t,hs[h],:] for t in range(sub)],1) if sub>1 else do_scr[slot,i,hs[h],:]
        otcp(m).wait()
        for i in range(nb):
            for h in range(hb):
                for t in range(sub):
                    B_=i*sub+t
                    dl_scr[h,:,B_*n:(B_+1)*n]=(do_scr[slot,B_,hs[h],:].astype(f32)*ot_scr[B_,hs[h],:].astype(f32)).sum(0,keepdims=True)
        @pl.when(m>0)
        def _(): otcp(m-1).start()
        rows=[(j,h) for j in range(nb) for h in range(hb)]
        def phase_a(r):
            j,h=rows[r]; ks=slice(j*BQ,(j+1)*BQ)
            for i in range(j,nb):
                cs=slice(i*BQ,(i+1)*BQ)
                t=dot(k_scr[h,ks,:],kv_scr[m,hs[h],cs])
                dp=dot(v_scr[h,ks,:],tile(h,i))
                sk=segk_ref[ks,:]
                ok=jnp.concatenate([sk]*(BQ//128),axis=1)==segq_ref[:,cs]
                if j==i: ok=ok&(rowi<=coli)
                p=jnp.exp(jnp.where(ok,t-lse_ref[m*hb+h,:,cs],NEG))
                p_scr[r%2,:,cs]=p.astype(bf16)
                ds_scr[r%2,:,cs]=(p*(dp-dl_scr[h,:,cs])).astype(bf16)
                yield
        def phase_b(r):
            j,h=rows[r]; js=slice(j*BQ,(j+1)*BQ); rs=slice(j*BQ,L)
            dos=jnp.concatenate([tile(h,i) for i in range(j,nb)],1)
            dv=dot(dos,p_scr[r%2,:,rs],NT)
            yield
            dk=dot(kv_scr[m,hs[h],rs],ds_scr[r%2,:,rs],NT)
            yield
            for i in range(j,nb):
                cs=slice(i*BQ,(i+1)*BQ)
                dq=dot(kv_scr[m,W+h*HD:W+(h+1)*HD,js],ds_scr[r%2,:,cs])
                if j==0: dq_scr[hs[h],cs]=dq
                else: dq_scr[hs[h],cs]+=dq
                yield
            kv_scr[m,W+h*HD:W+(h+1)*HD,js]=dk.astype(bf16)
            kv_scr[m,2*W+h*HD:2*W+(h+1)*HD,js]=dv.astype(bf16)
        merge(phase_a(0))
        for u in range(len(rows)):
            gs=[phase_b(u)]
            if u+1<len(rows): gs=[phase_a(u+1)]+gs
            merge(*gs)
        dq=dq_scr[...]
        sc_scr[...]+=(dq*kv_scr[m,:W,:].astype(f32)).sum(1,keepdims=True)/pd_ref[:,:1]
        kv_scr[m,:W,:]=(dq*pd_ref[:,:1]).astype(bf16)
        @pl.when(idx==0)
        def _():
            acp.wait()
            zsend(1,lambda ls: dwt(3,ls))
        @pl.when((idx==1)|(idx==2))
        def _():
            for c in range(D//256):
                ls=slice(c*256,(c+1)*256)
                dw_scr[m-1,:,ls]=dwt(m,ls).astype(bf16)
        @pl.when(idx==1)
        def _():
            qcp[2].start()
            diag(0)
            ld0=load(fb_ref.at[0],dw_scr.at[0],0)
            for m2 in (1,2): arrived(frow(m2),frs.at[m2])
            ld0.wait()
            zsend(2,lambda ls: dw_scr[0,:,ls].astype(f32)+big_scr[0:nC,ls].astype(f32)+big_scr[nC:2*nC,ls].astype(f32))
        @pl.when(idx==2)
        def _():
            qcp[1].start()
            diag(1)
        return 0
    def dwt(m,ls):
        return dot(kv_scr[m],a_scr[:,ls])
    lax.fori_loop(0,4,block,0)
    for m2 in (1,2): arrived(qr_scr.at[m2-1],qrs.at[m2])
    zsend(3,lambda ls: dwt(0,ls)+qr_scr[0,:,ls].astype(f32)+qr_scr[1,:,ls].astype(f32))
    wcp=[pltpu.make_async_copy(wts_ref.at[m],a_scr.at[pl.ds(m*nC,nC),:],kvl.at[m]) for m in range(4)]
    for cp in wcp: cp.start()
    for cp in wcp: cp.wait()

    def chunk(i):
        gl=kv_scr[:,:,pl.ds(pl.multiple_of(i*BQ,BQ),BQ)].reshape(4*nC,BQ)
        return dot(gl,a_scr[:4*nC,:],TN)
    order=[partner(q,m)*C+t for m in (3,1,2,0) for t in range(C)]
    def xload(e):
        b=order[e]
        return [pltpu.make_async_copy(xo_ref.at[b],xb_scr.at[0],xl.at[0,0]),pltpu.make_async_copy(gmid_ref.at[b],gb_scr.at[0],xl.at[1,0])]
    dxcp=[[rcopy(dxat(i,e),dxr_scr.at[back[i]-1,e],dxs.at[i,e],dxrs.at[back[i],e],pdev[i]) for e in range(NB)] for i in range(G-1)]
    def give(e):
        b=order[e]
        if sub>1: own_scr[...]=chunk(b)
        for i in range(G-1):
            if sub==1: big_scr[(i*NB+e)*n:(i*NB+e+1)*n,:]=chunk(b*G+pidx[i]).astype(bf16)
            else: big_scr[(i*NB+e)*n:(i*NB+e+1)*n,:]=own_scr[pl.ds(pl.multiple_of(pidx[i]*n,n),n),:].astype(bf16)
            dxcp[i][e].start()
    gicp=[]
    gparts=[]
    def take(e):
        b=order[e]
        for cp in xload(e): cp.start()
        if sub==1:
            gain=chunk(b*G+g0)
        else:
            own_scr[...]=chunk(b)
            gain=own_scr[pl.ds(pl.multiple_of(g0*n,n),n),:]
        for i in range(G-1):
            arrived(dxr_scr.at[fore[i]-1,e],dxrs.at[fore[i],e])
            gain=gain+dxr_scr[fore[i]-1,e].astype(f32)
        for cp in xload(e): cp.wait()
        x=xb_scr[0].astype(f32)
        inv=lax.rsqrt(jnp.mean(x*x,axis=-1,keepdims=True)+norm_eps)
        nx=x*inv
        dn=gain*gain_ref[...]
        gin=gb_scr[0]+inv*(dn-nx*jnp.mean(dn*nx,axis=-1,keepdims=True))
        gparts.append((gain*nx).reshape(n//8,8,D).sum(0))
        dxcp[0][e].wait_send()
        big_scr[e*n:(e+1)*n,:]=gin.astype(bf16)
        dst=gi_ref.at[lax.rem(q,2),pl.ds(pl.multiple_of((k*C+s)*n,n),n),:]
        rs=girs.at[(lax.rem(q,2)*2+k)*C+s]
        gicp.append((is_home()&(b==q*C+s),pltpu.make_async_copy(dxat(0,e),dst,rs),
                     rcopy(dxat(0,e),dst,gis.at[e],rs,(z,lax.div(q,2),lax.div(b,C),lax.rem(b,C)))))
        spread_start(gicp[-1:])
    give(0)
    for e in range(NB):
        if e+1<NB: give(e+1)
        take(e)
    gpart=gparts[0]
    for t in gparts[1:]: gpart=gpart+t
    vs_scr[...]=jnp.zeros_like(vs_scr)
    vs_scr[0:1,:]=gpart.sum(0,keepdims=True)
    vs_scr[1:2,:]=vec_ref[...].sum(0,keepdims=True)
    sc=sc_scr[0:HD,:]
    for h in range(1,hb): sc=sc+sc_scr[h*HD:(h+1)*HD,:]
    vs_scr[2:3,0:HD]=sc.T[0:1,:]
    me=(k*4+q)*C+s
    va_scr[me]=vs_scr[...]
    plane=list(itertools.product(range(2),range(4),range(C)))[1:]
    vacp=[rcopy(vs_scr,va_scr.at[me],vas.at[i],vars_.at[me],(z,lax.rem(k+a,2),lax.rem(q+b,4),lax.rem(s+c,C))) for i,(a,b,c) in enumerate(plane)]
    for cp in vacp: cp.start()
    final(0)
    for a,b,c in plane:
        o=(lax.rem(k+a,2)*4+lax.rem(q+b,4))*C+lax.rem(s+c,C)
        arrived(va_scr.at[o],vars_.at[o])
    t=va_scr[0]
    for i in range(1,8*C): t=t+va_scr[i]
    vb_scr[z]=t
    vbcp=[rcopy(vb_scr.at[z],vb_scr.at[z],vbs.at[j],vbrs.at[z],(zdev[j],k,q,s)) for j in range(1,Z)]
    for cp in vbcp: cp.start()
    final(1)
    for j in range(1,Z): arrived(vb_scr.at[zdev[j]],vbrs.at[zdev[j]])
    t=vb_scr[0]
    for i in range(1,Z): t=t+vb_scr[i]
    vo_ref[...]=t
    for e in range(2):
        arrived(gws[e].at[1-k],crs.at[e])
        ccp[e].wait_send()
    home_arrived(C,n,gi_ref,girs)
    spread_sent(gicp)
    for i in range(1,G-1):
        for e in range(NB): dxcp[i][e].wait_send()
    for m in (1,2):
        fcp[m].wait_send(); qcp[m].wait_send()
    for cp in vacp+vbcp: cp.wait_send()

def backward(Z, C, qkv, ot, do, lse, pd, segk, segq, ain, wts, xo, gmid, gain, vec, fb, R, Pn, Dd):
    NB,n,D=xo.shape; G=2*C; nC=wts.shape[1]; W=pd.shape[0]; hb=W//HD; L=segq.shape[1]
    V=pl.BlockSpec(memory_space=pltpu.VMEM); A=pl.BlockSpec(memory_space=pl.ANY)
    S=lambda *sh: pltpu.SemaphoreType.DMA(sh) if sh else pltpu.SemaphoreType.DMA
    M=lambda *sh: pltpu.VMEM(sh,bf16)
    F=lambda *sh: pltpu.VMEM(sh,f32)
    gw=jax.ShapeDtypeStruct((2,Dd,nC),f32)
    return pl.pallas_call(functools.partial(bwd_kernel,Z,C,n),
        out_shape=(jax.ShapeDtypeStruct((R,Pn,D),bf16),gw,gw,jax.ShapeDtypeStruct((8,D),f32)),
        in_specs=[A,A,A,V,V,V,V,A,A,A,A,V,V,A],out_specs=(A,V,V,V),
        scratch_shapes=[M(4,nC,L),M(hb,L,HD),M(hb,L,HD),M(2,BQ,L),M(2,BQ,L),F(W,L),F(hb,1,L),M(L,D),
            M(2,nC,D),M(2,nC,D),M(max(2*nC,(G-1)*NB*n),D),M(2,Z,D//Z,nC),M(4,Z,D//Z,nC),F(2,D//Z,nC),M(2,D//Z,nC),M(2,D//Z,nC),M(NB*G,W,n),M(2,NB*G,W,n),
            M(G-1,NB,n,D),F(BQ,D) if n<BQ else F(8,128),M(1,n,D),F(1,n,D),F(8*C,8,D),F(Z,8,D),F(8,D),F(W,1),
            S(4),S(4),S(4),S(4),S(4,Z),S(4,Z),S(2),S(2),S(2),S(2),S(G,NB),S(G,NB),S(NB),S(4*C),S(4),S(),S(),S(2),S(4),S(2,2),S(8*C),S(8*C),S(Z),S(Z)],
        compiler_params=pltpu.CompilerParams(collective_id=1,has_side_effects=True,vmem_limit_bytes=58*2**20),
        cost_estimate=pl.CostEstimate(flops=6*10**10,bytes_accessed=10**8,transcendentals=0),
        name="backward")(qkv,ot,do,lse,pd,segk,segq,ain.reshape(L,D),wts,xo,gmid,gain.reshape(1,D),vec,fb)

def finish_kernel(Ch, gi_ref, gwm_ref, gwq_ref, vo_ref, sf_ref, ig_ref, gq_ref, gk_ref, gv_ref, go_ref, gu_ref, gd_ref, ga_ref, gs_ref, gm_ref):
    ig_ref[...]=gi_ref[...].astype(f32)
    @pl.when(pl.program_id(0)==0)
    def _():
        def cols(ref,i):
            return jnp.concatenate([ref[0,:,i*Ch:(i+1)*Ch],ref[1,:,i*Ch:(i+1)*Ch]],1)
        for i,o in enumerate((gq_ref,gk_ref,gv_ref)): o[...]=cols(gwq_ref,i)
        go_ref[...]=cols(gwm_ref,0)
        gu_ref[...]=cols(gwm_ref,1)
        gd_ref[...]=cols(gwm_ref,2)
        ga_ref[...]=vo_ref[0,:]
        gm_ref[...]=vo_ref[1,:]
        gs_ref[...]=vo_ref[2,0:HD]*sf_ref[0,:]

def finish(gi, gwm, gwq, vo, sf):
    R,Pn,D=gi.shape; _,Dd,nC=gwm.shape; Ch=nC//3; T=4
    F=lambda *sh: jax.ShapeDtypeStruct(sh,f32)
    full=lambda *sh: pl.BlockSpec(sh,lambda i: (0,)*len(sh))
    row=pl.BlockSpec((R,Pn//T,D),lambda i:(0,i,0))
    shapes=[(Dd,2*Ch)]*6+[(D,),(HD,),(D,)]
    return pl.pallas_call(functools.partial(finish_kernel,Ch),grid=(T,),
        out_shape=(F(R,Pn,D),)+tuple(F(*sh) for sh in shapes),
        in_specs=[row,full(2,Dd,nC),full(2,Dd,nC),full(8,D),full(1,HD)],
        out_specs=(row,)+tuple(full(*sh) for sh in shapes),
        compiler_params=pltpu.CompilerParams(vmem_limit_bytes=60*2**20),
        name="finish")(gi,gwm,gwq,vo,sf.reshape(1,HD))


def make_local(Z, C):
    def local(tokens, segments, attn_gain, w_query, w_key, w_value, w_out, query_scale, mlp_gain, w_up, w_down, cotangent):
        R,Pn,D=tokens.shape
        Dd=w_query.shape[0]

        w1h,w2h,pd=prep(w_query,w_key,w_value,w_out,w_up,w_down,query_scale)
        xo,ain,wts,w2o,mix,qkv,ot,lse,segk,segq,coto=forward(Z,C,tokens,w1h,w2h,cotangent,attn_gain,pd,segments)
        _,block_out,do,gmid,fb,vec=middle(Z,C,mix,w2o,xo,cotangent,coto,mlp_gain)
        gi,gwm,gwq,vo=backward(Z,C,qkv,ot,do,lse,pd,segk,segq,ain,wts,xo,gmid,attn_gain,vec,fb,R,Pn,Dd)
        sf=(scale_base/math.sqrt(HD))*jax.nn.sigmoid(query_scale)
        ig,gq,gk,gv,go,gu,gd,ga,gs,gm=finish(gi,gwm,gwq,vo,sf)
        return (block_out,ig,ga,gq,gk,gv,go.T,gs,gm,gu,gd.T)
    return local

def solution(mesh):
    dp,T=mesh.shape["dp"],mesh.shape["tensor"]
    Z,C=dp//2,T//4
    fine=Mesh(mesh.devices.reshape(Z,2,4,C),AXES)
    dpx=("zz","core"); tx=("q","s")
    in_specs=(P(dpx,tx,None),P(dpx,None),P(),P(dpx,tx),P(dpx,tx),P(dpx,tx),P(tx,dpx),P(),P(),P(dpx,tx),P(tx,dpx),P(dpx,tx,None))
    out_specs=(P(dpx,tx,None),P(dpx,tx,None),P(),P(dpx,tx),P(dpx,tx),P(dpx,tx),P(tx,dpx),P(),P(),P(dpx,tx),P(tx,dpx))
    return jax.shard_map(make_local(Z,C),mesh=fine,in_specs=in_specs,out_specs=out_specs,check_vma=False)
```

```python
import functools
import itertools
import math
import jax, jax.numpy as jnp
from jax import lax
from jax.experimental import pallas as pl
from jax.experimental.pallas import tpu as pltpu
from jax.sharding import Mesh, PartitionSpec as P

AXES=("zz","core","q","s")
norm_eps = 1e-06
HD=80
BQ=256
NEG=-1e30
f32=jnp.float32; bf16=jnp.bfloat16
NT=(((1,),(1,)),((),()))
NN=(((1,),(0,)),((),()))
TN=(((0,),(0,)),((),()))
def dot(a,b,dims=NN): return lax.dot_general(a,b,dims,preferred_element_type=f32)

def merge(*gens):
    gens=list(gens)
    while gens:
        for g in list(gens):
            try: next(g)
            except StopIteration: gens.remove(g)


MESH=pl.DeviceIdType.MESH
scale_base = 1.442695041

def rcopy(src,dst,ss,rs,dev):
    return pltpu.make_async_remote_copy(src_ref=src,dst_ref=dst,send_sem=ss,recv_sem=rs,device_id=dev,device_id_type=MESH)

def transpose_rows(src, dst):
    P_,rows,cols=src.shape
    per=max(1,640//rows)
    for i in range(P_//per):
        dst[:,i*per*rows:(i+1)*per*rows]=src[i*per:(i+1)*per].reshape(per*rows,cols).T

def partner(q, m):
    return (q,q+1-2*lax.rem(q,2),lax.rem(q+2,4),3-q)[m]

def greet(Z, C):
    z,k,q,s=[lax.axis_index(a) for a in AXES]
    bar=pltpu.get_barrier_semaphore()
    plane=list(itertools.product(range(2),range(4),range(C)))[1:]
    column=[(j,a) for j in range(1,Z) for a in range(2)]
    for a,b,c in plane:
        pl.semaphore_signal(bar,inc=1,device_id=(z,lax.rem(k+a,2),lax.rem(q+b,4),lax.rem(s+c,C)),device_id_type=MESH)
    for j,a in column:
        pl.semaphore_signal(bar,inc=1,device_id=(lax.rem(z+j,Z),lax.rem(k+a,2),q,s),device_id_type=MESH)
    pl.semaphore_wait(bar,len(plane)+len(column))

def col_copies(Z, src, dst, ss, rs):
    z,k,q,s=[lax.axis_index(a) for a in AXES]
    out=[]
    for j in range(Z):
        for a in range(2):
            kk=lax.rem(k+a,2)
            if j==0 and a==0: out.append(pltpu.make_async_copy(src.at[k],dst.at[2*z+k],rs.at[2*z+k]))
            else: out.append(rcopy(src.at[kk],dst.at[2*z+k],ss.at[j*2+a],rs.at[2*z+k],(lax.rem(z+j,Z),kk,q,s)))
    return out

def spread_copies(C, n, src, dst, ss, rs):
    z,k,q,s=[lax.axis_index(a) for a in AXES]
    out=[]
    for rr in range(2):
        r=lax.rem(q+rr,2)
        for h in range(2):
            for s2 in range(C):
                i=(rr*2+h)*C+s2
                piece=src.at[r,pl.ds((h*C+s2)*n,n),:]
                out.append((rr,(k==h)&(q==2*k+r)&(s==s2),pltpu.make_async_copy(piece,dst.at[q*C+s],rs.at[q*C+s]),
                            rcopy(piece,dst.at[q*C+s],ss.at[i],rs.at[q*C+s],(z,h,2*k+r,s2))))
    return out

def is_home(): return lax.axis_index("core")==lax.div(lax.axis_index("q"),2)

def spread_near(cps, do):
    for rr,mine,loc,cp in cps:
        if rr==0:
            @pl.when(mine)
            def _(loc=loc):
                if do=="start": loc.start()
            @pl.when(jnp.logical_not(mine))
            def _(cp=cp): cp.start() if do=="start" else cp.wait_send()
        else:
            @pl.when(is_home())
            def _(cp=cp): cp.start() if do=="start" else cp.wait_send()

def spread_far(cps, do):
    for rr,mine,loc,cp in cps:
        if rr==1:
            @pl.when(jnp.logical_not(is_home()))
            def _(cp=cp): cp.start() if do=="start" else cp.wait_send()

def near_blocks(C):
    q=lax.axis_index("q")
    return [partner(q,m)*C+t for m in range(3) for t in range(C)]

def far_blocks(C):
    q=lax.axis_index("q")
    return [partner(q,3)*C+t for t in range(C)]

def spread_start(cps):
    for mine,loc,cp in cps:
        @pl.when(mine)
        def _(loc=loc): loc.start()
        @pl.when(jnp.logical_not(mine))
        def _(cp=cp): cp.start()

def spread_sent(cps):
    for mine,loc,cp in cps:
        @pl.when(jnp.logical_not(mine))
        def _(cp=cp): cp.wait_send()

def home_copies(C, n, src, dst, ss, rs):
    z,k,q,s=[lax.axis_index(a) for a in AXES]
    out=[]
    for b in range(4*C):
        to=dst.at[lax.rem(q,2),pl.ds(pl.multiple_of((k*C+s)*n,n),n),:]
        sem=rs.at[(lax.rem(q,2)*2+k)*C+s]
        out.append(((lax.div(q,2)==k)&(q==b//C)&(s==b%C),pltpu.make_async_copy(src.at[b],to,sem),
                    rcopy(src.at[b],to,ss.at[b],sem,(z,lax.div(q,2),b//C,b%C))))
    return out

def home_arrived(C, n, dst, rs):
    for r in range(2):
        for h in range(2):
            for s2 in range(C):
                arrived(dst.at[r,pl.ds((h*C+s2)*n,n),:],rs.at[(r*2+h)*C+s2])

def arrived(ref, sem):
    z,k,q,s=[lax.axis_index(a) for a in AXES]
    rcopy(ref,ref,sem,sem,(z,1-k,q,s)).wait_recv()

def fwd_kernel(Z, C, n, x_ref, w1_ref, w2_ref, cot_ref, gain_ref, pd_ref, seg_ref,
               xo_ref, ain_ref, wts_ref, w2o_ref, mix_ref, qkv_ref, ot_ref, lse_ref, segk_ref, segq_ref, coto_ref,
               xo_scr, ain_scr, wts_scr, qkv_scr, ot_scr, wa_scr, wb_scr, wd_scr, o3_scr, w2_scr, k_scr, s_scr, so_scr,
               tok_s, tok_r, ain_s, ain_r, a_s, a_r, b_s, b_r, dd_s, dd_r, o3_s, o3_r,
               wt_s, wt_r, hf_s, hf_r, w2_s, w2_r, gr_s, gr_r, loc_s, mix_s, mix_r, mixl, sg_s, sg_r, out_s, qo_s, cot_s, cot_r):
    z,k,q,s=[lax.axis_index(a) for a in AXES]
    G=2*C; g0=k*C+s; NB=4*C
    D=gain_ref.shape[1]; L=seg_ref.shape[1]; W=pd_ref.shape[0]; hb=W//HD; nb=L//BQ; nC=3*W
    peers=list(itertools.product(range(2),range(C)))[1:]
    pdev=[(z,lax.rem(k+gc,2),q,lax.rem(s+gs,C)) for gc,gs in peers]
    pidx=[lax.rem(k+gc,2)*C+lax.rem(s+gs,C) for gc,gs in peers]
    back=[gc*C+(C-gs)%C for gc,gs in peers]
    fore=[gc*C+gs for gc,gs in peers]
    chipdev=[(z,k,partner(q,m),s) for m in range(4)]
    toks=spread_copies(C,n,x_ref,xo_scr,tok_s,tok_r)
    cots=spread_copies(C,n,cot_ref,coto_ref,cot_s,cot_r)
    ca=col_copies(Z,w1_ref,wa_scr,a_s,a_r)
    cb=col_copies(Z,w2_ref,wb_scr,b_s,b_r)
    cd=col_copies(Z,o3_scr,wd_scr,dd_s,dd_r)
    o3=rcopy(w2_ref,o3_scr,o3_s,o3_r,chipdev[3])
    wcp=[rcopy(wts_scr.at[0],wts_scr.at[m],wt_s.at[m],wt_r.at[m],chipdev[m]) for m in (1,2)]
    h1=nC//32*16; half=[pl.ds(0,h1),pl.ds(h1,nC-h1)]
    hcp=[rcopy(wts_scr.at[1,half[0]],wts_scr.at[3,half[0]],hf_s.at[0],hf_r.at[0],chipdev[2]),
         rcopy(wts_scr.at[2,half[1]],wts_scr.at[3,half[1]],hf_s.at[1],hf_r.at[1],chipdev[1])]
    save=[pltpu.make_async_copy(xo_scr,xo_ref,out_s.at[0]),pltpu.make_async_copy(ain_scr,ain_ref,out_s.at[1])]
    wsave=[pltpu.make_async_copy(wts_scr.at[m],wts_ref.at[m],out_s.at[2+m]) for m in range(4)]
    def qsave(m): return [pltpu.make_async_copy(qkv_scr.at[m],qkv_ref.at[m],qo_s.at[0,m]),pltpu.make_async_copy(ot_scr.at[:,m],ot_ref.at[:,m],qo_s.at[1,m])]
    w2cp=[rcopy(w2_scr.at[0],w2_scr.at[m],w2_s.at[m],w2_r.at[m],chipdev[m]) for m in (1,2)]
    grp=[[rcopy(w2_scr.at[m],w2o_ref.at[back[i],m],gr_s.at[i,m],gr_r.at[back[i],m],pdev[i]) for i in range(G-1)] for m in range(4)]
    loc=[pltpu.make_async_copy(w2_scr.at[m],w2o_ref.at[0,m],loc_s.at[m]) for m in range(4)]
    def share(m):
        loc[m].start()
        for cp in grp[m]: cp.start()
    sgc=rcopy(seg_ref,so_scr,sg_s,sg_r,(z,1-k,q,s))
    greet(Z,C)
    sgc.start()
    for cp in ca: cp.start()
    spread_near(toks,"start"); spread_far(toks,"start")
    o3.start()
    sgc.wait_recv()
    sg=jnp.where(k==lax.div(q,2),seg_ref[...],so_scr[...])
    sg=jnp.where(lax.rem(q,2)==0,sg[0:1],sg[1:2]).astype(f32)
    segq_ref[...]=sg
    for c in range(L//BQ):
        segk_ref[c*BQ:(c+1)*BQ,:]=jnp.broadcast_to(sg[:,c*BQ:(c+1)*BQ],(128,BQ)).T
    for i in range(2*Z): arrived(wa_scr.at[i],a_r.at[i])
    for cp in cb: cp.start()
    transpose_rows(wa_scr,wts_scr.at[0])
    for cp in wcp: cp.start()
    wsave[0].start()
    ains=[]
    for j in range(NB):
        arrived(xo_scr.at[j],tok_r.at[j])
        x=xo_scr[j].astype(f32)
        inv=lax.rsqrt(jnp.mean(x*x,axis=-1,keepdims=True)+norm_eps)
        slot=j*G+g0
        ain_scr[slot]=(x*inv*gain_ref[...]).astype(bf16)
        for i in range(G-1):
            cp=rcopy(ain_scr.at[slot],ain_scr.at[slot],ain_s.at[i,j],ain_r.at[slot],pdev[i])
            cp.start(); ains.append(cp)
    for j in range(NB):
        for i in range(G-1): arrived(ain_scr.at[j*G+pidx[i]],ain_r.at[j*G+pidx[i]])
    for cp in save: cp.start()
    rowi=lax.broadcasted_iota(jnp.int32,(BQ,BQ),0)
    coli=lax.broadcasted_iota(jnp.int32,(BQ,BQ),1)
    hs=[slice(h*HD,(h+1)*HD) for h in range(hb)]
    CH=512; per=CH//n; sub=BQ//n

    def block(m,_):
        @pl.when(m==1)
        def _():
            for i in range(2*Z): arrived(wb_scr.at[i],b_r.at[i])
            arrived(o3_scr,o3_r)
            for cp in cd: cp.start()
            transpose_rows(wb_scr,w2_scr.at[0])
            for i in (1,2): arrived(wts_scr.at[i],wt_r.at[i])
            for cp in hcp+wsave[1:3]: cp.start()
            share(0)
        @pl.when(m==2)
        def _():
            for cp in w2cp: cp.start()
        @pl.when(m==3)
        def _():
            for i in range(2): arrived(wts_scr.at[3,half[i]],hf_r.at[i])
            wsave[3].start()
            spread_near(cots,"start")
        for c in range(L//CH):
            cs=slice(c*CH,(c+1)*CH)
            r=dot(wts_scr[m],ain_scr[c*per:(c+1)*per].reshape(CH,D),NT)
            qkv_scr[m,:W,cs]=(r[:W]*pd_ref[:,:1]).astype(bf16)
            qkv_scr[m,W:,cs]=r[W:].astype(bf16)
            for h in range(hb):
                k_scr[h,cs,:]=r[W+h*HD:W+(h+1)*HD].T.astype(bf16)
        units=[(i,h) for i in range(nb) for h in range(hb)]
        st={}
        def phase_a(u):
            i,h=units[u]; c0=i*BQ
            qi=qkv_scr[m,hs[h],c0:c0+BQ]
            sq=segq_ref[:,c0:c0+BQ]
            m8=None
            for j in range(i+1):
                t=dot(k_scr[h,j*BQ:(j+1)*BQ,:],qi)
                sk=segk_ref[j*BQ:(j+1)*BQ,:]
                ok=jnp.concatenate([sk]*(BQ//128),axis=1)==sq
                if j==i: ok=ok&(rowi<=coli)
                t=jnp.where(ok,t,NEG)
                s_scr[u%2,j*BQ:(j+1)*BQ,:]=t
                mm=t.reshape(BQ//8,8,BQ).max(0)
                m8=mm if m8 is None else jnp.maximum(m8,mm)
                yield
            st[u]=m8.max(0,keepdims=True)
        def phase_b(u):
            i,h=units[u]; c0=i*BQ
            mx=st[u]; l8=None; acc=None
            for j in range(i+1):
                p=jnp.exp(s_scr[u%2,j*BQ:(j+1)*BQ,:]-mx)
                ll=p.reshape(BQ//8,8,BQ).sum(0)
                l8=ll if l8 is None else l8+ll
                pv=dot(qkv_scr[m,2*W+h*HD:2*W+(h+1)*HD,j*BQ:(j+1)*BQ],p.astype(bf16))
                acc=pv if acc is None else acc+pv
                yield
            l=l8.sum(0,keepdims=True)
            o=(acc*(1.0/l)).astype(bf16)
            for t in range(sub): ot_scr[i*sub+t,m,hs[h],:]=o[:,t*n:(t+1)*n]
            lse_ref[m*hb+h,:,c0:c0+BQ]=mx+jnp.log(l)
        merge(phase_a(0))
        for u in range(len(units)):
            gs=[phase_b(u)]
            if u+1<len(units): gs=[phase_a(u+1)]+gs
            merge(*gs)
        for b in range(NB):
            pltpu.make_async_copy(ot_scr.at[b*G+g0,m],mix_ref.at[b,0,m],mixl.at[b,m]).start()
            for i in range(G-1):
                rcopy(ot_scr.at[b*G+pidx[i],m],mix_ref.at[b,back[i],m],mix_s.at[i,b,m],mix_r.at[back[i],b,m],pdev[i]).start()
        for cp in qsave(m): cp.start()
        return 0
    lax.fori_loop(0,4,block,0)
    for m in (1,2):
        arrived(w2_scr.at[m],w2_r.at[m])
        share(m)
    for i in range(2*Z): arrived(wd_scr.at[i],dd_r.at[i])
    transpose_rows(wd_scr,w2_scr.at[3])
    share(3)
    for i in range(G-1):
        for b in range(NB):
            for m in range(4):
                arrived(mix_ref.at[b,fore[i],m],mix_r.at[fore[i],b,m])
                rcopy(ot_scr.at[b*G+pidx[i],m],mix_ref.at[b,back[i],m],mix_s.at[i,b,m],mix_r.at[back[i],b,m],pdev[i]).wait_send()
        for m in range(4): arrived(w2o_ref.at[fore[i],m],gr_r.at[fore[i],m])
    for m in range(4):
        loc[m].wait()
        for cp in grp[m]: cp.wait_send()
    for cps in (ca,cb,cd):
        for cp in cps[1:]: cp.wait_send()
    for cp in wcp+hcp+w2cp+ains+[o3,sgc]: cp.wait_send()
    spread_near(toks,"sent"); spread_far(toks,"sent"); spread_near(cots,"sent")
    for b in near_blocks(C): arrived(coto_ref.at[b],cot_r.at[b])
    for cp in save+wsave: cp.wait()
    for m in range(4):
        for cp in qsave(m): cp.wait()
        for b in range(NB): pltpu.make_async_copy(ot_scr.at[b*G+g0,m],mix_ref.at[b,0,m],mixl.at[b,m]).wait()

def forward(Z, C, tokens, w1h, w2h, cot, gain, pd, seg):
    R,Pn,D=tokens.shape; G=2*C; n=Pn//G; _,Dd,nC=w1h.shape; NB=4*C
    L=seg.shape[1]; W=pd.shape[0]; hb=W//HD
    V=pl.BlockSpec(memory_space=pltpu.VMEM); A=pl.BlockSpec(memory_space=pl.ANY)
    S=lambda *sh: pltpu.SemaphoreType.DMA(sh) if sh else pltpu.SemaphoreType.DMA
    B=lambda *sh: jax.ShapeDtypeStruct(sh,bf16)
    F=lambda *sh: jax.ShapeDtypeStruct(sh,f32)
    M=lambda *sh: pltpu.VMEM(sh,bf16)
    col=M(2*Z,Dd,nC)
    return pl.pallas_call(functools.partial(fwd_kernel,Z,C,n),
        out_shape=(B(NB,n,D),B(NB*G,n,D),B(4,nC,D),B(G,4,nC,D),B(NB,G,4,W,n),B(4,nC,L),B(NB*G,4,W,n),F(4*hb,1,L),F(L,128),F(1,L),B(NB,n,D)),
        in_specs=[A,A,A,A,V,V,V],out_specs=(A,A,A,A,A,A,A,V,V,V,A),
        scratch_shapes=[M(NB,n,D),M(NB*G,n,D),M(4,nC,D),M(4,nC,L),M(NB*G,4,W,n),col,col,col,M(2,Dd,nC),M(4,nC,D),M(hb,L,HD),
            pltpu.VMEM((2,L,BQ),f32),pltpu.VMEM((R,L),jnp.int32),
            S(NB),S(NB),S(G-1,NB),S(NB*G),S(2*Z),S(2*Z),S(2*Z),S(2*Z),S(2*Z),S(2*Z),S(),S(),
            S(4),S(4),S(2),S(2),S(4),S(4),S(G-1,4),S(G,4),S(4),S(G-1,NB,4),S(G,NB,4),S(NB,4),S(),S(),S(6),S(2,4),S(NB),S(NB)],
        compiler_params=pltpu.CompilerParams(collective_id=0,has_side_effects=True,vmem_limit_bytes=60*2**20),
        cost_estimate=pl.CostEstimate(flops=3*10**10,bytes_accessed=10**8,transcendentals=0),
        name="forward")(tokens,w1h,w2h,cot,gain.reshape(1,D),pd,seg)

def prep_kernel(Ch, wq_ref, wk_ref, wv_ref, wo_ref, wu_ref, wd_ref, qs_ref, w1_ref, w2_ref, pd_ref):
    for ref,three in ((w1_ref,(wq_ref[...],wk_ref[...],wv_ref[...])),(w2_ref,(wo_ref[...],wu_ref[...],wd_ref[...]))):
        for i,w in enumerate(three):
            for h in range(2): ref[h,:,i*Ch:(i+1)*Ch]=w[:,h*Ch:(h+1)*Ch]
    v=qs_ref[...]
    per_dim=scale_base/math.sqrt(HD)*(jnp.maximum(v,0.0)+jnp.log(1.0+jnp.exp(-jnp.abs(v))))
    col=jnp.broadcast_to(per_dim,(128,HD)).T
    for h in range(pd_ref.shape[0]//HD): pd_ref[h*HD:(h+1)*HD,:]=col

def prep(wq, wk, wv, wo, wu, wd, qs):
    Dd,Ct=wq.shape; Ch=Ct//2
    B=jax.ShapeDtypeStruct((2,Dd,3*Ch),bf16)
    return pl.pallas_call(functools.partial(prep_kernel,Ch),out_shape=(B,B,jax.ShapeDtypeStruct((Ch,128),f32)),
        compiler_params=pltpu.CompilerParams(vmem_limit_bytes=60*2**20),name="prep")(wq,wk,wv,wo.T,wu,wd.T,qs.reshape(1,-1))


def mid_kernel(Z, C, n, mix_ref, w2_ref, xo_ref, cot_ref, coto_ref, gain_ref,
               bo_ref, bh_ref, do_ref, gm_ref, fb_ref, vec_ref,
               wo_scr, wu_scr, wd_scr, mi_scr, hid_scr, gup_scr, ga_scr, gt_scr, gs_scr, gr_scr, co_scr, up_scr, mid_scr,
               wl, dos, dors, dol, gss, grs, cot_s, cot_r, out_s, fo_s, bos, bors):
    z,k,q,s=[lax.axis_index(a) for a in AXES]
    G=2*C; g0=k*C+s; NB=4*C
    D=gain_ref.shape[1]; K4=wo_scr.shape[0]//G; Ch=K4//4; N=NB*n
    peers=list(itertools.product(range(2),range(C)))[1:]
    pdev=[(z,lax.rem(k+gc,2),q,lax.rem(s+gs,C)) for gc,gs in peers]
    pidx=[lax.rem(k+gc,2)*C+lax.rem(s+gs,C) for gc,gs in peers]
    back=[gc*C+(C-gs)%C for gc,gs in peers]
    fore=[gc*C+gs for gc,gs in peers]
    wcp=[]
    for i,dst in enumerate((wo_scr,wu_scr,wd_scr)):
        wcp.append([pltpu.make_async_copy(w2_ref.at[g,m,pl.ds(i*Ch,Ch),:],dst.at[pl.ds((g*4+m)*Ch,Ch),:],wl.at[i,g,m]) for g in range(G) for m in range(4)])
        for cp in wcp[i]: cp.start()
    cots=spread_copies(C,n,cot_ref,co_scr,cot_s,cot_r)
    greet(Z,C)
    spread_far(cots,"start")
    for b in near_blocks(C): pltpu.make_async_copy(coto_ref.at[b],co_scr.at[b],cot_r.at[b]).start()
    order=[partner(q,m)*C+(lax.rem(s+t,C)) for m in range(4) for t in range(C)]
    outs=[]
    def put(src,dst,sem):
        cp=pltpu.make_async_copy(src,dst,sem); cp.start(); outs.append(cp)
    vec_ref[...]=jnp.zeros_like(vec_ref)
    for cp in wcp[0]: cp.wait()
    def slot(e): return slice(e*n,(e+1)*n)
    def ahead(e):
        b=order[e]
        attn=dot(mix_ref[b].reshape(G*K4,n),wo_scr[...],TN)
        middle=xo_ref[b].astype(f32)+attn
        mid_scr[e]=middle
        inv=lax.rsqrt(jnp.mean(middle*middle,axis=-1,keepdims=True)+norm_eps)
        mi_scr[slot(e),:]=(middle*inv*gain_ref[...]).astype(bf16)
        yield
        if e==0:
            for cp in wcp[1]+wcp[2]: cp.wait()
        up=dot(mi_scr[slot(e),:],wu_scr[...],NT)
        up_scr[e]=up
        hid_scr[slot(e),:]=(up*(1.0/(1.0+jnp.exp(-up)))).astype(bf16)
        yield
        gs_scr[slot(e),:]=(mid_scr[e]+dot(hid_scr[slot(e),:],wd_scr[...])).astype(bf16)
        yield
    for e in range(0,NB,2):
        merge(ahead(e),ahead(e+1))
        for i in (e,e+1): put(gs_scr.at[slot(i)],bo_ref.at[order[i]],out_s.at[0,i])
    exch=[]
    home=[]
    boouts=list(outs); outs=[]
    def behind(e):
        b=order[e]
        gh=dot(co_scr[b],wd_scr[...],NT)
        up=up_scr[e]
        sg=1.0/(1.0+jnp.exp(-up))
        gup_scr[slot(e),:]=(gh*(sg*(1.0+up*(1.0-sg)))).astype(bf16)
        yield
        gmlp=dot(gup_scr[slot(e),:],wu_scr[...])
        middle=mid_scr[e]
        inv=lax.rsqrt(jnp.mean(middle*middle,axis=-1,keepdims=True)+norm_eps)
        n2=middle*inv
        dn=gmlp*gain_ref[...]
        gm=co_scr[b].astype(f32)+inv*(dn-n2*jnp.mean(dn*n2,axis=-1,keepdims=True))
        vec_ref[...]+=(gmlp*n2).reshape(n//8,8,D).sum(0)
        mid_scr[e]=gm
        ga_scr[slot(e),:]=gm.astype(bf16)
        yield
        gt_scr[e]=dot(wo_scr[...],ga_scr[slot(e),:],NT).astype(bf16).reshape(G,4,Ch,n)
        yield
    for e0 in range(0,NB,2):
        for e in (e0,e0+1):
            b=order[e]
            if e<3*C: pltpu.make_async_copy(coto_ref.at[b],co_scr.at[b],cot_r.at[b]).wait()
            else: arrived(co_scr.at[b],cot_r.at[b])
            boouts[e].wait()
            dst=bh_ref.at[lax.rem(q,2),pl.ds(pl.multiple_of((k*C+s)*n,n),n),:]
            rs=bors.at[(lax.rem(q,2)*2+k)*C+s]
            mine=is_home()&(b==q*C+s)
            home.append((mine,pltpu.make_async_copy(bo_ref.at[b],dst,rs),rcopy(bo_ref.at[b],dst,bos.at[e],rs,(z,lax.div(q,2),lax.div(b,C),lax.rem(b,C)))))
            spread_start(home[-1:])
        merge(behind(e0),behind(e0+1))
        for e in (e0,e0+1):
            b=order[e]
            put(mid_scr.at[e],gm_ref.at[b],out_s.at[1,e])
            lc=pltpu.make_async_copy(gt_scr.at[e,0],do_ref.at[b*G+g0],dol.at[e])
            lc.start(); exch.append(lc)
            for i in range(G-1):
                cp=rcopy(gt_scr.at[e,fore[i]],do_ref.at[b*G+g0],dos.at[i,e],dors.at[b*G+g0],pdev[i])
                cp.start(); exch.append(cp)
    def wgrad(i,g):
        cs=slice(g*K4,(g+1)*K4)
        if i==0: return dot(jnp.concatenate([mix_ref[b,g].reshape(K4,n) for b in order],1),ga_scr[...])
        if i==1: return dot(gup_scr[:,cs],mi_scr[...],TN)
        return dot(hid_scr[:,cs],jnp.concatenate([co_scr[b] for b in order],0),TN)
    for cp in outs: cp.wait()
    outs=[]
    def part(j,i): return pl.ds((j*3+i)*K4,K4)
    gcp=[[None]*3 for j in range(G-1)]
    for j in range(G-1):
        for i in range(3):
            gs_scr[part(j,i),:]=wgrad(i,fore[j]).astype(bf16)
            gcp[j][i]=rcopy(gs_scr.at[part(j,i)],gr_scr.at[back[j]-1,i],gss.at[j,i],grs.at[back[j]-1,i],pdev[j])
            gcp[j][i].start()
    for i in range(3):
        t=wgrad(i,0)
        for j in range(G-1):
            arrived(gr_scr.at[fore[j]-1,i],grs.at[fore[j]-1,i])
            t=t+gr_scr[fore[j]-1,i].astype(f32)
        gcp[0][i].wait_send()
        gs_scr[part(0,i),:]=t.astype(bf16)
        for m in range(4):
            put(gs_scr.at[pl.ds(i*K4+m*Ch,Ch)],fb_ref.at[m,pl.ds(i*Ch,Ch)],fo_s.at[i,m])
    for b in range(NB):
        for i in range(G-1): arrived(do_ref.at[b*G+pidx[i]],dors.at[b*G+pidx[i]])
    for i,cp in enumerate(exch):
        if i%G==0: cp.wait()
        else: cp.wait_send()
    for cps in gcp[1:]:
        for cp in cps: cp.wait_send()
    spread_far(cots,"sent")
    home_arrived(C,n,bh_ref,bors)
    spread_sent(home)
    for cp in outs: cp.wait()

def middle(Z, C, mix, w2o, xo, cot, coto, gain):
    NB,n,D=xo.shape; G=2*C; nC=w2o.shape[2]; Ch=nC//3; K4=4*Ch; N=NB*n
    V=pl.BlockSpec(memory_space=pltpu.VMEM); A=pl.BlockSpec(memory_space=pl.ANY)
    S=lambda *sh: pltpu.SemaphoreType.DMA(sh)
    M=lambda *sh: pltpu.VMEM(sh,bf16)
    B=lambda *sh: jax.ShapeDtypeStruct(sh,bf16)
    return pl.pallas_call(functools.partial(mid_kernel,Z,C,n),
        out_shape=(B(NB,n,D),B(*cot.shape),B(NB*G,4,Ch,n),jax.ShapeDtypeStruct((NB,n,D),f32),B(4,nC,D),jax.ShapeDtypeStruct((8,D),f32)),
        in_specs=[V,A,V,A,A,V],out_specs=(A,A,A,A,A,V),
        scratch_shapes=[M(G*K4,D)]*3+[M(N,G*K4) if i in (1,2) else M(N,D) for i in range(4)]+[M(NB,G,4,Ch,n),M((G-1)*3*K4,D),M(G-1,3,K4,D),M(NB,n,D),pltpu.VMEM((NB,n,G*K4),f32),pltpu.VMEM((NB,n,D),f32),
            S(3,G,4),S(G-1,NB),S(NB*G),S(NB),S(G-1,3),S(G-1,3),S(NB),S(NB),S(2,NB),S(3,4),S(NB),S(4*C)],
        compiler_params=pltpu.CompilerParams(collective_id=2,has_side_effects=True,vmem_limit_bytes=60*2**20),
        cost_estimate=pl.CostEstimate(flops=3*10**10,bytes_accessed=10**8,transcendentals=0),
        name="middle")(mix,w2o,xo,cot,coto,gain.reshape(1,D))

def bwd_kernel(Z, C, n, qkv_ref, ot_ref, do_ref, lse_ref, pd_ref, segk_ref, segq_ref, ain_ref, wts_ref,
               xo_ref, gmid_ref, gain_ref, vec_ref, fb_ref,
               gi_ref, gwm_ref, gwq_ref, vo_ref,
               kv_scr, k_scr, v_scr, p_scr, ds_scr, dq_scr, dl_scr, a_scr, dw_scr, qr_scr, big_scr, zs_scr, zr_scr, t3_scr, t3r_scr, tb_scr, ot_scr, do_scr,
               dxr_scr, own_scr, xb_scr, gb_scr, va_scr, vb_scr, vs_scr, sc_scr,
               fs, frs, qs, qrs, zss, zrs, t3s, t3rs, cs_, crs, dxs, dxrs, gis, girs, ld, al, otl, dol, kvl, xl, vas, vars_, vbs, vbrs):
    z,k,q,s=[lax.axis_index(a) for a in AXES]
    G=2*C; g0=k*C+s; NB=4*C
    D=gain_ref.shape[1]; L=segq_ref.shape[1]; W=pd_ref.shape[0]; hb=W//HD; nb=L//BQ; sub=BQ//n
    nC=3*W; Dd=gwm_ref.shape[1]
    peers=list(itertools.product(range(2),range(C)))[1:]
    pdev=[(z,lax.rem(k+gc,2),q,lax.rem(s+gs,C)) for gc,gs in peers]
    pidx=[lax.rem(k+gc,2)*C+lax.rem(s+gs,C) for gc,gs in peers]
    back=[gc*C+(C-gs)%C for gc,gs in peers]
    fore=[gc*C+gs for gc,gs in peers]
    chipdev=[(z,k,partner(q,m),s) for m in range(4)]
    core=(z,1-k,q,s)
    zdev=[lax.rem(z+j,Z) for j in range(Z)]
    def frow(m): return big_scr.at[pl.ds((m-1)*nC,nC)]
    def dxat(i,e): return big_scr.at[pl.ds((i*NB+e)*n,n)]
    fcp={m: rcopy(fb_ref.at[m],frow(m),fs.at[m],frs.at[m],chipdev[m]) for m in (1,2)}
    qcp={m: rcopy(dw_scr.at[m-1],qr_scr.at[m-1],qs.at[m],qrs.at[m],chipdev[m]) for m in (1,2)}
    zcp=[[rcopy(zs_scr.at[e%2,zdev[j]],zr_scr.at[e,z],zss.at[e,j],zrs.at[e,z],(zdev[j],k,q,s)) for j in range(1,Z)] for e in range(4)]
    t3cp=[rcopy(tb_scr.at[e],t3r_scr.at[e],t3s.at[e],t3rs.at[e],chipdev[3]) for e in range(2)]
    gws=(gwm_ref,gwq_ref)
    ccp=[rcopy(t3_scr.at[e,pl.ds(pl.multiple_of((1-k)*Dd,Dd),Dd),:],gws[e].at[k],cs_.at[e],crs.at[e],core) for e in range(2)]
    def load(src,dst,i):
        cp=pltpu.make_async_copy(src,dst,ld.at[i]); cp.start(); return cp
    def zsend(e, value):
        rows=D//Z; per=max(1,640//rows)
        for i in range(Z//per):
            ls=slice(i*per*rows,(i+1)*per*rows)
            zs_scr[e%2,i*per:(i+1)*per]=value(ls).T.reshape(per,rows,nC).astype(bf16)
        for cp in zcp[e]: cp.start()
    def zsum(e):
        for cp in zcp[e]: cp.wait_send()
        t=zs_scr[e%2,z].astype(f32)
        for j in range(1,Z):
            arrived(zr_scr.at[e,zdev[j]],zrs.at[e,zdev[j]])
            t=t+zr_scr[e,zdev[j]].astype(f32)
        return t
    def diag(e):
        tb_scr[e]=zsum(e).astype(bf16)
        t3cp[e].start()
    def final(e):
        t=zsum(2+e)
        arrived(t3r_scr.at[e],t3rs.at[e])
        t=t+t3r_scr[e].astype(f32)
        t3cp[e].wait_send()
        t3_scr[e]=t
        ccp[e].start()
        gws[e][k]=t3_scr[e,pl.ds(pl.multiple_of(k*Dd,Dd),Dd),:]
    kvcp=[pltpu.make_async_copy(qkv_ref.at[m],kv_scr.at[m],kvl.at[m]) for m in range(4)]
    for m in (3,2,1,0): kvcp[m].start()
    acp=pltpu.make_async_copy(ain_ref,a_scr,al)
    acp.start()
    def otcp(m): return pltpu.make_async_copy(ot_ref.at[:,m],ot_scr,otl)
    otcp(3).start()
    def docp(idx): return pltpu.make_async_copy(do_ref.at[:,3-idx],do_scr.at[lax.rem(idx,2)],dol.at[lax.rem(idx,2)])
    docp(0).start()
    greet(Z,C)
    for m in (1,2): fcp[m].start()
    load(fb_ref.at[3],dw_scr.at[0],0).wait()
    zsend(0,lambda ls: dw_scr[0,:,ls].astype(f32))
    sc_scr[...]=jnp.zeros_like(sc_scr)
    rowi=lax.broadcasted_iota(jnp.int32,(BQ,BQ),0)
    coli=lax.broadcasted_iota(jnp.int32,(BQ,BQ),1)
    hs=[slice(h*HD,(h+1)*HD) for h in range(hb)]

    def block(idx,_):
        m=3-idx
        pltpu.make_async_copy(qkv_ref.at[m],kv_scr.at[m],kvl.at[m]).wait()
        for h in range(hb):
            k_scr[h]=kv_scr[m,W+h*HD:W+(h+1)*HD,:].T
            v_scr[h]=kv_scr[m,2*W+h*HD:2*W+(h+1)*HD,:].T
        slot=lax.rem(idx,2)
        docp(idx).wait()
        @pl.when(idx<3)
        def _(): docp(idx+1).start()
        def tile(h,i):
            return jnp.concatenate([do_scr[slot,i*sub+t,hs[h],:] for t in range(sub)],1) if sub>1 else do_scr[slot,i,hs[h],:]
        otcp(m).wait()
        for i in range(nb):
            for h in range(hb):
                for t in range(sub):
                    B_=i*sub+t
                    dl_scr[h,:,B_*n:(B_+1)*n]=(do_scr[slot,B_,hs[h],:].astype(f32)*ot_scr[B_,hs[h],:].astype(f32)).sum(0,keepdims=True)
        @pl.when(m>0)
        def _(): otcp(m-1).start()
        rows=[(j,h) for j in range(nb) for h in range(hb)]
        def phase_a(r):
            j,h=rows[r]; ks=slice(j*BQ,(j+1)*BQ)
            for i in range(j,nb):
                cs=slice(i*BQ,(i+1)*BQ)
                t=dot(k_scr[h,ks,:],kv_scr[m,hs[h],cs])
                dp=dot(v_scr[h,ks,:],tile(h,i))
                sk=segk_ref[ks,:]
                ok=jnp.concatenate([sk]*(BQ//128),axis=1)==segq_ref[:,cs]
                if j==i: ok=ok&(rowi<=coli)
                p=jnp.exp(jnp.where(ok,t-lse_ref[m*hb+h,:,cs],NEG))
                p_scr[r%2,:,cs]=p.astype(bf16)
                ds_scr[r%2,:,cs]=(p*(dp-dl_scr[h,:,cs])).astype(bf16)
                yield
        def phase_b(r):
            j,h=rows[r]; js=slice(j*BQ,(j+1)*BQ); rs=slice(j*BQ,L)
            dos=jnp.concatenate([tile(h,i) for i in range(j,nb)],1)
            dv=dot(dos,p_scr[r%2,:,rs],NT)
            yield
            dk=dot(kv_scr[m,hs[h],rs],ds_scr[r%2,:,rs],NT)
            yield
            for i in range(j,nb):
                cs=slice(i*BQ,(i+1)*BQ)
                dq=dot(kv_scr[m,W+h*HD:W+(h+1)*HD,js],ds_scr[r%2,:,cs])
                if j==0: dq_scr[hs[h],cs]=dq
                else: dq_scr[hs[h],cs]+=dq
                yield
            kv_scr[m,W+h*HD:W+(h+1)*HD,js]=dk.astype(bf16)
            kv_scr[m,2*W+h*HD:2*W+(h+1)*HD,js]=dv.astype(bf16)
        merge(phase_a(0))
        for u in range(len(rows)):
            gs=[phase_b(u)]
            if u+1<len(rows): gs=[phase_a(u+1)]+gs
            merge(*gs)
        dq=dq_scr[...]
        sc_scr[...]+=(dq*kv_scr[m,:W,:].astype(f32)).sum(1,keepdims=True)/pd_ref[:,:1]
        kv_scr[m,:W,:]=(dq*pd_ref[:,:1]).astype(bf16)
        @pl.when(idx==0)
        def _():
            acp.wait()
            zsend(1,lambda ls: dwt(3,ls))
        @pl.when((idx==1)|(idx==2))
        def _():
            for c in range(D//256):
                ls=slice(c*256,(c+1)*256)
                dw_scr[m-1,:,ls]=dwt(m,ls).astype(bf16)
        @pl.when(idx==1)
        def _():
            qcp[2].start()
            diag(0)
            ld0=load(fb_ref.at[0],dw_scr.at[0],0)
            for m2 in (1,2): arrived(frow(m2),frs.at[m2])
            ld0.wait()
            zsend(2,lambda ls: dw_scr[0,:,ls].astype(f32)+big_scr[0:nC,ls].astype(f32)+big_scr[nC:2*nC,ls].astype(f32))
        @pl.when(idx==2)
        def _():
            qcp[1].start()
            diag(1)
        return 0
    def dwt(m,ls):
        return dot(kv_scr[m],a_scr[:,ls])
    lax.fori_loop(0,4,block,0)
    for m2 in (1,2): arrived(qr_scr.at[m2-1],qrs.at[m2])
    zsend(3,lambda ls: dwt(0,ls)+qr_scr[0,:,ls].astype(f32)+qr_scr[1,:,ls].astype(f32))
    wcp=[pltpu.make_async_copy(wts_ref.at[m],a_scr.at[pl.ds(m*nC,nC),:],kvl.at[m]) for m in range(4)]
    for cp in wcp: cp.start()
    for cp in wcp: cp.wait()

    def chunk(i):
        gl=kv_scr[:,:,pl.ds(pl.multiple_of(i*BQ,BQ),BQ)].reshape(4*nC,BQ)
        return dot(gl,a_scr[:4*nC,:],TN)
    order=[partner(q,m)*C+t for m in (3,1,2,0) for t in range(C)]
    def xload(e):
        b=order[e]
        return [pltpu.make_async_copy(xo_ref.at[b],xb_scr.at[0],xl.at[0,0]),pltpu.make_async_copy(gmid_ref.at[b],gb_scr.at[0],xl.at[1,0])]
    dxcp=[[rcopy(dxat(i,e),dxr_scr.at[back[i]-1,e],dxs.at[i,e],dxrs.at[back[i],e],pdev[i]) for e in range(NB)] for i in range(G-1)]
    def give(e):
        b=order[e]
        if sub>1: own_scr[...]=chunk(b)
        for i in range(G-1):
            if sub==1: big_scr[(i*NB+e)*n:(i*NB+e+1)*n,:]=chunk(b*G+pidx[i]).astype(bf16)
            else: big_scr[(i*NB+e)*n:(i*NB+e+1)*n,:]=own_scr[pl.ds(pl.multiple_of(pidx[i]*n,n),n),:].astype(bf16)
            dxcp[i][e].start()
    gicp=[]
    gparts=[]
    def take(e):
        b=order[e]
        for cp in xload(e): cp.start()
        if sub==1:
            gain=chunk(b*G+g0)
        else:
            own_scr[...]=chunk(b)
            gain=own_scr[pl.ds(pl.multiple_of(g0*n,n),n),:]
        for i in range(G-1):
            arrived(dxr_scr.at[fore[i]-1,e],dxrs.at[fore[i],e])
            gain=gain+dxr_scr[fore[i]-1,e].astype(f32)
        for cp in xload(e): cp.wait()
        x=xb_scr[0].astype(f32)
        inv=lax.rsqrt(jnp.mean(x*x,axis=-1,keepdims=True)+norm_eps)
        nx=x*inv
        dn=gain*gain_ref[...]
        gin=gb_scr[0]+inv*(dn-nx*jnp.mean(dn*nx,axis=-1,keepdims=True))
        gparts.append((gain*nx).reshape(n//8,8,D).sum(0))
        dxcp[0][e].wait_send()
        big_scr[e*n:(e+1)*n,:]=gin.astype(bf16)
        dst=gi_ref.at[lax.rem(q,2),pl.ds(pl.multiple_of((k*C+s)*n,n),n),:]
        rs=girs.at[(lax.rem(q,2)*2+k)*C+s]
        gicp.append((is_home()&(b==q*C+s),pltpu.make_async_copy(dxat(0,e),dst,rs),
                     rcopy(dxat(0,e),dst,gis.at[e],rs,(z,lax.div(q,2),lax.div(b,C),lax.rem(b,C)))))
        spread_start(gicp[-1:])
    give(0)
    for e in range(NB):
        if e+1<NB: give(e+1)
        take(e)
    gpart=gparts[0]
    for t in gparts[1:]: gpart=gpart+t
    vs_scr[...]=jnp.zeros_like(vs_scr)
    vs_scr[0:1,:]=gpart.sum(0,keepdims=True)
    vs_scr[1:2,:]=vec_ref[...].sum(0,keepdims=True)
    sc=sc_scr[0:HD,:]
    for h in range(1,hb): sc=sc+sc_scr[h*HD:(h+1)*HD,:]
    vs_scr[2:3,0:HD]=sc.T[0:1,:]
    me=(k*4+q)*C+s
    va_scr[me]=vs_scr[...]
    plane=list(itertools.product(range(2),range(4),range(C)))[1:]
    vacp=[rcopy(vs_scr,va_scr.at[me],vas.at[i],vars_.at[me],(z,lax.rem(k+a,2),lax.rem(q+b,4),lax.rem(s+c,C))) for i,(a,b,c) in enumerate(plane)]
    for cp in vacp: cp.start()
    final(0)
    for a,b,c in plane:
        o=(lax.rem(k+a,2)*4+lax.rem(q+b,4))*C+lax.rem(s+c,C)
        arrived(va_scr.at[o],vars_.at[o])
    t=va_scr[0]
    for i in range(1,8*C): t=t+va_scr[i]
    vb_scr[z]=t
    vbcp=[rcopy(vb_scr.at[z],vb_scr.at[z],vbs.at[j],vbrs.at[z],(zdev[j],k,q,s)) for j in range(1,Z)]
    for cp in vbcp: cp.start()
    final(1)
    for j in range(1,Z): arrived(vb_scr.at[zdev[j]],vbrs.at[zdev[j]])
    t=vb_scr[0]
    for i in range(1,Z): t=t+vb_scr[i]
    vo_ref[...]=t
    for e in range(2):
        arrived(gws[e].at[1-k],crs.at[e])
        ccp[e].wait_send()
    home_arrived(C,n,gi_ref,girs)
    spread_sent(gicp)
    for i in range(1,G-1):
        for e in range(NB): dxcp[i][e].wait_send()
    for m in (1,2):
        fcp[m].wait_send(); qcp[m].wait_send()
    for cp in vacp+vbcp: cp.wait_send()

def backward(Z, C, qkv, ot, do, lse, pd, segk, segq, ain, wts, xo, gmid, gain, vec, fb, R, Pn, Dd):
    NB,n,D=xo.shape; G=2*C; nC=wts.shape[1]; W=pd.shape[0]; hb=W//HD; L=segq.shape[1]
    V=pl.BlockSpec(memory_space=pltpu.VMEM); A=pl.BlockSpec(memory_space=pl.ANY)
    S=lambda *sh: pltpu.SemaphoreType.DMA(sh) if sh else pltpu.SemaphoreType.DMA
    M=lambda *sh: pltpu.VMEM(sh,bf16)
    F=lambda *sh: pltpu.VMEM(sh,f32)
    gw=jax.ShapeDtypeStruct((2,Dd,nC),f32)
    return pl.pallas_call(functools.partial(bwd_kernel,Z,C,n),
        out_shape=(jax.ShapeDtypeStruct((R,Pn,D),bf16),gw,gw,jax.ShapeDtypeStruct((8,D),f32)),
        in_specs=[A,A,A,V,V,V,V,A,A,A,A,V,V,A],out_specs=(A,V,V,V),
        scratch_shapes=[M(4,nC,L),M(hb,L,HD),M(hb,L,HD),M(2,BQ,L),M(2,BQ,L),F(W,L),F(hb,1,L),M(L,D),
            M(2,nC,D),M(2,nC,D),M(max(2*nC,(G-1)*NB*n),D),M(2,Z,D//Z,nC),M(4,Z,D//Z,nC),F(2,D//Z,nC),M(2,D//Z,nC),M(2,D//Z,nC),M(NB*G,W,n),M(2,NB*G,W,n),
            M(G-1,NB,n,D),F(BQ,D) if n<BQ else F(8,128),M(1,n,D),F(1,n,D),F(8*C,8,D),F(Z,8,D),F(8,D),F(W,1),
            S(4),S(4),S(4),S(4),S(4,Z),S(4,Z),S(2),S(2),S(2),S(2),S(G,NB),S(G,NB),S(NB),S(4*C),S(4),S(),S(),S(2),S(4),S(2,2),S(8*C),S(8*C),S(Z),S(Z)],
        compiler_params=pltpu.CompilerParams(collective_id=1,has_side_effects=True,vmem_limit_bytes=58*2**20),
        cost_estimate=pl.CostEstimate(flops=6*10**10,bytes_accessed=10**8,transcendentals=0),
        name="backward")(qkv,ot,do,lse,pd,segk,segq,ain.reshape(L,D),wts,xo,gmid,gain.reshape(1,D),vec,fb)

def finish_kernel(Ch, gi_ref, gwm_ref, gwq_ref, vo_ref, sf_ref, ig_ref, gq_ref, gk_ref, gv_ref, go_ref, gu_ref, gd_ref, ga_ref, gs_ref, gm_ref):
    ig_ref[...]=gi_ref[...].astype(f32)
    @pl.when(pl.program_id(0)==0)
    def _():
        def cols(ref,i):
            return jnp.concatenate([ref[0,:,i*Ch:(i+1)*Ch],ref[1,:,i*Ch:(i+1)*Ch]],1)
        for i,o in enumerate((gq_ref,gk_ref,gv_ref)): o[...]=cols(gwq_ref,i)
        go_ref[...]=cols(gwm_ref,0)
        gu_ref[...]=cols(gwm_ref,1)
        gd_ref[...]=cols(gwm_ref,2)
        ga_ref[...]=vo_ref[0,:]
        gm_ref[...]=vo_ref[1,:]
        gs_ref[...]=vo_ref[2,0:HD]*sf_ref[0,:]

def finish(gi, gwm, gwq, vo, sf):
    R,Pn,D=gi.shape; _,Dd,nC=gwm.shape; Ch=nC//3; T=4
    F=lambda *sh: jax.ShapeDtypeStruct(sh,f32)
    full=lambda *sh: pl.BlockSpec(sh,lambda i: (0,)*len(sh))
    row=pl.BlockSpec((R,Pn//T,D),lambda i:(0,i,0))
    shapes=[(Dd,2*Ch)]*6+[(D,),(HD,),(D,)]
    return pl.pallas_call(functools.partial(finish_kernel,Ch),grid=(T,),
        out_shape=(F(R,Pn,D),)+tuple(F(*sh) for sh in shapes),
        in_specs=[row,full(2,Dd,nC),full(2,Dd,nC),full(8,D),full(1,HD)],
        out_specs=(row,)+tuple(full(*sh) for sh in shapes),
        compiler_params=pltpu.CompilerParams(vmem_limit_bytes=60*2**20),
        name="finish")(gi,gwm,gwq,vo,sf.reshape(1,HD))


def make_local(Z, C):
    def local(tokens, segments, attn_gain, w_query, w_key, w_value, w_out, query_scale, mlp_gain, w_up, w_down, cotangent):
        R,Pn,D=tokens.shape
        Dd=w_query.shape[0]

        w1h,w2h,pd=prep(w_query,w_key,w_value,w_out,w_up,w_down,query_scale)
        xo,ain,wts,w2o,mix,qkv,ot,lse,segk,segq,coto=forward(Z,C,tokens,w1h,w2h,cotangent,attn_gain,pd,segments)
        _,block_out,do,gmid,fb,vec=middle(Z,C,mix,w2o,xo,cotangent,coto,mlp_gain)
        gi,gwm,gwq,vo=backward(Z,C,qkv,ot,do,lse,pd,segk,segq,ain,wts,xo,gmid,attn_gain,vec,fb,R,Pn,Dd)
        sf=(scale_base/math.sqrt(HD))*jax.nn.sigmoid(query_scale)
        ig,gq,gk,gv,go,gu,gd,ga,gs,gm=finish(gi,gwm,gwq,vo,sf)
        return (block_out,ig,ga,gq,gk,gv,go.T,gs,gm,gu,gd.T)
    return local

def solution(mesh):
    dp,T=mesh.shape["dp"],mesh.shape["tensor"]
    Z,C=dp//2,T//4
    fine=Mesh(mesh.devices.reshape(Z,2,4,C),AXES)
    dpx=("zz","core"); tx=("q","s")
    in_specs=(P(dpx,tx,None),P(dpx,None),P(),P(dpx,tx),P(dpx,tx),P(dpx,tx),P(tx,dpx),P(),P(),P(dpx,tx),P(tx,dpx),P(dpx,tx,None))
    out_specs=(P(dpx,tx,None),P(dpx,tx,None),P(),P(dpx,tx),P(dpx,tx),P(dpx,tx),P(tx,dpx),P(),P(),P(dpx,tx),P(tx,dpx))
    return jax.shard_map(make_local(Z,C),mesh=fine,in_specs=in_specs,out_specs=out_specs,check_vma=False)
```

```python
import functools
import itertools
import math
import jax, jax.numpy as jnp
from jax import lax
from jax.experimental import pallas as pl
from jax.experimental.pallas import tpu as pltpu
from jax.sharding import Mesh, PartitionSpec as P

AXES=("zz","core","q","s")
norm_eps = 1e-06
HD=80
BQ=256
NEG=-1e30
f32=jnp.float32; bf16=jnp.bfloat16
NT=(((1,),(1,)),((),()))
NN=(((1,),(0,)),((),()))
TN=(((0,),(0,)),((),()))
def dot(a,b,dims=NN): return lax.dot_general(a,b,dims,preferred_element_type=f32)

def merge(*gens):
    gens=list(gens)
    while gens:
        for g in list(gens):
            try: next(g)
            except StopIteration: gens.remove(g)


MESH=pl.DeviceIdType.MESH
scale_base = 1.442695041

def rcopy(src,dst,ss,rs,dev):
    return pltpu.make_async_remote_copy(src_ref=src,dst_ref=dst,send_sem=ss,recv_sem=rs,device_id=dev,device_id_type=MESH)

def transpose_rows(src, dst):
    P_,rows,cols=src.shape
    per=max(1,640//rows)
    for i in range(P_//per):
        dst[:,i*per*rows:(i+1)*per*rows]=src[i*per:(i+1)*per].reshape(per*rows,cols).T

def partner(q, m):
    return (q,q+1-2*lax.rem(q,2),lax.rem(q+2,4),3-q)[m]

def greet(Z, C):
    z,k,q,s=[lax.axis_index(a) for a in AXES]
    bar=pltpu.get_barrier_semaphore()
    plane=list(itertools.product(range(2),range(4),range(C)))[1:]
    column=[(j,a) for j in range(1,Z) for a in range(2)]
    for a,b,c in plane:
        pl.semaphore_signal(bar,inc=1,device_id=(z,lax.rem(k+a,2),lax.rem(q+b,4),lax.rem(s+c,C)),device_id_type=MESH)
    for j,a in column:
        pl.semaphore_signal(bar,inc=1,device_id=(lax.rem(z+j,Z),lax.rem(k+a,2),q,s),device_id_type=MESH)
    pl.semaphore_wait(bar,len(plane)+len(column))

def col_copies(Z, src, dst, ss, rs):
    z,k,q,s=[lax.axis_index(a) for a in AXES]
    out=[]
    for j in range(Z):
        for a in range(2):
            kk=lax.rem(k+a,2)
            if j==0 and a==0: out.append(pltpu.make_async_copy(src.at[k],dst.at[2*z+k],rs.at[2*z+k]))
            else: out.append(rcopy(src.at[kk],dst.at[2*z+k],ss.at[j*2+a],rs.at[2*z+k],(lax.rem(z+j,Z),kk,q,s)))
    return out

def spread_copies(C, n, src, dst, ss, rs):
    z,k,q,s=[lax.axis_index(a) for a in AXES]
    out=[]
    for rr in range(2):
        r=lax.rem(q+rr,2)
        for h in range(2):
            for s2 in range(C):
                i=(rr*2+h)*C+s2
                piece=src.at[r,pl.ds((h*C+s2)*n,n),:]
                out.append((rr,(k==h)&(q==2*k+r)&(s==s2),pltpu.make_async_copy(piece,dst.at[q*C+s],rs.at[q*C+s]),
                            rcopy(piece,dst.at[q*C+s],ss.at[i],rs.at[q*C+s],(z,h,2*k+r,s2))))
    return out

def is_home(): return lax.axis_index("core")==lax.div(lax.axis_index("q"),2)

def spread_near(cps, do):
    for rr,mine,loc,cp in cps:
        if rr==0:
            @pl.when(mine)
            def _(loc=loc):
                if do=="start": loc.start()
            @pl.when(jnp.logical_not(mine))
            def _(cp=cp): cp.start() if do=="start" else cp.wait_send()
        else:
            @pl.when(is_home())
            def _(cp=cp): cp.start() if do=="start" else cp.wait_send()

def spread_far(cps, do):
    for rr,mine,loc,cp in cps:
        if rr==1:
            @pl.when(jnp.logical_not(is_home()))
            def _(cp=cp): cp.start() if do=="start" else cp.wait_send()

def near_blocks(C):
    q=lax.axis_index("q")
    return [partner(q,m)*C+t for m in range(3) for t in range(C)]

def far_blocks(C):
    q=lax.axis_index("q")
    return [partner(q,3)*C+t for t in range(C)]

def spread_start(cps):
    for mine,loc,cp in cps:
        @pl.when(mine)
        def _(loc=loc): loc.start()
        @pl.when(jnp.logical_not(mine))
        def _(cp=cp): cp.start()

def spread_sent(cps):
    for mine,loc,cp in cps:
        @pl.when(jnp.logical_not(mine))
        def _(cp=cp): cp.wait_send()

def home_copies(C, n, src, dst, ss, rs):
    z,k,q,s=[lax.axis_index(a) for a in AXES]
    out=[]
    for b in range(4*C):
        to=dst.at[lax.rem(q,2),pl.ds(pl.multiple_of((k*C+s)*n,n),n),:]
        sem=rs.at[(lax.rem(q,2)*2+k)*C+s]
        out.append(((lax.div(q,2)==k)&(q==b//C)&(s==b%C),pltpu.make_async_copy(src.at[b],to,sem),
                    rcopy(src.at[b],to,ss.at[b],sem,(z,lax.div(q,2),b//C,b%C))))
    return out

def home_arrived(C, n, dst, rs):
    for r in range(2):
        for h in range(2):
            for s2 in range(C):
                arrived(dst.at[r,pl.ds((h*C+s2)*n,n),:],rs.at[(r*2+h)*C+s2])

def arrived(ref, sem):
    z,k,q,s=[lax.axis_index(a) for a in AXES]
    rcopy(ref,ref,sem,sem,(z,1-k,q,s)).wait_recv()

def fwd_kernel(Z, C, n, x_ref, w1_ref, w2_ref, cot_ref, gain_ref, pd_ref, seg_ref,
               xo_ref, ain_ref, wts_ref, w2o_ref, mix_ref, qkv_ref, ot_ref, lse_ref, segk_ref, segq_ref, coto_ref,
               xo_scr, ain_scr, wts_scr, qkv_scr, ot_scr, wa_scr, wb_scr, wd_scr, o3_scr, w2_scr, k_scr, s_scr, so_scr,
               tok_s, tok_r, ain_s, ain_r, a_s, a_r, b_s, b_r, dd_s, dd_r, o3_s, o3_r,
               wt_s, wt_r, hf_s, hf_r, w2_s, w2_r, gr_s, gr_r, loc_s, mix_s, mix_r, mixl, sg_s, sg_r, out_s, qo_s, cot_s, cot_r):
    z,k,q,s=[lax.axis_index(a) for a in AXES]
    G=2*C; g0=k*C+s; NB=4*C
    D=gain_ref.shape[1]; L=seg_ref.shape[1]; W=pd_ref.shape[0]; hb=W//HD; nb=L//BQ; nC=3*W
    peers=list(itertools.product(range(2),range(C)))[1:]
    pdev=[(z,lax.rem(k+gc,2),q,lax.rem(s+gs,C)) for gc,gs in peers]
    pidx=[lax.rem(k+gc,2)*C+lax.rem(s+gs,C) for gc,gs in peers]
    back=[gc*C+(C-gs)%C for gc,gs in peers]
    fore=[gc*C+gs for gc,gs in peers]
    chipdev=[(z,k,partner(q,m),s) for m in range(4)]
    toks=spread_copies(C,n,x_ref,xo_scr,tok_s,tok_r)
    cots=spread_copies(C,n,cot_ref,coto_ref,cot_s,cot_r)
    ca=col_copies(Z,w1_ref,wa_scr,a_s,a_r)
    cb=col_copies(Z,w2_ref,wb_scr,b_s,b_r)
    cd=col_copies(Z,o3_scr,wd_scr,dd_s,dd_r)
    o3=rcopy(w2_ref,o3_scr,o3_s,o3_r,chipdev[3])
    wcp=[rcopy(wts_scr.at[0],wts_scr.at[m],wt_s.at[m],wt_r.at[m],chipdev[m]) for m in (1,2)]
    h1=nC//32*16; half=[pl.ds(0,h1),pl.ds(h1,nC-h1)]
    hcp=[rcopy(wts_scr.at[1,half[0]],wts_scr.at[3,half[0]],hf_s.at[0],hf_r.at[0],chipdev[2]),
         rcopy(wts_scr.at[2,half[1]],wts_scr.at[3,half[1]],hf_s.at[1],hf_r.at[1],chipdev[1])]
    save=[pltpu.make_async_copy(xo_scr,xo_ref,out_s.at[0]),pltpu.make_async_copy(ain_scr,ain_ref,out_s.at[1])]
    wsave=[pltpu.make_async_copy(wts_scr.at[m],wts_ref.at[m],out_s.at[2+m]) for m in range(4)]
    def qsave(m): return [pltpu.make_async_copy(qkv_scr.at[m],qkv_ref.at[m],qo_s.at[0,m]),pltpu.make_async_copy(ot_scr.at[:,m],ot_ref.at[:,m],qo_s.at[1,m])]
    w2cp=[rcopy(w2_scr.at[0],w2_scr.at[m],w2_s.at[m],w2_r.at[m],chipdev[m]) for m in (1,2)]
    grp=[[rcopy(w2_scr.at[m],w2o_ref.at[back[i],m],gr_s.at[i,m],gr_r.at[back[i],m],pdev[i]) for i in range(G-1)] for m in range(4)]
    loc=[pltpu.make_async_copy(w2_scr.at[m],w2o_ref.at[0,m],loc_s.at[m]) for m in range(4)]
    def share(m):
        loc[m].start()
        for cp in grp[m]: cp.start()
    sgc=rcopy(seg_ref,so_scr,sg_s,sg_r,(z,1-k,q,s))
    greet(Z,C)
    sgc.start()
    for cp in ca: cp.start()
    spread_near(toks,"start"); spread_far(toks,"start")
    o3.start()
    sgc.wait_recv()
    sg=jnp.where(k==lax.div(q,2),seg_ref[...],so_scr[...])
    sg=jnp.where(lax.rem(q,2)==0,sg[0:1],sg[1:2]).astype(f32)
    segq_ref[...]=sg
    for c in range(L//BQ):
        segk_ref[c*BQ:(c+1)*BQ,:]=jnp.broadcast_to(sg[:,c*BQ:(c+1)*BQ],(128,BQ)).T
    for i in range(2*Z): arrived(wa_scr.at[i],a_r.at[i])
    for cp in cb: cp.start()
    transpose_rows(wa_scr,wts_scr.at[0])
    for cp in wcp: cp.start()
    wsave[0].start()
    ains=[]
    for j in range(NB):
        arrived(xo_scr.at[j],tok_r.at[j])
        x=xo_scr[j].astype(f32)
        inv=lax.rsqrt(jnp.mean(x*x,axis=-1,keepdims=True)+norm_eps)
        slot=j*G+g0
        ain_scr[slot]=(x*inv*gain_ref[...]).astype(bf16)
        for i in range(G-1):
            cp=rcopy(ain_scr.at[slot],ain_scr.at[slot],ain_s.at[i,j],ain_r.at[slot],pdev[i])
            cp.start(); ains.append(cp)
    for j in range(NB):
        for i in range(G-1): arrived(ain_scr.at[j*G+pidx[i]],ain_r.at[j*G+pidx[i]])
    for cp in save: cp.start()
    rowi=lax.broadcasted_iota(jnp.int32,(BQ,BQ),0)
    coli=lax.broadcasted_iota(jnp.int32,(BQ,BQ),1)
    hs=[slice(h*HD,(h+1)*HD) for h in range(hb)]
    CH=512; per=CH//n; sub=BQ//n

    def block(m,_):
        @pl.when(m==1)
        def _():
            for i in range(2*Z): arrived(wb_scr.at[i],b_r.at[i])
            arrived(o3_scr,o3_r)
            for cp in cd: cp.start()
            transpose_rows(wb_scr,w2_scr.at[0])
            for i in (1,2): arrived(wts_scr.at[i],wt_r.at[i])
            for cp in hcp+wsave[1:3]: cp.start()
            share(0)
        @pl.when(m==2)
        def _():
            for cp in w2cp: cp.start()
        @pl.when(m==3)
        def _():
            for i in range(2): arrived(wts_scr.at[3,half[i]],hf_r.at[i])
            wsave[3].start()
            spread_near(cots,"start")
        for c in range(L//CH):
            cs=slice(c*CH,(c+1)*CH)
            r=dot(wts_scr[m],ain_scr[c*per:(c+1)*per].reshape(CH,D),NT)
            qkv_scr[m,:W,cs]=(r[:W]*pd_ref[:,:1]).astype(bf16)
            qkv_scr[m,W:,cs]=r[W:].astype(bf16)
            for h in range(hb):
                k_scr[h,cs,:]=r[W+h*HD:W+(h+1)*HD].T.astype(bf16)
        units=[(i,h) for i in range(nb) for h in range(hb)]
        st={}
        def phase_a(u):
            i,h=units[u]; c0=i*BQ
            qi=qkv_scr[m,hs[h],c0:c0+BQ]
            sq=segq_ref[:,c0:c0+BQ]
            m8=None
            for j in range(i+1):
                t=dot(k_scr[h,j*BQ:(j+1)*BQ,:],qi)
                sk=segk_ref[j*BQ:(j+1)*BQ,:]
                ok=jnp.concatenate([sk]*(BQ//128),axis=1)==sq
                if j==i: ok=ok&(rowi<=coli)
                t=jnp.where(ok,t,NEG)
                s_scr[u%2,j*BQ:(j+1)*BQ,:]=t
                mm=t.reshape(BQ//8,8,BQ).max(0)
                m8=mm if m8 is None else jnp.maximum(m8,mm)
                yield
            st[u]=m8.max(0,keepdims=True)
        def phase_b(u):
            i,h=units[u]; c0=i*BQ
            mx=st[u]; l8=None; acc=None
            for j in range(i+1):
                p=jnp.exp(s_scr[u%2,j*BQ:(j+1)*BQ,:]-mx)
                ll=p.reshape(BQ//8,8,BQ).sum(0)
                l8=ll if l8 is None else l8+ll
                pv=dot(qkv_scr[m,2*W+h*HD:2*W+(h+1)*HD,j*BQ:(j+1)*BQ],p.astype(bf16))
                acc=pv if acc is None else acc+pv
                yield
            l=l8.sum(0,keepdims=True)
            o=(acc*(1.0/l)).astype(bf16)
            for t in range(sub): ot_scr[i*sub+t,m,hs[h],:]=o[:,t*n:(t+1)*n]
            lse_ref[m*hb+h,:,c0:c0+BQ]=mx+jnp.log(l)
        merge(phase_a(0))
        for u in range(len(units)):
            gs=[phase_b(u)]
            if u+1<len(units): gs=[phase_a(u+1)]+gs
            merge(*gs)
        for b in range(NB):
            pltpu.make_async_copy(ot_scr.at[b*G+g0,m],mix_ref.at[b,0,m],mixl.at[b,m]).start()
            for i in range(G-1):
                rcopy(ot_scr.at[b*G+pidx[i],m],mix_ref.at[b,back[i],m],mix_s.at[i,b,m],mix_r.at[back[i],b,m],pdev[i]).start()
        for cp in qsave(m): cp.start()
        return 0
    lax.fori_loop(0,4,block,0)
    for m in (1,2):
        arrived(w2_scr.at[m],w2_r.at[m])
        share(m)
    for i in range(2*Z): arrived(wd_scr.at[i],dd_r.at[i])
    transpose_rows(wd_scr,w2_scr.at[3])
    share(3)
    for i in range(G-1):
        for b in range(NB):
            for m in range(4):
                arrived(mix_ref.at[b,fore[i],m],mix_r.at[fore[i],b,m])
                rcopy(ot_scr.at[b*G+pidx[i],m],mix_ref.at[b,back[i],m],mix_s.at[i,b,m],mix_r.at[back[i],b,m],pdev[i]).wait_send()
        for m in range(4): arrived(w2o_ref.at[fore[i],m],gr_r.at[fore[i],m])
    for m in range(4):
        loc[m].wait()
        for cp in grp[m]: cp.wait_send()
    for cps in (ca,cb,cd):
        for cp in cps[1:]: cp.wait_send()
    for cp in wcp+hcp+w2cp+ains+[o3,sgc]: cp.wait_send()
    spread_near(toks,"sent"); spread_far(toks,"sent"); spread_near(cots,"sent")
    for b in near_blocks(C): arrived(coto_ref.at[b],cot_r.at[b])
    for cp in save+wsave: cp.wait()
    for m in range(4):
        for cp in qsave(m): cp.wait()
        for b in range(NB): pltpu.make_async_copy(ot_scr.at[b*G+g0,m],mix_ref.at[b,0,m],mixl.at[b,m]).wait()

def forward(Z, C, tokens, w1h, w2h, cot, gain, pd, seg):
    R,Pn,D=tokens.shape; G=2*C; n=Pn//G; _,Dd,nC=w1h.shape; NB=4*C
    L=seg.shape[1]; W=pd.shape[0]; hb=W//HD
    V=pl.BlockSpec(memory_space=pltpu.VMEM); A=pl.BlockSpec(memory_space=pl.ANY)
    S=lambda *sh: pltpu.SemaphoreType.DMA(sh) if sh else pltpu.SemaphoreType.DMA
    B=lambda *sh: jax.ShapeDtypeStruct(sh,bf16)
    F=lambda *sh: jax.ShapeDtypeStruct(sh,f32)
    M=lambda *sh: pltpu.VMEM(sh,bf16)
    col=M(2*Z,Dd,nC)
    return pl.pallas_call(functools.partial(fwd_kernel,Z,C,n),
        out_shape=(B(NB,n,D),B(NB*G,n,D),B(4,nC,D),B(G,4,nC,D),B(NB,G,4,W,n),B(4,nC,L),B(NB*G,4,W,n),F(4*hb,1,L),F(L,128),F(1,L),B(NB,n,D)),
        in_specs=[A,A,A,A,V,V,V],out_specs=(A,A,A,A,A,A,A,V,V,V,A),
        scratch_shapes=[M(NB,n,D),M(NB*G,n,D),M(4,nC,D),M(4,nC,L),M(NB*G,4,W,n),col,col,col,M(2,Dd,nC),M(4,nC,D),M(hb,L,HD),
            pltpu.VMEM((2,L,BQ),f32),pltpu.VMEM((R,L),jnp.int32),
            S(NB),S(NB),S(G-1,NB),S(NB*G),S(2*Z),S(2*Z),S(2*Z),S(2*Z),S(2*Z),S(2*Z),S(),S(),
            S(4),S(4),S(2),S(2),S(4),S(4),S(G-1,4),S(G,4),S(4),S(G-1,NB,4),S(G,NB,4),S(NB,4),S(),S(),S(6),S(2,4),S(NB),S(NB)],
        compiler_params=pltpu.CompilerParams(collective_id=0,has_side_effects=True,vmem_limit_bytes=60*2**20),
        cost_estimate=pl.CostEstimate(flops=3*10**10,bytes_accessed=10**8,transcendentals=0),
        name="forward")(tokens,w1h,w2h,cot,gain.reshape(1,D),pd,seg)

def prep_kernel(Ch, wq_ref, wk_ref, wv_ref, wo_ref, wu_ref, wd_ref, qs_ref, w1_ref, w2_ref, pd_ref):
    for ref,three in ((w1_ref,(wq_ref[...],wk_ref[...],wv_ref[...])),(w2_ref,(wo_ref[...],wu_ref[...],wd_ref[...]))):
        for i,w in enumerate(three):
            for h in range(2): ref[h,:,i*Ch:(i+1)*Ch]=w[:,h*Ch:(h+1)*Ch]
    v=qs_ref[...]
    per_dim=scale_base/math.sqrt(HD)*(jnp.maximum(v,0.0)+jnp.log(1.0+jnp.exp(-jnp.abs(v))))
    col=jnp.broadcast_to(per_dim,(128,HD)).T
    for h in range(pd_ref.shape[0]//HD): pd_ref[h*HD:(h+1)*HD,:]=col

def prep(wq, wk, wv, wo, wu, wd, qs):
    Dd,Ct=wq.shape; Ch=Ct//2
    B=jax.ShapeDtypeStruct((2,Dd,3*Ch),bf16)
    return pl.pallas_call(functools.partial(prep_kernel,Ch),out_shape=(B,B,jax.ShapeDtypeStruct((Ch,128),f32)),
        compiler_params=pltpu.CompilerParams(vmem_limit_bytes=60*2**20),name="prep")(wq,wk,wv,wo.T,wu,wd.T,qs.reshape(1,-1))


def mid_kernel(Z, C, n, mix_ref, w2_ref, xo_ref, cot_ref, coto_ref, gain_ref,
               bo_ref, bh_ref, do_ref, gm_ref, fb_ref, vec_ref,
               wo_scr, wu_scr, wd_scr, mi_scr, hid_scr, gup_scr, ga_scr, gt_scr, gs_scr, gr_scr, co_scr, up_scr, mid_scr,
               wl, dos, dors, dol, gss, grs, cot_s, cot_r, out_s, fo_s, bos, bors):
    z,k,q,s=[lax.axis_index(a) for a in AXES]
    G=2*C; g0=k*C+s; NB=4*C
    D=gain_ref.shape[1]; K4=wo_scr.shape[0]//G; Ch=K4//4; N=NB*n
    peers=list(itertools.product(range(2),range(C)))[1:]
    pdev=[(z,lax.rem(k+gc,2),q,lax.rem(s+gs,C)) for gc,gs in peers]
    pidx=[lax.rem(k+gc,2)*C+lax.rem(s+gs,C) for gc,gs in peers]
    back=[gc*C+(C-gs)%C for gc,gs in peers]
    fore=[gc*C+gs for gc,gs in peers]
    wcp=[]
    for i,dst in enumerate((wo_scr,wu_scr,wd_scr)):
        wcp.append([pltpu.make_async_copy(w2_ref.at[g,m,pl.ds(i*Ch,Ch),:],dst.at[pl.ds((g*4+m)*Ch,Ch),:],wl.at[i,g,m]) for g in range(G) for m in range(4)])
        for cp in wcp[i]: cp.start()
    cots=spread_copies(C,n,cot_ref,co_scr,cot_s,cot_r)
    greet(Z,C)
    spread_far(cots,"start")
    for b in near_blocks(C): pltpu.make_async_copy(coto_ref.at[b],co_scr.at[b],cot_r.at[b]).start()
    order=[partner(q,m)*C+(lax.rem(s+t,C)) for m in range(4) for t in range(C)]
    outs=[]
    def put(src,dst,sem):
        cp=pltpu.make_async_copy(src,dst,sem); cp.start(); outs.append(cp)
    vec_ref[...]=jnp.zeros_like(vec_ref)
    for cp in wcp[0]: cp.wait()
    def slot(e): return slice(e*n,(e+1)*n)
    def ahead(e):
        b=order[e]
        attn=dot(mix_ref[b].reshape(G*K4,n),wo_scr[...],TN)
        middle=xo_ref[b].astype(f32)+attn
        mid_scr[e]=middle
        inv=lax.rsqrt(jnp.mean(middle*middle,axis=-1,keepdims=True)+norm_eps)
        mi_scr[slot(e),:]=(middle*inv*gain_ref[...]).astype(bf16)
        yield
        if e==0:
            for cp in wcp[1]+wcp[2]: cp.wait()
        up=dot(mi_scr[slot(e),:],wu_scr[...],NT)
        up_scr[e]=up
        hid_scr[slot(e),:]=(up*(1.0/(1.0+jnp.exp(-up)))).astype(bf16)
        yield
        gs_scr[slot(e),:]=(mid_scr[e]+dot(hid_scr[slot(e),:],wd_scr[...])).astype(bf16)
        yield
    for e in range(0,NB,2):
        merge(ahead(e),ahead(e+1))
        for i in (e,e+1): put(gs_scr.at[slot(i)],bo_ref.at[order[i]],out_s.at[0,i])
    exch=[]
    home=[]
    boouts=list(outs); outs=[]
    def behind(e):
        b=order[e]
        gh=dot(co_scr[b],wd_scr[...],NT)
        up=up_scr[e]
        sg=1.0/(1.0+jnp.exp(-up))
        gup_scr[slot(e),:]=(gh*(sg*(1.0+up*(1.0-sg)))).astype(bf16)
        yield
        gmlp=dot(gup_scr[slot(e),:],wu_scr[...])
        middle=mid_scr[e]
        inv=lax.rsqrt(jnp.mean(middle*middle,axis=-1,keepdims=True)+norm_eps)
        n2=middle*inv
        dn=gmlp*gain_ref[...]
        gm=co_scr[b].astype(f32)+inv*(dn-n2*jnp.mean(dn*n2,axis=-1,keepdims=True))
        vec_ref[...]+=(gmlp*n2).reshape(n//8,8,D).sum(0)
        mid_scr[e]=gm
        ga_scr[slot(e),:]=gm.astype(bf16)
        yield
        gt_scr[e]=dot(wo_scr[...],ga_scr[slot(e),:],NT).astype(bf16).reshape(G,4,Ch,n)
        yield
    for e0 in range(0,NB,2):
        for e in (e0,e0+1):
            b=order[e]
            if e<3*C: pltpu.make_async_copy(coto_ref.at[b],co_scr.at[b],cot_r.at[b]).wait()
            else: arrived(co_scr.at[b],cot_r.at[b])
            boouts[e].wait()
            dst=bh_ref.at[lax.rem(q,2),pl.ds(pl.multiple_of((k*C+s)*n,n),n),:]
            rs=bors.at[(lax.rem(q,2)*2+k)*C+s]
            mine=is_home()&(b==q*C+s)
            home.append((mine,pltpu.make_async_copy(bo_ref.at[b],dst,rs),rcopy(bo_ref.at[b],dst,bos.at[e],rs,(z,lax.div(q,2),lax.div(b,C),lax.rem(b,C)))))
            spread_start(home[-1:])
        merge(behind(e0),behind(e0+1))
        for e in (e0,e0+1):
            b=order[e]
            put(mid_scr.at[e],gm_ref.at[b],out_s.at[1,e])
            lc=pltpu.make_async_copy(gt_scr.at[e,0],do_ref.at[b*G+g0],dol.at[e])
            lc.start(); exch.append(lc)
            for i in range(G-1):
                cp=rcopy(gt_scr.at[e,fore[i]],do_ref.at[b*G+g0],dos.at[i,e],dors.at[b*G+g0],pdev[i])
                cp.start(); exch.append(cp)
    def wgrad(i,g):
        cs=slice(g*K4,(g+1)*K4)
        if i==0: return dot(jnp.concatenate([mix_ref[b,g].reshape(K4,n) for b in order],1),ga_scr[...])
        if i==1: return dot(gup_scr[:,cs],mi_scr[...],TN)
        return dot(hid_scr[:,cs],jnp.concatenate([co_scr[b] for b in order],0),TN)
    for cp in outs: cp.wait()
    outs=[]
    def part(j,i): return pl.ds((j*3+i)*K4,K4)
    gcp=[[None]*3 for j in range(G-1)]
    for j in range(G-1):
        for i in range(3):
            gs_scr[part(j,i),:]=wgrad(i,fore[j]).astype(bf16)
            gcp[j][i]=rcopy(gs_scr.at[part(j,i)],gr_scr.at[back[j]-1,i],gss.at[j,i],grs.at[back[j]-1,i],pdev[j])
            gcp[j][i].start()
    for i in range(3):
        t=wgrad(i,0)
        for j in range(G-1):
            arrived(gr_scr.at[fore[j]-1,i],grs.at[fore[j]-1,i])
            t=t+gr_scr[fore[j]-1,i].astype(f32)
        gcp[0][i].wait_send()
        gs_scr[part(0,i),:]=t.astype(bf16)
        for m in range(4):
            put(gs_scr.at[pl.ds(i*K4+m*Ch,Ch)],fb_ref.at[m,pl.ds(i*Ch,Ch)],fo_s.at[i,m])
    for b in range(NB):
        for i in range(G-1): arrived(do_ref.at[b*G+pidx[i]],dors.at[b*G+pidx[i]])
    for i,cp in enumerate(exch):
        if i%G==0: cp.wait()
        else: cp.wait_send()
    for cps in gcp[1:]:
        for cp in cps: cp.wait_send()
    spread_far(cots,"sent")
    home_arrived(C,n,bh_ref,bors)
    spread_sent(home)
    for cp in outs: cp.wait()

def middle(Z, C, mix, w2o, xo, cot, coto, gain):
    NB,n,D=xo.shape; G=2*C; nC=w2o.shape[2]; Ch=nC//3; K4=4*Ch; N=NB*n
    V=pl.BlockSpec(memory_space=pltpu.VMEM); A=pl.BlockSpec(memory_space=pl.ANY)
    S=lambda *sh: pltpu.SemaphoreType.DMA(sh)
    M=lambda *sh: pltpu.VMEM(sh,bf16)
    B=lambda *sh: jax.ShapeDtypeStruct(sh,bf16)
    return pl.pallas_call(functools.partial(mid_kernel,Z,C,n),
        out_shape=(B(NB,n,D),B(*cot.shape),B(NB*G,4,Ch,n),jax.ShapeDtypeStruct((NB,n,D),f32),B(4,nC,D),jax.ShapeDtypeStruct((8,D),f32)),
        in_specs=[V,A,V,A,A,V],out_specs=(A,A,A,A,A,V),
        scratch_shapes=[M(G*K4,D)]*3+[M(N,G*K4) if i in (1,2) else M(N,D) for i in range(4)]+[M(NB,G,4,Ch,n),M((G-1)*3*K4,D),M(G-1,3,K4,D),M(NB,n,D),pltpu.VMEM((NB,n,G*K4),f32),pltpu.VMEM((NB,n,D),f32),
            S(3,G,4),S(G-1,NB),S(NB*G),S(NB),S(G-1,3),S(G-1,3),S(NB),S(NB),S(2,NB),S(3,4),S(NB),S(4*C)],
        compiler_params=pltpu.CompilerParams(collective_id=2,has_side_effects=True,vmem_limit_bytes=60*2**20),
        cost_estimate=pl.CostEstimate(flops=3*10**10,bytes_accessed=10**8,transcendentals=0),
        name="middle")(mix,w2o,xo,cot,coto,gain.reshape(1,D))

def bwd_kernel(Z, C, n, qkv_ref, ot_ref, do_ref, lse_ref, pd_ref, segk_ref, segq_ref, ain_ref, wts_ref,
               xo_ref, gmid_ref, gain_ref, vec_ref, fb_ref,
               gi_ref, gwm_ref, gwq_ref, vo_ref,
               kv_scr, k_scr, v_scr, p_scr, ds_scr, dq_scr, dl_scr, a_scr, dw_scr, qr_scr, big_scr, zs_scr, zr_scr, t3_scr, t3r_scr, tb_scr, ot_scr, do_scr,
               dxr_scr, wx_scr, own_scr, xb_scr, gb_scr, va_scr, vb_scr, vs_scr, sc_scr,
               fs, frs, qs, qrs, zss, zrs, t3s, t3rs, cs_, crs, dxs, dxrs, gis, girs, ld, al, otl, dol, kvl, wtl, xl, vas, vars_, vbs, vbrs):
    z,k,q,s=[lax.axis_index(a) for a in AXES]
    G=2*C; g0=k*C+s; NB=4*C
    D=gain_ref.shape[1]; L=segq_ref.shape[1]; W=pd_ref.shape[0]; hb=W//HD; nb=L//BQ; sub=BQ//n
    nC=3*W; Dd=gwm_ref.shape[1]
    peers=list(itertools.product(range(2),range(C)))[1:]
    pdev=[(z,lax.rem(k+gc,2),q,lax.rem(s+gs,C)) for gc,gs in peers]
    pidx=[lax.rem(k+gc,2)*C+lax.rem(s+gs,C) for gc,gs in peers]
    back=[gc*C+(C-gs)%C for gc,gs in peers]
    fore=[gc*C+gs for gc,gs in peers]
    chipdev=[(z,k,partner(q,m),s) for m in range(4)]
    core=(z,1-k,q,s)
    zdev=[lax.rem(z+j,Z) for j in range(Z)]
    def frow(m): return big_scr.at[pl.ds((m-1)*nC,nC)]
    def dxat(i,e): return big_scr.at[pl.ds((i*NB+e)*n,n)]
    fcp={m: rcopy(fb_ref.at[m],frow(m),fs.at[m],frs.at[m],chipdev[m]) for m in (1,2)}
    qcp={m: rcopy(dw_scr.at[m-1],qr_scr.at[m-1],qs.at[m],qrs.at[m],chipdev[m]) for m in (1,2)}
    slot_of=(0,1,0,0)
    zcp=[[rcopy(zs_scr.at[slot_of[e],zdev[j]],zr_scr.at[e%3,z],zss.at[e,j],zrs.at[e,z],(zdev[j],k,q,s)) for j in range(1,Z)] for e in range(4)]
    t3cp=[rcopy(tb_scr,t3r_scr.at[e],t3s.at[e],t3rs.at[e],chipdev[3]) for e in range(2)]
    gws=(gwm_ref,gwq_ref)
    ccp=[rcopy(t3_scr.at[pl.ds(pl.multiple_of((1-k)*Dd,Dd),Dd),:],gws[e].at[k],cs_.at[e],crs.at[e],core) for e in range(2)]
    def wcopy(m): return pltpu.make_async_copy(wts_ref.at[m],(dw_scr.at[m] if m<2 else wx_scr.at[m-2]),wtl.at[m])
    def load(src,dst,i):
        cp=pltpu.make_async_copy(src,dst,ld.at[i]); cp.start(); return cp
    def zsend(e, value):
        rows=D//Z; per=max(1,640//rows)
        for i in range(Z//per):
            ls=slice(i*per*rows,(i+1)*per*rows)
            zs_scr[slot_of[e],i*per:(i+1)*per]=value(ls).T.reshape(per,rows,nC).astype(bf16)
        for cp in zcp[e]: cp.start()
    def zsum(e):
        for cp in zcp[e]: cp.wait_send()
        t=zs_scr[slot_of[e],z].astype(f32)
        for j in range(1,Z):
            arrived(zr_scr.at[e%3,zdev[j]],zrs.at[e,zdev[j]])
            t=t+zr_scr[e%3,zdev[j]].astype(f32)
        return t
    def diag(e):
        tb_scr[...]=zsum(e).astype(bf16)
        t3cp[e].start()
    def final(e):
        t=zsum(2+e)
        arrived(t3r_scr.at[e],t3rs.at[e])
        t=t+t3r_scr[e].astype(f32)
        t3cp[e].wait_send()
        if e==1: ccp[0].wait_send()
        t3_scr[...]=t
        ccp[e].start()
        gws[e][k]=t3_scr[pl.ds(pl.multiple_of(k*Dd,Dd),Dd),:]
    kvcp=[pltpu.make_async_copy(qkv_ref.at[m],kv_scr.at[m],kvl.at[m]) for m in range(4)]
    for m in (1,2,3,0): kvcp[m].start()
    acp=pltpu.make_async_copy(ain_ref,a_scr,al)
    acp.start()
    def otcp(m): return pltpu.make_async_copy(ot_ref.at[:,m],ot_scr,otl)
    otcp(1).start()
    def docp(idx): return pltpu.make_async_copy(do_ref.at[:,lax.rem(idx+1,4)],do_scr.at[lax.rem(idx,2)],dol.at[lax.rem(idx,2)])
    docp(0).start()
    greet(Z,C)
    for m in (1,2): fcp[m].start()
    load(fb_ref.at[3],dw_scr.at[0],0).wait()
    zsend(0,lambda ls: dw_scr[0,:,ls].astype(f32))
    ld0=load(fb_ref.at[0],dw_scr.at[1],1)
    sc_scr[...]=jnp.zeros_like(sc_scr)
    rowi=lax.broadcasted_iota(jnp.int32,(BQ,BQ),0)
    coli=lax.broadcasted_iota(jnp.int32,(BQ,BQ),1)
    hs=[slice(h*HD,(h+1)*HD) for h in range(hb)]

    def block(idx,_):
        m=lax.rem(idx+1,4)
        pltpu.make_async_copy(qkv_ref.at[m],kv_scr.at[m],kvl.at[m]).wait()
        for h in range(hb):
            k_scr[h]=kv_scr[m,W+h*HD:W+(h+1)*HD,:].T
            v_scr[h]=kv_scr[m,2*W+h*HD:2*W+(h+1)*HD,:].T
        slot=lax.rem(idx,2)
        docp(idx).wait()
        @pl.when(idx<3)
        def _(): docp(idx+1).start()
        def tile(h,i):
            return jnp.concatenate([do_scr[slot,i*sub+t,hs[h],:] for t in range(sub)],1) if sub>1 else do_scr[slot,i,hs[h],:]
        otcp(m).wait()
        for i in range(nb):
            for h in range(hb):
                for t in range(sub):
                    B_=i*sub+t
                    dl_scr[h,:,B_*n:(B_+1)*n]=(do_scr[slot,B_,hs[h],:].astype(f32)*ot_scr[B_,hs[h],:].astype(f32)).sum(0,keepdims=True)
        @pl.when(idx<3)
        def _(): otcp(lax.rem(idx+2,4)).start()
        rows=[(j,h) for j in range(nb) for h in range(hb)]
        def phase_a(r):
            j,h=rows[r]; ks=slice(j*BQ,(j+1)*BQ)
            for i in range(j,nb):
                cs=slice(i*BQ,(i+1)*BQ)
                t=dot(k_scr[h,ks,:],kv_scr[m,hs[h],cs])
                dp=dot(v_scr[h,ks,:],tile(h,i))
                sk=segk_ref[ks,:]
                ok=jnp.concatenate([sk]*(BQ//128),axis=1)==segq_ref[:,cs]
                if j==i: ok=ok&(rowi<=coli)
                p=jnp.exp(jnp.where(ok,t-lse_ref[m*hb+h,:,cs],NEG))
                p_scr[r%2,:,cs]=p.astype(bf16)
                ds_scr[r%2,:,cs]=(p*(dp-dl_scr[h,:,cs])).astype(bf16)
                yield
        def phase_b(r):
            j,h=rows[r]; js=slice(j*BQ,(j+1)*BQ); rs=slice(j*BQ,L)
            dos=jnp.concatenate([tile(h,i) for i in range(j,nb)],1)
            dv=dot(dos,p_scr[r%2,:,rs],NT)
            yield
            dk=dot(kv_scr[m,hs[h],rs],ds_scr[r%2,:,rs],NT)
            yield
            for i in range(j,nb):
                cs=slice(i*BQ,(i+1)*BQ)
                dq=dot(kv_scr[m,W+h*HD:W+(h+1)*HD,js],ds_scr[r%2,:,cs])
                if j==0: dq_scr[hs[h],cs]=dq
                else: dq_scr[hs[h],cs]+=dq
                yield
            kv_scr[m,W+h*HD:W+(h+1)*HD,js]=dk.astype(bf16)
            kv_scr[m,2*W+h*HD:2*W+(h+1)*HD,js]=dv.astype(bf16)
        def attend(part):
            merge(phase_a(part[0]))
            for u in part:
                gs=[phase_b(u)]
                if u+1<=part[-1]: gs=[phase_a(u+1)]+gs
                merge(*gs)
        attend(range(2*hb))
        @pl.when(idx==1)
        def _():
            diag(0)
            for m2 in (1,2): arrived(frow(m2),frs.at[m2])
            ld0.wait()
            zsend(2,lambda ls: dw_scr[1,:,ls].astype(f32)+big_scr[0:nC,ls].astype(f32)+big_scr[nC:2*nC,ls].astype(f32))
        @pl.when(idx==3)
        def _():
            final(0)
            for m2 in (1,2): qcp[m2].wait_send()
            for m2 in range(4): wcopy(m2).start()
        attend(range(2*hb,len(rows)))
        dq=dq_scr[...]
        sc_scr[...]+=(dq*kv_scr[m,:W,:].astype(f32)).sum(1,keepdims=True)/pd_ref[:,:1]
        kv_scr[m,:W,:]=(dq*pd_ref[:,:1]).astype(bf16)
        @pl.when(idx==0)
        def _(): acp.wait()
        @pl.when(idx<2)
        def _():
            for c in range(D//256):
                ls=slice(c*256,(c+1)*256)
                dw_scr[m-1,:,ls]=dwt(m,ls).astype(bf16)
        @pl.when(idx==0)
        def _():
            qcp[1].start()
        @pl.when(idx==1)
        def _(): qcp[2].start()
        @pl.when(idx==2)
        def _(): zsend(1,lambda ls: dwt(3,ls))
        return 0
    def dwt(m,ls):
        return dot(kv_scr[m],a_scr[:,ls])
    lax.fori_loop(0,4,block,0)
    for m in range(4): wcopy(m).wait()

    def chunk(i):
        gl=kv_scr[:,:,pl.ds(pl.multiple_of(i*BQ,BQ),BQ)].reshape(4*nC,BQ)
        return dot(gl,jnp.concatenate([dw_scr[...].reshape(2*nC,D),wx_scr[...].reshape(2*nC,D)],0),TN)
    order=[partner(q,m)*C+t for m in (3,1,2,0) for t in range(C)]
    def xload(e):
        b=order[e]
        return [pltpu.make_async_copy(xo_ref.at[b],xb_scr.at[0],xl.at[0,0]),pltpu.make_async_copy(gmid_ref.at[b],gb_scr.at[0],xl.at[1,0])]
    dxcp=[[rcopy(dxat(i,e),dxr_scr.at[back[i]-1,e],dxs.at[i,e],dxrs.at[back[i],e],pdev[i]) for e in range(NB)] for i in range(G-1)]
    def give(e):
        b=order[e]
        if sub>1: own_scr[...]=chunk(b)
        for i in range(G-1):
            if sub==1: big_scr[(i*NB+e)*n:(i*NB+e+1)*n,:]=chunk(b*G+pidx[i]).astype(bf16)
            else: big_scr[(i*NB+e)*n:(i*NB+e+1)*n,:]=own_scr[pl.ds(pl.multiple_of(pidx[i]*n,n),n),:].astype(bf16)
            dxcp[i][e].start()
    gicp=[]
    gparts=[]
    def take(e):
        b=order[e]
        for cp in xload(e): cp.start()
        if sub==1:
            gain=chunk(b*G+g0)
        else:
            own_scr[...]=chunk(b)
            gain=own_scr[pl.ds(pl.multiple_of(g0*n,n),n),:]
        for i in range(G-1):
            arrived(dxr_scr.at[fore[i]-1,e],dxrs.at[fore[i],e])
            gain=gain+dxr_scr[fore[i]-1,e].astype(f32)
        for cp in xload(e): cp.wait()
        x=xb_scr[0].astype(f32)
        inv=lax.rsqrt(jnp.mean(x*x,axis=-1,keepdims=True)+norm_eps)
        nx=x*inv
        dn=gain*gain_ref[...]
        gin=gb_scr[0]+inv*(dn-nx*jnp.mean(dn*nx,axis=-1,keepdims=True))
        gparts.append((gain*nx).reshape(n//8,8,D).sum(0))
        dxcp[0][e].wait_send()
        big_scr[e*n:(e+1)*n,:]=gin.astype(bf16)
        dst=gi_ref.at[lax.rem(q,2),pl.ds(pl.multiple_of((k*C+s)*n,n),n),:]
        rs=girs.at[(lax.rem(q,2)*2+k)*C+s]
        gicp.append((is_home()&(b==q*C+s),pltpu.make_async_copy(dxat(0,e),dst,rs),
                     rcopy(dxat(0,e),dst,gis.at[e],rs,(z,lax.div(q,2),lax.div(b,C),lax.rem(b,C)))))
        spread_start(gicp[-1:])
    give(0)
    for e in range(NB):
        if e+1<NB: give(e+1)
        take(e)
        if e==0:
            for m2 in (1,2): arrived(qr_scr.at[m2-1],qrs.at[m2])
            zsend(3,lambda ls: dwt(0,ls)+qr_scr[0,:,ls].astype(f32)+qr_scr[1,:,ls].astype(f32))
            diag(1)
    gpart=gparts[0]
    for t in gparts[1:]: gpart=gpart+t
    vs_scr[...]=jnp.zeros_like(vs_scr)
    vs_scr[0:1,:]=gpart.sum(0,keepdims=True)
    vs_scr[1:2,:]=vec_ref[...].sum(0,keepdims=True)
    sc=sc_scr[0:HD,:]
    for h in range(1,hb): sc=sc+sc_scr[h*HD:(h+1)*HD,:]
    vs_scr[2:3,0:HD]=sc.T[0:1,:]
    me=(k*4+q)*C+s
    va_scr[me]=vs_scr[...]
    plane=list(itertools.product(range(2),range(4),range(C)))[1:]
    vacp=[rcopy(vs_scr,va_scr.at[me],vas.at[i],vars_.at[me],(z,lax.rem(k+a,2),lax.rem(q+b,4),lax.rem(s+c,C))) for i,(a,b,c) in enumerate(plane)]
    for cp in vacp: cp.start()
    for a,b,c in plane:
        o=(lax.rem(k+a,2)*4+lax.rem(q+b,4))*C+lax.rem(s+c,C)
        arrived(va_scr.at[o],vars_.at[o])
    t=va_scr[0]
    for i in range(1,8*C): t=t+va_scr[i]
    vb_scr[z]=t
    vbcp=[rcopy(vb_scr.at[z],vb_scr.at[z],vbs.at[j],vbrs.at[z],(zdev[j],k,q,s)) for j in range(1,Z)]
    for cp in vbcp: cp.start()
    final(1)
    for j in range(1,Z): arrived(vb_scr.at[zdev[j]],vbrs.at[zdev[j]])
    t=vb_scr[0]
    for i in range(1,Z): t=t+vb_scr[i]
    vo_ref[...]=t
    for e in range(2):
        arrived(gws[e].at[1-k],crs.at[e])
        if e==1: ccp[e].wait_send()
    home_arrived(C,n,gi_ref,girs)
    spread_sent(gicp)
    for i in range(1,G-1):
        for e in range(NB): dxcp[i][e].wait_send()
    for m in (1,2):
        fcp[m].wait_send()
    for cp in vacp+vbcp: cp.wait_send()

def backward(Z, C, qkv, ot, do, lse, pd, segk, segq, ain, wts, xo, gmid, gain, vec, fb, R, Pn, Dd):
    NB,n,D=xo.shape; G=2*C; nC=wts.shape[1]; W=pd.shape[0]; hb=W//HD; L=segq.shape[1]
    V=pl.BlockSpec(memory_space=pltpu.VMEM); A=pl.BlockSpec(memory_space=pl.ANY)
    S=lambda *sh: pltpu.SemaphoreType.DMA(sh) if sh else pltpu.SemaphoreType.DMA
    M=lambda *sh: pltpu.VMEM(sh,bf16)
    F=lambda *sh: pltpu.VMEM(sh,f32)
    gw=jax.ShapeDtypeStruct((2,Dd,nC),f32)
    return pl.pallas_call(functools.partial(bwd_kernel,Z,C,n),
        out_shape=(jax.ShapeDtypeStruct((R,Pn,D),bf16),gw,gw,jax.ShapeDtypeStruct((8,D),f32)),
        in_specs=[A,A,A,V,V,V,V,A,A,A,A,V,V,A],out_specs=(A,V,V,V),
        scratch_shapes=[M(4,nC,L),M(hb,L,HD),M(hb,L,HD),M(2,BQ,L),M(2,BQ,L),F(W,L),F(hb,1,L),M(L,D),
            M(2,nC,D),M(2,nC,D),M(max(2*nC,(G-1)*NB*n),D),M(2,Z,D//Z,nC),M(3,Z,D//Z,nC),F(D//Z,nC),M(2,D//Z,nC),M(D//Z,nC),M(NB*G,W,n),M(2,NB*G,W,n),
            M(G-1,NB,n,D),M(2,nC,D),F(BQ,D) if n<BQ else F(8,128),M(1,n,D),F(1,n,D),F(8*C,8,D),F(Z,8,D),F(8,D),F(W,1),
            S(4),S(4),S(4),S(4),S(4,Z),S(4,Z),S(2),S(2),S(2),S(2),S(G,NB),S(G,NB),S(NB),S(4*C),S(4),S(),S(),S(2),S(4),S(4),S(2,2),S(8*C),S(8*C),S(Z),S(Z)],
        compiler_params=pltpu.CompilerParams(collective_id=1,has_side_effects=True,vmem_limit_bytes=61*2**20),
        cost_estimate=pl.CostEstimate(flops=6*10**10,bytes_accessed=10**8,transcendentals=0),
        name="backward")(qkv,ot,do,lse,pd,segk,segq,ain.reshape(L,D),wts,xo,gmid,gain.reshape(1,D),vec,fb)

def finish_kernel(Ch, gi_ref, gwm_ref, gwq_ref, vo_ref, sf_ref, ig_ref, gq_ref, gk_ref, gv_ref, go_ref, gu_ref, gd_ref, ga_ref, gs_ref, gm_ref):
    ig_ref[...]=gi_ref[...].astype(f32)
    @pl.when(pl.program_id(0)==0)
    def _():
        def cols(ref,i):
            return jnp.concatenate([ref[0,:,i*Ch:(i+1)*Ch],ref[1,:,i*Ch:(i+1)*Ch]],1)
        for i,o in enumerate((gq_ref,gk_ref,gv_ref)): o[...]=cols(gwq_ref,i)
        go_ref[...]=cols(gwm_ref,0)
        gu_ref[...]=cols(gwm_ref,1)
        gd_ref[...]=cols(gwm_ref,2)
        ga_ref[...]=vo_ref[0,:]
        gm_ref[...]=vo_ref[1,:]
        gs_ref[...]=vo_ref[2,0:HD]*sf_ref[0,:]

def finish(gi, gwm, gwq, vo, sf):
    R,Pn,D=gi.shape; _,Dd,nC=gwm.shape; Ch=nC//3; T=4
    F=lambda *sh: jax.ShapeDtypeStruct(sh,f32)
    full=lambda *sh: pl.BlockSpec(sh,lambda i: (0,)*len(sh))
    row=pl.BlockSpec((R,Pn//T,D),lambda i:(0,i,0))
    shapes=[(Dd,2*Ch)]*6+[(D,),(HD,),(D,)]
    return pl.pallas_call(functools.partial(finish_kernel,Ch),grid=(T,),
        out_shape=(F(R,Pn,D),)+tuple(F(*sh) for sh in shapes),
        in_specs=[row,full(2,Dd,nC),full(2,Dd,nC),full(8,D),full(1,HD)],
        out_specs=(row,)+tuple(full(*sh) for sh in shapes),
        compiler_params=pltpu.CompilerParams(vmem_limit_bytes=60*2**20),
        name="finish")(gi,gwm,gwq,vo,sf.reshape(1,HD))


def make_local(Z, C):
    def local(tokens, segments, attn_gain, w_query, w_key, w_value, w_out, query_scale, mlp_gain, w_up, w_down, cotangent):
        R,Pn,D=tokens.shape
        Dd=w_query.shape[0]

        w1h,w2h,pd=prep(w_query,w_key,w_value,w_out,w_up,w_down,query_scale)
        xo,ain,wts,w2o,mix,qkv,ot,lse,segk,segq,coto=forward(Z,C,tokens,w1h,w2h,cotangent,attn_gain,pd,segments)
        _,block_out,do,gmid,fb,vec=middle(Z,C,mix,w2o,xo,cotangent,coto,mlp_gain)
        gi,gwm,gwq,vo=backward(Z,C,qkv,ot,do,lse,pd,segk,segq,ain,wts,xo,gmid,attn_gain,vec,fb,R,Pn,Dd)
        sf=(scale_base/math.sqrt(HD))*jax.nn.sigmoid(query_scale)
        ig,gq,gk,gv,go,gu,gd,ga,gs,gm=finish(gi,gwm,gwq,vo,sf)
        return (block_out,ig,ga,gq,gk,gv,go.T,gs,gm,gu,gd.T)
    return local

def solution(mesh):
    dp,T=mesh.shape["dp"],mesh.shape["tensor"]
    Z,C=dp//2,T//4
    fine=Mesh(mesh.devices.reshape(Z,2,4,C),AXES)
    dpx=("zz","core"); tx=("q","s")
    in_specs=(P(dpx,tx,None),P(dpx,None),P(),P(dpx,tx),P(dpx,tx),P(dpx,tx),P(tx,dpx),P(),P(),P(dpx,tx),P(tx,dpx),P(dpx,tx,None))
    out_specs=(P(dpx,tx,None),P(dpx,tx,None),P(),P(dpx,tx),P(dpx,tx),P(dpx,tx),P(tx,dpx),P(),P(),P(dpx,tx),P(tx,dpx))
    return jax.shard_map(make_local(Z,C),mesh=fine,in_specs=in_specs,out_specs=out_specs,check_vma=False)
```

```python
import functools
import itertools
import math
import jax, jax.numpy as jnp
from jax import lax
from jax.experimental import pallas as pl
from jax.experimental.pallas import tpu as pltpu
from jax.sharding import Mesh, PartitionSpec as P

AXES=("zz","core","q","s")
norm_eps = 1e-06
HD=80
BQ=256
NEG=-1e30
f32=jnp.float32; bf16=jnp.bfloat16
NT=(((1,),(1,)),((),()))
NN=(((1,),(0,)),((),()))
TN=(((0,),(0,)),((),()))
def dot(a,b,dims=NN): return lax.dot_general(a,b,dims,preferred_element_type=f32)

def merge(*gens):
    gens=list(gens)
    while gens:
        for g in list(gens):
            try: next(g)
            except StopIteration: gens.remove(g)


MESH=pl.DeviceIdType.MESH
scale_base = 1.442695041

def rcopy(src,dst,ss,rs,dev):
    return pltpu.make_async_remote_copy(src_ref=src,dst_ref=dst,send_sem=ss,recv_sem=rs,device_id=dev,device_id_type=MESH)

def transpose_rows(src, dst):
    P_,rows,cols=src.shape
    per=max(1,640//rows)
    for i in range(P_//per):
        dst[:,i*per*rows:(i+1)*per*rows]=src[i*per:(i+1)*per].reshape(per*rows,cols).T

def partner(q, m):
    return (q,q+1-2*lax.rem(q,2),lax.rem(q+2,4),3-q)[m]

def greet(Z, C):
    z,k,q,s=[lax.axis_index(a) for a in AXES]
    bar=pltpu.get_barrier_semaphore()
    plane=list(itertools.product(range(2),range(4),range(C)))[1:]
    column=[(j,a) for j in range(1,Z) for a in range(2)]
    for a,b,c in plane:
        pl.semaphore_signal(bar,inc=1,device_id=(z,lax.rem(k+a,2),lax.rem(q+b,4),lax.rem(s+c,C)),device_id_type=MESH)
    for j,a in column:
        pl.semaphore_signal(bar,inc=1,device_id=(lax.rem(z+j,Z),lax.rem(k+a,2),q,s),device_id_type=MESH)
    pl.semaphore_wait(bar,len(plane)+len(column))

def col_copies(Z, src, dst, ss, rs):
    z,k,q,s=[lax.axis_index(a) for a in AXES]
    out=[]
    for j in range(Z):
        for a in range(2):
            kk=lax.rem(k+a,2)
            if j==0 and a==0: out.append(pltpu.make_async_copy(src.at[k],dst.at[2*z+k],rs.at[2*z+k]))
            else: out.append(rcopy(src.at[kk],dst.at[2*z+k],ss.at[j*2+a],rs.at[2*z+k],(lax.rem(z+j,Z),kk,q,s)))
    return out

def spread_copies(C, n, src, dst, ss, rs):
    z,k,q,s=[lax.axis_index(a) for a in AXES]
    out=[]
    for rr in range(2):
        r=lax.rem(q+rr,2)
        for h in range(2):
            for s2 in range(C):
                i=(rr*2+h)*C+s2
                piece=src.at[r,pl.ds((h*C+s2)*n,n),:]
                out.append((rr,(k==h)&(q==2*k+r)&(s==s2),pltpu.make_async_copy(piece,dst.at[q*C+s],rs.at[q*C+s]),
                            rcopy(piece,dst.at[q*C+s],ss.at[i],rs.at[q*C+s],(z,h,2*k+r,s2))))
    return out

def is_home(): return lax.axis_index("core")==lax.div(lax.axis_index("q"),2)

def spread_near(cps, do):
    for rr,mine,loc,cp in cps:
        if rr==0:
            @pl.when(mine)
            def _(loc=loc):
                if do=="start": loc.start()
            @pl.when(jnp.logical_not(mine))
            def _(cp=cp): cp.start() if do=="start" else cp.wait_send()
        else:
            @pl.when(is_home())
            def _(cp=cp): cp.start() if do=="start" else cp.wait_send()

def spread_far(cps, do):
    for rr,mine,loc,cp in cps:
        if rr==1:
            @pl.when(jnp.logical_not(is_home()))
            def _(cp=cp): cp.start() if do=="start" else cp.wait_send()

def near_blocks(C):
    q=lax.axis_index("q")
    return [partner(q,m)*C+t for m in range(3) for t in range(C)]

def far_blocks(C):
    q=lax.axis_index("q")
    return [partner(q,3)*C+t for t in range(C)]

def spread_start(cps):
    for mine,loc,cp in cps:
        @pl.when(mine)
        def _(loc=loc): loc.start()
        @pl.when(jnp.logical_not(mine))
        def _(cp=cp): cp.start()

def spread_sent(cps):
    for mine,loc,cp in cps:
        @pl.when(jnp.logical_not(mine))
        def _(cp=cp): cp.wait_send()

def home_copies(C, n, src, dst, ss, rs):
    z,k,q,s=[lax.axis_index(a) for a in AXES]
    out=[]
    for b in range(4*C):
        to=dst.at[lax.rem(q,2),pl.ds(pl.multiple_of((k*C+s)*n,n),n),:]
        sem=rs.at[(lax.rem(q,2)*2+k)*C+s]
        out.append(((lax.div(q,2)==k)&(q==b//C)&(s==b%C),pltpu.make_async_copy(src.at[b],to,sem),
                    rcopy(src.at[b],to,ss.at[b],sem,(z,lax.div(q,2),b//C,b%C))))
    return out

def home_arrived(C, n, dst, rs):
    for r in range(2):
        for h in range(2):
            for s2 in range(C):
                arrived(dst.at[r,pl.ds((h*C+s2)*n,n),:],rs.at[(r*2+h)*C+s2])

def arrived(ref, sem):
    z,k,q,s=[lax.axis_index(a) for a in AXES]
    rcopy(ref,ref,sem,sem,(z,1-k,q,s)).wait_recv()

def fwd_kernel(Z, C, n, x_ref, w1_ref, w2_ref, cot_ref, gain_ref, pd_ref, seg_ref,
               xo_ref, ain_ref, wts_ref, w2o_ref, mix_ref, qkv_ref, ot_ref, lse_ref, segk_ref, segq_ref, coto_ref,
               xo_scr, ain_scr, wts_scr, qkv_scr, ot_scr, wa_scr, wb_scr, wd_scr, o3_scr, w2_scr, k_scr, s_scr, so_scr,
               tok_s, tok_r, ain_s, ain_r, a_s, a_r, b_s, b_r, dd_s, dd_r, o3_s, o3_r,
               wt_s, wt_r, hf_s, hf_r, w2_s, w2_r, gr_s, gr_r, loc_s, mix_s, mix_r, mixl, sg_s, sg_r, out_s, qo_s, cot_s, cot_r):
    z,k,q,s=[lax.axis_index(a) for a in AXES]
    G=2*C; g0=k*C+s; NB=4*C
    D=gain_ref.shape[1]; L=seg_ref.shape[1]; W=pd_ref.shape[0]; hb=W//HD; nb=L//BQ; nC=3*W
    peers=list(itertools.product(range(2),range(C)))[1:]
    pdev=[(z,lax.rem(k+gc,2),q,lax.rem(s+gs,C)) for gc,gs in peers]
    pidx=[lax.rem(k+gc,2)*C+lax.rem(s+gs,C) for gc,gs in peers]
    back=[gc*C+(C-gs)%C for gc,gs in peers]
    fore=[gc*C+gs for gc,gs in peers]
    chipdev=[(z,k,partner(q,m),s) for m in range(4)]
    toks=spread_copies(C,n,x_ref,xo_scr,tok_s,tok_r)
    cots=spread_copies(C,n,cot_ref,coto_ref,cot_s,cot_r)
    ca=col_copies(Z,w1_ref,wa_scr,a_s,a_r)
    cb=col_copies(Z,w2_ref,wb_scr,b_s,b_r)
    cd=col_copies(Z,o3_scr,wd_scr,dd_s,dd_r)
    o3=rcopy(w2_ref,o3_scr,o3_s,o3_r,chipdev[3])
    wcp=[rcopy(wts_scr.at[0],wts_scr.at[m],wt_s.at[m],wt_r.at[m],chipdev[m]) for m in (1,2)]
    h1=nC//32*16; half=[pl.ds(0,h1),pl.ds(h1,nC-h1)]
    hcp=[rcopy(wts_scr.at[1,half[0]],wts_scr.at[3,half[0]],hf_s.at[0],hf_r.at[0],chipdev[2]),
         rcopy(wts_scr.at[2,half[1]],wts_scr.at[3,half[1]],hf_s.at[1],hf_r.at[1],chipdev[1])]
    save=[pltpu.make_async_copy(xo_scr,xo_ref,out_s.at[0]),pltpu.make_async_copy(ain_scr,ain_ref,out_s.at[1])]
    wsave=[pltpu.make_async_copy(wts_scr.at[m],wts_ref.at[m],out_s.at[2+m]) for m in range(4)]
    def qsave(m): return [pltpu.make_async_copy(qkv_scr.at[m],qkv_ref.at[m],qo_s.at[0,m]),pltpu.make_async_copy(ot_scr.at[:,m],ot_ref.at[:,m],qo_s.at[1,m])]
    w2cp=[rcopy(w2_scr.at[0],w2_scr.at[m],w2_s.at[m],w2_r.at[m],chipdev[m]) for m in (1,2)]
    grp=[[rcopy(w2_scr.at[m],w2o_ref.at[back[i],m],gr_s.at[i,m],gr_r.at[back[i],m],pdev[i]) for i in range(G-1)] for m in range(4)]
    loc=[pltpu.make_async_copy(w2_scr.at[m],w2o_ref.at[0,m],loc_s.at[m]) for m in range(4)]
    def share(m):
        loc[m].start()
        for cp in grp[m]: cp.start()
    sgc=rcopy(seg_ref,so_scr,sg_s,sg_r,(z,1-k,q,s))
    greet(Z,C)
    sgc.start()
    for cp in ca: cp.start()
    spread_near(toks,"start"); spread_far(toks,"start")
    o3.start()
    sgc.wait_recv()
    sg=jnp.where(k==lax.div(q,2),seg_ref[...],so_scr[...])
    sg=jnp.where(lax.rem(q,2)==0,sg[0:1],sg[1:2]).astype(f32)
    segq_ref[...]=sg
    for c in range(L//BQ):
        segk_ref[c*BQ:(c+1)*BQ,:]=jnp.broadcast_to(sg[:,c*BQ:(c+1)*BQ],(128,BQ)).T
    for i in range(2*Z): arrived(wa_scr.at[i],a_r.at[i])
    for cp in cb: cp.start()
    transpose_rows(wa_scr,wts_scr.at[0])
    for cp in wcp: cp.start()
    wsave[0].start()
    ains=[]
    for j in range(NB):
        arrived(xo_scr.at[j],tok_r.at[j])
        x=xo_scr[j].astype(f32)
        inv=lax.rsqrt(jnp.mean(x*x,axis=-1,keepdims=True)+norm_eps)
        slot=j*G+g0
        ain_scr[slot]=(x*inv*gain_ref[...]).astype(bf16)
        for i in range(G-1):
            cp=rcopy(ain_scr.at[slot],ain_scr.at[slot],ain_s.at[i,j],ain_r.at[slot],pdev[i])
            cp.start(); ains.append(cp)
    for j in range(NB):
        for i in range(G-1): arrived(ain_scr.at[j*G+pidx[i]],ain_r.at[j*G+pidx[i]])
    for cp in save: cp.start()
    rowi=lax.broadcasted_iota(jnp.int32,(BQ,BQ),0)
    coli=lax.broadcasted_iota(jnp.int32,(BQ,BQ),1)
    hs=[slice(h*HD,(h+1)*HD) for h in range(hb)]
    CH=512; per=CH//n; sub=BQ//n

    def block(m,_):
        @pl.when(m==1)
        def _():
            for i in range(2*Z): arrived(wb_scr.at[i],b_r.at[i])
            arrived(o3_scr,o3_r)
            for cp in cd: cp.start()
            transpose_rows(wb_scr,w2_scr.at[0])
            for i in (1,2): arrived(wts_scr.at[i],wt_r.at[i])
            for cp in hcp+wsave[1:3]: cp.start()
            share(0)
        @pl.when(m==2)
        def _():
            for cp in w2cp: cp.start()
        @pl.when(m==3)
        def _():
            for i in range(2): arrived(wts_scr.at[3,half[i]],hf_r.at[i])
            wsave[3].start()
            spread_near(cots,"start")
        for c in range(L//CH):
            cs=slice(c*CH,(c+1)*CH)
            r=dot(wts_scr[m],ain_scr[c*per:(c+1)*per].reshape(CH,D),NT)
            qkv_scr[m,:W,cs]=(r[:W]*pd_ref[:,:1]).astype(bf16)
            qkv_scr[m,W:,cs]=r[W:].astype(bf16)
            for h in range(hb):
                k_scr[h,cs,:]=r[W+h*HD:W+(h+1)*HD].T.astype(bf16)
        units=[(i,h) for i in range(nb) for h in range(hb)]
        st={}
        def phase_a(u):
            i,h=units[u]; c0=i*BQ
            qi=qkv_scr[m,hs[h],c0:c0+BQ]
            sq=segq_ref[:,c0:c0+BQ]
            m8=None
            for j in range(i+1):
                t=dot(k_scr[h,j*BQ:(j+1)*BQ,:],qi)
                sk=segk_ref[j*BQ:(j+1)*BQ,:]
                ok=jnp.concatenate([sk]*(BQ//128),axis=1)==sq
                if j==i: ok=ok&(rowi<=coli)
                t=jnp.where(ok,t,NEG)
                s_scr[u%2,j*BQ:(j+1)*BQ,:]=t
                mm=t.reshape(BQ//8,8,BQ).max(0)
                m8=mm if m8 is None else jnp.maximum(m8,mm)
                yield
            st[u]=m8.max(0,keepdims=True)
        def phase_b(u):
            i,h=units[u]; c0=i*BQ
            mx=st[u]; l8=None; acc=None
            for j in range(i+1):
                p=jnp.exp(s_scr[u%2,j*BQ:(j+1)*BQ,:]-mx)
                ll=p.reshape(BQ//8,8,BQ).sum(0)
                l8=ll if l8 is None else l8+ll
                pv=dot(qkv_scr[m,2*W+h*HD:2*W+(h+1)*HD,j*BQ:(j+1)*BQ],p.astype(bf16))
                acc=pv if acc is None else acc+pv
                yield
            l=l8.sum(0,keepdims=True)
            o=(acc*(1.0/l)).astype(bf16)
            for t in range(sub): ot_scr[i*sub+t,m,hs[h],:]=o[:,t*n:(t+1)*n]
            lse_ref[m*hb+h,:,c0:c0+BQ]=mx+jnp.log(l)
        merge(phase_a(0))
        for u in range(len(units)):
            gs=[phase_b(u)]
            if u+1<len(units): gs=[phase_a(u+1)]+gs
            merge(*gs)
        for b in range(NB):
            pltpu.make_async_copy(ot_scr.at[b*G+g0,m],mix_ref.at[b,0,m],mixl.at[b,m]).start()
            for i in range(G-1):
                rcopy(ot_scr.at[b*G+pidx[i],m],mix_ref.at[b,back[i],m],mix_s.at[i,b,m],mix_r.at[back[i],b,m],pdev[i]).start()
        for cp in qsave(m): cp.start()
        return 0
    lax.fori_loop(0,4,block,0)
    for m in (1,2):
        arrived(w2_scr.at[m],w2_r.at[m])
        share(m)
    for i in range(2*Z): arrived(wd_scr.at[i],dd_r.at[i])
    transpose_rows(wd_scr,w2_scr.at[3])
    share(3)
    for i in range(G-1):
        for b in range(NB):
            for m in range(4):
                arrived(mix_ref.at[b,fore[i],m],mix_r.at[fore[i],b,m])
                rcopy(ot_scr.at[b*G+pidx[i],m],mix_ref.at[b,back[i],m],mix_s.at[i,b,m],mix_r.at[back[i],b,m],pdev[i]).wait_send()
        for m in range(4): arrived(w2o_ref.at[fore[i],m],gr_r.at[fore[i],m])
    for m in range(4):
        loc[m].wait()
        for cp in grp[m]: cp.wait_send()
    for cps in (ca,cb,cd):
        for cp in cps[1:]: cp.wait_send()
    for cp in wcp+hcp+w2cp+ains+[o3,sgc]: cp.wait_send()
    spread_near(toks,"sent"); spread_far(toks,"sent"); spread_near(cots,"sent")
    for b in near_blocks(C): arrived(coto_ref.at[b],cot_r.at[b])
    for cp in save+wsave: cp.wait()
    for m in range(4):
        for cp in qsave(m): cp.wait()
        for b in range(NB): pltpu.make_async_copy(ot_scr.at[b*G+g0,m],mix_ref.at[b,0,m],mixl.at[b,m]).wait()

def forward(Z, C, tokens, w1h, w2h, cot, gain, pd, seg):
    R,Pn,D=tokens.shape; G=2*C; n=Pn//G; _,Dd,nC=w1h.shape; NB=4*C
    L=seg.shape[1]; W=pd.shape[0]; hb=W//HD
    V=pl.BlockSpec(memory_space=pltpu.VMEM); A=pl.BlockSpec(memory_space=pl.ANY)
    S=lambda *sh: pltpu.SemaphoreType.DMA(sh) if sh else pltpu.SemaphoreType.DMA
    B=lambda *sh: jax.ShapeDtypeStruct(sh,bf16)
    F=lambda *sh: jax.ShapeDtypeStruct(sh,f32)
    M=lambda *sh: pltpu.VMEM(sh,bf16)
    col=M(2*Z,Dd,nC)
    return pl.pallas_call(functools.partial(fwd_kernel,Z,C,n),
        out_shape=(B(NB,n,D),B(NB*G,n,D),B(4,nC,D),B(G,4,nC,D),B(NB,G,4,W,n),B(4,nC,L),B(NB*G,4,W,n),F(4*hb,1,L),F(L,128),F(1,L),B(NB,n,D)),
        in_specs=[A,A,A,A,V,V,V],out_specs=(A,A,A,A,A,A,A,V,V,V,A),
        scratch_shapes=[M(NB,n,D),M(NB*G,n,D),M(4,nC,D),M(4,nC,L),M(NB*G,4,W,n),col,col,col,M(2,Dd,nC),M(4,nC,D),M(hb,L,HD),
            pltpu.VMEM((2,L,BQ),f32),pltpu.VMEM((R,L),jnp.int32),
            S(NB),S(NB),S(G-1,NB),S(NB*G),S(2*Z),S(2*Z),S(2*Z),S(2*Z),S(2*Z),S(2*Z),S(),S(),
            S(4),S(4),S(2),S(2),S(4),S(4),S(G-1,4),S(G,4),S(4),S(G-1,NB,4),S(G,NB,4),S(NB,4),S(),S(),S(6),S(2,4),S(NB),S(NB)],
        compiler_params=pltpu.CompilerParams(collective_id=0,has_side_effects=True,vmem_limit_bytes=60*2**20),
        cost_estimate=pl.CostEstimate(flops=3*10**10,bytes_accessed=10**8,transcendentals=0),
        name="forward")(tokens,w1h,w2h,cot,gain.reshape(1,D),pd,seg)

def prep_kernel(Ch, wq_ref, wk_ref, wv_ref, wo_ref, wu_ref, wd_ref, qs_ref, w1_ref, w2_ref, pd_ref):
    for ref,three in ((w1_ref,(wq_ref[...],wk_ref[...],wv_ref[...])),(w2_ref,(wo_ref[...],wu_ref[...],wd_ref[...]))):
        for i,w in enumerate(three):
            for h in range(2): ref[h,:,i*Ch:(i+1)*Ch]=w[:,h*Ch:(h+1)*Ch]
    v=qs_ref[...]
    per_dim=scale_base/math.sqrt(HD)*(jnp.maximum(v,0.0)+jnp.log(1.0+jnp.exp(-jnp.abs(v))))
    col=jnp.broadcast_to(per_dim,(128,HD)).T
    for h in range(pd_ref.shape[0]//HD): pd_ref[h*HD:(h+1)*HD,:]=col

def prep(wq, wk, wv, wo, wu, wd, qs):
    Dd,Ct=wq.shape; Ch=Ct//2
    B=jax.ShapeDtypeStruct((2,Dd,3*Ch),bf16)
    return pl.pallas_call(functools.partial(prep_kernel,Ch),out_shape=(B,B,jax.ShapeDtypeStruct((Ch,128),f32)),
        compiler_params=pltpu.CompilerParams(vmem_limit_bytes=60*2**20),name="prep")(wq,wk,wv,wo.T,wu,wd.T,qs.reshape(1,-1))


def mid_kernel(Z, C, n, mixh_ref, w2_ref, xoh_ref, cot_ref, coto_ref, gain_ref,
               bo_ref, bh_ref, do_ref, gm_ref, fb_ref, vec_ref,
               wo_scr, wu_scr, wd_scr, mi_scr, hid_scr, gup_scr, ga_scr, gt_scr, gs_scr, gr_scr, co_scr, up_scr, mid_scr, mix_ref, xo_ref,
               wl, dos, dors, dol, gss, grs, cot_s, cot_r, out_s, fo_s, bos, bors, inl):
    z,k,q,s=[lax.axis_index(a) for a in AXES]
    G=2*C; g0=k*C+s; NB=4*C
    D=gain_ref.shape[1]; K4=wo_scr.shape[0]//G; Ch=K4//4; N=NB*n
    peers=list(itertools.product(range(2),range(C)))[1:]
    pdev=[(z,lax.rem(k+gc,2),q,lax.rem(s+gs,C)) for gc,gs in peers]
    pidx=[lax.rem(k+gc,2)*C+lax.rem(s+gs,C) for gc,gs in peers]
    back=[gc*C+(C-gs)%C for gc,gs in peers]
    fore=[gc*C+gs for gc,gs in peers]
    wcp=[]
    for i,dst in enumerate((wo_scr,wu_scr,wd_scr)):
        wcp.append([pltpu.make_async_copy(w2_ref.at[g,m,pl.ds(i*Ch,Ch),:],dst.at[pl.ds((g*4+m)*Ch,Ch),:],wl.at[i,g,m]) for g in range(G) for m in range(4)])
        for cp in wcp[i]: cp.start()
        if i==0:
            ins=[pltpu.make_async_copy(mixh_ref,mix_ref,inl.at[0]),pltpu.make_async_copy(xoh_ref,xo_ref,inl.at[1])]
            for cp in ins: cp.start()
    cots=spread_copies(C,n,cot_ref,co_scr,cot_s,cot_r)
    greet(Z,C)
    spread_far(cots,"start")
    for b in near_blocks(C): pltpu.make_async_copy(coto_ref.at[b],co_scr.at[b],cot_r.at[b]).start()
    order=[partner(q,m)*C+(lax.rem(s+t,C)) for m in range(4) for t in range(C)]
    outs=[]
    def put(src,dst,sem):
        cp=pltpu.make_async_copy(src,dst,sem); cp.start(); outs.append(cp)
    vec_ref[...]=jnp.zeros_like(vec_ref)
    for cp in wcp[0]+ins: cp.wait()
    def slot(e): return slice(e*n,(e+1)*n)
    def ahead(e):
        b=order[e]
        attn=dot(mix_ref[b].reshape(G*K4,n),wo_scr[...],TN)
        middle=xo_ref[b].astype(f32)+attn
        mid_scr[e]=middle
        inv=lax.rsqrt(jnp.mean(middle*middle,axis=-1,keepdims=True)+norm_eps)
        mi_scr[slot(e),:]=(middle*inv*gain_ref[...]).astype(bf16)
        yield
        if e==0:
            for cp in wcp[1]+wcp[2]: cp.wait()
        up=dot(mi_scr[slot(e),:],wu_scr[...],NT)
        up_scr[e]=up
        hid_scr[slot(e),:]=(up*(1.0/(1.0+jnp.exp(-up)))).astype(bf16)
        yield
        gs_scr[slot(e),:]=(mid_scr[e]+dot(hid_scr[slot(e),:],wd_scr[...])).astype(bf16)
        yield
    for e in range(0,NB,2):
        merge(ahead(e),ahead(e+1))
        for i in (e,e+1): put(gs_scr.at[slot(i)],bo_ref.at[order[i]],out_s.at[0,i])
    exch=[]
    home=[]
    boouts=list(outs); outs=[]
    def behind(e):
        b=order[e]
        gh=dot(co_scr[b],wd_scr[...],NT)
        up=up_scr[e]
        sg=1.0/(1.0+jnp.exp(-up))
        gup_scr[slot(e),:]=(gh*(sg*(1.0+up*(1.0-sg)))).astype(bf16)
        yield
        gmlp=dot(gup_scr[slot(e),:],wu_scr[...])
        middle=mid_scr[e]
        inv=lax.rsqrt(jnp.mean(middle*middle,axis=-1,keepdims=True)+norm_eps)
        n2=middle*inv
        dn=gmlp*gain_ref[...]
        gm=co_scr[b].astype(f32)+inv*(dn-n2*jnp.mean(dn*n2,axis=-1,keepdims=True))
        vec_ref[...]+=(gmlp*n2).reshape(n//8,8,D).sum(0)
        mid_scr[e]=gm
        ga_scr[slot(e),:]=gm.astype(bf16)
        yield
        gt_scr[e]=dot(wo_scr[...],ga_scr[slot(e),:],NT).astype(bf16).reshape(G,4,Ch,n)
        yield
    for e0 in range(0,NB,2):
        for e in (e0,e0+1):
            b=order[e]
            if e<3*C: pltpu.make_async_copy(coto_ref.at[b],co_scr.at[b],cot_r.at[b]).wait()
            else: arrived(co_scr.at[b],cot_r.at[b])
            boouts[e].wait()
            dst=bh_ref.at[lax.rem(q,2),pl.ds(pl.multiple_of((k*C+s)*n,n),n),:]
            rs=bors.at[(lax.rem(q,2)*2+k)*C+s]
            mine=is_home()&(b==q*C+s)
            home.append((mine,pltpu.make_async_copy(bo_ref.at[b],dst,rs),rcopy(bo_ref.at[b],dst,bos.at[e],rs,(z,lax.div(q,2),lax.div(b,C),lax.rem(b,C)))))
            spread_start(home[-1:])
        merge(behind(e0),behind(e0+1))
        for e in (e0,e0+1):
            b=order[e]
            put(mid_scr.at[e],gm_ref.at[b],out_s.at[1,e])
            lc=pltpu.make_async_copy(gt_scr.at[e,0],do_ref.at[b*G+g0],dol.at[e])
            lc.start(); exch.append(lc)
            for i in range(G-1):
                cp=rcopy(gt_scr.at[e,fore[i]],do_ref.at[b*G+g0],dos.at[i,e],dors.at[b*G+g0],pdev[i])
                cp.start(); exch.append(cp)
    def wgrad(i,g):
        cs=slice(g*K4,(g+1)*K4)
        if i==0: return dot(jnp.concatenate([mix_ref[b,g].reshape(K4,n) for b in order],1),ga_scr[...])
        if i==1: return dot(gup_scr[:,cs],mi_scr[...],TN)
        return dot(hid_scr[:,cs],jnp.concatenate([co_scr[b] for b in order],0),TN)
    for cp in outs: cp.wait()
    outs=[]
    def part(j,i): return pl.ds((j*3+i)*K4,K4)
    gcp=[[None]*3 for j in range(G-1)]
    for j in range(G-1):
        for i in range(3):
            gs_scr[part(j,i),:]=wgrad(i,fore[j]).astype(bf16)
            gcp[j][i]=rcopy(gs_scr.at[part(j,i)],gr_scr.at[back[j]-1,i],gss.at[j,i],grs.at[back[j]-1,i],pdev[j])
            gcp[j][i].start()
    for i in range(3):
        t=wgrad(i,0)
        for j in range(G-1):
            arrived(gr_scr.at[fore[j]-1,i],grs.at[fore[j]-1,i])
            t=t+gr_scr[fore[j]-1,i].astype(f32)
        gcp[0][i].wait_send()
        gs_scr[part(0,i),:]=t.astype(bf16)
        for m in range(4):
            put(gs_scr.at[pl.ds(i*K4+m*Ch,Ch)],fb_ref.at[m,pl.ds(i*Ch,Ch)],fo_s.at[i,m])
    for b in range(NB):
        for i in range(G-1): arrived(do_ref.at[b*G+pidx[i]],dors.at[b*G+pidx[i]])
    for i,cp in enumerate(exch):
        if i%G==0: cp.wait()
        else: cp.wait_send()
    for cps in gcp[1:]:
        for cp in cps: cp.wait_send()
    spread_far(cots,"sent")
    home_arrived(C,n,bh_ref,bors)
    spread_sent(home)
    for cp in outs: cp.wait()

def middle(Z, C, mix, w2o, xo, cot, coto, gain):
    NB,n,D=xo.shape; G=2*C; nC=w2o.shape[2]; Ch=nC//3; K4=4*Ch; N=NB*n
    V=pl.BlockSpec(memory_space=pltpu.VMEM); A=pl.BlockSpec(memory_space=pl.ANY)
    S=lambda *sh: pltpu.SemaphoreType.DMA(sh)
    M=lambda *sh: pltpu.VMEM(sh,bf16)
    B=lambda *sh: jax.ShapeDtypeStruct(sh,bf16)
    return pl.pallas_call(functools.partial(mid_kernel,Z,C,n),
        out_shape=(B(NB,n,D),B(*cot.shape),B(NB*G,4,Ch,n),jax.ShapeDtypeStruct((NB,n,D),f32),B(4,nC,D),jax.ShapeDtypeStruct((8,D),f32)),
        in_specs=[A,A,A,A,A,V],out_specs=(A,A,A,A,A,V),
        scratch_shapes=[M(G*K4,D)]*3+[M(N,G*K4) if i in (1,2) else M(N,D) for i in range(4)]+[M(NB,G,4,Ch,n),M((G-1)*3*K4,D),M(G-1,3,K4,D),M(NB,n,D),pltpu.VMEM((NB,n,G*K4),f32),pltpu.VMEM((NB,n,D),f32),M(NB,G,4,Ch,n),M(NB,n,D),
            S(3,G,4),S(G-1,NB),S(NB*G),S(NB),S(G-1,3),S(G-1,3),S(NB),S(NB),S(2,NB),S(3,4),S(NB),S(4*C),S(2)],
        compiler_params=pltpu.CompilerParams(collective_id=2,has_side_effects=True,vmem_limit_bytes=60*2**20),
        cost_estimate=pl.CostEstimate(flops=3*10**10,bytes_accessed=10**8,transcendentals=0),
        name="middle")(mix,w2o,xo,cot,coto,gain.reshape(1,D))

def bwd_kernel(Z, C, n, qkv_ref, ot_ref, do_ref, lse_ref, pd_ref, segk_ref, segq_ref, ain_ref, wts_ref,
               xo_ref, gmid_ref, gain_ref, vec_ref, fb_ref,
               gi_ref, gwm_ref, gwq_ref, vo_ref,
               kv_scr, k_scr, v_scr, p_scr, ds_scr, dq_scr, dl_scr, a_scr, dw_scr, qr_scr, big_scr, zs_scr, zr_scr, t3_scr, t3r_scr, tb_scr, ot_scr, do_scr,
               dxr_scr, wx_scr, own_scr, xb_scr, gb_scr, va_scr, vb_scr, vs_scr, sc_scr,
               fs, frs, qs, qrs, zss, zrs, t3s, t3rs, cs_, crs, dxs, dxrs, gis, girs, ld, al, otl, dol, kvl, wtl, xl, vas, vars_, vbs, vbrs):
    z,k,q,s=[lax.axis_index(a) for a in AXES]
    G=2*C; g0=k*C+s; NB=4*C
    D=gain_ref.shape[1]; L=segq_ref.shape[1]; W=pd_ref.shape[0]; hb=W//HD; nb=L//BQ; sub=BQ//n
    nC=3*W; Dd=gwm_ref.shape[1]
    peers=list(itertools.product(range(2),range(C)))[1:]
    pdev=[(z,lax.rem(k+gc,2),q,lax.rem(s+gs,C)) for gc,gs in peers]
    pidx=[lax.rem(k+gc,2)*C+lax.rem(s+gs,C) for gc,gs in peers]
    back=[gc*C+(C-gs)%C for gc,gs in peers]
    fore=[gc*C+gs for gc,gs in peers]
    chipdev=[(z,k,partner(q,m),s) for m in range(4)]
    core=(z,1-k,q,s)
    zdev=[lax.rem(z+j,Z) for j in range(Z)]
    def frow(m): return big_scr.at[pl.ds((m-1)*nC,nC)]
    def dxat(i,e): return big_scr.at[pl.ds((i*NB+e)*n,n)]
    fcp={m: rcopy(fb_ref.at[m],frow(m),fs.at[m],frs.at[m],chipdev[m]) for m in (1,2)}
    qcp={m: rcopy(dw_scr.at[m-1],qr_scr.at[m-1],qs.at[m],qrs.at[m],chipdev[m]) for m in (1,2)}
    slot_of=(0,1,0,0)
    zcp=[[rcopy(zs_scr.at[slot_of[e],zdev[j]],zr_scr.at[e%3,z],zss.at[e,j],zrs.at[e,z],(zdev[j],k,q,s)) for j in range(1,Z)] for e in range(4)]
    t3cp=[rcopy(tb_scr,t3r_scr.at[e],t3s.at[e],t3rs.at[e],chipdev[3]) for e in range(2)]
    gws=(gwm_ref,gwq_ref)
    ccp=[rcopy(t3_scr.at[pl.ds(pl.multiple_of((1-k)*Dd,Dd),Dd),:],gws[e].at[k],cs_.at[e],crs.at[e],core) for e in range(2)]
    def wcopy(m): return pltpu.make_async_copy(wts_ref.at[m],(dw_scr.at[m] if m<2 else wx_scr.at[m-2]),wtl.at[m])
    def load(src,dst,i):
        cp=pltpu.make_async_copy(src,dst,ld.at[i]); cp.start(); return cp
    def zsend(e, value):
        rows=D//Z; per=max(1,640//rows)
        for i in range(Z//per):
            ls=slice(i*per*rows,(i+1)*per*rows)
            zs_scr[slot_of[e],i*per:(i+1)*per]=value(ls).T.reshape(per,rows,nC).astype(bf16)
        for cp in zcp[e]: cp.start()
    def zsum(e):
        for cp in zcp[e]: cp.wait_send()
        t=zs_scr[slot_of[e],z].astype(f32)
        for j in range(1,Z):
            arrived(zr_scr.at[e%3,zdev[j]],zrs.at[e,zdev[j]])
            t=t+zr_scr[e%3,zdev[j]].astype(f32)
        return t
    def diag(e):
        tb_scr[...]=zsum(e).astype(bf16)
        t3cp[e].start()
    def final(e):
        t=zsum(2+e)
        arrived(t3r_scr.at[e],t3rs.at[e])
        t=t+t3r_scr[e].astype(f32)
        t3cp[e].wait_send()
        if e==1: ccp[0].wait_send()
        t3_scr[...]=t
        ccp[e].start()
        gws[e][k]=t3_scr[pl.ds(pl.multiple_of(k*Dd,Dd),Dd),:]
    first=load(fb_ref.at[3],dw_scr.at[0],0)
    kvcp=[pltpu.make_async_copy(qkv_ref.at[m],kv_scr.at[m],kvl.at[m]) for m in range(4)]
    kvcp[1].start()
    acp=pltpu.make_async_copy(ain_ref,a_scr,al)
    def otcp(m): return pltpu.make_async_copy(ot_ref.at[:,m],ot_scr,otl)
    otcp(1).start()
    def docp(idx): return pltpu.make_async_copy(do_ref.at[:,lax.rem(idx+1,4)],do_scr.at[lax.rem(idx,2)],dol.at[lax.rem(idx,2)])
    docp(0).start()
    greet(Z,C)
    for m in (1,2): fcp[m].start()
    first.wait()
    zsend(0,lambda ls: dw_scr[0,:,ls].astype(f32))
    ld0=load(fb_ref.at[0],dw_scr.at[1],1)
    acp.start()
    for m in (2,3,0): kvcp[m].start()
    sc_scr[...]=jnp.zeros_like(sc_scr)
    rowi=lax.broadcasted_iota(jnp.int32,(BQ,BQ),0)
    coli=lax.broadcasted_iota(jnp.int32,(BQ,BQ),1)
    hs=[slice(h*HD,(h+1)*HD) for h in range(hb)]

    def block(idx,_):
        m=lax.rem(idx+1,4)
        pltpu.make_async_copy(qkv_ref.at[m],kv_scr.at[m],kvl.at[m]).wait()
        for h in range(hb):
            k_scr[h]=kv_scr[m,W+h*HD:W+(h+1)*HD,:].T
            v_scr[h]=kv_scr[m,2*W+h*HD:2*W+(h+1)*HD,:].T
        slot=lax.rem(idx,2)
        docp(idx).wait()
        @pl.when(idx<3)
        def _(): docp(idx+1).start()
        def tile(h,i):
            return jnp.concatenate([do_scr[slot,i*sub+t,hs[h],:] for t in range(sub)],1) if sub>1 else do_scr[slot,i,hs[h],:]
        otcp(m).wait()
        for i in range(nb):
            for h in range(hb):
                for t in range(sub):
                    B_=i*sub+t
                    dl_scr[h,:,B_*n:(B_+1)*n]=(do_scr[slot,B_,hs[h],:].astype(f32)*ot_scr[B_,hs[h],:].astype(f32)).sum(0,keepdims=True)
        @pl.when(idx<3)
        def _(): otcp(lax.rem(idx+2,4)).start()
        rows=[(j,h) for j in range(nb) for h in range(hb)]
        def phase_a(r):
            j,h=rows[r]; ks=slice(j*BQ,(j+1)*BQ)
            for i in range(j,nb):
                cs=slice(i*BQ,(i+1)*BQ)
                t=dot(k_scr[h,ks,:],kv_scr[m,hs[h],cs])
                dp=dot(v_scr[h,ks,:],tile(h,i))
                sk=segk_ref[ks,:]
                ok=jnp.concatenate([sk]*(BQ//128),axis=1)==segq_ref[:,cs]
                if j==i: ok=ok&(rowi<=coli)
                p=jnp.exp(jnp.where(ok,t-lse_ref[m*hb+h,:,cs],NEG))
                p_scr[r%2,:,cs]=p.astype(bf16)
                ds_scr[r%2,:,cs]=(p*(dp-dl_scr[h,:,cs])).astype(bf16)
                yield
        def phase_b(r):
            j,h=rows[r]; js=slice(j*BQ,(j+1)*BQ); rs=slice(j*BQ,L)
            dos=jnp.concatenate([tile(h,i) for i in range(j,nb)],1)
            dv=dot(dos,p_scr[r%2,:,rs],NT)
            yield
            dk=dot(kv_scr[m,hs[h],rs],ds_scr[r%2,:,rs],NT)
            yield
            for i in range(j,nb):
                cs=slice(i*BQ,(i+1)*BQ)
                dq=dot(kv_scr[m,W+h*HD:W+(h+1)*HD,js],ds_scr[r%2,:,cs])
                if j==0: dq_scr[hs[h],cs]=dq
                else: dq_scr[hs[h],cs]+=dq
                yield
            kv_scr[m,W+h*HD:W+(h+1)*HD,js]=dk.astype(bf16)
            kv_scr[m,2*W+h*HD:2*W+(h+1)*HD,js]=dv.astype(bf16)
        def attend(part):
            merge(phase_a(part[0]))
            for u in part:
                gs=[phase_b(u)]
                if u+1<=part[-1]: gs=[phase_a(u+1)]+gs
                merge(*gs)
        attend(range(2*hb))
        @pl.when(idx==1)
        def _():
            diag(0)
            for m2 in (1,2): arrived(frow(m2),frs.at[m2])
            ld0.wait()
            zsend(2,lambda ls: dw_scr[1,:,ls].astype(f32)+big_scr[0:nC,ls].astype(f32)+big_scr[nC:2*nC,ls].astype(f32))
        @pl.when(idx==3)
        def _():
            final(0)
            for m2 in (1,2): qcp[m2].wait_send()
            for m2 in range(4): wcopy(m2).start()
        attend(range(2*hb,len(rows)))
        dq=dq_scr[...]
        sc_scr[...]+=(dq*kv_scr[m,:W,:].astype(f32)).sum(1,keepdims=True)/pd_ref[:,:1]
        kv_scr[m,:W,:]=(dq*pd_ref[:,:1]).astype(bf16)
        @pl.when(idx==0)
        def _(): acp.wait()
        @pl.when(idx<2)
        def _():
            for c in range(D//256):
                ls=slice(c*256,(c+1)*256)
                dw_scr[m-1,:,ls]=dwt(m,ls).astype(bf16)
        @pl.when(idx==0)
        def _():
            qcp[1].start()
        @pl.when(idx==1)
        def _(): qcp[2].start()
        @pl.when(idx==2)
        def _(): zsend(1,lambda ls: dwt(3,ls))
        return 0
    def dwt(m,ls):
        return dot(kv_scr[m],a_scr[:,ls])
    lax.fori_loop(0,4,block,0)
    for m in range(4): wcopy(m).wait()

    def chunk(i):
        gl=kv_scr[:,:,pl.ds(pl.multiple_of(i*BQ,BQ),BQ)].reshape(4*nC,BQ)
        return dot(gl,jnp.concatenate([dw_scr[...].reshape(2*nC,D),wx_scr[...].reshape(2*nC,D)],0),TN)
    order=[partner(q,m)*C+t for m in (3,1,2,0) for t in range(C)]
    def xload(e):
        b=order[e]
        return [pltpu.make_async_copy(xo_ref.at[b],xb_scr.at[0],xl.at[0,0]),pltpu.make_async_copy(gmid_ref.at[b],gb_scr.at[0],xl.at[1,0])]
    dxcp=[[rcopy(dxat(i,e),dxr_scr.at[back[i]-1,e],dxs.at[i,e],dxrs.at[back[i],e],pdev[i]) for e in range(NB)] for i in range(G-1)]
    def give(e):
        b=order[e]
        if sub>1: own_scr[...]=chunk(b)
        for i in range(G-1):
            if sub==1: big_scr[(i*NB+e)*n:(i*NB+e+1)*n,:]=chunk(b*G+pidx[i]).astype(bf16)
            else: big_scr[(i*NB+e)*n:(i*NB+e+1)*n,:]=own_scr[pl.ds(pl.multiple_of(pidx[i]*n,n),n),:].astype(bf16)
            dxcp[i][e].start()
    gicp=[]
    gparts=[]
    def take(e):
        b=order[e]
        for cp in xload(e): cp.start()
        if sub==1:
            gain=chunk(b*G+g0)
        else:
            own_scr[...]=chunk(b)
            gain=own_scr[pl.ds(pl.multiple_of(g0*n,n),n),:]
        for i in range(G-1):
            arrived(dxr_scr.at[fore[i]-1,e],dxrs.at[fore[i],e])
            gain=gain+dxr_scr[fore[i]-1,e].astype(f32)
        for cp in xload(e): cp.wait()
        x=xb_scr[0].astype(f32)
        inv=lax.rsqrt(jnp.mean(x*x,axis=-1,keepdims=True)+norm_eps)
        nx=x*inv
        dn=gain*gain_ref[...]
        gin=gb_scr[0]+inv*(dn-nx*jnp.mean(dn*nx,axis=-1,keepdims=True))
        gparts.append((gain*nx).reshape(n//8,8,D).sum(0))
        dxcp[0][e].wait_send()
        big_scr[e*n:(e+1)*n,:]=gin.astype(bf16)
        dst=gi_ref.at[lax.rem(q,2),pl.ds(pl.multiple_of((k*C+s)*n,n),n),:]
        rs=girs.at[(lax.rem(q,2)*2+k)*C+s]
        gicp.append((is_home()&(b==q*C+s),pltpu.make_async_copy(dxat(0,e),dst,rs),
                     rcopy(dxat(0,e),dst,gis.at[e],rs,(z,lax.div(q,2),lax.div(b,C),lax.rem(b,C)))))
        spread_start(gicp[-1:])
    give(0)
    for e in range(NB):
        if e+1<NB: give(e+1)
        take(e)
        if e==0:
            for m2 in (1,2): arrived(qr_scr.at[m2-1],qrs.at[m2])
            zsend(3,lambda ls: dwt(0,ls)+qr_scr[0,:,ls].astype(f32)+qr_scr[1,:,ls].astype(f32))
            diag(1)
    gpart=gparts[0]
    for t in gparts[1:]: gpart=gpart+t
    vs_scr[...]=jnp.zeros_like(vs_scr)
    vs_scr[0:1,:]=gpart.sum(0,keepdims=True)
    vs_scr[1:2,:]=vec_ref[...].sum(0,keepdims=True)
    sc=sc_scr[0:HD,:]
    for h in range(1,hb): sc=sc+sc_scr[h*HD:(h+1)*HD,:]
    vs_scr[2:3,0:HD]=sc.T[0:1,:]
    me=(k*4+q)*C+s
    va_scr[me]=vs_scr[...]
    plane=list(itertools.product(range(2),range(4),range(C)))[1:]
    vacp=[rcopy(vs_scr,va_scr.at[me],vas.at[i],vars_.at[me],(z,lax.rem(k+a,2),lax.rem(q+b,4),lax.rem(s+c,C))) for i,(a,b,c) in enumerate(plane)]
    for cp in vacp: cp.start()
    for a,b,c in plane:
        o=(lax.rem(k+a,2)*4+lax.rem(q+b,4))*C+lax.rem(s+c,C)
        arrived(va_scr.at[o],vars_.at[o])
    t=va_scr[0]
    for i in range(1,8*C): t=t+va_scr[i]
    vb_scr[z]=t
    vbcp=[rcopy(vb_scr.at[z],vb_scr.at[z],vbs.at[j],vbrs.at[z],(zdev[j],k,q,s)) for j in range(1,Z)]
    for cp in vbcp: cp.start()
    final(1)
    for j in range(1,Z): arrived(vb_scr.at[zdev[j]],vbrs.at[zdev[j]])
    t=vb_scr[0]
    for i in range(1,Z): t=t+vb_scr[i]
    vo_ref[...]=t
    for e in range(2):
        arrived(gws[e].at[1-k],crs.at[e])
        if e==1: ccp[e].wait_send()
    home_arrived(C,n,gi_ref,girs)
    spread_sent(gicp)
    for i in range(1,G-1):
        for e in range(NB): dxcp[i][e].wait_send()
    for m in (1,2):
        fcp[m].wait_send()
    for cp in vacp+vbcp: cp.wait_send()

def backward(Z, C, qkv, ot, do, lse, pd, segk, segq, ain, wts, xo, gmid, gain, vec, fb, R, Pn, Dd):
    NB,n,D=xo.shape; G=2*C; nC=wts.shape[1]; W=pd.shape[0]; hb=W//HD; L=segq.shape[1]
    V=pl.BlockSpec(memory_space=pltpu.VMEM); A=pl.BlockSpec(memory_space=pl.ANY)
    S=lambda *sh: pltpu.SemaphoreType.DMA(sh) if sh else pltpu.SemaphoreType.DMA
    M=lambda *sh: pltpu.VMEM(sh,bf16)
    F=lambda *sh: pltpu.VMEM(sh,f32)
    gw=jax.ShapeDtypeStruct((2,Dd,nC),f32)
    return pl.pallas_call(functools.partial(bwd_kernel,Z,C,n),
        out_shape=(jax.ShapeDtypeStruct((R,Pn,D),bf16),gw,gw,jax.ShapeDtypeStruct((8,D),f32)),
        in_specs=[A,A,A,V,V,V,V,A,A,A,A,V,V,A],out_specs=(A,V,V,V),
        scratch_shapes=[M(4,nC,L),M(hb,L,HD),M(hb,L,HD),M(2,BQ,L),M(2,BQ,L),F(W,L),F(hb,1,L),M(L,D),
            M(2,nC,D),M(2,nC,D),M(max(2*nC,(G-1)*NB*n),D),M(2,Z,D//Z,nC),M(3,Z,D//Z,nC),F(D//Z,nC),M(2,D//Z,nC),M(D//Z,nC),M(NB*G,W,n),M(2,NB*G,W,n),
            M(G-1,NB,n,D),M(2,nC,D),F(BQ,D) if n<BQ else F(8,128),M(1,n,D),F(1,n,D),F(8*C,8,D),F(Z,8,D),F(8,D),F(W,1),
            S(4),S(4),S(4),S(4),S(4,Z),S(4,Z),S(2),S(2),S(2),S(2),S(G,NB),S(G,NB),S(NB),S(4*C),S(4),S(),S(),S(2),S(4),S(4),S(2,2),S(8*C),S(8*C),S(Z),S(Z)],
        compiler_params=pltpu.CompilerParams(collective_id=1,has_side_effects=True,vmem_limit_bytes=61*2**20),
        cost_estimate=pl.CostEstimate(flops=6*10**10,bytes_accessed=10**8,transcendentals=0),
        name="backward")(qkv,ot,do,lse,pd,segk,segq,ain.reshape(L,D),wts,xo,gmid,gain.reshape(1,D),vec,fb)

def finish_kernel(Ch, gi_ref, gwm_ref, gwq_ref, vo_ref, sf_ref, ig_ref, gq_ref, gk_ref, gv_ref, go_ref, gu_ref, gd_ref, ga_ref, gs_ref, gm_ref):
    ig_ref[...]=gi_ref[...].astype(f32)
    @pl.when(pl.program_id(0)==0)
    def _():
        def cols(ref,i):
            return jnp.concatenate([ref[0,:,i*Ch:(i+1)*Ch],ref[1,:,i*Ch:(i+1)*Ch]],1)
        for i,o in enumerate((gq_ref,gk_ref,gv_ref)): o[...]=cols(gwq_ref,i)
        go_ref[...]=cols(gwm_ref,0)
        gu_ref[...]=cols(gwm_ref,1)
        gd_ref[...]=cols(gwm_ref,2)
        ga_ref[...]=vo_ref[0,:]
        gm_ref[...]=vo_ref[1,:]
        gs_ref[...]=vo_ref[2,0:HD]*sf_ref[0,:]

def finish(gi, gwm, gwq, vo, sf):
    R,Pn,D=gi.shape; _,Dd,nC=gwm.shape; Ch=nC//3; T=4
    F=lambda *sh: jax.ShapeDtypeStruct(sh,f32)
    full=lambda *sh: pl.BlockSpec(sh,lambda i: (0,)*len(sh))
    row=pl.BlockSpec((R,Pn//T,D),lambda i:(0,i,0))
    shapes=[(Dd,2*Ch)]*6+[(D,),(HD,),(D,)]
    return pl.pallas_call(functools.partial(finish_kernel,Ch),grid=(T,),
        out_shape=(F(R,Pn,D),)+tuple(F(*sh) for sh in shapes),
        in_specs=[row,full(2,Dd,nC),full(2,Dd,nC),full(8,D),full(1,HD)],
        out_specs=(row,)+tuple(full(*sh) for sh in shapes),
        compiler_params=pltpu.CompilerParams(vmem_limit_bytes=60*2**20),
        name="finish")(gi,gwm,gwq,vo,sf.reshape(1,HD))


def make_local(Z, C):
    def local(tokens, segments, attn_gain, w_query, w_key, w_value, w_out, query_scale, mlp_gain, w_up, w_down, cotangent):
        R,Pn,D=tokens.shape
        Dd=w_query.shape[0]

        w1h,w2h,pd=prep(w_query,w_key,w_value,w_out,w_up,w_down,query_scale)
        xo,ain,wts,w2o,mix,qkv,ot,lse,segk,segq,coto=forward(Z,C,tokens,w1h,w2h,cotangent,attn_gain,pd,segments)
        _,block_out,do,gmid,fb,vec=middle(Z,C,mix,w2o,xo,cotangent,coto,mlp_gain)
        gi,gwm,gwq,vo=backward(Z,C,qkv,ot,do,lse,pd,segk,segq,ain,wts,xo,gmid,attn_gain,vec,fb,R,Pn,Dd)
        sf=(scale_base/math.sqrt(HD))*jax.nn.sigmoid(query_scale)
        ig,gq,gk,gv,go,gu,gd,ga,gs,gm=finish(gi,gwm,gwq,vo,sf)
        return (block_out,ig,ga,gq,gk,gv,go.T,gs,gm,gu,gd.T)
    return local

def solution(mesh):
    dp,T=mesh.shape["dp"],mesh.shape["tensor"]
    Z,C=dp//2,T//4
    fine=Mesh(mesh.devices.reshape(Z,2,4,C),AXES)
    dpx=("zz","core"); tx=("q","s")
    in_specs=(P(dpx,tx,None),P(dpx,None),P(),P(dpx,tx),P(dpx,tx),P(dpx,tx),P(tx,dpx),P(),P(),P(dpx,tx),P(tx,dpx),P(dpx,tx,None))
    out_specs=(P(dpx,tx,None),P(dpx,tx,None),P(),P(dpx,tx),P(dpx,tx),P(dpx,tx),P(tx,dpx),P(),P(),P(dpx,tx),P(tx,dpx))
    return jax.shard_map(make_local(Z,C),mesh=fine,in_specs=in_specs,out_specs=out_specs,check_vma=False)
```

```python
import functools
import itertools
import math
import jax, jax.numpy as jnp
from jax import lax
from jax.experimental import pallas as pl
from jax.experimental.pallas import tpu as pltpu
from jax.sharding import Mesh, PartitionSpec as P

AXES=("zz","core","q","s")
norm_eps = 1e-06
HD=80
BQ=256
NEG=-1e30
f32=jnp.float32; bf16=jnp.bfloat16
NT=(((1,),(1,)),((),()))
NN=(((1,),(0,)),((),()))
TN=(((0,),(0,)),((),()))
def dot(a,b,dims=NN): return lax.dot_general(a,b,dims,preferred_element_type=f32)

def merge(*gens):
    gens=list(gens)
    while gens:
        for g in list(gens):
            try: next(g)
            except StopIteration: gens.remove(g)


MESH=pl.DeviceIdType.MESH
scale_base = 1.442695041

def rcopy(src,dst,ss,rs,dev):
    return pltpu.make_async_remote_copy(src_ref=src,dst_ref=dst,send_sem=ss,recv_sem=rs,device_id=dev,device_id_type=MESH)

def transpose_rows(src, dst):
    P_,rows,cols=src.shape
    per=max(1,640//rows)
    for i in range(P_//per):
        dst[:,i*per*rows:(i+1)*per*rows]=src[i*per:(i+1)*per].reshape(per*rows,cols).T

def partner(q, m):
    return (q,q+1-2*lax.rem(q,2),lax.rem(q+2,4),3-q)[m]

def greet(Z, C):
    z,k,q,s=[lax.axis_index(a) for a in AXES]
    bar=pltpu.get_barrier_semaphore()
    plane=list(itertools.product(range(2),range(4),range(C)))[1:]
    column=[(j,a) for j in range(1,Z) for a in range(2)]
    for a,b,c in plane:
        pl.semaphore_signal(bar,inc=1,device_id=(z,lax.rem(k+a,2),lax.rem(q+b,4),lax.rem(s+c,C)),device_id_type=MESH)
    for j,a in column:
        pl.semaphore_signal(bar,inc=1,device_id=(lax.rem(z+j,Z),lax.rem(k+a,2),q,s),device_id_type=MESH)
    pl.semaphore_wait(bar,len(plane)+len(column))

def col_copies(Z, src, dst, ss, rs):
    z,k,q,s=[lax.axis_index(a) for a in AXES]
    out=[]
    for j in range(Z):
        for a in range(2):
            kk=lax.rem(k+a,2)
            if j==0 and a==0: out.append(pltpu.make_async_copy(src.at[k],dst.at[2*z+k],rs.at[2*z+k]))
            else: out.append(rcopy(src.at[kk],dst.at[2*z+k],ss.at[j*2+a],rs.at[2*z+k],(lax.rem(z+j,Z),kk,q,s)))
    return out

def spread_copies(C, n, src, dst, ss, rs):
    z,k,q,s=[lax.axis_index(a) for a in AXES]
    out=[]
    for rr in range(2):
        r=lax.rem(q+rr,2)
        for h in range(2):
            for s2 in range(C):
                i=(rr*2+h)*C+s2
                piece=src.at[r,pl.ds((h*C+s2)*n,n),:]
                out.append((rr,(k==h)&(q==2*k+r)&(s==s2),pltpu.make_async_copy(piece,dst.at[q*C+s],rs.at[q*C+s]),
                            rcopy(piece,dst.at[q*C+s],ss.at[i],rs.at[q*C+s],(z,h,2*k+r,s2))))
    return out

def is_home(): return lax.axis_index("core")==lax.div(lax.axis_index("q"),2)

def spread_near(cps, do):
    for rr,mine,loc,cp in cps:
        if rr==0:
            @pl.when(mine)
            def _(loc=loc):
                if do=="start": loc.start()
            @pl.when(jnp.logical_not(mine))
            def _(cp=cp): cp.start() if do=="start" else cp.wait_send()
        else:
            @pl.when(is_home())
            def _(cp=cp): cp.start() if do=="start" else cp.wait_send()

def spread_far(cps, do):
    for rr,mine,loc,cp in cps:
        if rr==1:
            @pl.when(jnp.logical_not(is_home()))
            def _(cp=cp): cp.start() if do=="start" else cp.wait_send()

def near_blocks(C):
    q=lax.axis_index("q")
    return [partner(q,m)*C+t for m in range(3) for t in range(C)]

def far_blocks(C):
    q=lax.axis_index("q")
    return [partner(q,3)*C+t for t in range(C)]

def spread_start(cps):
    for mine,loc,cp in cps:
        @pl.when(mine)
        def _(loc=loc): loc.start()
        @pl.when(jnp.logical_not(mine))
        def _(cp=cp): cp.start()

def spread_sent(cps):
    for mine,loc,cp in cps:
        @pl.when(jnp.logical_not(mine))
        def _(cp=cp): cp.wait_send()

def home_copies(C, n, src, dst, ss, rs):
    z,k,q,s=[lax.axis_index(a) for a in AXES]
    out=[]
    for b in range(4*C):
        to=dst.at[lax.rem(q,2),pl.ds(pl.multiple_of((k*C+s)*n,n),n),:]
        sem=rs.at[(lax.rem(q,2)*2+k)*C+s]
        out.append(((lax.div(q,2)==k)&(q==b//C)&(s==b%C),pltpu.make_async_copy(src.at[b],to,sem),
                    rcopy(src.at[b],to,ss.at[b],sem,(z,lax.div(q,2),b//C,b%C))))
    return out

def home_arrived(C, n, dst, rs):
    for r in range(2):
        for h in range(2):
            for s2 in range(C):
                arrived(dst.at[r,pl.ds((h*C+s2)*n,n),:],rs.at[(r*2+h)*C+s2])

def arrived(ref, sem):
    z,k,q,s=[lax.axis_index(a) for a in AXES]
    rcopy(ref,ref,sem,sem,(z,1-k,q,s)).wait_recv()

def fwd_kernel(Z, C, n, x_ref, w1_ref, w2_ref, cot_ref, gain_ref, pd_ref, seg_ref,
               xo_ref, ain_ref, wts_ref, w2o_ref, mix_ref, qkv_ref, ot_ref, lse_ref, segk_ref, segq_ref, coto_ref,
               xo_scr, ain_scr, wts_scr, qkv_scr, ot_scr, wa_scr, wb_scr, wd_scr, o3_scr, w2_scr, k_scr, s_scr, so_scr,
               tok_s, tok_r, ain_s, ain_r, a_s, a_r, b_s, b_r, dd_s, dd_r, o3_s, o3_r,
               wt_s, wt_r, hf_s, hf_r, w2_s, w2_r, gr_s, gr_r, loc_s, mix_s, mix_r, mixl, sg_s, sg_r, out_s, qo_s, cot_s, cot_r):
    z,k,q,s=[lax.axis_index(a) for a in AXES]
    G=2*C; g0=k*C+s; NB=4*C
    D=gain_ref.shape[1]; L=seg_ref.shape[1]; W=pd_ref.shape[0]; hb=W//HD; nb=L//BQ; nC=3*W
    peers=list(itertools.product(range(2),range(C)))[1:]
    pdev=[(z,lax.rem(k+gc,2),q,lax.rem(s+gs,C)) for gc,gs in peers]
    pidx=[lax.rem(k+gc,2)*C+lax.rem(s+gs,C) for gc,gs in peers]
    back=[gc*C+(C-gs)%C for gc,gs in peers]
    fore=[gc*C+gs for gc,gs in peers]
    chipdev=[(z,k,partner(q,m),s) for m in range(4)]
    toks=spread_copies(C,n,x_ref,xo_scr,tok_s,tok_r)
    cots=spread_copies(C,n,cot_ref,coto_ref,cot_s,cot_r)
    ca=col_copies(Z,w1_ref,wa_scr,a_s,a_r)
    cb=col_copies(Z,w2_ref,wb_scr,b_s,b_r)
    cd=col_copies(Z,o3_scr,wd_scr,dd_s,dd_r)
    o3=rcopy(w2_ref,o3_scr,o3_s,o3_r,chipdev[3])
    wcp=[rcopy(wts_scr.at[0],wts_scr.at[m],wt_s.at[m],wt_r.at[m],chipdev[m]) for m in (1,2)]
    h1=nC//32*16; half=[pl.ds(0,h1),pl.ds(h1,nC-h1)]
    hcp=[rcopy(wts_scr.at[1,half[0]],wts_scr.at[3,half[0]],hf_s.at[0],hf_r.at[0],chipdev[2]),
         rcopy(wts_scr.at[2,half[1]],wts_scr.at[3,half[1]],hf_s.at[1],hf_r.at[1],chipdev[1])]
    save=[pltpu.make_async_copy(xo_scr,xo_ref,out_s.at[0]),pltpu.make_async_copy(ain_scr,ain_ref,out_s.at[1])]
    wsave=[pltpu.make_async_copy(wts_scr.at[m],wts_ref.at[m],out_s.at[2+m]) for m in range(4)]
    def qsave(m): return [pltpu.make_async_copy(qkv_scr.at[m],qkv_ref.at[m],qo_s.at[0,m]),pltpu.make_async_copy(ot_scr.at[:,m],ot_ref.at[:,m],qo_s.at[1,m])]
    w2cp=[rcopy(w2_scr.at[0],w2_scr.at[m],w2_s.at[m],w2_r.at[m],chipdev[m]) for m in (1,2)]
    grp=[[rcopy(w2_scr.at[m],w2o_ref.at[back[i],m],gr_s.at[i,m],gr_r.at[back[i],m],pdev[i]) for i in range(G-1)] for m in range(4)]
    loc=[pltpu.make_async_copy(w2_scr.at[m],w2o_ref.at[0,m],loc_s.at[m]) for m in range(4)]
    def share(m):
        loc[m].start()
        for cp in grp[m]: cp.start()
    sgc=rcopy(seg_ref,so_scr,sg_s,sg_r,(z,1-k,q,s))
    greet(Z,C)
    sgc.start()
    for cp in ca: cp.start()
    spread_near(toks,"start"); spread_far(toks,"start")
    o3.start()
    sgc.wait_recv()
    sg=jnp.where(k==lax.div(q,2),seg_ref[...],so_scr[...])
    sg=jnp.where(lax.rem(q,2)==0,sg[0:1],sg[1:2]).astype(f32)
    segq_ref[...]=sg
    for c in range(L//BQ):
        segk_ref[c*BQ:(c+1)*BQ,:]=jnp.broadcast_to(sg[:,c*BQ:(c+1)*BQ],(128,BQ)).T
    for i in range(2*Z): arrived(wa_scr.at[i],a_r.at[i])
    for cp in cb: cp.start()
    transpose_rows(wa_scr,wts_scr.at[0])
    for cp in wcp: cp.start()
    wsave[0].start()
    ains=[]
    for j in range(NB):
        arrived(xo_scr.at[j],tok_r.at[j])
        x=xo_scr[j].astype(f32)
        inv=lax.rsqrt(jnp.mean(x*x,axis=-1,keepdims=True)+norm_eps)
        slot=j*G+g0
        ain_scr[slot]=(x*inv*gain_ref[...]).astype(bf16)
        for i in range(G-1):
            cp=rcopy(ain_scr.at[slot],ain_scr.at[slot],ain_s.at[i,j],ain_r.at[slot],pdev[i])
            cp.start(); ains.append(cp)
    for j in range(NB):
        for i in range(G-1): arrived(ain_scr.at[j*G+pidx[i]],ain_r.at[j*G+pidx[i]])
    for cp in save: cp.start()
    rowi=lax.broadcasted_iota(jnp.int32,(BQ,BQ),0)
    coli=lax.broadcasted_iota(jnp.int32,(BQ,BQ),1)
    hs=[slice(h*HD,(h+1)*HD) for h in range(hb)]
    CH=512; per=CH//n; sub=BQ//n

    def block(m,_):
        @pl.when(m==1)
        def _():
            for i in range(2*Z): arrived(wb_scr.at[i],b_r.at[i])
            arrived(o3_scr,o3_r)
            for cp in cd: cp.start()
            transpose_rows(wb_scr,w2_scr.at[0])
            for i in (1,2): arrived(wts_scr.at[i],wt_r.at[i])
            for cp in hcp+wsave[1:3]: cp.start()
            share(0)
        @pl.when(m==2)
        def _():
            for cp in w2cp: cp.start()
        @pl.when(m==3)
        def _():
            for i in range(2): arrived(wts_scr.at[3,half[i]],hf_r.at[i])
            wsave[3].start()
            spread_near(cots,"start")
        for c in range(L//CH):
            cs=slice(c*CH,(c+1)*CH)
            r=dot(wts_scr[m],ain_scr[c*per:(c+1)*per].reshape(CH,D),NT)
            qkv_scr[m,:W,cs]=(r[:W]*pd_ref[:,:1]).astype(bf16)
            qkv_scr[m,W:,cs]=r[W:].astype(bf16)
            for h in range(hb):
                k_scr[h,cs,:]=r[W+h*HD:W+(h+1)*HD].T.astype(bf16)
        units=[(i,h) for i in range(nb) for h in range(hb)]
        st={}
        def phase_a(u):
            i,h=units[u]; c0=i*BQ
            qi=qkv_scr[m,hs[h],c0:c0+BQ]
            sq=segq_ref[:,c0:c0+BQ]
            m8=None
            for j in range(i+1):
                t=dot(k_scr[h,j*BQ:(j+1)*BQ,:],qi)
                sk=segk_ref[j*BQ:(j+1)*BQ,:]
                ok=jnp.concatenate([sk]*(BQ//128),axis=1)==sq
                if j==i: ok=ok&(rowi<=coli)
                t=jnp.where(ok,t,NEG)
                s_scr[u%2,j*BQ:(j+1)*BQ,:]=t
                mm=t.reshape(BQ//8,8,BQ).max(0)
                m8=mm if m8 is None else jnp.maximum(m8,mm)
                yield
            st[u]=m8.max(0,keepdims=True)
        def phase_b(u):
            i,h=units[u]; c0=i*BQ
            mx=st[u]; l8=None; acc=None
            for j in range(i+1):
                p=jnp.exp(s_scr[u%2,j*BQ:(j+1)*BQ,:]-mx)
                ll=p.reshape(BQ//8,8,BQ).sum(0)
                l8=ll if l8 is None else l8+ll
                pv=dot(qkv_scr[m,2*W+h*HD:2*W+(h+1)*HD,j*BQ:(j+1)*BQ],p.astype(bf16))
                acc=pv if acc is None else acc+pv
                yield
            l=l8.sum(0,keepdims=True)
            o=(acc*(1.0/l)).astype(bf16)
            for t in range(sub): ot_scr[i*sub+t,m,hs[h],:]=o[:,t*n:(t+1)*n]
            lse_ref[m*hb+h,:,c0:c0+BQ]=mx+jnp.log(l)
        merge(phase_a(0))
        for u in range(len(units)):
            gs=[phase_b(u)]
            if u+1<len(units): gs=[phase_a(u+1)]+gs
            merge(*gs)
        for b in range(NB):
            pltpu.make_async_copy(ot_scr.at[b*G+g0,m],mix_ref.at[b,0,m],mixl.at[b,m]).start()
            for i in range(G-1):
                rcopy(ot_scr.at[b*G+pidx[i],m],mix_ref.at[b,back[i],m],mix_s.at[i,b,m],mix_r.at[back[i],b,m],pdev[i]).start()
        for cp in qsave(m): cp.start()
        return 0
    lax.fori_loop(0,4,block,0)
    for m in (1,2):
        arrived(w2_scr.at[m],w2_r.at[m])
        share(m)
    for i in range(2*Z): arrived(wd_scr.at[i],dd_r.at[i])
    transpose_rows(wd_scr,w2_scr.at[3])
    share(3)
    for i in range(G-1):
        for b in range(NB):
            for m in range(4):
                arrived(mix_ref.at[b,fore[i],m],mix_r.at[fore[i],b,m])
                rcopy(ot_scr.at[b*G+pidx[i],m],mix_ref.at[b,back[i],m],mix_s.at[i,b,m],mix_r.at[back[i],b,m],pdev[i]).wait_send()
        for m in range(4): arrived(w2o_ref.at[fore[i],m],gr_r.at[fore[i],m])
    for m in range(4):
        loc[m].wait()
        for cp in grp[m]: cp.wait_send()
    for cps in (ca,cb,cd):
        for cp in cps[1:]: cp.wait_send()
    for cp in wcp+hcp+w2cp+ains+[o3,sgc]: cp.wait_send()
    spread_near(toks,"sent"); spread_far(toks,"sent"); spread_near(cots,"sent")
    for b in near_blocks(C): arrived(coto_ref.at[b],cot_r.at[b])
    for cp in save+wsave: cp.wait()
    for m in range(4):
        for cp in qsave(m): cp.wait()
        for b in range(NB): pltpu.make_async_copy(ot_scr.at[b*G+g0,m],mix_ref.at[b,0,m],mixl.at[b,m]).wait()

def forward(Z, C, tokens, w1h, w2h, cot, gain, pd, seg):
    R,Pn,D=tokens.shape; G=2*C; n=Pn//G; _,Dd,nC=w1h.shape; NB=4*C
    L=seg.shape[1]; W=pd.shape[0]; hb=W//HD
    V=pl.BlockSpec(memory_space=pltpu.VMEM); A=pl.BlockSpec(memory_space=pl.ANY)
    S=lambda *sh: pltpu.SemaphoreType.DMA(sh) if sh else pltpu.SemaphoreType.DMA
    B=lambda *sh: jax.ShapeDtypeStruct(sh,bf16)
    F=lambda *sh: jax.ShapeDtypeStruct(sh,f32)
    M=lambda *sh: pltpu.VMEM(sh,bf16)
    col=M(2*Z,Dd,nC)
    return pl.pallas_call(functools.partial(fwd_kernel,Z,C,n),
        out_shape=(B(NB,n,D),B(NB*G,n,D),B(4,nC,D),B(G,4,nC,D),B(NB,G,4,W,n),B(4,nC,L),B(NB*G,4,W,n),F(4*hb,1,L),F(L,128),F(1,L),B(NB,n,D)),
        in_specs=[A,A,A,A,V,V,V],out_specs=(A,A,A,A,A,A,A,V,V,V,A),
        scratch_shapes=[M(NB,n,D),M(NB*G,n,D),M(4,nC,D),M(4,nC,L),M(NB*G,4,W,n),col,col,col,M(2,Dd,nC),M(4,nC,D),M(hb,L,HD),
            pltpu.VMEM((2,L,BQ),f32),pltpu.VMEM((R,L),jnp.int32),
            S(NB),S(NB),S(G-1,NB),S(NB*G),S(2*Z),S(2*Z),S(2*Z),S(2*Z),S(2*Z),S(2*Z),S(),S(),
            S(4),S(4),S(2),S(2),S(4),S(4),S(G-1,4),S(G,4),S(4),S(G-1,NB,4),S(G,NB,4),S(NB,4),S(),S(),S(6),S(2,4),S(NB),S(NB)],
        compiler_params=pltpu.CompilerParams(collective_id=0,has_side_effects=True,vmem_limit_bytes=60*2**20),
        cost_estimate=pl.CostEstimate(flops=3*10**10,bytes_accessed=10**8,transcendentals=0),
        name="forward")(tokens,w1h,w2h,cot,gain,pd,seg)

def prep_kernel(Ch, wq_ref, wk_ref, wv_ref, wo_ref, wu_ref, wd_ref, qs_ref, ga_ref, gm_ref, w1_ref, w2_ref, pd_ref, gar_ref, gmr_ref):
    gar_ref[0,:]=ga_ref[...]
    gmr_ref[0,:]=gm_ref[...]
    for ref,three in ((w1_ref,(wq_ref[...],wk_ref[...],wv_ref[...])),(w2_ref,(wo_ref[...],wu_ref[...],wd_ref[...]))):
        for i,w in enumerate(three):
            for h in range(2): ref[h,:,i*Ch:(i+1)*Ch]=w[:,h*Ch:(h+1)*Ch]
    v=qs_ref[...]
    per_dim=scale_base/math.sqrt(HD)*(jnp.maximum(v,0.0)+jnp.log(1.0+jnp.exp(-jnp.abs(v))))
    col=jnp.broadcast_to(per_dim,(128,HD)).T
    for h in range(pd_ref.shape[0]//HD): pd_ref[h*HD:(h+1)*HD,:]=col

def prep(wq, wk, wv, wo, wu, wd, qs, ga, gm):
    Dd,Ct=wq.shape; Ch=Ct//2
    B=jax.ShapeDtypeStruct((2,Dd,3*Ch),bf16)
    return pl.pallas_call(functools.partial(prep_kernel,Ch),out_shape=(B,B,jax.ShapeDtypeStruct((Ch,128),f32))+(jax.ShapeDtypeStruct((1,ga.shape[0]),f32),)*2,
        compiler_params=pltpu.CompilerParams(vmem_limit_bytes=60*2**20),name="prep")(wq,wk,wv,wo.T,wu,wd.T,qs.reshape(1,-1),ga,gm)


def mid_kernel(Z, C, n, mixh_ref, w2_ref, xoh_ref, cot_ref, coto_ref, gain_ref,
               bo_ref, bh_ref, do_ref, gm_ref, fb_ref, vec_ref,
               wo_scr, wu_scr, wd_scr, mi_scr, hid_scr, gup_scr, ga_scr, gt_scr, gs_scr, gr_scr, co_scr, up_scr, mid_scr, mix_ref, xo_ref,
               wl, dos, dors, dol, gss, grs, cot_s, cot_r, out_s, fo_s, bos, bors, inl):
    z,k,q,s=[lax.axis_index(a) for a in AXES]
    G=2*C; g0=k*C+s; NB=4*C
    D=gain_ref.shape[1]; K4=wo_scr.shape[0]//G; Ch=K4//4; N=NB*n
    peers=list(itertools.product(range(2),range(C)))[1:]
    pdev=[(z,lax.rem(k+gc,2),q,lax.rem(s+gs,C)) for gc,gs in peers]
    pidx=[lax.rem(k+gc,2)*C+lax.rem(s+gs,C) for gc,gs in peers]
    back=[gc*C+(C-gs)%C for gc,gs in peers]
    fore=[gc*C+gs for gc,gs in peers]
    wcp=[]
    for i,dst in enumerate((wo_scr,wu_scr,wd_scr)):
        wcp.append([pltpu.make_async_copy(w2_ref.at[g,m,pl.ds(i*Ch,Ch),:],dst.at[pl.ds((g*4+m)*Ch,Ch),:],wl.at[i,g,m]) for g in range(G) for m in range(4)])
        for cp in wcp[i]: cp.start()
        if i==0:
            ins=[pltpu.make_async_copy(mixh_ref,mix_ref,inl.at[0]),pltpu.make_async_copy(xoh_ref,xo_ref,inl.at[1])]
            for cp in ins: cp.start()
    cots=spread_copies(C,n,cot_ref,co_scr,cot_s,cot_r)
    greet(Z,C)
    spread_far(cots,"start")
    for b in near_blocks(C): pltpu.make_async_copy(coto_ref.at[b],co_scr.at[b],cot_r.at[b]).start()
    order=[partner(q,m)*C+(lax.rem(s+t,C)) for m in range(4) for t in range(C)]
    outs=[]
    def put(src,dst,sem):
        cp=pltpu.make_async_copy(src,dst,sem); cp.start(); outs.append(cp)
    vec_ref[...]=jnp.zeros_like(vec_ref)
    for cp in wcp[0]+ins: cp.wait()
    def slot(e): return slice(e*n,(e+1)*n)
    def ahead(e):
        b=order[e]
        attn=dot(mix_ref[b].reshape(G*K4,n),wo_scr[...],TN)
        middle=xo_ref[b].astype(f32)+attn
        mid_scr[e]=middle
        inv=lax.rsqrt(jnp.mean(middle*middle,axis=-1,keepdims=True)+norm_eps)
        mi_scr[slot(e),:]=(middle*inv*gain_ref[...]).astype(bf16)
        yield
        if e==0:
            for cp in wcp[1]+wcp[2]: cp.wait()
        up=dot(mi_scr[slot(e),:],wu_scr[...],NT)
        up_scr[e]=up
        hid_scr[slot(e),:]=(up*(1.0/(1.0+jnp.exp(-up)))).astype(bf16)
        yield
        gs_scr[slot(e),:]=(mid_scr[e]+dot(hid_scr[slot(e),:],wd_scr[...])).astype(bf16)
        yield
    for e in range(0,NB,2):
        merge(ahead(e),ahead(e+1))
        for i in (e,e+1): put(gs_scr.at[slot(i)],bo_ref.at[order[i]],out_s.at[0,i])
    exch=[]
    home=[]
    boouts=list(outs); outs=[]
    def behind(e):
        b=order[e]
        gh=dot(co_scr[b],wd_scr[...],NT)
        up=up_scr[e]
        sg=1.0/(1.0+jnp.exp(-up))
        gup_scr[slot(e),:]=(gh*(sg*(1.0+up*(1.0-sg)))).astype(bf16)
        yield
        gmlp=dot(gup_scr[slot(e),:],wu_scr[...])
        middle=mid_scr[e]
        inv=lax.rsqrt(jnp.mean(middle*middle,axis=-1,keepdims=True)+norm_eps)
        n2=middle*inv
        dn=gmlp*gain_ref[...]
        gm=co_scr[b].astype(f32)+inv*(dn-n2*jnp.mean(dn*n2,axis=-1,keepdims=True))
        vec_ref[...]+=(gmlp*n2).reshape(n//8,8,D).sum(0)
        mid_scr[e]=gm
        ga_scr[slot(e),:]=gm.astype(bf16)
        yield
        gt_scr[e]=dot(wo_scr[...],ga_scr[slot(e),:],NT).astype(bf16).reshape(G,4,Ch,n)
        yield
    for e0 in range(0,NB,2):
        for e in (e0,e0+1):
            b=order[e]
            if e<3*C: pltpu.make_async_copy(coto_ref.at[b],co_scr.at[b],cot_r.at[b]).wait()
            else: arrived(co_scr.at[b],cot_r.at[b])
            boouts[e].wait()
            dst=bh_ref.at[lax.rem(q,2),pl.ds(pl.multiple_of((k*C+s)*n,n),n),:]
            rs=bors.at[(lax.rem(q,2)*2+k)*C+s]
            mine=is_home()&(b==q*C+s)
            home.append((mine,pltpu.make_async_copy(bo_ref.at[b],dst,rs),rcopy(bo_ref.at[b],dst,bos.at[e],rs,(z,lax.div(q,2),lax.div(b,C),lax.rem(b,C)))))
            spread_start(home[-1:])
        merge(behind(e0),behind(e0+1))
        for e in (e0,e0+1):
            b=order[e]
            put(mid_scr.at[e],gm_ref.at[b],out_s.at[1,e])
            lc=pltpu.make_async_copy(gt_scr.at[e,0],do_ref.at[b*G+g0],dol.at[e])
            lc.start(); exch.append(lc)
            for i in range(G-1):
                cp=rcopy(gt_scr.at[e,fore[i]],do_ref.at[b*G+g0],dos.at[i,e],dors.at[b*G+g0],pdev[i])
                cp.start(); exch.append(cp)
    def wgrad(i,g):
        cs=slice(g*K4,(g+1)*K4)
        if i==0: return dot(jnp.concatenate([mix_ref[b,g].reshape(K4,n) for b in order],1),ga_scr[...])
        if i==1: return dot(gup_scr[:,cs],mi_scr[...],TN)
        return dot(hid_scr[:,cs],jnp.concatenate([co_scr[b] for b in order],0),TN)
    for cp in outs: cp.wait()
    outs=[]
    def part(j,i): return pl.ds((j*3+i)*K4,K4)
    gcp=[[None]*3 for j in range(G-1)]
    for j in range(G-1):
        for i in range(3):
            gs_scr[part(j,i),:]=wgrad(i,fore[j]).astype(bf16)
            gcp[j][i]=rcopy(gs_scr.at[part(j,i)],gr_scr.at[back[j]-1,i],gss.at[j,i],grs.at[back[j]-1,i],pdev[j])
            gcp[j][i].start()
    for i in range(3):
        t=wgrad(i,0)
        for j in range(G-1):
            arrived(gr_scr.at[fore[j]-1,i],grs.at[fore[j]-1,i])
            t=t+gr_scr[fore[j]-1,i].astype(f32)
        gcp[0][i].wait_send()
        gs_scr[part(0,i),:]=t.astype(bf16)
        for m in range(4):
            put(gs_scr.at[pl.ds(i*K4+m*Ch,Ch)],fb_ref.at[m,pl.ds(i*Ch,Ch)],fo_s.at[i,m])
    for b in range(NB):
        for i in range(G-1): arrived(do_ref.at[b*G+pidx[i]],dors.at[b*G+pidx[i]])
    for i,cp in enumerate(exch):
        if i%G==0: cp.wait()
        else: cp.wait_send()
    for cps in gcp[1:]:
        for cp in cps: cp.wait_send()
    spread_far(cots,"sent")
    home_arrived(C,n,bh_ref,bors)
    spread_sent(home)
    for cp in outs: cp.wait()

def middle(Z, C, mix, w2o, xo, cot, coto, gain):
    NB,n,D=xo.shape; G=2*C; nC=w2o.shape[2]; Ch=nC//3; K4=4*Ch; N=NB*n
    V=pl.BlockSpec(memory_space=pltpu.VMEM); A=pl.BlockSpec(memory_space=pl.ANY)
    S=lambda *sh: pltpu.SemaphoreType.DMA(sh)
    M=lambda *sh: pltpu.VMEM(sh,bf16)
    B=lambda *sh: jax.ShapeDtypeStruct(sh,bf16)
    return pl.pallas_call(functools.partial(mid_kernel,Z,C,n),
        out_shape=(B(NB,n,D),B(*cot.shape),B(NB*G,4,Ch,n),jax.ShapeDtypeStruct((NB,n,D),f32),B(4,nC,D),jax.ShapeDtypeStruct((8,D),f32)),
        in_specs=[A,A,A,A,A,V],out_specs=(A,A,A,A,A,V),
        scratch_shapes=[M(G*K4,D)]*3+[M(N,G*K4) if i in (1,2) else M(N,D) for i in range(4)]+[M(NB,G,4,Ch,n),M((G-1)*3*K4,D),M(G-1,3,K4,D),M(NB,n,D),pltpu.VMEM((NB,n,G*K4),f32),pltpu.VMEM((NB,n,D),f32),M(NB,G,4,Ch,n),M(NB,n,D),
            S(3,G,4),S(G-1,NB),S(NB*G),S(NB),S(G-1,3),S(G-1,3),S(NB),S(NB),S(2,NB),S(3,4),S(NB),S(4*C),S(2)],
        compiler_params=pltpu.CompilerParams(collective_id=2,has_side_effects=True,vmem_limit_bytes=60*2**20),
        cost_estimate=pl.CostEstimate(flops=3*10**10,bytes_accessed=10**8,transcendentals=0),
        name="middle")(mix,w2o,xo,cot,coto,gain)

def bwd_kernel(Z, C, n, qkv_ref, ot_ref, do_ref, lse_ref, pd_ref, segk_ref, segq_ref, ain_ref, wts_ref,
               xo_ref, gmid_ref, gain_ref, vec_ref, fb_ref,
               gi_ref, gwm_ref, gwq_ref, vo_ref,
               kv_scr, k_scr, v_scr, p_scr, ds_scr, dq_scr, dl_scr, a_scr, dw_scr, qr_scr, big_scr, zs_scr, zr_scr, t3_scr, t3r_scr, tb_scr, ot_scr, do_scr,
               dxr_scr, wx_scr, own_scr, xb_scr, gb_scr, va_scr, vb_scr, vs_scr, sc_scr,
               fs, frs, qs, qrs, zss, zrs, t3s, t3rs, cs_, crs, dxs, dxrs, gis, girs, ld, al, otl, dol, kvl, wtl, xl, vas, vars_, vbs, vbrs):
    z,k,q,s=[lax.axis_index(a) for a in AXES]
    G=2*C; g0=k*C+s; NB=4*C
    D=gain_ref.shape[1]; L=segq_ref.shape[1]; W=pd_ref.shape[0]; hb=W//HD; nb=L//BQ; sub=BQ//n
    nC=3*W; Dd=gwm_ref.shape[1]
    peers=list(itertools.product(range(2),range(C)))[1:]
    pdev=[(z,lax.rem(k+gc,2),q,lax.rem(s+gs,C)) for gc,gs in peers]
    pidx=[lax.rem(k+gc,2)*C+lax.rem(s+gs,C) for gc,gs in peers]
    back=[gc*C+(C-gs)%C for gc,gs in peers]
    fore=[gc*C+gs for gc,gs in peers]
    chipdev=[(z,k,partner(q,m),s) for m in range(4)]
    core=(z,1-k,q,s)
    zdev=[lax.rem(z+j,Z) for j in range(Z)]
    def frow(m): return big_scr.at[pl.ds((m-1)*nC,nC)]
    def dxat(i,e): return big_scr.at[pl.ds((i*NB+e)*n,n)]
    fcp={m: rcopy(fb_ref.at[m],frow(m),fs.at[m],frs.at[m],chipdev[m]) for m in (1,2)}
    qcp={m: rcopy(dw_scr.at[m-1],qr_scr.at[m-1],qs.at[m],qrs.at[m],chipdev[m]) for m in (1,2)}
    slot_of=(0,1,0,0)
    zcp=[[rcopy(zs_scr.at[slot_of[e],zdev[j]],zr_scr.at[e%3,z],zss.at[e,j],zrs.at[e,z],(zdev[j],k,q,s)) for j in range(1,Z)] for e in range(4)]
    t3cp=[rcopy(tb_scr,t3r_scr.at[e],t3s.at[e],t3rs.at[e],chipdev[3]) for e in range(2)]
    gws=(gwm_ref,gwq_ref)
    ccp=[rcopy(t3_scr.at[pl.ds(pl.multiple_of((1-k)*Dd,Dd),Dd),:],gws[e].at[k],cs_.at[e],crs.at[e],core) for e in range(2)]
    def wcopy(m): return pltpu.make_async_copy(wts_ref.at[m],(dw_scr.at[m] if m<2 else wx_scr.at[m-2]),wtl.at[m])
    def load(src,dst,i):
        cp=pltpu.make_async_copy(src,dst,ld.at[i]); cp.start(); return cp
    def zsend(e, value):
        rows=D//Z; per=max(1,640//rows)
        for i in range(Z//per):
            ls=slice(i*per*rows,(i+1)*per*rows)
            zs_scr[slot_of[e],i*per:(i+1)*per]=value(ls).T.reshape(per,rows,nC).astype(bf16)
        for cp in zcp[e]: cp.start()
    def zsum(e):
        for cp in zcp[e]: cp.wait_send()
        t=zs_scr[slot_of[e],z].astype(f32)
        for j in range(1,Z):
            arrived(zr_scr.at[e%3,zdev[j]],zrs.at[e,zdev[j]])
            t=t+zr_scr[e%3,zdev[j]].astype(f32)
        return t
    def diag(e):
        tb_scr[...]=zsum(e).astype(bf16)
        t3cp[e].start()
    def final(e):
        t=zsum(2+e)
        arrived(t3r_scr.at[e],t3rs.at[e])
        t=t+t3r_scr[e].astype(f32)
        t3cp[e].wait_send()
        if e==1: ccp[0].wait_send()
        t3_scr[...]=t
        ccp[e].start()
        gws[e][k]=t3_scr[pl.ds(pl.multiple_of(k*Dd,Dd),Dd),:]
    first=load(fb_ref.at[3],dw_scr.at[0],0)
    kvcp=[pltpu.make_async_copy(qkv_ref.at[m],kv_scr.at[m],kvl.at[m]) for m in range(4)]
    kvcp[1].start()
    acp=pltpu.make_async_copy(ain_ref,a_scr,al)
    def otcp(m): return pltpu.make_async_copy(ot_ref.at[:,m],ot_scr,otl)
    otcp(1).start()
    def docp(idx): return pltpu.make_async_copy(do_ref.at[:,lax.rem(idx+1,4)],do_scr.at[lax.rem(idx,2)],dol.at[lax.rem(idx,2)])
    docp(0).start()
    greet(Z,C)
    for m in (1,2): fcp[m].start()
    first.wait()
    zsend(0,lambda ls: dw_scr[0,:,ls].astype(f32))
    ld0=load(fb_ref.at[0],dw_scr.at[1],1)
    acp.start()
    for m in (2,3,0): kvcp[m].start()
    sc_scr[...]=jnp.zeros_like(sc_scr)
    rowi=lax.broadcasted_iota(jnp.int32,(BQ,BQ),0)
    coli=lax.broadcasted_iota(jnp.int32,(BQ,BQ),1)
    hs=[slice(h*HD,(h+1)*HD) for h in range(hb)]

    def block(idx,_):
        m=lax.rem(idx+1,4)
        pltpu.make_async_copy(qkv_ref.at[m],kv_scr.at[m],kvl.at[m]).wait()
        for h in range(hb):
            k_scr[h]=kv_scr[m,W+h*HD:W+(h+1)*HD,:].T
            v_scr[h]=kv_scr[m,2*W+h*HD:2*W+(h+1)*HD,:].T
        slot=lax.rem(idx,2)
        docp(idx).wait()
        @pl.when(idx<3)
        def _(): docp(idx+1).start()
        def tile(h,i):
            return jnp.concatenate([do_scr[slot,i*sub+t,hs[h],:] for t in range(sub)],1) if sub>1 else do_scr[slot,i,hs[h],:]
        otcp(m).wait()
        for i in range(nb):
            for h in range(hb):
                for t in range(sub):
                    B_=i*sub+t
                    dl_scr[h,:,B_*n:(B_+1)*n]=(do_scr[slot,B_,hs[h],:].astype(f32)*ot_scr[B_,hs[h],:].astype(f32)).sum(0,keepdims=True)
        @pl.when(idx<3)
        def _(): otcp(lax.rem(idx+2,4)).start()
        rows=[(j,h) for j in range(nb) for h in range(hb)]
        def phase_a(r):
            j,h=rows[r]; ks=slice(j*BQ,(j+1)*BQ)
            for i in range(j,nb):
                cs=slice(i*BQ,(i+1)*BQ)
                t=dot(k_scr[h,ks,:],kv_scr[m,hs[h],cs])
                dp=dot(v_scr[h,ks,:],tile(h,i))
                sk=segk_ref[ks,:]
                ok=jnp.concatenate([sk]*(BQ//128),axis=1)==segq_ref[:,cs]
                if j==i: ok=ok&(rowi<=coli)
                p=jnp.exp(jnp.where(ok,t-lse_ref[m*hb+h,:,cs],NEG))
                p_scr[r%2,:,cs]=p.astype(bf16)
                ds_scr[r%2,:,cs]=(p*(dp-dl_scr[h,:,cs])).astype(bf16)
                yield
        def phase_b(r):
            j,h=rows[r]; js=slice(j*BQ,(j+1)*BQ); rs=slice(j*BQ,L)
            dos=jnp.concatenate([tile(h,i) for i in range(j,nb)],1)
            dv=dot(dos,p_scr[r%2,:,rs],NT)
            yield
            dk=dot(kv_scr[m,hs[h],rs],ds_scr[r%2,:,rs],NT)
            yield
            for i in range(j,nb):
                cs=slice(i*BQ,(i+1)*BQ)
                dq=dot(kv_scr[m,W+h*HD:W+(h+1)*HD,js],ds_scr[r%2,:,cs])
                if j==0: dq_scr[hs[h],cs]=dq
                else: dq_scr[hs[h],cs]+=dq
                yield
            kv_scr[m,W+h*HD:W+(h+1)*HD,js]=dk.astype(bf16)
            kv_scr[m,2*W+h*HD:2*W+(h+1)*HD,js]=dv.astype(bf16)
        def attend(part):
            merge(phase_a(part[0]))
            for u in part:
                gs=[phase_b(u)]
                if u+1<=part[-1]: gs=[phase_a(u+1)]+gs
                merge(*gs)
        attend(range(2*hb))
        @pl.when(idx==1)
        def _():
            diag(0)
            for m2 in (1,2): arrived(frow(m2),frs.at[m2])
            ld0.wait()
            zsend(2,lambda ls: dw_scr[1,:,ls].astype(f32)+big_scr[0:nC,ls].astype(f32)+big_scr[nC:2*nC,ls].astype(f32))
        @pl.when(idx==3)
        def _():
            final(0)
            for m2 in (1,2): qcp[m2].wait_send()
            for m2 in range(4): wcopy(m2).start()
        attend(range(2*hb,len(rows)))
        dq=dq_scr[...]
        sc_scr[...]+=(dq*kv_scr[m,:W,:].astype(f32)).sum(1,keepdims=True)/pd_ref[:,:1]
        kv_scr[m,:W,:]=(dq*pd_ref[:,:1]).astype(bf16)
        @pl.when(idx==0)
        def _(): acp.wait()
        @pl.when(idx<2)
        def _():
            for c in range(D//256):
                ls=slice(c*256,(c+1)*256)
                dw_scr[m-1,:,ls]=dwt(m,ls).astype(bf16)
        @pl.when(idx==0)
        def _():
            qcp[1].start()
        @pl.when(idx==1)
        def _(): qcp[2].start()
        @pl.when(idx==2)
        def _(): zsend(1,lambda ls: dwt(3,ls))
        return 0
    def dwt(m,ls):
        return dot(kv_scr[m],a_scr[:,ls])
    lax.fori_loop(0,4,block,0)
    for m in range(4): wcopy(m).wait()

    def chunk(i):
        gl=kv_scr[:,:,pl.ds(pl.multiple_of(i*BQ,BQ),BQ)].reshape(4*nC,BQ)
        return dot(gl,jnp.concatenate([dw_scr[...].reshape(2*nC,D),wx_scr[...].reshape(2*nC,D)],0),TN)
    order=[partner(q,m)*C+t for m in (3,1,2,0) for t in range(C)]
    def xload(e):
        b=order[e]
        return [pltpu.make_async_copy(xo_ref.at[b],xb_scr.at[0],xl.at[0,0]),pltpu.make_async_copy(gmid_ref.at[b],gb_scr.at[0],xl.at[1,0])]
    dxcp=[[rcopy(dxat(i,e),dxr_scr.at[back[i]-1,e],dxs.at[i,e],dxrs.at[back[i],e],pdev[i]) for e in range(NB)] for i in range(G-1)]
    def give(e):
        b=order[e]
        if sub>1: own_scr[...]=chunk(b)
        for i in range(G-1):
            if sub==1: big_scr[(i*NB+e)*n:(i*NB+e+1)*n,:]=chunk(b*G+pidx[i]).astype(bf16)
            else: big_scr[(i*NB+e)*n:(i*NB+e+1)*n,:]=own_scr[pl.ds(pl.multiple_of(pidx[i]*n,n),n),:].astype(bf16)
            dxcp[i][e].start()
    gicp=[]
    gparts=[]
    def take(e):
        b=order[e]
        for cp in xload(e): cp.start()
        if sub==1:
            gain=chunk(b*G+g0)
        else:
            own_scr[...]=chunk(b)
            gain=own_scr[pl.ds(pl.multiple_of(g0*n,n),n),:]
        for i in range(G-1):
            arrived(dxr_scr.at[fore[i]-1,e],dxrs.at[fore[i],e])
            gain=gain+dxr_scr[fore[i]-1,e].astype(f32)
        for cp in xload(e): cp.wait()
        x=xb_scr[0].astype(f32)
        inv=lax.rsqrt(jnp.mean(x*x,axis=-1,keepdims=True)+norm_eps)
        nx=x*inv
        dn=gain*gain_ref[...]
        gin=gb_scr[0]+inv*(dn-nx*jnp.mean(dn*nx,axis=-1,keepdims=True))
        gparts.append((gain*nx).reshape(n//8,8,D).sum(0))
        dxcp[0][e].wait_send()
        big_scr[e*n:(e+1)*n,:]=gin.astype(bf16)
        dst=gi_ref.at[lax.rem(q,2),pl.ds(pl.multiple_of((k*C+s)*n,n),n),:]
        rs=girs.at[(lax.rem(q,2)*2+k)*C+s]
        gicp.append((is_home()&(b==q*C+s),pltpu.make_async_copy(dxat(0,e),dst,rs),
                     rcopy(dxat(0,e),dst,gis.at[e],rs,(z,lax.div(q,2),lax.div(b,C),lax.rem(b,C)))))
        spread_start(gicp[-1:])
    give(0)
    for e in range(NB):
        if e+1<NB: give(e+1)
        take(e)
        if e==0:
            for m2 in (1,2): arrived(qr_scr.at[m2-1],qrs.at[m2])
            zsend(3,lambda ls: dwt(0,ls)+qr_scr[0,:,ls].astype(f32)+qr_scr[1,:,ls].astype(f32))
            diag(1)
    gpart=gparts[0]
    for t in gparts[1:]: gpart=gpart+t
    vs_scr[...]=jnp.zeros_like(vs_scr)
    vs_scr[0:1,:]=gpart.sum(0,keepdims=True)
    vs_scr[1:2,:]=vec_ref[...].sum(0,keepdims=True)
    sc=sc_scr[0:HD,:]
    for h in range(1,hb): sc=sc+sc_scr[h*HD:(h+1)*HD,:]
    vs_scr[2:3,0:HD]=sc.T[0:1,:]
    me=(k*4+q)*C+s
    va_scr[me]=vs_scr[...]
    plane=list(itertools.product(range(2),range(4),range(C)))[1:]
    vacp=[rcopy(vs_scr,va_scr.at[me],vas.at[i],vars_.at[me],(z,lax.rem(k+a,2),lax.rem(q+b,4),lax.rem(s+c,C))) for i,(a,b,c) in enumerate(plane)]
    for cp in vacp: cp.start()
    for a,b,c in plane:
        o=(lax.rem(k+a,2)*4+lax.rem(q+b,4))*C+lax.rem(s+c,C)
        arrived(va_scr.at[o],vars_.at[o])
    t=va_scr[0]
    for i in range(1,8*C): t=t+va_scr[i]
    vb_scr[z]=t
    vbcp=[rcopy(vb_scr.at[z],vb_scr.at[z],vbs.at[j],vbrs.at[z],(zdev[j],k,q,s)) for j in range(1,Z)]
    for cp in vbcp: cp.start()
    final(1)
    for j in range(1,Z): arrived(vb_scr.at[zdev[j]],vbrs.at[zdev[j]])
    t=vb_scr[0]
    for i in range(1,Z): t=t+vb_scr[i]
    vo_ref[...]=t
    for e in range(2):
        arrived(gws[e].at[1-k],crs.at[e])
        if e==1: ccp[e].wait_send()
    home_arrived(C,n,gi_ref,girs)
    spread_sent(gicp)
    for i in range(1,G-1):
        for e in range(NB): dxcp[i][e].wait_send()
    for m in (1,2):
        fcp[m].wait_send()
    for cp in vacp+vbcp: cp.wait_send()

def backward(Z, C, qkv, ot, do, lse, pd, segk, segq, ain, wts, xo, gmid, gain, vec, fb, R, Pn, Dd):
    NB,n,D=xo.shape; G=2*C; nC=wts.shape[1]; W=pd.shape[0]; hb=W//HD; L=segq.shape[1]
    V=pl.BlockSpec(memory_space=pltpu.VMEM); A=pl.BlockSpec(memory_space=pl.ANY)
    S=lambda *sh: pltpu.SemaphoreType.DMA(sh) if sh else pltpu.SemaphoreType.DMA
    M=lambda *sh: pltpu.VMEM(sh,bf16)
    F=lambda *sh: pltpu.VMEM(sh,f32)
    gw=jax.ShapeDtypeStruct((2,Dd,nC),f32)
    return pl.pallas_call(functools.partial(bwd_kernel,Z,C,n),
        out_shape=(jax.ShapeDtypeStruct((R,Pn,D),bf16),gw,gw,jax.ShapeDtypeStruct((8,D),f32)),
        in_specs=[A,A,A,V,V,V,V,A,A,A,A,V,V,A],out_specs=(A,V,V,V),
        scratch_shapes=[M(4,nC,L),M(hb,L,HD),M(hb,L,HD),M(2,BQ,L),M(2,BQ,L),F(W,L),F(hb,1,L),M(L,D),
            M(2,nC,D),M(2,nC,D),M(max(2*nC,(G-1)*NB*n),D),M(2,Z,D//Z,nC),M(3,Z,D//Z,nC),F(D//Z,nC),M(2,D//Z,nC),M(D//Z,nC),M(NB*G,W,n),M(2,NB*G,W,n),
            M(G-1,NB,n,D),M(2,nC,D),F(BQ,D) if n<BQ else F(8,128),M(1,n,D),F(1,n,D),F(8*C,8,D),F(Z,8,D),F(8,D),F(W,1),
            S(4),S(4),S(4),S(4),S(4,Z),S(4,Z),S(2),S(2),S(2),S(2),S(G,NB),S(G,NB),S(NB),S(4*C),S(4),S(),S(),S(2),S(4),S(4),S(2,2),S(8*C),S(8*C),S(Z),S(Z)],
        compiler_params=pltpu.CompilerParams(collective_id=1,has_side_effects=True,vmem_limit_bytes=61*2**20),
        cost_estimate=pl.CostEstimate(flops=6*10**10,bytes_accessed=10**8,transcendentals=0),
        name="backward")(qkv,ot,do,lse,pd,segk,segq,ain.reshape(L,D),wts,xo,gmid,gain,vec,fb)

def finish_kernel(Ch, gi_ref, gwm_ref, gwq_ref, vo_ref, sf_ref, ig_ref, gq_ref, gk_ref, gv_ref, go_ref, gu_ref, gd_ref, ga_ref, gs_ref, gm_ref):
    ig_ref[...]=gi_ref[...].astype(f32)
    @pl.when(pl.program_id(0)==0)
    def _():
        def cols(ref,i):
            return jnp.concatenate([ref[0,:,i*Ch:(i+1)*Ch],ref[1,:,i*Ch:(i+1)*Ch]],1)
        for i,o in enumerate((gq_ref,gk_ref,gv_ref)): o[...]=cols(gwq_ref,i)
        go_ref[...]=cols(gwm_ref,0)
        gu_ref[...]=cols(gwm_ref,1)
        gd_ref[...]=cols(gwm_ref,2)
        ga_ref[...]=vo_ref[0,:]
        gm_ref[...]=vo_ref[1,:]
        gs_ref[...]=vo_ref[2,0:HD]*sf_ref[0,:]

def finish(gi, gwm, gwq, vo, sf):
    R,Pn,D=gi.shape; _,Dd,nC=gwm.shape; Ch=nC//3; T=4
    F=lambda *sh: jax.ShapeDtypeStruct(sh,f32)
    full=lambda *sh: pl.BlockSpec(sh,lambda i: (0,)*len(sh))
    row=pl.BlockSpec((R,Pn//T,D),lambda i:(0,i,0))
    shapes=[(Dd,2*Ch)]*6+[(D,),(HD,),(D,)]
    return pl.pallas_call(functools.partial(finish_kernel,Ch),grid=(T,),
        out_shape=(F(R,Pn,D),)+tuple(F(*sh) for sh in shapes),
        in_specs=[row,full(2,Dd,nC),full(2,Dd,nC),full(8,D),full(1,HD)],
        out_specs=(row,)+tuple(full(*sh) for sh in shapes),
        compiler_params=pltpu.CompilerParams(vmem_limit_bytes=60*2**20),
        name="finish")(gi,gwm,gwq,vo,sf.reshape(1,HD))


def make_local(Z, C):
    def local(tokens, segments, attn_gain, w_query, w_key, w_value, w_out, query_scale, mlp_gain, w_up, w_down, cotangent):
        R,Pn,D=tokens.shape
        Dd=w_query.shape[0]

        w1h,w2h,pd,attn_gain,mlp_gain=prep(w_query,w_key,w_value,w_out,w_up,w_down,query_scale,attn_gain,mlp_gain)
        xo,ain,wts,w2o,mix,qkv,ot,lse,segk,segq,coto=forward(Z,C,tokens,w1h,w2h,cotangent,attn_gain,pd,segments)
        _,block_out,do,gmid,fb,vec=middle(Z,C,mix,w2o,xo,cotangent,coto,mlp_gain)
        gi,gwm,gwq,vo=backward(Z,C,qkv,ot,do,lse,pd,segk,segq,ain,wts,xo,gmid,attn_gain,vec,fb,R,Pn,Dd)
        sf=(scale_base/math.sqrt(HD))*jax.nn.sigmoid(query_scale)
        ig,gq,gk,gv,go,gu,gd,ga,gs,gm=finish(gi,gwm,gwq,vo,sf)
        return (block_out,ig,ga,gq,gk,gv,go.T,gs,gm,gu,gd.T)
    return local

def solution(mesh):
    dp,T=mesh.shape["dp"],mesh.shape["tensor"]
    Z,C=dp//2,T//4
    fine=Mesh(mesh.devices.reshape(Z,2,4,C),AXES)
    dpx=("zz","core"); tx=("q","s")
    in_specs=(P(dpx,tx,None),P(dpx,None),P(),P(dpx,tx),P(dpx,tx),P(dpx,tx),P(tx,dpx),P(),P(),P(dpx,tx),P(tx,dpx),P(dpx,tx,None))
    out_specs=(P(dpx,tx,None),P(dpx,tx,None),P(),P(dpx,tx),P(dpx,tx),P(dpx,tx),P(tx,dpx),P(),P(),P(dpx,tx),P(tx,dpx))
    return jax.shard_map(make_local(Z,C),mesh=fine,in_specs=in_specs,out_specs=out_specs,check_vma=False)
```
